32 devices in a mesh: seq: 4 (over y, x), fsdp: 4 (over z), grp: 2 (over core).
Axes of the slice: x: 2, y: 2, z: 4, core: 2. Of those that a mesh axis runs over, the one named last changes fastest.
Arguments:
- latents: bfloat16 [2, 8, 1024, 1024], P(None, ('fsdp', 'grp'), 'seq'), may hold values from -6 to 6
- conditioning: float32 [2, 8, 1024], P(None, ('fsdp', 'grp')), may hold values from -6 to 6
- cotangent: bfloat16 [2, 8, 1024, 1024], P(None, ('fsdp', 'grp'), 'seq'), may hold values from -6 to 6
- owner_list: int32 [18], replicated, may hold values from 0 to 1, as said below
- master: float32 [30, 1024, 1024], P('grp', ('seq', 'fsdp')), may hold values from -2 to 2
- moment_one: float32 [30, 1024, 1024], P('grp', ('seq', 'fsdp')), may hold values from -4000 to 4000
- moment_two: float32 [30, 1024, 1024], P('grp', ('seq', 'fsdp')), may hold values from 1 to 10000000
- biases: float32 [14, 1024], replicated, may hold values from -2 to 2
- bias_moment_one: float32 [14, 1024], replicated, may hold values from -4000 to 4000
- bias_moment_two: float32 [14, 1024], replicated, may hold values from 1 to 10000000
Outputs:
- output: bfloat16 [2, 8, 1024, 1024], P(None, ('fsdp', 'grp'), 'seq')
- input_grad: float32 [2, 8, 1024, 1024], P(None, ('fsdp', 'grp'), 'seq')
- cond_grad: float32 [2, 8, 1024], P(None, ('fsdp', 'grp'))
- new_master: float32 [30, 1024, 1024], P('grp', ('seq', 'fsdp'))
- new_moment_one: float32 [30, 1024, 1024], P('grp', ('seq', 'fsdp'))
- new_moment_two: float32 [30, 1024, 1024], P('grp', ('seq', 'fsdp'))
- new_copies: bfloat16 [30, 1024, 1024], P('grp', ('seq', 'fsdp'))
- new_biases: float32 [14, 1024], replicated
- new_bias_one: float32 [14, 1024], replicated
- new_bias_two: float32 [14, 1024], replicated
The draws below stay inside these ranges and needn't reach their ends.
Inputs may be any that keep to these rules, and one draw needn't show every extreme that they name: Block b's master copy and moments lie in slot 15 * owner_list[b] + (the number of earlier blocks with the same owner); no group is named more than 15 times, and one is named exactly 15 times.
All inputs are finite; a program needn't handle non-finite values.
Results may differ from the reference program's by a relative error of at most 0.028.
Values may be sent and summed in bfloat16 or wider, within the bound.
A program may use at most 448 MiB of HBM per device.

```python
import math
import jax
import jax.numpy as jnp
from jax import lax

D = 1024
HEADS = 16
HD = 64
L = 1024
MICRO = 2
STEP = 5
NBLK = 18
NBIAS = 14
LAT = 8
CAP = 15
N_GRP = 2


WEIGHT_FACTORS = [1.0, 1.0, 1.0, 4.0, 1.0, 1.0, 1.0, 1.0, 0.5, 0.5, 0.5, 0.5, 1.0, 1.0, 1.0, 1.0, 1.0, 1.0]


GRAD_FACTORS = [0.5, 0.5, 0.7, 0.18, 0.33, 0.33, 0.33, 0.33, 0.59, 0.59, 0.59, 0.59, 0.65, 0.65, 0.7, 0.3, 0.3, 0.6]


BIAS_FACTORS = [0.37, 0.5, 0.78, 0.24, 0.24, 0.24, 0.24, 0.65, 1.0, 1.0, 1.1, 0.5, 0.5, 0.9]


def owner_table(key):
    key_full = jax.random.fold_in(key, 101)
    key_other = jax.random.fold_in(key, 102)
    key_order = jax.random.fold_in(key, 103)
    full_group = jax.random.randint(key_full, (), 0, N_GRP, dtype=jnp.int32)
    others = jax.random.permutation(key_other, (N_GRP - 1) * CAP)[:NBLK - CAP].astype(jnp.int32)
    among = others // CAP
    groups = (among + jnp.where(among >= full_group, 1, 0)).astype(jnp.int32)
    listed = jnp.concatenate([jnp.full((CAP,), full_group, jnp.int32), groups])
    order = jax.random.permutation(key_order, NBLK).astype(jnp.int32)
    return listed[order].astype(jnp.int32)


def slot_factors(key, factors, empty_factor):
    owners = owner_table(key)
    position = jnp.arange(NBLK, dtype=jnp.int32)
    same = owners[:, None] == owners[None, :]
    before = position[None, :] < position[:, None]
    ranks = jnp.sum(jnp.where(same & before, 1, 0), axis=1).astype(jnp.int32)
    slots = owners * CAP + ranks
    picks = slots[None, :] == jnp.arange(N_GRP * CAP, dtype=jnp.int32)[:, None]
    table = jnp.asarray(factors, jnp.float32)
    filled = jnp.sum(jnp.where(picks, table[None, :], 0.0), axis=1)
    return jnp.where(jnp.any(picks, axis=1), filled, empty_factor)


def draw_owner_list(key, part):
    return owner_table(key)


def draw_master(key, part):
    scales = slot_factors(key, WEIGHT_FACTORS, 1.0) * D ** (-0.5)
    key = jax.random.fold_in(key, 3)
    entries = jax.random.truncated_normal(key, -3.5, 3.5, (N_GRP * CAP, D, D), jnp.float32)
    return entries * scales[:, None, None]


def draw_moment_one(key, part):
    scales = slot_factors(key, GRAD_FACTORS, 0.5) * math.sqrt(MICRO * LAT * L)
    key = jax.random.fold_in(key, 5)
    entries = jax.random.normal(key, (N_GRP * CAP, D, D), jnp.float32)
    return entries * scales[:, None, None]


def draw_moment_two(key, part):
    scales = slot_factors(key, GRAD_FACTORS, 0.5) * math.sqrt(MICRO * LAT * L)
    key = jax.random.fold_in(key, 7)
    ratio = jnp.exp(jax.random.uniform(key, (N_GRP * CAP, D, D), jnp.float32, 0.0, math.log(4.0)))
    return ratio * (scales * scales)[:, None, None]


def draw_bias_moment_one(key, part):
    key = jax.random.fold_in(key, 9)
    scales = jnp.asarray(BIAS_FACTORS, jnp.float32) * math.sqrt(MICRO * LAT * L)
    entries = jax.random.normal(key, (NBIAS, D), jnp.float32)
    return entries * scales[:, None]


def draw_bias_moment_two(key, part):
    key = jax.random.fold_in(key, 11)
    scales = jnp.asarray(BIAS_FACTORS, jnp.float32) * math.sqrt(MICRO * LAT * L)
    ratio = jnp.exp(jax.random.uniform(key, (NBIAS, D), jnp.float32, 0.0, math.log(4.0)))
    return ratio * (scales * scales)[:, None]


def level_of(stream_key, extent, pieces, least, high):
    def one(dim, shards_of):
        draws = jax.random.uniform(jax.random.fold_in(jax.random.fold_in(stream_key, 6), dim), (shards_of,), jnp.float32, least / len(pieces), high / len(pieces))
        return jnp.repeat(jnp.exp(draws), extent[dim] // shards_of).reshape((-1,) + (1,) * (len(extent) - dim - 1))

    gain = one(*pieces[0])
    for cut in pieces[1:]:
        gain = gain * one(*cut)
    return gain


def normal_values(rng, shape, deviation, limit, pieces=(), kind=jnp.bfloat16):
    loudness = level_of(rng, shape, pieces, -0.22, 0.18) if pieces else 1.0
    values = jax.random.normal(rng, shape, jnp.float32) * deviation * loudness
    return jnp.minimum(jnp.maximum(values, -limit), limit).astype(kind)


def setup_inputs(seed: int = 0) -> dict:
    keys = jax.random.split(jax.random.key(seed), 11)
    return {
        "latents": normal_values(keys[0], (MICRO, LAT, L, D), 1.0, 6.0, ((1, 8), (2, 4))),
        "conditioning": normal_values(keys[1], (MICRO, LAT, D), 1.0, 6.0, ((1, 8),), jnp.float32),
        "cotangent": normal_values(keys[2], (MICRO, LAT, L, D), 1.0, 6.0, ((1, 8), (2, 4))),
        "owner_list": draw_owner_list(jax.random.fold_in(keys[10], 71), 0),
        "master": draw_master(jax.random.fold_in(keys[10], 71), 0),
        "moment_one": draw_moment_one(jax.random.fold_in(keys[10], 71), 0),
        "moment_two": draw_moment_two(jax.random.fold_in(keys[10], 71), 0),
        "biases": normal_values(keys[7], (NBIAS, D), 0.3, 2.0, (), jnp.float32),
        "bias_moment_one": draw_bias_moment_one(jax.random.fold_in(keys[10], 71), 0),
        "bias_moment_two": draw_bias_moment_two(jax.random.fold_in(keys[10], 71), 0),
    }


EPS_NORM = 1e-06
BETA_ONE = 0.5
BETA_TWO = 0.5
RATE_WEIGHT = 0.03
RATE_BIAS = 0.1
DECAY = 0.1
ADAM_EPS = 1e-08

@jax.custom_vjp
def low(v):
    return lax.optimization_barrier(v.astype(jnp.bfloat16)).astype(jnp.float32)

@jax.custom_vjp
def low_back(v):
    return v

def low_keep(v):
    return (low(v), None)

def low_pass(kept, grad):
    return (grad,)

def back_keep(v):
    return (v, None)

def back_low(kept, grad):
    return (low(grad),)
low.defvjp(low_keep, low_pass)
low_back.defvjp(back_keep, back_low)

def round_both(values):
    return low_back(low(values))

def exact_dot(spec, left, right):
    return jnp.einsum(spec, left, right, precision=lax.Precision.HIGHEST)

def modulate(values, scale, shift):
    centre = lax.optimization_barrier(jnp.mean(values, axis=-1, keepdims=True))
    centred = values - centre
    spread = lax.optimization_barrier(jnp.mean(centred * centred, axis=-1, keepdims=True))
    return centred * lax.rsqrt(spread + EPS_NORM) * (1.0 + scale) + shift

def slot_numbers(owner_list, capacity):
    blocks = owner_list.shape[0]
    position = jnp.arange(blocks, dtype=jnp.int32)
    same = owner_list[:, None] == owner_list[None, :]
    before = position[None, :] < position[:, None]
    slot_ranks = lax.optimization_barrier(jnp.sum(jnp.where(same & before, 1, 0), axis=1)).astype(jnp.int32)
    return (slot_ranks, (owner_list * capacity + slot_ranks).astype(jnp.int32))

def attention(query_low, key_low, value_low):
    factor = 1.0 / math.sqrt(HD)
    query_heads = query_low.reshape(L, HEADS, HD)
    key_heads = key_low.reshape(L, HEADS, HD)
    value_heads = value_low.reshape(L, HEADS, HD)
    scores = low_back(exact_dot('qhd,khd->hqk', query_heads, key_heads) * factor)
    weights_low = low(jax.nn.softmax(scores, axis=-1))
    return exact_dot('hqk,khd->qhd', weights_low, value_heads).reshape(L, D)

def latent_forward(weight_bank, bias_bank, tokens, condition):
    silu_low = low(jax.nn.silu(condition))
    modulation = low_back(exact_dot('d,kde->ke', silu_low, weight_bank[12:18]) + bias_bank[8:14])
    hidden = low(modulate(tokens, modulation[1], modulation[0]))
    query_low = round_both(exact_dot('td,de->te', hidden, weight_bank[0]) + bias_bank[0])
    key_low = round_both(exact_dot('td,de->te', hidden, weight_bank[1]))
    value_low = round_both(exact_dot('td,de->te', hidden, weight_bank[2]) + bias_bank[1])
    attended = round_both(attention(query_low, key_low, value_low))
    branch = low_back(exact_dot('td,de->te', attended, weight_bank[3]) + bias_bank[2])
    middle = tokens + modulation[2] * branch
    hidden_two = low(modulate(middle, modulation[4], modulation[3]))
    upper_pre = low_back(exact_dot('td,jde->tje', hidden_two, weight_bank[4:8]) + bias_bank[3:7])
    active = low(jax.nn.gelu(upper_pre, approximate=True))
    mlp_out = low_back(exact_dot('tjd,jde->te', active, weight_bank[8:12]) + bias_bank[7])
    return middle + modulation[5] * mlp_out

def adam_step(param, grad, one, two, rate):
    next_one = BETA_ONE * one + (1.0 - BETA_ONE) * grad
    next_two = BETA_TWO * two + (1.0 - BETA_TWO) * grad * grad
    fix_one = 1.0 - BETA_ONE ** STEP
    fix_two = 1.0 - BETA_TWO ** STEP
    update = next_one / fix_one / (jnp.sqrt(next_two / fix_two) + ADAM_EPS)
    return (param - rate * (update + DECAY * param), next_one, next_two)

def reference(latents, conditioning, cotangent, owner_list, master, moment_one, moment_two, biases, bias_moment_one, bias_moment_two):
    slot_ranks, slot_index = slot_numbers(owner_list, CAP)
    chosen = jnp.take(master, slot_index, axis=0)
    weights = lax.optimization_barrier(chosen.astype(jnp.bfloat16)).astype(jnp.float32)
    values = latents.astype(jnp.float32)
    step_fn = jax.checkpoint(latent_forward)

    def forward(weight_bank, bias_bank, token_bank, cond_bank):
        flat_tokens = token_bank.reshape(MICRO * LAT, L, D)
        flat_cond = cond_bank.reshape(MICRO * LAT, D)

        def one_latent(latent_pair):
            return step_fn(weight_bank, bias_bank, latent_pair[0], latent_pair[1])
        result = lax.map(one_latent, (flat_tokens, flat_cond))
        return result.reshape(MICRO, LAT, L, D)
    result, pull_back = jax.vjp(forward, weights, biases, values, conditioning)
    grad_weights, grad_biases, input_grad, cond_grad = pull_back(cotangent.astype(jnp.float32))
    new_blocks, next_one, next_two = adam_step(chosen, grad_weights, jnp.take(moment_one, slot_index, axis=0), jnp.take(moment_two, slot_index, axis=0), RATE_WEIGHT)
    new_master = master.at[slot_index].set(new_blocks)
    new_moment_one = moment_one.at[slot_index].set(next_one)
    new_moment_two = moment_two.at[slot_index].set(next_two)
    new_copies = new_master.astype(jnp.bfloat16)
    new_biases, new_bias_one, new_bias_two = adam_step(biases, grad_biases, bias_moment_one, bias_moment_two, RATE_BIAS)
    return (result.astype(jnp.bfloat16), input_grad, cond_grad, new_master, new_moment_one, new_moment_two, new_copies, new_biases, new_bias_one, new_bias_two)
```

```python
import functools
import math

import jax
import jax.numpy as jnp
from jax import lax
from jax.experimental import pallas as pl
from jax.experimental.pallas import tpu as pltpu
from jax.sharding import PartitionSpec as P

HD = 64
STEP = 5
EPS_NORM = 1e-06
BETA_ONE = 0.5
BETA_TWO = 0.5
RATE_WEIGHT = 0.03
RATE_BIAS = 0.1
DECAY = 0.1
ADAM_EPS = 1e-08

MESH = pl.DeviceIdType.MESH
ANY = pl.BlockSpec(memory_space=pl.ANY)
VMEM = pl.BlockSpec(memory_space=pltpu.VMEM)
F32 = jnp.float32
BF16 = jnp.bfloat16
DMA = pltpu.SemaphoreType.DMA
LINEAR = 12


def params(cid, vmem=48):
    return pltpu.CompilerParams(
        collective_id=cid, has_side_effects=True, vmem_limit_bytes=vmem * 1024 * 1024
    )


def remote(src, dst, send_sem, recv_sem, device):
    return pltpu.make_async_remote_copy(
        src_ref=src,
        dst_ref=dst,
        send_sem=send_sem,
        recv_sem=recv_sem,
        device_id=device,
        device_id_type=MESH,
    )


class Place:
    def __init__(self, sizes):
        self.S, self.F, self.G = sizes
        self.s = lax.axis_index("seq")
        self.f = lax.axis_index("fsdp")
        self.g = lax.axis_index("grp")
        self.c = lax.rem(self.g, 2)
        self.base = self.g - self.c
        self.sib = self.base + 1 - self.c
        odd = lax.rem(self.s, 2)
        self.sx = self.s + 1 - 2 * odd
        self.sy = lax.rem(self.s + 2, 4)
        self.sa = self.sx + self.c * (self.sy - self.sx)
        self.sb = self.sy + self.c * (self.sx - self.sy)

    def sibling(self):
        return (self.s, self.f, self.sib)


def meet(devices):
    bar = pltpu.get_barrier_semaphore()
    for device in devices:
        pl.semaphore_signal(bar, inc=1, device_id=device, device_id_type=MESH)
    pl.semaphore_wait(bar, len(devices))


def meet_loop(count, device_of):
    bar = pltpu.get_barrier_semaphore()

    def one(i, carry):
        pl.semaphore_signal(bar, inc=1, device_id=device_of(i), device_id_type=MESH)
        return carry

    lax.fori_loop(1, count, one, 0)
    pl.semaphore_wait(bar, count - 1)


def slot_tables(owner_list, group, capacity):
    blocks = owner_list.shape[0]
    position = jnp.arange(blocks, dtype=jnp.int32)
    same = owner_list[:, None] == owner_list[None, :]
    before = position[None, :] < position[:, None]
    ranks = jnp.sum(jnp.where(same & before, 1, 0), axis=1).astype(jnp.int32)
    mine = owner_list == group
    slots = jnp.arange(capacity, dtype=jnp.int32)
    holds = mine[None, :] & (ranks[None, :] == slots[:, None])
    slot_block = jnp.sum(jnp.where(holds, position[None, :], 0), axis=1).astype(jnp.int32)
    slot_live = jnp.any(holds, axis=1).astype(jnp.int32)
    block_slot = jnp.where(mine, ranks, 0).astype(jnp.int32)
    return block_slot, mine.astype(jnp.int32), slot_block, slot_live


def pick_kernel(slot_ref, mine_ref, master_ref, out_ref):
    keep = mine_ref[pl.program_id(0)] > 0
    out_ref[...] = jnp.where(keep, master_ref[...], 0.0).astype(BF16)


def pick_blocks(master, block_slot, mine):
    blocks = block_slot.shape[0]
    rows, width = master.shape[1:]
    return pl.pallas_call(
        pick_kernel,
        out_shape=jax.ShapeDtypeStruct((blocks, rows, width), BF16),
        grid_spec=pltpu.PrefetchScalarGridSpec(
            num_scalar_prefetch=2,
            grid=(blocks,),
            in_specs=[pl.BlockSpec((1, rows, width), lambda b, slot, own: (slot[b], 0, 0))],
            out_specs=pl.BlockSpec((1, rows, width), lambda b, slot, own: (b, 0, 0)),
        ),
        name="pick_blocks",
    )(block_slot, mine, master)


def adam_step(param, grad, one, two, rate):
    next_one = BETA_ONE * one + (1.0 - BETA_ONE) * grad
    next_two = BETA_TWO * two + (1.0 - BETA_TWO) * grad * grad
    fix_one = 1.0 - BETA_ONE**STEP
    fix_two = 1.0 - BETA_TWO**STEP
    update = next_one / fix_one / (jnp.sqrt(next_two / fix_two) + ADAM_EPS)
    return (param - rate * (update + DECAY * param), next_one, next_two)


def adam_kernel(block_ref, live_ref, master, grad, one, two, o_master, o_one, o_two, o_copy):
    live = live_ref[pl.program_id(0)] > 0
    stepped, next_one, next_two = adam_step(
        master[...], grad[...].astype(F32), one[...], two[...], RATE_WEIGHT
    )
    new = jnp.where(live, stepped, master[...])
    o_master[...] = new
    o_one[...] = jnp.where(live, next_one, one[...])
    o_two[...] = jnp.where(live, next_two, two[...])
    o_copy[...] = new.astype(BF16)


def adam_slots(master, grads, one, two, slot_block, slot_live):
    slots, rows, width = master.shape
    by_slot = pl.BlockSpec((1, rows, width), lambda j, block, live: (j, 0, 0))
    by_block = pl.BlockSpec((1, rows, width), lambda j, block, live: (block[j], 0, 0))
    shape = jax.ShapeDtypeStruct(master.shape, F32)
    return pl.pallas_call(
        adam_kernel,
        out_shape=(shape, shape, shape, jax.ShapeDtypeStruct(master.shape, BF16)),
        grid_spec=pltpu.PrefetchScalarGridSpec(
            num_scalar_prefetch=2,
            grid=(slots,),
            in_specs=[by_slot, by_block, by_slot, by_slot],
            out_specs=(by_slot, by_slot, by_slot, by_slot),
        ),
        name="adam_slots",
    )(slot_block, slot_live, master, grads, one, two)


def share_kernel(sizes, blocks_ref, cond_ref, theirs_ref, conds_ref, ws, wr, cs, cr, ls):
    at = Place(sizes)
    half = theirs_ref.shape[2]
    count = at.F * at.G
    me = at.f * at.G + at.g

    def device_of(i):
        n = lax.rem(me + i, count)
        return (at.s, lax.div(n, at.G), lax.rem(n, at.G))

    meet_loop(count, device_of)

    def to_group(i):
        g = lax.rem(at.g + i, at.G)
        return remote(
            blocks_ref.at[:, pl.ds(pl.multiple_of(lax.rem(g, 2) * half, half), half), :],
            theirs_ref.at[at.G - 1 - i],
            ws.at[i],
            wr.at[at.G - 1 - i],
            (at.s, at.f, g),
        )

    def from_group(j):
        return remote(
            blocks_ref.at[:, pl.ds(0, half), :], theirs_ref.at[j], ws.at[0], wr.at[j], (at.s, at.f, at.g)
        )

    for i in range(1, at.G):
        to_group(i).start()
    own = pltpu.make_async_copy(cond_ref, conds_ref.at[me], ls)
    own.start()

    def cond_to(i):
        return remote(cond_ref, conds_ref.at[me], cs.at[i], cr.at[me], device_of(i))

    def cond_from(i):
        n = lax.rem(me + count - i, count)
        return remote(cond_ref, conds_ref.at[n], cs.at[i], cr.at[n], device_of(i))

    lax.fori_loop(1, count, lambda i, u: (cond_to(i).start(), u)[1], 0)
    own.wait()
    for i in range(1, at.G):
        to_group(i).wait_send()
        from_group(i - 1).wait_recv()
    lax.fori_loop(1, count, lambda i, u: (cond_to(i).wait_send(), u)[1], 0)
    lax.fori_loop(1, count, lambda i, u: (cond_from(i).wait_recv(), u)[1], 0)


def share(sizes, blocks, cond):
    S, F, G = sizes
    count, rows, width = blocks.shape
    return pl.pallas_call(
        functools.partial(share_kernel, sizes),
        out_shape=(
            jax.ShapeDtypeStruct((G - 1, count, rows // 2, width), BF16),
            jax.ShapeDtypeStruct((F * G,) + cond.shape, F32),
        ),
        in_specs=[ANY, ANY],
        out_specs=(ANY, ANY),
        scratch_shapes=[DMA((G,)), DMA((G,)), DMA((F * G,)), DMA((F * G,)), DMA],
        compiler_params=params(1),
        name="share_blocks",
    )(blocks, cond)


def token_move(at, j):
    return (2 * j + at.c, at.f, at.base + lax.div(at.s, 2))


def gather_kernel(
    sizes, shard, modp, lat, cot, bank, modr, tok, ctok, ls, zs, zr, as_, ar, bs, br, cs, cr, ms, mr, ts, tr, tl
):
    at = Place(sizes)
    S, F = at.S, at.F
    K = shard.shape[0]
    T = 2 * S * F
    me = (at.s * F + at.f) * 2 + at.c
    quarter = lat.shape[1]

    def device_of(i):
        n = lax.rem(me + i, T)
        return (lax.div(n, 2 * F), lax.rem(lax.div(n, 2), F), at.base + lax.rem(n, 2))

    meet_loop(T, device_of)

    def mod_to(i):
        n = lax.rem(me + i, T)
        return remote(modp.at[lax.div(n, 2)], modr.at[me], ms.at[i], mr.at[me], device_of(i))

    def mod_from(i):
        n = lax.rem(me + T - i, T)
        return remote(modp.at[0], modr.at[n], ms.at[i], mr.at[n], device_of(i))

    def tok_to(j, which):
        src, dst = ((lat, tok), (cot, ctok))[which]
        place = pl.ds(pl.multiple_of(lax.rem(at.s, 2) * quarter, quarter), quarter)
        return remote(
            src.at[j], dst.at[place], ts.at[which, j], tr.at[which, lax.rem(at.s, 2)], token_move(at, j)
        )

    def tok_from(j, which):
        src, dst = ((lat, tok), (cot, ctok))[which]
        return remote(
            src.at[0],
            dst.at[pl.ds(j * quarter, quarter)],
            ts.at[which, j],
            tr.at[which, j],
            token_move(at, j),
        )

    def tok_local(j, which):
        src, dst = ((lat, tok), (cot, ctok))[which]
        place = pl.ds(pl.multiple_of(lax.rem(at.s, 2) * quarter, quarter), quarter)
        return pltpu.make_async_copy(src.at[j], dst.at[place], tl.at[which])

    def stays(j):
        return (2 * j + at.c == at.s) & (lax.div(at.s, 2) == at.c)

    def comes(j):
        return jnp.logical_not((2 * at.c + j == at.s) & (lax.rem(at.s, 2) == at.c))

    def tok_start(which):
        for j in range(2):
            @pl.when(stays(j))
            def _():
                tok_local(j, which).start()

            @pl.when(jnp.logical_not(stays(j)))
            def _():
                tok_to(j, which).start()

    def tok_finish(which):
        for j in range(2):
            @pl.when(stays(j))
            def _():
                tok_local(j, which).wait()

            @pl.when(jnp.logical_not(stays(j)))
            def _():
                tok_to(j, which).wait_send()

            @pl.when(comes(j))
            def _():
                tok_from(j, which).wait_recv()

    lax.fori_loop(1, T, lambda i, u: (mod_to(i).start(), u)[1], 0)
    mine = pltpu.make_async_copy(modp.at[at.s * F + at.f], modr.at[me], tl.at[2])
    mine.start()
    tok_start(0)

    def own(k):
        return pltpu.make_async_copy(shard.at[k], bank.at[k, at.s, at.f, at.c], ls.at[k])

    def z_to(k, i):
        f = lax.rem(at.f + i, F)
        return remote(
            shard.at[k], bank.at[k, at.s, at.f, at.c], zs.at[k, i], zr.at[k, i], (at.s, f, at.g)
        )

    def z_from(k, i):
        f = lax.rem(at.f + F - i, F)
        return remote(shard.at[k], bank.at[k, at.s, f, at.c], zs.at[k, i], zr.at[k, i], (at.s, f, at.g))

    def a_copy(k, s):
        line = bank.at[k, s, :, at.c]
        return remote(line, line, as_.at[k], ar.at[k], (at.sa, at.f, at.g))

    def b_copy(k, s, n):
        line = bank.at[k, s, :, at.c]
        return remote(line, line, bs.at[k, n], br.at[k, n], (at.sb, at.f, at.g))

    sd = at.S - 1 - at.s

    def c_copy(k, s, n, core):
        line = bank.at[k, s, :, core]
        return remote(line, line, cs.at[k, n], cr.at[k, n], at.sibling())

    def z_start(k):
        own(k).start()
        for i in range(1, F):
            z_to(k, i).start()

    z_start(0)
    z_start(1)

    def step(k, carry):
        @pl.when(k + 2 < K)
        def _():
            z_start(k + 2)

        @pl.when(k < K)
        def _():
            own(k).wait()
            for i in range(1, F):
                z_from(k, i).wait_recv()
            a_copy(k, at.s).start()
            c_copy(k, at.s, 0, at.c).start()

        @pl.when((k >= 1) & (k <= K))
        def _():
            a_copy(k - 1, at.sa).wait_recv()
            b_copy(k - 1, at.s, 0).start()
            b_copy(k - 1, at.sa, 1).start()
            c_copy(k - 1, at.sa, 1, at.c).start()

        @pl.when(k >= 2)
        def _():
            b_copy(k - 2, at.sb, 0).wait_recv()
            c_copy(k - 2, at.sb, 2, at.c).start()
            b_copy(k - 2, sd, 1).wait_recv()
            c_copy(k - 2, sd, 3, at.c).start()

        return carry

    lax.fori_loop(0, K + 2, step, 0)
    tok_start(1)

    def finish(k, carry):
        for i in range(1, F):
            z_to(k, i).wait_send()
        a_copy(k, at.s).wait_send()
        b_copy(k, at.s, 0).wait_send()
        b_copy(k, at.sa, 1).wait_send()
        for n, s in enumerate((at.s, at.sa, at.sb, sd)):
            c_copy(k, s, n, at.c).wait_send()
        for n, s in enumerate((at.s, at.sb, at.sa, sd)):
            c_copy(k, s, n, 1 - at.c).wait_recv()
        return carry

    lax.fori_loop(0, K, finish, 0)
    tok_finish(0)
    tok_finish(1)
    mine.wait()
    lax.fori_loop(1, T, lambda i, u: (mod_to(i).wait_send(), u)[1], 0)
    lax.fori_loop(1, T, lambda i, u: (mod_from(i).wait_recv(), u)[1], 0)


def gather(sizes, shard, modp, lat, cot):
    S, F, G = sizes
    K, half, width = shard.shape
    T = 2 * S * F
    tokens = 2 * lat.shape[1]
    return pl.pallas_call(
        functools.partial(gather_kernel, sizes),
        out_shape=(
            jax.ShapeDtypeStruct((K, S, F, 2, half, width), BF16),
            jax.ShapeDtypeStruct((T,) + modp.shape[1:], F32),
            jax.ShapeDtypeStruct((tokens, width), BF16),
            jax.ShapeDtypeStruct((tokens, width), BF16),
        ),
        in_specs=[ANY] * 4,
        out_specs=(ANY,) * 4,
        scratch_shapes=[
            DMA((K,)),
            DMA((K, F)),
            DMA((K, F)),
            DMA((K,)),
            DMA((K,)),
            DMA((K, 2)),
            DMA((K, 2)),
            DMA((K, 4)),
            DMA((K, 4)),
            DMA((T,)),
            DMA((T,)),
            DMA((2, 2)),
            DMA((2, 2)),
            DMA((3,)),
        ],
        compiler_params=params(2),
        name="gather_blocks",
    )(shard, modp, lat, cot)


def to_heads_kernel(sizes, count, *refs):
    at = Place(sizes)
    ins, outs, (ls, ss, rs) = refs[:count], refs[count : 2 * count], refs[2 * count :]
    tokens, width = ins[0].shape
    half = width // 2
    meet([at.sibling()])
    here = pl.ds(pl.multiple_of(at.c * tokens, tokens), tokens)
    there = pl.ds(pl.multiple_of((1 - at.c) * tokens, tokens), tokens)
    keep = pl.ds(pl.multiple_of(at.c * half, half), half)
    give = pl.ds(pl.multiple_of((1 - at.c) * half, half), half)
    for n in range(count):
        remote(ins[n].at[:, give], outs[n].at[here], ss.at[n], rs.at[n], at.sibling()).start()
        pltpu.make_async_copy(ins[n].at[:, keep], outs[n].at[here], ls.at[n]).start()
    for n in range(count):
        remote(ins[n].at[:, give], outs[n].at[here], ss.at[n], rs.at[n], at.sibling()).wait_send()
        remote(ins[n].at[:, give], outs[n].at[there], ss.at[n], rs.at[n], at.sibling()).wait_recv()
        pltpu.make_async_copy(ins[n].at[:, keep], outs[n].at[here], ls.at[n]).wait()


def to_tokens_kernel(sizes, count, *refs):
    at = Place(sizes)
    ins, outs, (ls, ss, rs) = refs[:count], refs[count : 2 * count], refs[2 * count :]
    tokens, half = ins[0].shape[0] // 2, ins[0].shape[1]
    meet([at.sibling()])
    keep = pl.ds(pl.multiple_of(at.c * tokens, tokens), tokens)
    give = pl.ds(pl.multiple_of((1 - at.c) * tokens, tokens), tokens)
    here = pl.ds(pl.multiple_of(at.c * half, half), half)
    there = pl.ds(pl.multiple_of((1 - at.c) * half, half), half)
    for n in range(count):
        remote(ins[n].at[give], outs[n].at[:, here], ss.at[n], rs.at[n], at.sibling()).start()
        pltpu.make_async_copy(ins[n].at[keep], outs[n].at[:, here], ls.at[n]).start()
    for n in range(count):
        remote(ins[n].at[give], outs[n].at[:, here], ss.at[n], rs.at[n], at.sibling()).wait_send()
        remote(ins[n].at[give], outs[n].at[:, there], ss.at[n], rs.at[n], at.sibling()).wait_recv()
        pltpu.make_async_copy(ins[n].at[keep], outs[n].at[:, here], ls.at[n]).wait()


def exchange(sizes, kernel, cid, name, arrays):
    count = len(arrays)
    rows, width = arrays[0].shape
    shape = (2 * rows, width // 2) if kernel is to_heads_kernel else (rows // 2, 2 * width)
    return pl.pallas_call(
        functools.partial(kernel, sizes, count),
        out_shape=tuple(jax.ShapeDtypeStruct(shape, BF16) for _ in arrays),
        in_specs=[ANY] * count,
        out_specs=(ANY,) * count,
        scratch_shapes=[DMA((count,)), DMA((count,)), DMA((count,))],
        compiler_params=params(cid),
        name=name,
    )(*arrays)


ROWS = 256
NT = (((1,), (1,)), ((), ()))
NN = (((1,), (0,)), ((), ()))


def dot(left, right, dims):
    return lax.dot_general(left, right, dims, preferred_element_type=F32)


def attend_kernel(q_ref, k_ref, v_ref, a_ref, lse_ref):
    length = q_ref.shape[0]
    factor = 1.0 / math.sqrt(HD)
    for h in range(2):
        cols = slice(h * HD, (h + 1) * HD)
        key = k_ref[:, cols]
        value = v_ref[:, cols]
        for r in range(0, length, ROWS):
            rows = slice(r, r + ROWS)
            scores = dot(q_ref[rows, cols], key, NT)
            high = jnp.max(scores, axis=1, keepdims=True)
            weights = jnp.exp((scores - high) * factor)
            total = jnp.sum(weights, axis=1, keepdims=True)
            out = dot(weights.astype(BF16), value, NN) / total
            a_ref[rows, cols] = out.astype(BF16)
            lse_ref[rows, cols] = jnp.broadcast_to(high * factor + jnp.log(total), (ROWS, HD))


def attend(q, k, v):
    length, width = q.shape
    pair = pl.BlockSpec((length, 2 * HD), lambda n: (0, n))
    return pl.pallas_call(
        attend_kernel,
        out_shape=(
            jax.ShapeDtypeStruct((length, width), BF16),
            jax.ShapeDtypeStruct((length, width), F32),
        ),
        grid=(width // (2 * HD),),
        in_specs=[pair] * 3,
        out_specs=(pair, pair),
        compiler_params=pltpu.CompilerParams(vmem_limit_bytes=48 * 1024 * 1024),
        name="attend",
    )(q, k, v)


def attend_back_kernel(q_ref, k_ref, v_ref, a_ref, lse_ref, da_ref, dq_ref, dk_ref, dv_ref):
    length = q_ref.shape[0]
    factor = 1.0 / math.sqrt(HD)
    for h in range(2):
        cols = slice(h * HD, (h + 1) * HD)
        key = k_ref[:, cols]
        value = v_ref[:, cols]
        dk = jnp.zeros((HD, length), F32)
        dv = jnp.zeros((HD, length), F32)
        for r in range(0, length, ROWS):
            rows = slice(r, r + ROWS)
            query = q_ref[rows, cols]
            grad = da_ref[rows, cols]
            lse = lse_ref[rows, h * HD : h * HD + 1]
            scores = dot(query, key, NT)
            probs = jnp.exp(scores * factor - lse)
            row_dot = jnp.sum(
                grad.astype(F32) * a_ref[rows, cols].astype(F32), axis=1, keepdims=True
            )
            weight_grad = dot(grad, value, NT)
            score_grad = (probs * (weight_grad - row_dot)).astype(BF16)
            dq_ref[rows, cols] = (dot(score_grad, key, NN) * factor).astype(BF16)
            dk = dk + dot(query.T, score_grad, NN)
            dv = dv + dot(grad.T, probs.astype(BF16), NN)
        dk_ref[:, cols] = (dk * factor).T.astype(BF16)
        dv_ref[:, cols] = dv.T.astype(BF16)


def attend_back(q, k, v, a, lse, da):
    length, width = q.shape
    pair = pl.BlockSpec((length, 2 * HD), lambda n: (0, n))
    shape = jax.ShapeDtypeStruct((length, width), BF16)
    return pl.pallas_call(
        attend_back_kernel,
        out_shape=(shape, shape, shape),
        grid=(width // (2 * HD),),
        in_specs=[pair] * 6,
        out_specs=(pair, pair, pair),
        compiler_params=pltpu.CompilerParams(vmem_limit_bytes=48 * 1024 * 1024),
        name="attend_back",
    )(q, k, v, a, lse, da)


def reduce_kernel(
    sizes, grads, small, out_tok, in_tok, red, smalls, out_lat, in_lat,
    mine, r0, r1, r2, r3, total, sv, sw,
    ls, cs, cr, bs, br, as_, ar, zs, zr, os_, vs, vr, ws, wr, wl, ts, tr, tl,
):
    at = Place(sizes)
    S, F, G = sizes
    K = grads.shape[0]
    half, width = red.shape[1:]
    count = S * F * G
    me = (at.s * F + at.f) * G + at.g
    quarter = out_lat.shape[1]
    sd = S - 1 - at.s

    def device_of(i):
        n = lax.rem(me + i, count)
        return (lax.div(n, F * G), lax.rem(lax.div(n, G), F), lax.rem(n, G))

    meet_loop(count, device_of)

    def c_copy(k):
        return remote(grads.at[k, :, :, 1 - at.c], r0.at[k], cs.at[k], cr.at[k], at.sibling())

    def own(k):
        return pltpu.make_async_copy(grads.at[k, :, :, at.c], mine.at[k], ls.at[k])

    def b_copy(k, s, n):
        return remote(mine.at[k, s], r1.at[k, n], bs.at[k, n], br.at[k, n], (at.sb, at.f, at.g))

    def a_copy(k):
        return remote(mine.at[k, at.sa], r2.at[k], as_.at[k], ar.at[k], (at.sa, at.f, at.g))

    def z_to(k, i):
        f = lax.rem(at.f + i, F)
        return remote(mine.at[k, at.s, f], r3.at[k, i], zs.at[k, i], zr.at[k, i], (at.s, f, at.g))

    def out_copy(k):
        return pltpu.make_async_copy(total.at[k], red.at[k], os_.at[k])

    small_swap = remote(small, sv, vs, vr, at.sibling())
    small_swap.start()
    own(0).start()
    c_copy(0).start()
    own(1).start()
    c_copy(1).start()

    def back_device(j):
        return (2 * at.c + j, at.f, at.base + lax.rem(at.s, 2))

    def back_stays(j):
        return (2 * at.c + j == at.s) & (lax.rem(at.s, 2) == at.c)

    def back_comes(m):
        return jnp.logical_not((2 * m + at.c == at.s) & (lax.div(at.s, 2) == at.c))

    def back_to(j, which):
        src, dst = ((out_tok, out_lat), (in_tok, in_lat))[which]
        m = lax.div(at.s, 2)
        return remote(
            src.at[pl.ds(j * quarter, quarter)], dst.at[m], ts.at[which, j], tr.at[which, m], back_device(j)
        )

    def back_from(m, which):
        src, dst = ((out_tok, out_lat), (in_tok, in_lat))[which]
        return remote(
            src.at[pl.ds(0, quarter)], dst.at[m], ts.at[which, m], tr.at[which, m], back_device(m)
        )

    def back_local(j, which):
        src, dst = ((out_tok, out_lat), (in_tok, in_lat))[which]
        return pltpu.make_async_copy(
            src.at[pl.ds(j * quarter, quarter)], dst.at[lax.div(at.s, 2)], tl.at[which]
        )

    def back_start(which):
        for j in range(2):
            @pl.when(back_stays(j))
            def _():
                back_local(j, which).start()

            @pl.when(jnp.logical_not(back_stays(j)))
            def _():
                back_to(j, which).start()

    def back_finish(which):
        for j in range(2):
            @pl.when(back_stays(j))
            def _():
                back_local(j, which).wait()

            @pl.when(jnp.logical_not(back_stays(j)))
            def _():
                back_to(j, which).wait_send()

            @pl.when(back_comes(j))
            def _():
                back_from(j, which).wait_recv()

    small_swap.wait()
    sw[...] = small[...] + sv[...]

    chip = lax.div(me, 2)
    part = small.shape[0] // 2
    sent = pl.ds(pl.multiple_of(at.c * part, part), part)

    def small_device(i):
        n = lax.rem(me - at.c + 2 + i, count)
        return (lax.div(n, F * G), lax.rem(lax.div(n, G), F), lax.rem(n, G))

    def small_to(i):
        return remote(
            sw.at[sent], smalls.at[chip, sent], ws.at[i], wr.at[chip, at.c], small_device(i)
        )

    def small_from(i):
        n = lax.rem(me - at.c + 2 + i, count)
        there = lax.div(n, 2)
        core = lax.rem(n, 2)
        rows = pl.ds(pl.multiple_of(core * part, part), part)
        return remote(sw.at[rows], smalls.at[there, rows], ws.at[i], wr.at[there, core], small_device(i))

    small_own = pltpu.make_async_copy(sw, smalls.at[chip], wl)
    small_own.start()
    lax.fori_loop(0, count - 2, lambda i, u: (small_to(i).start(), u)[1], 0)

    def add_line(dst, src):
        def one(f, carry):
            dst[f] = (dst[f].astype(F32) + src[f].astype(F32)).astype(BF16)
            return carry

        lax.fori_loop(0, F, one, 0)

    def step(k, carry):
        @pl.when(k + 2 < K)
        def _():
            own(k + 2).start()
            c_copy(k + 2).start()

        @pl.when(k < K)
        def _():
            own(k).wait()
            c_copy(k).wait_recv()

            def one(n, carry):
                s = lax.div(n, F)
                f = lax.rem(n, F)
                mine[k, s, f] = (mine[k, s, f].astype(F32) + r0[k, s, f].astype(F32)).astype(BF16)
                return carry

            lax.fori_loop(0, S * F, one, 0)
            b_copy(k, at.sb, 0).start()
            b_copy(k, sd, 1).start()

        @pl.when((k >= 1) & (k <= K))
        def _():
            b_copy(k - 1, at.sb, 0).wait_recv()
            b_copy(k - 1, sd, 1).wait_recv()
            add_line(mine.at[k - 1, at.s], r1.at[k - 1, 0])
            add_line(mine.at[k - 1, at.sa], r1.at[k - 1, 1])
            a_copy(k - 1).start()

        @pl.when((k >= 2) & (k <= K + 1))
        def _():
            a_copy(k - 2).wait_recv()
            add_line(mine.at[k - 2, at.s], r2.at[k - 2])
            for i in range(1, F):
                z_to(k - 2, i).start()

        @pl.when(k >= 3)
        def _():
            for i in range(1, F):
                z_to(k - 3, i).wait_recv()
            value = mine[k - 3, at.s, at.f].astype(F32)
            for i in range(1, F):
                value = value + r3[k - 3, i].astype(F32)
            total[k - 3] = value
            out_copy(k - 3).start()

        return carry

    lax.fori_loop(0, K + 3, step, 0)
    back_start(0)
    back_start(1)

    def finish(k, carry):
        c_copy(k).wait_send()
        b_copy(k, at.sb, 0).wait_send()
        b_copy(k, sd, 1).wait_send()
        a_copy(k).wait_send()
        for i in range(1, F):
            z_to(k, i).wait_send()
        out_copy(k).wait()
        return carry

    lax.fori_loop(0, K, finish, 0)
    back_finish(0)
    back_finish(1)
    small_own.wait()
    lax.fori_loop(0, count - 2, lambda i, u: (small_to(i).wait_send(), u)[1], 0)
    lax.fori_loop(0, count - 2, lambda i, u: (small_from(i).wait_recv(), u)[1], 0)


def reduce_grads(sizes, grads, small, out_tok, in_tok):
    S, F, G = sizes
    K, _, _, _, half, width = grads.shape
    quarter = out_tok.shape[0] // 2
    count = S * F * G
    part = (K, F, half, width)
    return pl.pallas_call(
        functools.partial(reduce_kernel, sizes),
        out_shape=(
            jax.ShapeDtypeStruct((K, half, width), F32),
            jax.ShapeDtypeStruct((count // 2,) + small.shape, F32),
            jax.ShapeDtypeStruct((2, quarter, width), BF16),
            jax.ShapeDtypeStruct((2, quarter, width), BF16),
        ),
        in_specs=[ANY, VMEM, ANY, ANY],
        out_specs=(ANY,) * 4,
        scratch_shapes=[
            pltpu.VMEM((K, S, F, half, width), BF16),
            pltpu.VMEM((K, S, F, half, width), BF16),
            pltpu.VMEM((K, 2, F, half, width), BF16),
            pltpu.VMEM((K, F, half, width), BF16),
            pltpu.VMEM((K, F, half, width), BF16),
            pltpu.VMEM((K, half, width), F32),
            pltpu.VMEM(small.shape, F32),
            pltpu.VMEM(small.shape, F32),
            DMA((K,)),
            DMA((K,)),
            DMA((K,)),
            DMA((K, 2)),
            DMA((K, 2)),
            DMA((K,)),
            DMA((K,)),
            DMA((K, F)),
            DMA((K, F)),
            DMA((K,)),
            DMA,
            DMA,
            DMA((count,)),
            DMA((count // 2, 2)),
            DMA,
            DMA((2, 2)),
            DMA((2, 2)),
            DMA((2,)),
        ],
        compiler_params=params(7, 60),
        name="reduce_grads",
    )(grads, small, out_tok, in_tok)


def settle_kernel(sizes, red, cg, theirs, cgs, gs, gr, cs, cr, cl):
    at = Place(sizes)
    S, F, G = sizes
    T = 2 * S * F
    me = (at.s * F + at.f) * 2 + at.c
    others = [lax.rem(at.g + i, G) for i in range(1, G)]

    def device_of(i):
        n = lax.rem(me + i, T)
        return (lax.div(n, 2 * F), lax.rem(lax.div(n, 2), F), at.base + lax.rem(n, 2))

    bar = pltpu.get_barrier_semaphore()

    def greet(i, carry):
        pl.semaphore_signal(bar, inc=1, device_id=device_of(i), device_id_type=MESH)
        return carry

    lax.fori_loop(1, T, greet, 0)
    extra = 0
    if G > 2:
        for g in others:
            pl.semaphore_signal(bar, inc=1, device_id=(at.s, at.f, g), device_id_type=MESH)
        extra = G - 1
    pl.semaphore_wait(bar, T - 1 + extra)

    def to_group(i):
        return remote(
            red, theirs.at[G - 1 - i], gs.at[i], gr.at[G - 1 - i], (at.s, at.f, lax.rem(at.g + i, G))
        )

    for i in range(1, G):
        to_group(i).start()

    def cond_to(i):
        return remote(cg, cgs.at[me], cs.at[i], cr.at[me], device_of(i))

    def cond_from(i):
        n = lax.rem(me + T - i, T)
        return remote(cg, cgs.at[n], cs.at[i], cr.at[n], device_of(i))

    own = pltpu.make_async_copy(cg, cgs.at[me], cl)
    own.start()
    lax.fori_loop(1, T, lambda i, u: (cond_to(i).start(), u)[1], 0)
    own.wait()
    for i in range(1, G):
        to_group(i).wait()
    lax.fori_loop(1, T, lambda i, u: (cond_to(i).wait_send(), u)[1], 0)
    lax.fori_loop(1, T, lambda i, u: (cond_from(i).wait_recv(), u)[1], 0)


def settle(sizes, red, cg):
    S, F, G = sizes
    T = 2 * S * F
    return pl.pallas_call(
        functools.partial(settle_kernel, sizes),
        out_shape=(
            jax.ShapeDtypeStruct((G - 1,) + red.shape, F32),
            jax.ShapeDtypeStruct((T,) + cg.shape, F32),
        ),
        in_specs=[ANY, ANY],
        out_specs=(ANY, ANY),
        scratch_shapes=[DMA((G,)), DMA((G,)), DMA((T,)), DMA((T,)), DMA],
        compiler_params=params(8),
        name="settle_rows",
    )(red, cg)


def normed(values):
    centre = jnp.mean(values, axis=-1, keepdims=True)
    centred = values - centre
    spread = jnp.mean(centred * centred, axis=-1, keepdims=True)
    inverse = lax.rsqrt(spread + EPS_NORM)
    return centred * inverse, inverse


def norm_back(grad, scaled, inverse, scale):
    inner = grad * (1.0 + scale)
    mean_inner = jnp.mean(inner, axis=-1, keepdims=True)
    mean_scaled = jnp.mean(inner * scaled, axis=-1, keepdims=True)
    part = inverse * (inner - mean_inner - scaled * mean_scaled)
    return part, jnp.sum(grad * scaled, axis=0), jnp.sum(grad, axis=0)


def matmul(left, right):
    return jnp.einsum("td,de->te", left, right, preferred_element_type=F32)


def matmul_t(left, right):
    return jnp.einsum("te,de->td", left, right, preferred_element_type=F32)


def weight_grad(left, right):
    return jnp.einsum("td,te->de", left, right, preferred_element_type=F32).astype(BF16)


def gelu_tanh(values):
    return jax.nn.gelu(values, approximate=True)


def per_device(
    sizes,
    latents,
    conditioning,
    cotangent,
    owner_list,
    master,
    moment_one,
    moment_two,
    biases,
    bias_moment_one,
    bias_moment_two,
):
    S, F, G = sizes
    capacity, rows, width = master.shape
    half = rows // 2
    blocks = owner_list.shape[0]
    s, f, g = lax.axis_index("seq"), lax.axis_index("fsdp"), lax.axis_index("grp")
    core = g % 2
    pair = g // 2
    T = S * F

    block_slot, mine, slot_block, slot_live = slot_tables(owner_list, g, capacity)
    picked = pick_blocks(master, block_slot, mine)
    cond_pad = jnp.pad(conditioning[:, 0], ((0, 6), (0, 0)))
    theirs, conds = share(sizes, picked, cond_pad)
    shard = lax.dynamic_slice_in_dim(picked, core * half, half, 1)
    for i in range(G - 1):
        shard = shard + theirs[i]
    linear, modulation_rows = shard[:LINEAR], shard[LINEAR:]

    silu_all = jax.nn.silu(conds[:, :2]).astype(BF16).reshape(F, G // 2, 2, 2, width)
    silu_pair = lax.dynamic_index_in_dim(silu_all, pair, 1, keepdims=False)
    silu_pair = silu_pair.transpose(2, 1, 0, 3).reshape(T, width)
    first_row = (s * F + f) * rows + core * half
    silu_rows = lax.dynamic_slice_in_dim(silu_pair, first_row, half, 1)
    mod_part = jnp.einsum("tr,jre->tje", silu_rows, modulation_rows, preferred_element_type=F32)
    mod_part = jnp.pad(mod_part, ((0, 0), (0, 2), (0, 0)))

    bank, mod_parts, tokens, grad_low = gather(
        sizes, linear, mod_part, latents[:, 0], cotangent[:, 0]
    )
    bank = bank.reshape(LINEAR, width, width)
    modulation = jnp.sum(mod_parts, axis=0)[:6] + biases[8:14]
    shift_one, scale_one, gate_one, shift_two, scale_two, gate_two = (
        modulation[j : j + 1] for j in range(6)
    )

    values = tokens.astype(F32)
    scaled_one, inverse_one = normed(values)
    hidden = (scaled_one * (1.0 + scale_one) + shift_one).astype(BF16)
    query = (matmul(hidden, bank[0]) + biases[0]).astype(BF16)
    key = matmul(hidden, bank[1]).astype(BF16)
    value = (matmul(hidden, bank[2]) + biases[1]).astype(BF16)
    head_query, head_key, head_value = exchange(
        sizes, to_heads_kernel, 3, "qkv_to_heads", (query, key, value)
    )
    head_out, lse = attend(head_query, head_key, head_value)
    (attended,) = exchange(sizes, to_tokens_kernel, 4, "out_to_tokens", (head_out,))
    branch = matmul(attended, bank[3]) + biases[2]
    middle = values + gate_one * branch
    scaled_two, inverse_two = normed(middle)
    hidden_two = (scaled_two * (1.0 + scale_two) + shift_two).astype(BF16)
    upper = jnp.einsum("td,jde->jte", hidden_two, bank[4:8], preferred_element_type=F32)
    upper = upper + biases[3:7][:, None]
    active, gelu_pull = jax.vjp(gelu_tanh, upper)
    active = active.astype(BF16)
    mlp_out = (
        jnp.einsum("jtd,jde->te", active, bank[8:12], preferred_element_type=F32) + biases[7]
    )
    result = (middle + gate_two * mlp_out).astype(BF16)

    grad_out = grad_low.astype(F32)
    d_gate_two = jnp.sum(grad_out * mlp_out, axis=0)
    mlp_grad = (gate_two * grad_out).astype(BF16)
    active_grad = jnp.einsum("te,jde->jtd", mlp_grad, bank[8:12], preferred_element_type=F32)
    upper_grad = gelu_pull(active_grad)[0].astype(BF16)
    hidden_two_grad = jnp.einsum("jte,jde->td", upper_grad, bank[4:8], preferred_element_type=F32)
    middle_part, d_scale_two, d_shift_two = norm_back(
        hidden_two_grad, scaled_two, inverse_two, scale_two
    )
    middle_grad = grad_out + middle_part
    d_gate_one = jnp.sum(middle_grad * branch, axis=0)
    branch_grad = (gate_one * middle_grad).astype(BF16)
    attended_grad = matmul_t(branch_grad, bank[3]).astype(BF16)
    (head_grad,) = exchange(sizes, to_heads_kernel, 5, "grad_to_heads", (attended_grad,))
    head_grads = attend_back(head_query, head_key, head_value, head_out, lse, head_grad)
    query_grad, key_grad, value_grad = exchange(
        sizes, to_tokens_kernel, 6, "grads_to_tokens", head_grads
    )
    hidden_grad = (
        matmul_t(query_grad, bank[0]) + matmul_t(key_grad, bank[1]) + matmul_t(value_grad, bank[2])
    )
    values_part, d_scale_one, d_shift_one = norm_back(
        hidden_grad, scaled_one, inverse_one, scale_one
    )
    input_grad = (middle_grad + values_part).astype(BF16)

    grads = jnp.concatenate(
        [
            weight_grad(hidden, query_grad)[None],
            weight_grad(hidden, key_grad)[None],
            weight_grad(hidden, value_grad)[None],
            weight_grad(attended, branch_grad)[None],
            jnp.einsum("td,jte->jde", hidden_two, upper_grad, preferred_element_type=F32).astype(BF16),
            jnp.einsum("jtd,te->jde", active, mlp_grad, preferred_element_type=F32).astype(BF16),
        ],
        axis=0,
    )
    small = jnp.concatenate(
        [
            jnp.stack(
                [d_shift_one, d_scale_one, d_gate_one, d_shift_two, d_scale_two, d_gate_two]
            ),
            jnp.sum(query_grad.astype(F32), axis=0)[None],
            jnp.sum(value_grad.astype(F32), axis=0)[None],
            jnp.sum(branch_grad.astype(F32), axis=0)[None],
            jnp.sum(upper_grad.astype(F32), axis=1),
            jnp.sum(mlp_grad.astype(F32), axis=0)[None],
            jnp.zeros((2, width), F32),
        ],
        axis=0,
    )
    reduced, smalls, out_lat, in_lat = reduce_grads(
        sizes, grads.reshape(LINEAR, S, F, 2, half, width), small, result, input_grad
    )

    smalls = smalls.reshape(S, F, G // 2, 16, width)
    mod_grad = smalls[:, :, :, :6].astype(BF16)
    mod_grad_pair = lax.dynamic_index_in_dim(mod_grad, pair, 2, keepdims=False).reshape(T, 6, width)
    cond_rows = jnp.einsum("tje,jre->tr", mod_grad_pair, modulation_rows, preferred_element_type=F32)
    cond_rows = jnp.pad(cond_rows, ((0, 0), (0, 128 - half)))
    theirs_red, cond_all = settle(sizes, reduced, cond_rows)

    silu_every = silu_all.transpose(3, 2, 0, 1, 4).reshape(S * F * (G // 2), width)
    silu_mine = lax.dynamic_slice_in_dim(silu_every, (s * F + f) * rows, rows, 1)
    mod_weight_grads = jnp.einsum(
        "nr,nje->jre", silu_mine, mod_grad.reshape(-1, 6, width), preferred_element_type=F32
    )
    halves = [jnp.zeros_like(reduced), jnp.zeros_like(reduced)]
    for i in range(G):
        part = reduced if i == G - 1 else theirs_red[i]
        parity = (g + 1 + i) % 2
        halves = [halves[h] + jnp.where(parity == h, part, 0.0) for h in range(2)]
    linear_grads = jnp.concatenate(halves, axis=1)
    weight_grads = jnp.concatenate([linear_grads, mod_weight_grads], axis=0)

    new_master, new_one, new_two, new_copies = adam_slots(
        master, weight_grads, moment_one, moment_two, slot_block, slot_live
    )

    cond_full = cond_all[:, :, :half].reshape(S, F, 2, T, half)
    cond_full = cond_full.transpose(3, 0, 1, 2, 4).reshape(2, 2, F, width)
    cond_mine = lax.dynamic_index_in_dim(cond_full, core, 1, keepdims=False)
    cond_mine = lax.dynamic_index_in_dim(cond_mine, f, 1, keepdims=False)
    _, silu_pull = jax.vjp(jax.nn.silu, conditioning)
    cond_grad = silu_pull(cond_mine[:, None])[0]

    bias_sums = jnp.sum(smalls[:, :, :, 6:14], axis=(0, 1, 2))
    mod_sums = jnp.sum(mod_grad.astype(F32), axis=(0, 1, 2))
    bias_total = jnp.concatenate([bias_sums, mod_sums], axis=0)
    new_biases, new_bias_one, new_bias_two = adam_step(
        biases, bias_total, bias_moment_one, bias_moment_two, RATE_BIAS
    )
    return (
        out_lat[:, None],
        in_lat[:, None].astype(F32),
        cond_grad,
        new_master,
        new_one,
        new_two,
        new_copies,
        new_biases,
        new_bias_one,
        new_bias_two,
    )


def solution(mesh):
    sizes = (mesh.shape["seq"], mesh.shape["fsdp"], mesh.shape["grp"])
    tokens = P(None, ("fsdp", "grp"), "seq", None)
    vector = P(None, ("fsdp", "grp"), None)
    slots = P("grp", ("seq", "fsdp"), None)
    in_specs = (tokens, vector, tokens, P(), slots, slots, slots, P(), P(), P())
    out_specs = (tokens, tokens, vector, slots, slots, slots, slots, P(), P(), P())
    return jax.shard_map(
        functools.partial(per_device, sizes),
        mesh=mesh,
        in_specs=in_specs,
        out_specs=out_specs,
        check_vma=False,
    )
```

```python
import functools
import math

import jax
import jax.numpy as jnp
from jax import lax
from jax.experimental import pallas as pl
from jax.experimental.pallas import tpu as pltpu
from jax.sharding import PartitionSpec as P

HD = 64
STEP = 5
EPS_NORM = 1e-06
BETA_ONE = 0.5
BETA_TWO = 0.5
RATE_WEIGHT = 0.03
RATE_BIAS = 0.1
DECAY = 0.1
ADAM_EPS = 1e-08

MESH = pl.DeviceIdType.MESH
ANY = pl.BlockSpec(memory_space=pl.ANY)
VMEM = pl.BlockSpec(memory_space=pltpu.VMEM)
F32 = jnp.float32
BF16 = jnp.bfloat16
DMA = pltpu.SemaphoreType.DMA
LINEAR = 12


def params(cid, vmem=48):
    return pltpu.CompilerParams(
        collective_id=cid, has_side_effects=True, vmem_limit_bytes=vmem * 1024 * 1024
    )


def remote(src, dst, send_sem, recv_sem, device):
    return pltpu.make_async_remote_copy(
        src_ref=src,
        dst_ref=dst,
        send_sem=send_sem,
        recv_sem=recv_sem,
        device_id=device,
        device_id_type=MESH,
    )


class Place:
    def __init__(self, sizes):
        self.S, self.F, self.G = sizes
        self.s = lax.axis_index("seq")
        self.f = lax.axis_index("fsdp")
        self.g = lax.axis_index("grp")
        self.c = lax.rem(self.g, 2)
        self.base = self.g - self.c
        self.sib = self.base + 1 - self.c
        odd = lax.rem(self.s, 2)
        self.sx = self.s + 1 - 2 * odd
        self.sy = lax.rem(self.s + 2, 4)
        self.sa = self.sx + self.c * (self.sy - self.sx)
        self.sb = self.sy + self.c * (self.sx - self.sy)

    def sibling(self):
        return (self.s, self.f, self.sib)


def meet(devices):
    bar = pltpu.get_barrier_semaphore()
    for device in devices:
        pl.semaphore_signal(bar, inc=1, device_id=device, device_id_type=MESH)
    pl.semaphore_wait(bar, len(devices))


def meet_loop(count, device_of):
    bar = pltpu.get_barrier_semaphore()

    def one(i, carry):
        pl.semaphore_signal(bar, inc=1, device_id=device_of(i), device_id_type=MESH)
        return carry

    lax.fori_loop(1, count, one, 0)
    pl.semaphore_wait(bar, count - 1)


def slot_tables(owner_list, group, capacity):
    blocks = owner_list.shape[0]
    position = jnp.arange(blocks, dtype=jnp.int32)
    same = owner_list[:, None] == owner_list[None, :]
    before = position[None, :] < position[:, None]
    ranks = jnp.sum(jnp.where(same & before, 1, 0), axis=1).astype(jnp.int32)
    mine = owner_list == group
    slots = jnp.arange(capacity, dtype=jnp.int32)
    holds = mine[None, :] & (ranks[None, :] == slots[:, None])
    slot_block = jnp.sum(jnp.where(holds, position[None, :], 0), axis=1).astype(jnp.int32)
    slot_live = jnp.any(holds, axis=1).astype(jnp.int32)
    block_slot = jnp.where(mine, ranks, 0).astype(jnp.int32)
    return block_slot, mine.astype(jnp.int32), slot_block, slot_live


def pick_kernel(slot_ref, mine_ref, master_ref, out_ref, buf, sems):
    blocks = out_ref.shape[0]

    def fetch(b):
        return pltpu.make_async_copy(master_ref.at[slot_ref[b]], buf.at[b], sems.at[b])

    for b in range(blocks):
        fetch(b).start()
    for b in range(blocks):
        fetch(b).wait()
        out_ref[b] = jnp.where(mine_ref[b] > 0, buf[b], 0.0).astype(BF16)


def pick_blocks(master, block_slot, mine):
    blocks = block_slot.shape[0]
    rows, width = master.shape[1:]
    scalars = pl.BlockSpec(memory_space=pltpu.SMEM)
    return pl.pallas_call(
        pick_kernel,
        out_shape=jax.ShapeDtypeStruct((blocks, rows, width), BF16),
        in_specs=[scalars, scalars, ANY],
        out_specs=VMEM,
        scratch_shapes=[pltpu.VMEM((blocks, rows, width), F32), DMA((blocks,))],
        compiler_params=pltpu.CompilerParams(vmem_limit_bytes=32 * 1024 * 1024),
        name="pick_blocks",
    )(block_slot, mine, master)


def adam_step(param, grad, one, two, rate):
    next_one = BETA_ONE * one + (1.0 - BETA_ONE) * grad
    next_two = BETA_TWO * two + (1.0 - BETA_TWO) * grad * grad
    fix_one = 1.0 - BETA_ONE**STEP
    fix_two = 1.0 - BETA_TWO**STEP
    update = next_one / fix_one / (jnp.sqrt(next_two / fix_two) + ADAM_EPS)
    return (param - rate * (update + DECAY * param), next_one, next_two)


def adam_kernel(block_ref, live_ref, master, grad, one, two, o_master, o_one, o_two, o_copy):
    live = live_ref[pl.program_id(0)] > 0
    stepped, next_one, next_two = adam_step(
        master[...], grad[...].astype(F32), one[...], two[...], RATE_WEIGHT
    )
    new = jnp.where(live, stepped, master[...])
    o_master[...] = new
    o_one[...] = jnp.where(live, next_one, one[...])
    o_two[...] = jnp.where(live, next_two, two[...])
    o_copy[...] = new.astype(BF16)


def adam_slots(master, grads, one, two, slot_block, slot_live):
    slots, rows, width = master.shape
    by_slot = pl.BlockSpec((1, rows, width), lambda j, block, live: (j, 0, 0))
    by_block = pl.BlockSpec((1, rows, width), lambda j, block, live: (block[j], 0, 0))
    shape = jax.ShapeDtypeStruct(master.shape, F32)
    return pl.pallas_call(
        adam_kernel,
        out_shape=(shape, shape, shape, jax.ShapeDtypeStruct(master.shape, BF16)),
        grid_spec=pltpu.PrefetchScalarGridSpec(
            num_scalar_prefetch=2,
            grid=(slots,),
            in_specs=[by_slot, by_block, by_slot, by_slot],
            out_specs=(by_slot, by_slot, by_slot, by_slot),
        ),
        name="adam_slots",
    )(slot_block, slot_live, master, grads, one, two)


def share_kernel(sizes, blocks_ref, cond_ref, theirs_ref, conds_ref, ws, wr, cs, cr, ls):
    at = Place(sizes)
    half = theirs_ref.shape[2]
    count = at.F * at.G
    me = at.f * at.G + at.g

    def device_of(i):
        n = lax.rem(me + i, count)
        return (at.s, lax.div(n, at.G), lax.rem(n, at.G))

    meet_loop(count, device_of)

    def to_group(i):
        g = lax.rem(at.g + i, at.G)
        return remote(
            blocks_ref.at[:, pl.ds(pl.multiple_of(lax.rem(g, 2) * half, half), half), :],
            theirs_ref.at[at.G - 1 - i],
            ws.at[i],
            wr.at[at.G - 1 - i],
            (at.s, at.f, g),
        )

    def from_group(j):
        return remote(
            blocks_ref.at[:, pl.ds(0, half), :], theirs_ref.at[j], ws.at[0], wr.at[j], (at.s, at.f, at.g)
        )

    for i in range(1, at.G):
        to_group(i).start()
    own = pltpu.make_async_copy(cond_ref, conds_ref.at[me], ls)
    own.start()

    def cond_to(i):
        return remote(cond_ref, conds_ref.at[me], cs.at[i], cr.at[me], device_of(i))

    def cond_from(i):
        n = lax.rem(me + count - i, count)
        return remote(cond_ref, conds_ref.at[n], cs.at[i], cr.at[n], device_of(i))

    lax.fori_loop(1, count, lambda i, u: (cond_to(i).start(), u)[1], 0)
    own.wait()
    for i in range(1, at.G):
        to_group(i).wait_send()
        from_group(i - 1).wait_recv()
    lax.fori_loop(1, count, lambda i, u: (cond_to(i).wait_send(), u)[1], 0)
    lax.fori_loop(1, count, lambda i, u: (cond_from(i).wait_recv(), u)[1], 0)


def share(sizes, blocks, cond):
    S, F, G = sizes
    count, rows, width = blocks.shape
    return pl.pallas_call(
        functools.partial(share_kernel, sizes),
        out_shape=(
            jax.ShapeDtypeStruct((G - 1, count, rows // 2, width), BF16),
            jax.ShapeDtypeStruct((F * G,) + cond.shape, F32),
        ),
        in_specs=[ANY, ANY],
        out_specs=(ANY, ANY),
        scratch_shapes=[DMA((G,)), DMA((G,)), DMA((F * G,)), DMA((F * G,)), DMA],
        compiler_params=params(1),
        name="share_blocks",
    )(blocks, cond)


def token_move(at, j):
    return (2 * j + at.c, at.f, at.base + lax.div(at.s, 2))


ROWS = 256
CHUNK = 32
NT = (((1,), (1,)), ((), ()))
NN = (((1,), (0,)), ((), ()))
TN = (((0,), (0,)), ((), ()))


def dot(left, right, dims=NN):
    return lax.dot_general(left, right, dims, preferred_element_type=F32)


def loop(count, body):
    def one(i, carry):
        body(i)
        return carry

    lax.fori_loop(0, count, one, 0)


def aligned(index, size):
    return pl.ds(pl.multiple_of(index * size, size), size)


def norm_rows(values):
    centre = jnp.mean(values, axis=-1, keepdims=True)
    centred = values - centre
    spread = jnp.mean(centred * centred, axis=-1, keepdims=True)
    inverse = lax.rsqrt(spread + EPS_NORM)
    return centred * inverse, inverse


def attend_pair(q_ref, k_ref, v_ref, a_ref, lse_ref, pair):
    length = q_ref.shape[0]
    factor = 1.0 / math.sqrt(HD)
    for h in range(2):
        cols = slice((2 * pair + h) * HD, (2 * pair + h + 1) * HD)
        key = k_ref[:, cols]
        value = v_ref[:, cols]
        for r in range(0, length, ROWS):
            rows = slice(r, r + ROWS)
            scores = dot(q_ref[rows, cols], key, NT)
            high = jnp.max(scores, axis=1, keepdims=True)
            weights = jnp.exp((scores - high) * factor)
            total = jnp.sum(weights, axis=1, keepdims=True)
            out = dot(weights.astype(BF16), value, NN) / total
            a_ref[rows, cols] = out.astype(BF16)
            lse_ref[rows, cols] = jnp.broadcast_to(high * factor + jnp.log(total), (ROWS, HD))


def forward_kernel(sizes, *refs):
    (
        shard, modp, lat, cot, bias,
        bank, mod_o, tok_o, ctok, hid_o, heads_o, head_a_o, lse_o, att_o, branch_o, mid_o, hid2_o, up_o, act_o, mlp_o, res_o,
        modr, mod, xv, hid, stage, heads, head_a, lse, att, branch, mid, hid2, up, act, mlp, res, wbuf,
        ls, zs, zr, as_, ar, bs, br, cs, cr, ms, mr, ts, tr, tl, ws, xs, xr, save_sem,
    ) = refs
    at = Place(sizes)
    S, F = at.S, at.F
    K = shard.shape[0]
    T = 2 * S * F
    me = (at.s * F + at.f) * 2 + at.c
    quarter = lat.shape[1]
    tokens, width = xv.shape
    part = width // 2
    tiles = width // ROWS

    def device_of(i):
        n = lax.rem(me + i, T)
        return (lax.div(n, 2 * F), lax.rem(lax.div(n, 2), F), at.base + lax.rem(n, 2))

    meet_loop(T, device_of)

    def mod_to(i):
        n = lax.rem(me + i, T)
        return remote(modp.at[lax.div(n, 2)], modr.at[me], ms.at[i], mr.at[me], device_of(i))

    def mod_from(i):
        n = lax.rem(me + T - i, T)
        return remote(modp.at[0], modr.at[n], ms.at[i], mr.at[n], device_of(i))

    mod_own = pltpu.make_async_copy(modp.at[at.s * F + at.f], modr.at[me], tl.at[2])

    def tok_move(j, which):
        return (2 * j + at.c, at.f, at.base + lax.div(at.s, 2))

    def tok_refs(which):
        return ((lat, xv), (cot, ctok))[which]

    def tok_to(j, which):
        src, dst = tok_refs(which)
        place = aligned(lax.rem(at.s, 2), quarter)
        return remote(
            src.at[j], dst.at[place], ts.at[which, j], tr.at[which, lax.rem(at.s, 2)], tok_move(j, which)
        )

    def tok_from(j, which):
        src, dst = tok_refs(which)
        place = pl.ds(j * quarter, quarter)
        return remote(src.at[0], dst.at[place], ts.at[which, j], tr.at[which, j], tok_move(j, which))

    def tok_local(j, which):
        src, dst = tok_refs(which)
        return pltpu.make_async_copy(src.at[j], dst.at[aligned(lax.rem(at.s, 2), quarter)], tl.at[which])

    def stays(j):
        return (2 * j + at.c == at.s) & (lax.div(at.s, 2) == at.c)

    def comes(j):
        return jnp.logical_not((2 * at.c + j == at.s) & (lax.rem(at.s, 2) == at.c))

    def tok_start(which):
        for j in range(2):
            @pl.when(stays(j))
            def _():
                tok_local(j, which).start()

            @pl.when(jnp.logical_not(stays(j)))
            def _():
                tok_to(j, which).start()

    def tok_finish(which):
        for j in range(2):
            @pl.when(stays(j))
            def _():
                tok_local(j, which).wait()

            @pl.when(jnp.logical_not(stays(j)))
            def _():
                tok_to(j, which).wait_send()

            @pl.when(comes(j))
            def _():
                tok_from(j, which).wait_recv()

    def own(k):
        return pltpu.make_async_copy(shard.at[k], bank.at[k, at.s, at.f, at.c], ls.at[k])

    def z_to(k, i):
        f = lax.rem(at.f + i, F)
        return remote(
            shard.at[k], bank.at[k, at.s, at.f, at.c], zs.at[k, i], zr.at[k, i], (at.s, f, at.g)
        )

    def z_from(k, i):
        f = lax.rem(at.f + F - i, F)
        return remote(shard.at[k], bank.at[k, at.s, f, at.c], zs.at[k, i], zr.at[k, i], (at.s, f, at.g))

    def a_copy(k, s):
        line = bank.at[k, s, :, at.c]
        return remote(line, line, as_.at[k], ar.at[k], (at.sa, at.f, at.g))

    def b_copy(k, s, n):
        line = bank.at[k, s, :, at.c]
        return remote(line, line, bs.at[k, n], br.at[k, n], (at.sb, at.f, at.g))

    sd = S - 1 - at.s

    def c_copy(k, s, n, core):
        line = bank.at[k, s, :, core]
        return remote(line, line, cs.at[k, n], cr.at[k, n], at.sibling())

    def z_start(k):
        own(k).start()
        for i in range(1, F):
            z_to(k, i).start()

    def step(t):
        if t + 2 < K:
            z_start(t + 2)
        if t < K:
            own(t).wait()
            for i in range(1, F):
                z_from(t, i).wait_recv()
            a_copy(t, at.s).start()
            c_copy(t, at.s, 0, at.c).start()
        if 1 <= t <= K:
            a_copy(t - 1, at.sa).wait_recv()
            b_copy(t - 1, at.s, 0).start()
            b_copy(t - 1, at.sa, 1).start()
            c_copy(t - 1, at.sa, 1, at.c).start()
        if t >= 2:
            b_copy(t - 2, at.sb, 0).wait_recv()
            c_copy(t - 2, at.sb, 2, at.c).start()
            b_copy(t - 2, sd, 1).wait_recv()
            c_copy(t - 2, sd, 3, at.c).start()

    def fetch(k):
        return pltpu.make_async_copy(bank.at[k], wbuf.at[k % 2], ws.at[k % 2])

    def arrive(k):
        for n, s in enumerate((at.s, at.sb, at.sa, sd)):
            c_copy(k, s, n, 1 - at.c).wait_recv()
        fetch(k).start()
        fetch(k).wait()

    def weights(k, cols):
        return wbuf[k % 2, :, :, :, :, cols].reshape(width, ROWS)

    saves = []

    def save(src, dst):
        copy = pltpu.make_async_copy(src, dst, save_sem.at[len(saves)])
        copy.start()
        saves.append(copy)
        return copy

    def prepare():
        mod_own.wait()
        loop(T - 1, lambda i: mod_from(i + 1).wait_recv())
        total = modr[0]
        for n in range(1, T):
            total = total + modr[n]
        mod[...] = total
        mod[0:6] = mod[0:6] + bias[8:14]
        save(mod, mod_o)
        tok_finish(0)
        save(xv, tok_o)

        def one(i):
            rows = aligned(i, CHUNK)
            scaled, _ = norm_rows(xv[rows].astype(F32))
            hid[rows] = (scaled * (1.0 + mod[1:2]) + mod[0:1]).astype(BF16)

        loop(tokens // CHUNK, one)
        save(hid, hid_o)

    def swap(n):
        return remote(
            stage.at[n], heads.at[n, aligned(at.c, tokens)], xs.at[n], xr.at[n], at.sibling()
        )

    def swap_from(n):
        return remote(
            stage.at[n], heads.at[n, aligned(1 - at.c, tokens)], xs.at[n], xr.at[n], at.sibling()
        )

    def project(n, bias_row):
        def one(i, core, dst):
            tile = core * (part // ROWS) + i
            cols = aligned(tile, ROWS)
            value = dot(hid[...], weights(n, cols))
            if bias_row is not None:
                value = value + bias[bias_row : bias_row + 1, cols]
            dst[:, aligned(i, ROWS)] = value.astype(BF16)

        loop(part // ROWS, lambda i: one(i, 1 - at.c, stage.at[n]))
        swap(n).start()
        loop(part // ROWS, lambda i: one(i, at.c, heads.at[n, aligned(at.c, tokens)]))

    def attend_part(pair):
        if pair == 0:
            for n in range(3):
                swap_from(n).wait_recv()
                save(heads.at[n], heads_o.at[n])
        attend_pair(heads.at[0], heads.at[1], heads.at[2], head_a, lse, pair)

    def give_out():
        return remote(
            head_a.at[aligned(1 - at.c, tokens)], att.at[:, aligned(at.c, part)], xs.at[3], xr.at[3], at.sibling()
        )

    def give_from():
        return remote(
            head_a.at[aligned(at.c, tokens)], att.at[:, aligned(1 - at.c, part)], xs.at[3], xr.at[3], at.sibling()
        )

    def send_attended():
        give_out().start()
        att[:, aligned(at.c, part)] = head_a[aligned(at.c, tokens)]
        save(head_a, head_a_o)
        save(lse, lse_o)

    def output_projection():
        give_from().wait_recv()
        save(att, att_o)

        def one(i):
            cols = aligned(i, ROWS)
            branch[:, cols] = dot(att[...], weights(3, cols)) + bias[2:3, cols]

        loop(tiles, one)
        save(branch, branch_o)

        def rest(i):
            rows = aligned(i, CHUNK)
            middle = xv[rows].astype(F32) + mod[2:3] * branch[rows]
            mid[rows] = middle
            scaled, _ = norm_rows(middle)
            hid2[rows] = (scaled * (1.0 + mod[4:5]) + mod[3:4]).astype(BF16)

        loop(tokens // CHUNK, rest)
        save(mid, mid_o)
        save(hid2, hid2_o)

    up_saves = []

    def upper(j):
        if j >= 2:
            up_saves[j - 2].wait()

        def one(i):
            cols = aligned(i, ROWS)
            value = dot(hid2[...], weights(4 + j, cols)) + bias[3 + j : 4 + j, cols]
            up[j % 2, :, cols] = value
            act[j, :, cols] = jax.nn.gelu(value, approximate=True).astype(BF16)

        loop(tiles, one)
        up_saves.append(save(up.at[j % 2], up_o.at[j]))
        save(act.at[j], act_o.at[j])

    def lower(j):
        def one(i):
            cols = aligned(i, ROWS)
            value = dot(act[j], weights(8 + j, cols))
            mlp[:, cols] = value + (bias[7:8, cols] if j == 0 else mlp[:, cols])

        loop(tiles, one)

    def finish_forward():
        save(mlp, mlp_o)

        def one(i):
            rows = aligned(i, CHUNK)
            res[rows] = (mid[rows] + mod[5:6] * mlp[rows]).astype(BF16)

        loop(tokens // CHUNK, one)
        save(res, res_o)

    loop(T - 1, lambda i: mod_to(i + 1).start())
    mod_own.start()
    tok_start(0)
    z_start(0)
    z_start(1)
    for t in range(K + 2):
        step(t)
        if t == 1:
            prepare()
        if t in (2, 3, 4):
            arrive(t - 2)
            project(t - 2, (0, None, 1)[t - 2])
        if 5 <= t <= 8:
            attend_part(t - 5)
        if t == 8:
            send_attended()
            arrive(3)
            arrive(4)
        if t == 9:
            output_projection()
            upper(0)
            arrive(5)
            upper(1)
        if t == 10:
            tok_start(1)
        if t in (10, 11):
            arrive(t - 4)
            upper(t - 8)
        if t in (12, 13):
            if t == 12:
                arrive(8)
                lower(0)
                arrive(9)
                lower(1)
            arrive(t - 2)
            lower(t - 10)
    finish_forward()

    def finish(k):
        for i in range(1, F):
            z_to(k, i).wait_send()
        a_copy(k, at.s).wait_send()
        b_copy(k, at.s, 0).wait_send()
        b_copy(k, at.sa, 1).wait_send()
        for n, s in enumerate((at.s, at.sa, at.sb, sd)):
            c_copy(k, s, n, at.c).wait_send()

    loop(K, finish)
    for n in range(3):
        swap(n).wait_send()
    give_out().wait_send()
    tok_finish(1)
    loop(T - 1, lambda i: mod_to(i + 1).wait_send())
    for copy in saves:
        if not any(copy is done for done in up_saves[:2]):
            copy.wait()


def forward(sizes, shard, modp, lat, cot, bias):
    S, F, G = sizes
    K, half, width = shard.shape
    T = 2 * S * F
    tokens = 2 * lat.shape[1]
    length, part = 2 * tokens, width // 2
    low = lambda *shape: (shape, BF16)
    high = lambda *shape: (shape, F32)
    outs = (
        low(K, S, F, 2, half, width),
        high(8, width),
        low(tokens, width),
        low(tokens, width),
        low(tokens, width),
        low(3, length, part),
        low(length, part),
        high(length, part),
        low(tokens, width),
        high(tokens, width),
        high(tokens, width),
        low(tokens, width),
        high(4, tokens, width),
        low(4, tokens, width),
        high(tokens, width),
        low(tokens, width),
    )
    scratch = (
        high(T, 8, width),
        high(8, width),
        low(tokens, width),
        low(tokens, width),
        low(3, tokens, part),
        low(3, length, part),
        low(length, part),
        high(length, part),
        low(tokens, width),
        high(tokens, width),
        high(tokens, width),
        low(tokens, width),
        high(2, tokens, width),
        low(4, tokens, width),
        high(tokens, width),
        low(tokens, width),
        low(2, S, F, 2, half, width),
    )
    return pl.pallas_call(
        functools.partial(forward_kernel, sizes),
        out_shape=tuple(jax.ShapeDtypeStruct(*o) for o in outs),
        in_specs=[ANY] * 4 + [VMEM],
        out_specs=(ANY,) * len(outs),
        scratch_shapes=[pltpu.VMEM(*s) for s in scratch]
        + [
            DMA((K,)),
            DMA((K, F)),
            DMA((K, F)),
            DMA((K,)),
            DMA((K,)),
            DMA((K, 2)),
            DMA((K, 2)),
            DMA((K, 4)),
            DMA((K, 4)),
            DMA((T,)),
            DMA((T,)),
            DMA((2, 2)),
            DMA((2, 2)),
            DMA((3,)),
            DMA((2,)),
            DMA((4,)),
            DMA((4,)),
            DMA((24,)),
        ],
        compiler_params=params(2, 60),
        name="forward",
    )(shard, modp, lat, cot, bias)


def to_heads_kernel(sizes, count, *refs):
    at = Place(sizes)
    ins, outs, (ls, ss, rs) = refs[:count], refs[count : 2 * count], refs[2 * count :]
    tokens, width = ins[0].shape
    half = width // 2
    meet([at.sibling()])
    here = pl.ds(pl.multiple_of(at.c * tokens, tokens), tokens)
    there = pl.ds(pl.multiple_of((1 - at.c) * tokens, tokens), tokens)
    keep = pl.ds(pl.multiple_of(at.c * half, half), half)
    give = pl.ds(pl.multiple_of((1 - at.c) * half, half), half)
    for n in range(count):
        remote(ins[n].at[:, give], outs[n].at[here], ss.at[n], rs.at[n], at.sibling()).start()
        pltpu.make_async_copy(ins[n].at[:, keep], outs[n].at[here], ls.at[n]).start()
    for n in range(count):
        remote(ins[n].at[:, give], outs[n].at[here], ss.at[n], rs.at[n], at.sibling()).wait_send()
        remote(ins[n].at[:, give], outs[n].at[there], ss.at[n], rs.at[n], at.sibling()).wait_recv()
        pltpu.make_async_copy(ins[n].at[:, keep], outs[n].at[here], ls.at[n]).wait()


def to_tokens_kernel(sizes, count, *refs):
    at = Place(sizes)
    ins, outs, (ls, ss, rs) = refs[:count], refs[count : 2 * count], refs[2 * count :]
    tokens, half = ins[0].shape[0] // 2, ins[0].shape[1]
    meet([at.sibling()])
    keep = pl.ds(pl.multiple_of(at.c * tokens, tokens), tokens)
    give = pl.ds(pl.multiple_of((1 - at.c) * tokens, tokens), tokens)
    here = pl.ds(pl.multiple_of(at.c * half, half), half)
    there = pl.ds(pl.multiple_of((1 - at.c) * half, half), half)
    for n in range(count):
        remote(ins[n].at[give], outs[n].at[:, here], ss.at[n], rs.at[n], at.sibling()).start()
        pltpu.make_async_copy(ins[n].at[keep], outs[n].at[:, here], ls.at[n]).start()
    for n in range(count):
        remote(ins[n].at[give], outs[n].at[:, here], ss.at[n], rs.at[n], at.sibling()).wait_send()
        remote(ins[n].at[give], outs[n].at[:, there], ss.at[n], rs.at[n], at.sibling()).wait_recv()
        pltpu.make_async_copy(ins[n].at[keep], outs[n].at[:, here], ls.at[n]).wait()


def exchange(sizes, kernel, cid, name, arrays):
    count = len(arrays)
    rows, width = arrays[0].shape
    shape = (2 * rows, width // 2) if kernel is to_heads_kernel else (rows // 2, 2 * width)
    return pl.pallas_call(
        functools.partial(kernel, sizes, count),
        out_shape=tuple(jax.ShapeDtypeStruct(shape, BF16) for _ in arrays),
        in_specs=[ANY] * count,
        out_specs=(ANY,) * count,
        scratch_shapes=[DMA((count,)), DMA((count,)), DMA((count,))],
        compiler_params=params(cid),
        name=name,
    )(*arrays)


def attend_back_kernel(q_ref, k_ref, v_ref, a_ref, lse_ref, da_ref, dq_ref, dk_ref, dv_ref):
    length = q_ref.shape[0]
    factor = 1.0 / math.sqrt(HD)
    for h in range(2):
        cols = slice(h * HD, (h + 1) * HD)
        key = k_ref[:, cols]
        value = v_ref[:, cols]
        dk = jnp.zeros((HD, length), F32)
        dv = jnp.zeros((HD, length), F32)
        for r in range(0, length, ROWS):
            rows = slice(r, r + ROWS)
            query = q_ref[rows, cols]
            grad = da_ref[rows, cols]
            lse = lse_ref[rows, h * HD : h * HD + 1]
            scores = dot(query, key, NT)
            probs = jnp.exp(scores * factor - lse)
            row_dot = jnp.sum(
                grad.astype(F32) * a_ref[rows, cols].astype(F32), axis=1, keepdims=True
            )
            weight_grad = dot(grad, value, NT)
            score_grad = (probs * (weight_grad - row_dot)).astype(BF16)
            dq_ref[rows, cols] = (dot(score_grad, key, NN) * factor).astype(BF16)
            dk = dk + dot(query.T, score_grad, NN)
            dv = dv + dot(grad.T, probs.astype(BF16), NN)
        dk_ref[:, cols] = (dk * factor).T.astype(BF16)
        dv_ref[:, cols] = dv.T.astype(BF16)


def attend_back(q, k, v, a, lse, da):
    length, width = q.shape
    pair = pl.BlockSpec((length, 2 * HD), lambda n: (0, n))
    shape = jax.ShapeDtypeStruct((length, width), BF16)
    return pl.pallas_call(
        attend_back_kernel,
        out_shape=(shape, shape, shape),
        grid=(width // (2 * HD),),
        in_specs=[pair] * 6,
        out_specs=(pair, pair, pair),
        compiler_params=pltpu.CompilerParams(vmem_limit_bytes=48 * 1024 * 1024),
        name="attend_back",
    )(q, k, v, a, lse, da)


def reduce_kernel(
    sizes, grads, small, out_tok, in_tok, red, smalls, out_lat, in_lat,
    mine, r0, r1, r2, r3, total, sv, sw,
    ls, cs, cr, bs, br, as_, ar, zs, zr, os_, vs, vr, ws, wr, wl, ts, tr, tl,
):
    at = Place(sizes)
    S, F, G = sizes
    K = grads.shape[0]
    half, width = red.shape[1:]
    count = S * F * G
    me = (at.s * F + at.f) * G + at.g
    quarter = out_lat.shape[1]
    sd = S - 1 - at.s

    def device_of(i):
        n = lax.rem(me + i, count)
        return (lax.div(n, F * G), lax.rem(lax.div(n, G), F), lax.rem(n, G))

    meet_loop(count, device_of)

    def c_copy(k):
        return remote(grads.at[k, :, :, 1 - at.c], r0.at[k], cs.at[k], cr.at[k], at.sibling())

    def own(k):
        return pltpu.make_async_copy(grads.at[k, :, :, at.c], mine.at[k], ls.at[k])

    def b_copy(k, s, n):
        return remote(mine.at[k, s], r1.at[k, n], bs.at[k, n], br.at[k, n], (at.sb, at.f, at.g))

    def a_copy(k):
        return remote(mine.at[k, at.sa], r2.at[k], as_.at[k], ar.at[k], (at.sa, at.f, at.g))

    def z_to(k, i):
        f = lax.rem(at.f + i, F)
        return remote(mine.at[k, at.s, f], r3.at[k, i], zs.at[k, i], zr.at[k, i], (at.s, f, at.g))

    def out_copy(k):
        return pltpu.make_async_copy(total.at[k], red.at[k], os_.at[k])

    small_swap = remote(small, sv, vs, vr, at.sibling())
    small_swap.start()
    own(0).start()
    c_copy(0).start()
    own(1).start()
    c_copy(1).start()

    def back_device(j):
        return (2 * at.c + j, at.f, at.base + lax.rem(at.s, 2))

    def back_stays(j):
        return (2 * at.c + j == at.s) & (lax.rem(at.s, 2) == at.c)

    def back_comes(m):
        return jnp.logical_not((2 * m + at.c == at.s) & (lax.div(at.s, 2) == at.c))

    def back_to(j, which):
        src, dst = ((out_tok, out_lat), (in_tok, in_lat))[which]
        m = lax.div(at.s, 2)
        return remote(
            src.at[pl.ds(j * quarter, quarter)], dst.at[m], ts.at[which, j], tr.at[which, m], back_device(j)
        )

    def back_from(m, which):
        src, dst = ((out_tok, out_lat), (in_tok, in_lat))[which]
        return remote(
            src.at[pl.ds(0, quarter)], dst.at[m], ts.at[which, m], tr.at[which, m], back_device(m)
        )

    def back_local(j, which):
        src, dst = ((out_tok, out_lat), (in_tok, in_lat))[which]
        return pltpu.make_async_copy(
            src.at[pl.ds(j * quarter, quarter)], dst.at[lax.div(at.s, 2)], tl.at[which]
        )

    def back_start(which):
        for j in range(2):
            @pl.when(back_stays(j))
            def _():
                back_local(j, which).start()

            @pl.when(jnp.logical_not(back_stays(j)))
            def _():
                back_to(j, which).start()

    def back_finish(which):
        for j in range(2):
            @pl.when(back_stays(j))
            def _():
                back_local(j, which).wait()

            @pl.when(jnp.logical_not(back_stays(j)))
            def _():
                back_to(j, which).wait_send()

            @pl.when(back_comes(j))
            def _():
                back_from(j, which).wait_recv()

    small_swap.wait()
    sw[...] = small[...] + sv[...]

    chip = lax.div(me, 2)
    part = small.shape[0] // 2
    sent = pl.ds(pl.multiple_of(at.c * part, part), part)

    def small_device(i):
        n = lax.rem(me - at.c + 2 + i, count)
        return (lax.div(n, F * G), lax.rem(lax.div(n, G), F), lax.rem(n, G))

    def small_to(i):
        return remote(
            sw.at[sent], smalls.at[chip, sent], ws.at[i], wr.at[chip, at.c], small_device(i)
        )

    def small_from(i):
        n = lax.rem(me - at.c + 2 + i, count)
        there = lax.div(n, 2)
        core = lax.rem(n, 2)
        rows = pl.ds(pl.multiple_of(core * part, part), part)
        return remote(sw.at[rows], smalls.at[there, rows], ws.at[i], wr.at[there, core], small_device(i))

    small_own = pltpu.make_async_copy(sw, smalls.at[chip], wl)
    small_own.start()
    lax.fori_loop(0, count - 2, lambda i, u: (small_to(i).start(), u)[1], 0)

    def add_line(dst, src):
        def one(f, carry):
            dst[f] = (dst[f].astype(F32) + src[f].astype(F32)).astype(BF16)
            return carry

        lax.fori_loop(0, F, one, 0)

    def step(k, carry):
        @pl.when(k + 2 < K)
        def _():
            own(k + 2).start()
            c_copy(k + 2).start()

        @pl.when(k < K)
        def _():
            own(k).wait()
            c_copy(k).wait_recv()

            def one(n, carry):
                s = lax.div(n, F)
                f = lax.rem(n, F)
                mine[k, s, f] = (mine[k, s, f].astype(F32) + r0[k, s, f].astype(F32)).astype(BF16)
                return carry

            lax.fori_loop(0, S * F, one, 0)
            b_copy(k, at.sb, 0).start()
            b_copy(k, sd, 1).start()

        @pl.when((k >= 1) & (k <= K))
        def _():
            b_copy(k - 1, at.sb, 0).wait_recv()
            b_copy(k - 1, sd, 1).wait_recv()
            add_line(mine.at[k - 1, at.s], r1.at[k - 1, 0])
            add_line(mine.at[k - 1, at.sa], r1.at[k - 1, 1])
            a_copy(k - 1).start()

        @pl.when((k >= 2) & (k <= K + 1))
        def _():
            a_copy(k - 2).wait_recv()
            add_line(mine.at[k - 2, at.s], r2.at[k - 2])
            for i in range(1, F):
                z_to(k - 2, i).start()

        @pl.when(k >= 3)
        def _():
            for i in range(1, F):
                z_to(k - 3, i).wait_recv()
            value = mine[k - 3, at.s, at.f].astype(F32)
            for i in range(1, F):
                value = value + r3[k - 3, i].astype(F32)
            total[k - 3] = value
            out_copy(k - 3).start()

        return carry

    lax.fori_loop(0, K + 3, step, 0)
    back_start(0)
    back_start(1)

    def finish(k, carry):
        c_copy(k).wait_send()
        b_copy(k, at.sb, 0).wait_send()
        b_copy(k, sd, 1).wait_send()
        a_copy(k).wait_send()
        for i in range(1, F):
            z_to(k, i).wait_send()
        out_copy(k).wait()
        return carry

    lax.fori_loop(0, K, finish, 0)
    back_finish(0)
    back_finish(1)
    small_own.wait()
    lax.fori_loop(0, count - 2, lambda i, u: (small_to(i).wait_send(), u)[1], 0)
    lax.fori_loop(0, count - 2, lambda i, u: (small_from(i).wait_recv(), u)[1], 0)


def reduce_grads(sizes, grads, small, out_tok, in_tok):
    S, F, G = sizes
    K, _, _, _, half, width = grads.shape
    quarter = out_tok.shape[0] // 2
    count = S * F * G
    part = (K, F, half, width)
    return pl.pallas_call(
        functools.partial(reduce_kernel, sizes),
        out_shape=(
            jax.ShapeDtypeStruct((K, half, width), F32),
            jax.ShapeDtypeStruct((count // 2,) + small.shape, F32),
            jax.ShapeDtypeStruct((2, quarter, width), BF16),
            jax.ShapeDtypeStruct((2, quarter, width), BF16),
        ),
        in_specs=[ANY, VMEM, ANY, ANY],
        out_specs=(ANY,) * 4,
        scratch_shapes=[
            pltpu.VMEM((K, S, F, half, width), BF16),
            pltpu.VMEM((K, S, F, half, width), BF16),
            pltpu.VMEM((K, 2, F, half, width), BF16),
            pltpu.VMEM((K, F, half, width), BF16),
            pltpu.VMEM((K, F, half, width), BF16),
            pltpu.VMEM((K, half, width), F32),
            pltpu.VMEM(small.shape, F32),
            pltpu.VMEM(small.shape, F32),
            DMA((K,)),
            DMA((K,)),
            DMA((K,)),
            DMA((K, 2)),
            DMA((K, 2)),
            DMA((K,)),
            DMA((K,)),
            DMA((K, F)),
            DMA((K, F)),
            DMA((K,)),
            DMA,
            DMA,
            DMA((count,)),
            DMA((count // 2, 2)),
            DMA,
            DMA((2, 2)),
            DMA((2, 2)),
            DMA((2,)),
        ],
        compiler_params=params(7, 60),
        name="reduce_grads",
    )(grads, small, out_tok, in_tok)


def settle_kernel(sizes, red, cg, theirs, cgs, gs, gr, cs, cr, cl):
    at = Place(sizes)
    S, F, G = sizes
    T = 2 * S * F
    me = (at.s * F + at.f) * 2 + at.c
    others = [lax.rem(at.g + i, G) for i in range(1, G)]

    def device_of(i):
        n = lax.rem(me + i, T)
        return (lax.div(n, 2 * F), lax.rem(lax.div(n, 2), F), at.base + lax.rem(n, 2))

    bar = pltpu.get_barrier_semaphore()

    def greet(i, carry):
        pl.semaphore_signal(bar, inc=1, device_id=device_of(i), device_id_type=MESH)
        return carry

    lax.fori_loop(1, T, greet, 0)
    extra = 0
    if G > 2:
        for g in others:
            pl.semaphore_signal(bar, inc=1, device_id=(at.s, at.f, g), device_id_type=MESH)
        extra = G - 1
    pl.semaphore_wait(bar, T - 1 + extra)

    def to_group(i):
        return remote(
            red, theirs.at[G - 1 - i], gs.at[i], gr.at[G - 1 - i], (at.s, at.f, lax.rem(at.g + i, G))
        )

    for i in range(1, G):
        to_group(i).start()

    def cond_to(i):
        return remote(cg, cgs.at[me], cs.at[i], cr.at[me], device_of(i))

    def cond_from(i):
        n = lax.rem(me + T - i, T)
        return remote(cg, cgs.at[n], cs.at[i], cr.at[n], device_of(i))

    own = pltpu.make_async_copy(cg, cgs.at[me], cl)
    own.start()
    lax.fori_loop(1, T, lambda i, u: (cond_to(i).start(), u)[1], 0)
    own.wait()
    for i in range(1, G):
        to_group(i).wait()
    lax.fori_loop(1, T, lambda i, u: (cond_to(i).wait_send(), u)[1], 0)
    lax.fori_loop(1, T, lambda i, u: (cond_from(i).wait_recv(), u)[1], 0)


def settle(sizes, red, cg):
    S, F, G = sizes
    T = 2 * S * F
    return pl.pallas_call(
        functools.partial(settle_kernel, sizes),
        out_shape=(
            jax.ShapeDtypeStruct((G - 1,) + red.shape, F32),
            jax.ShapeDtypeStruct((T,) + cg.shape, F32),
        ),
        in_specs=[ANY, ANY],
        out_specs=(ANY, ANY),
        scratch_shapes=[DMA((G,)), DMA((G,)), DMA((T,)), DMA((T,)), DMA],
        compiler_params=params(8),
        name="settle_rows",
    )(red, cg)


def norm_back(grad, scaled, inverse, scale):
    inner = grad * (1.0 + scale)
    mean_inner = jnp.mean(inner, axis=-1, keepdims=True)
    mean_scaled = jnp.mean(inner * scaled, axis=-1, keepdims=True)
    part = inverse * (inner - mean_inner - scaled * mean_scaled)
    return part, jnp.sum(grad * scaled, axis=0), jnp.sum(grad, axis=0)


def matmul(left, right):
    return jnp.einsum("td,de->te", left, right, preferred_element_type=F32)


def matmul_t(left, right):
    return jnp.einsum("te,de->td", left, right, preferred_element_type=F32)


def weight_grad(left, right):
    return jnp.einsum("td,te->de", left, right, preferred_element_type=F32).astype(BF16)


def gelu_tanh(values):
    return jax.nn.gelu(values, approximate=True)


def per_device(
    sizes,
    latents,
    conditioning,
    cotangent,
    owner_list,
    master,
    moment_one,
    moment_two,
    biases,
    bias_moment_one,
    bias_moment_two,
):
    S, F, G = sizes
    capacity, rows, width = master.shape
    half = rows // 2
    blocks = owner_list.shape[0]
    s, f, g = lax.axis_index("seq"), lax.axis_index("fsdp"), lax.axis_index("grp")
    core = g % 2
    pair = g // 2
    T = S * F

    block_slot, mine, slot_block, slot_live = slot_tables(owner_list, g, capacity)
    picked = pick_blocks(master, block_slot, mine)
    cond_pad = jnp.pad(conditioning[:, 0], ((0, 6), (0, 0)))
    theirs, conds = share(sizes, picked, cond_pad)
    shard = lax.dynamic_slice_in_dim(picked, core * half, half, 1)
    for i in range(G - 1):
        shard = shard + theirs[i]
    linear, modulation_rows = shard[:LINEAR], shard[LINEAR:]

    silu_all = jax.nn.silu(conds[:, :2]).astype(BF16).reshape(F, G // 2, 2, 2, width)
    silu_pair = lax.dynamic_index_in_dim(silu_all, pair, 1, keepdims=False)
    silu_pair = silu_pair.transpose(2, 1, 0, 3).reshape(T, width)
    first_row = (s * F + f) * rows + core * half
    silu_rows = lax.dynamic_slice_in_dim(silu_pair, first_row, half, 1)
    mod_part = jnp.einsum("tr,jre->tje", silu_rows, modulation_rows, preferred_element_type=F32)
    mod_part = jnp.pad(mod_part, ((0, 0), (0, 2), (0, 0)))

    bias_rows = jnp.pad(biases, ((0, 2), (0, 0)))
    (
        bank, modulation, tokens, grad_low, hidden, heads, head_out, lse, attended, branch,
        middle, hidden_two, upper, active, mlp_out, result,
    ) = forward(sizes, linear, mod_part, latents[:, 0], cotangent[:, 0], bias_rows)
    bank = bank.reshape(LINEAR, width, width)
    shift_one, scale_one, gate_one, shift_two, scale_two, gate_two = (
        modulation[j : j + 1] for j in range(6)
    )
    head_query, head_key, head_value = heads[0], heads[1], heads[2]
    scaled_one, inverse_one = norm_rows(tokens.astype(F32))
    scaled_two, inverse_two = norm_rows(middle)
    _, gelu_pull = jax.vjp(gelu_tanh, upper)

    grad_out = grad_low.astype(F32)
    d_gate_two = jnp.sum(grad_out * mlp_out, axis=0)
    mlp_grad = (gate_two * grad_out).astype(BF16)
    active_grad = jnp.einsum("te,jde->jtd", mlp_grad, bank[8:12], preferred_element_type=F32)
    upper_grad = gelu_pull(active_grad)[0].astype(BF16)
    hidden_two_grad = jnp.einsum("jte,jde->td", upper_grad, bank[4:8], preferred_element_type=F32)
    middle_part, d_scale_two, d_shift_two = norm_back(
        hidden_two_grad, scaled_two, inverse_two, scale_two
    )
    middle_grad = grad_out + middle_part
    d_gate_one = jnp.sum(middle_grad * branch, axis=0)
    branch_grad = (gate_one * middle_grad).astype(BF16)
    attended_grad = matmul_t(branch_grad, bank[3]).astype(BF16)
    (head_grad,) = exchange(sizes, to_heads_kernel, 5, "grad_to_heads", (attended_grad,))
    head_grads = attend_back(head_query, head_key, head_value, head_out, lse, head_grad)
    query_grad, key_grad, value_grad = exchange(
        sizes, to_tokens_kernel, 6, "grads_to_tokens", head_grads
    )
    hidden_grad = (
        matmul_t(query_grad, bank[0]) + matmul_t(key_grad, bank[1]) + matmul_t(value_grad, bank[2])
    )
    values_part, d_scale_one, d_shift_one = norm_back(
        hidden_grad, scaled_one, inverse_one, scale_one
    )
    input_grad = (middle_grad + values_part).astype(BF16)

    grads = jnp.concatenate(
        [
            weight_grad(hidden, query_grad)[None],
            weight_grad(hidden, key_grad)[None],
            weight_grad(hidden, value_grad)[None],
            weight_grad(attended, branch_grad)[None],
            jnp.einsum("td,jte->jde", hidden_two, upper_grad, preferred_element_type=F32).astype(BF16),
            jnp.einsum("jtd,te->jde", active, mlp_grad, preferred_element_type=F32).astype(BF16),
        ],
        axis=0,
    )
    small = jnp.concatenate(
        [
            jnp.stack(
                [d_shift_one, d_scale_one, d_gate_one, d_shift_two, d_scale_two, d_gate_two]
            ),
            jnp.sum(query_grad.astype(F32), axis=0)[None],
            jnp.sum(value_grad.astype(F32), axis=0)[None],
            jnp.sum(branch_grad.astype(F32), axis=0)[None],
            jnp.sum(upper_grad.astype(F32), axis=1),
            jnp.sum(mlp_grad.astype(F32), axis=0)[None],
            jnp.zeros((2, width), F32),
        ],
        axis=0,
    )
    reduced, smalls, out_lat, in_lat = reduce_grads(
        sizes, grads.reshape(LINEAR, S, F, 2, half, width), small, result, input_grad
    )

    smalls = smalls.reshape(S, F, G // 2, 16, width)
    mod_grad = smalls[:, :, :, :6].astype(BF16)
    mod_grad_pair = lax.dynamic_index_in_dim(mod_grad, pair, 2, keepdims=False).reshape(T, 6, width)
    cond_rows = jnp.einsum("tje,jre->tr", mod_grad_pair, modulation_rows, preferred_element_type=F32)
    cond_rows = jnp.pad(cond_rows, ((0, 0), (0, 128 - half)))
    theirs_red, cond_all = settle(sizes, reduced, cond_rows)

    silu_every = silu_all.transpose(3, 2, 0, 1, 4).reshape(S * F * (G // 2), width)
    silu_mine = lax.dynamic_slice_in_dim(silu_every, (s * F + f) * rows, rows, 1)
    mod_weight_grads = jnp.einsum(
        "nr,nje->jre", silu_mine, mod_grad.reshape(-1, 6, width), preferred_element_type=F32
    )
    halves = [jnp.zeros_like(reduced), jnp.zeros_like(reduced)]
    for i in range(G):
        part = reduced if i == G - 1 else theirs_red[i]
        parity = (g + 1 + i) % 2
        halves = [halves[h] + jnp.where(parity == h, part, 0.0) for h in range(2)]
    linear_grads = jnp.concatenate(halves, axis=1)
    weight_grads = jnp.concatenate([linear_grads, mod_weight_grads], axis=0)

    new_master, new_one, new_two, new_copies = adam_slots(
        master, weight_grads, moment_one, moment_two, slot_block, slot_live
    )

    cond_full = cond_all[:, :, :half].reshape(S, F, 2, T, half)
    cond_full = cond_full.transpose(3, 0, 1, 2, 4).reshape(2, 2, F, width)
    cond_mine = lax.dynamic_index_in_dim(cond_full, core, 1, keepdims=False)
    cond_mine = lax.dynamic_index_in_dim(cond_mine, f, 1, keepdims=False)
    _, silu_pull = jax.vjp(jax.nn.silu, conditioning)
    cond_grad = silu_pull(cond_mine[:, None])[0]

    bias_sums = jnp.sum(smalls[:, :, :, 6:14], axis=(0, 1, 2))
    mod_sums = jnp.sum(mod_grad.astype(F32), axis=(0, 1, 2))
    bias_total = jnp.concatenate([bias_sums, mod_sums], axis=0)
    new_biases, new_bias_one, new_bias_two = adam_step(
        biases, bias_total, bias_moment_one, bias_moment_two, RATE_BIAS
    )
    return (
        out_lat[:, None],
        in_lat[:, None].astype(F32),
        cond_grad,
        new_master,
        new_one,
        new_two,
        new_copies,
        new_biases,
        new_bias_one,
        new_bias_two,
    )


def solution(mesh):
    sizes = (mesh.shape["seq"], mesh.shape["fsdp"], mesh.shape["grp"])
    tokens = P(None, ("fsdp", "grp"), "seq", None)
    vector = P(None, ("fsdp", "grp"), None)
    slots = P("grp", ("seq", "fsdp"), None)
    in_specs = (tokens, vector, tokens, P(), slots, slots, slots, P(), P(), P())
    out_specs = (tokens, tokens, vector, slots, slots, slots, slots, P(), P(), P())
    return jax.shard_map(
        functools.partial(per_device, sizes),
        mesh=mesh,
        in_specs=in_specs,
        out_specs=out_specs,
        check_vma=False,
    )
```

```python
import functools
import math

import jax
import jax.numpy as jnp
from jax import lax
from jax.experimental import pallas as pl
from jax.experimental.pallas import tpu as pltpu
from jax.sharding import PartitionSpec as P

HD = 64
STEP = 5
EPS_NORM = 1e-06
BETA_ONE = 0.5
BETA_TWO = 0.5
RATE_WEIGHT = 0.03
RATE_BIAS = 0.1
DECAY = 0.1
ADAM_EPS = 1e-08

MESH = pl.DeviceIdType.MESH
ANY = pl.BlockSpec(memory_space=pl.ANY)
VMEM = pl.BlockSpec(memory_space=pltpu.VMEM)
F32 = jnp.float32
BF16 = jnp.bfloat16
DMA = pltpu.SemaphoreType.DMA
LINEAR = 12


def params(cid, vmem=48):
    return pltpu.CompilerParams(
        collective_id=cid, has_side_effects=True, vmem_limit_bytes=vmem * 1024 * 1024
    )


def remote(src, dst, send_sem, recv_sem, device):
    return pltpu.make_async_remote_copy(
        src_ref=src,
        dst_ref=dst,
        send_sem=send_sem,
        recv_sem=recv_sem,
        device_id=device,
        device_id_type=MESH,
    )


class Place:
    def __init__(self, sizes):
        self.S, self.F, self.G = sizes
        self.s = lax.axis_index("seq")
        self.f = lax.axis_index("fsdp")
        self.g = lax.axis_index("grp")
        self.c = lax.rem(self.g, 2)
        self.base = self.g - self.c
        self.sib = self.base + 1 - self.c
        odd = lax.rem(self.s, 2)
        self.sx = self.s + 1 - 2 * odd
        self.sy = lax.rem(self.s + 2, 4)
        self.sa = self.sx + self.c * (self.sy - self.sx)
        self.sb = self.sy + self.c * (self.sx - self.sy)

    def sibling(self):
        return (self.s, self.f, self.sib)


def meet(devices):
    bar = pltpu.get_barrier_semaphore()
    for device in devices:
        pl.semaphore_signal(bar, inc=1, device_id=device, device_id_type=MESH)
    pl.semaphore_wait(bar, len(devices))


def meet_loop(count, device_of):
    bar = pltpu.get_barrier_semaphore()

    def one(i, carry):
        pl.semaphore_signal(bar, inc=1, device_id=device_of(i), device_id_type=MESH)
        return carry

    lax.fori_loop(1, count, one, 0)
    pl.semaphore_wait(bar, count - 1)


def slot_tables(owner_list, group, capacity):
    blocks = owner_list.shape[0]
    position = jnp.arange(blocks, dtype=jnp.int32)
    same = owner_list[:, None] == owner_list[None, :]
    before = position[None, :] < position[:, None]
    ranks = jnp.sum(jnp.where(same & before, 1, 0), axis=1).astype(jnp.int32)
    mine = owner_list == group
    slots = jnp.arange(capacity, dtype=jnp.int32)
    holds = mine[None, :] & (ranks[None, :] == slots[:, None])
    slot_block = jnp.sum(jnp.where(holds, position[None, :], 0), axis=1).astype(jnp.int32)
    slot_live = jnp.any(holds, axis=1).astype(jnp.int32)
    block_slot = jnp.where(mine, ranks, 0).astype(jnp.int32)
    return block_slot, mine.astype(jnp.int32), slot_block, slot_live


def pick_kernel(slot_ref, mine_ref, master_ref, out_ref, buf, sems):
    blocks = out_ref.shape[0]

    def fetch(b):
        return pltpu.make_async_copy(master_ref.at[slot_ref[b]], buf.at[b], sems.at[b])

    for b in range(blocks):
        fetch(b).start()
    for b in range(blocks):
        fetch(b).wait()
        out_ref[b] = jnp.where(mine_ref[b] > 0, buf[b], 0.0).astype(BF16)


def pick_blocks(master, block_slot, mine):
    blocks = block_slot.shape[0]
    rows, width = master.shape[1:]
    scalars = pl.BlockSpec(memory_space=pltpu.SMEM)
    return pl.pallas_call(
        pick_kernel,
        out_shape=jax.ShapeDtypeStruct((blocks, rows, width), BF16),
        in_specs=[scalars, scalars, ANY],
        out_specs=VMEM,
        scratch_shapes=[pltpu.VMEM((blocks, rows, width), F32), DMA((blocks,))],
        compiler_params=pltpu.CompilerParams(vmem_limit_bytes=32 * 1024 * 1024),
        name="pick_blocks",
    )(block_slot, mine, master)


def adam_step(param, grad, one, two, rate):
    next_one = BETA_ONE * one + (1.0 - BETA_ONE) * grad
    next_two = BETA_TWO * two + (1.0 - BETA_TWO) * grad * grad
    fix_one = 1.0 - BETA_ONE**STEP
    fix_two = 1.0 - BETA_TWO**STEP
    update = next_one / fix_one / (jnp.sqrt(next_two / fix_two) + ADAM_EPS)
    return (param - rate * (update + DECAY * param), next_one, next_two)


def adam_kernel(block_ref, live_ref, master, grad, one, two, o_master, o_one, o_two, o_copy):
    live = live_ref[pl.program_id(0)] > 0
    stepped, next_one, next_two = adam_step(
        master[...], grad[...].astype(F32), one[...], two[...], RATE_WEIGHT
    )
    new = jnp.where(live, stepped, master[...])
    o_master[...] = new
    o_one[...] = jnp.where(live, next_one, one[...])
    o_two[...] = jnp.where(live, next_two, two[...])
    o_copy[...] = new.astype(BF16)


def adam_slots(master, grads, one, two, slot_block, slot_live):
    slots, rows, width = master.shape
    by_slot = pl.BlockSpec((1, rows, width), lambda j, block, live: (j, 0, 0))
    by_block = pl.BlockSpec((1, rows, width), lambda j, block, live: (block[j], 0, 0))
    shape = jax.ShapeDtypeStruct(master.shape, F32)
    return pl.pallas_call(
        adam_kernel,
        out_shape=(shape, shape, shape, jax.ShapeDtypeStruct(master.shape, BF16)),
        grid_spec=pltpu.PrefetchScalarGridSpec(
            num_scalar_prefetch=2,
            grid=(slots,),
            in_specs=[by_slot, by_block, by_slot, by_slot],
            out_specs=(by_slot, by_slot, by_slot, by_slot),
        ),
        name="adam_slots",
    )(slot_block, slot_live, master, grads, one, two)


def share_kernel(sizes, blocks_ref, cond_ref, theirs_ref, conds_ref, ws, wr, cs, cr, ls):
    at = Place(sizes)
    half = theirs_ref.shape[2]
    count = at.F * at.G
    me = at.f * at.G + at.g

    def device_of(i):
        n = lax.rem(me + i, count)
        return (at.s, lax.div(n, at.G), lax.rem(n, at.G))

    meet_loop(count, device_of)

    def to_group(i):
        g = lax.rem(at.g + i, at.G)
        return remote(
            blocks_ref.at[:, pl.ds(pl.multiple_of(lax.rem(g, 2) * half, half), half), :],
            theirs_ref.at[at.G - 1 - i],
            ws.at[i],
            wr.at[at.G - 1 - i],
            (at.s, at.f, g),
        )

    def from_group(j):
        return remote(
            blocks_ref.at[:, pl.ds(0, half), :], theirs_ref.at[j], ws.at[0], wr.at[j], (at.s, at.f, at.g)
        )

    for i in range(1, at.G):
        to_group(i).start()
    own = pltpu.make_async_copy(cond_ref, conds_ref.at[me], ls)
    own.start()

    def cond_to(i):
        return remote(cond_ref, conds_ref.at[me], cs.at[i], cr.at[me], device_of(i))

    def cond_from(i):
        n = lax.rem(me + count - i, count)
        return remote(cond_ref, conds_ref.at[n], cs.at[i], cr.at[n], device_of(i))

    lax.fori_loop(1, count, lambda i, u: (cond_to(i).start(), u)[1], 0)
    own.wait()
    for i in range(1, at.G):
        to_group(i).wait_send()
        from_group(i - 1).wait_recv()
    lax.fori_loop(1, count, lambda i, u: (cond_to(i).wait_send(), u)[1], 0)
    lax.fori_loop(1, count, lambda i, u: (cond_from(i).wait_recv(), u)[1], 0)


def share(sizes, blocks, cond):
    S, F, G = sizes
    count, rows, width = blocks.shape
    return pl.pallas_call(
        functools.partial(share_kernel, sizes),
        out_shape=(
            jax.ShapeDtypeStruct((G - 1, count, rows // 2, width), BF16),
            jax.ShapeDtypeStruct((F * G,) + cond.shape, F32),
        ),
        in_specs=[ANY, ANY],
        out_specs=(ANY, ANY),
        scratch_shapes=[DMA((G,)), DMA((G,)), DMA((F * G,)), DMA((F * G,)), DMA],
        compiler_params=params(1),
        name="share_blocks",
    )(blocks, cond)


def token_move(at, j):
    return (2 * j + at.c, at.f, at.base + lax.div(at.s, 2))


ROWS = 256
CHUNK = 32
NT = (((1,), (1,)), ((), ()))
NN = (((1,), (0,)), ((), ()))
TN = (((0,), (0,)), ((), ()))


def dot(left, right, dims=NN):
    return lax.dot_general(left, right, dims, preferred_element_type=F32)


def loop(count, body):
    def one(i, carry):
        body(i)
        return carry

    lax.fori_loop(0, count, one, 0)


def aligned(index, size):
    return pl.ds(pl.multiple_of(index * size, size), size)


def norm_rows(values):
    centre = jnp.mean(values, axis=-1, keepdims=True)
    centred = values - centre
    spread = jnp.mean(centred * centred, axis=-1, keepdims=True)
    inverse = lax.rsqrt(spread + EPS_NORM)
    return centred * inverse, inverse


def attend_pair(q_ref, k_ref, v_ref, a_ref, lse_ref, pair):
    length = q_ref.shape[0]
    factor = 1.0 / math.sqrt(HD)
    for h in range(2):
        cols = slice((2 * pair + h) * HD, (2 * pair + h + 1) * HD)
        key = k_ref[:, cols]
        value = v_ref[:, cols]
        for r in range(0, length, ROWS):
            rows = slice(r, r + ROWS)
            scores = dot(q_ref[rows, cols], key, NT)
            high = jnp.max(scores, axis=1, keepdims=True)
            weights = jnp.exp((scores - high) * factor)
            total = jnp.sum(weights, axis=1, keepdims=True)
            out = dot(weights.astype(BF16), value, NN) / total
            a_ref[rows, cols] = out.astype(BF16)
            lse_ref[rows, cols] = jnp.broadcast_to(high * factor + jnp.log(total), (ROWS, HD))


def forward_kernel(sizes, *refs):
    (
        shard, modp, lat, cot, bias,
        bank, mod_o, tok_o, ctok, hid_o, heads_o, head_a_o, lse_o, att_o, branch_o, mid_o, hid2_o, up_o, act_o, mlp_o, res_o,
        modr, mod, xv, hid, stage, heads, head_a, lse, att, branch, mid, hid2, up, act, mlp, res, wbuf,
        ls, zs, zr, as_, ar, bs, br, cs, cr, ms, mr, ts, tr, tl, ws, xs, xr, save_sem,
    ) = refs
    at = Place(sizes)
    S, F = at.S, at.F
    K = shard.shape[0]
    T = 2 * S * F
    me = (at.s * F + at.f) * 2 + at.c
    quarter = lat.shape[1]
    tokens, width = xv.shape
    part = width // 2
    tiles = width // ROWS

    def device_of(i):
        n = lax.rem(me + i, T)
        return (lax.div(n, 2 * F), lax.rem(lax.div(n, 2), F), at.base + lax.rem(n, 2))

    meet_loop(T, device_of)

    def mod_to(i):
        n = lax.rem(me + i, T)
        return remote(modp.at[lax.div(n, 2)], modr.at[me], ms.at[i], mr.at[me], device_of(i))

    def mod_from(i):
        n = lax.rem(me + T - i, T)
        return remote(modp.at[0], modr.at[n], ms.at[i], mr.at[n], device_of(i))

    mod_own = pltpu.make_async_copy(modp.at[at.s * F + at.f], modr.at[me], tl.at[2])

    def tok_move(j, which):
        return (2 * j + at.c, at.f, at.base + lax.div(at.s, 2))

    def tok_refs(which):
        return ((lat, xv), (cot, ctok))[which]

    def tok_to(j, which):
        src, dst = tok_refs(which)
        place = aligned(lax.rem(at.s, 2), quarter)
        return remote(
            src.at[j], dst.at[place], ts.at[which, j], tr.at[which, lax.rem(at.s, 2)], tok_move(j, which)
        )

    def tok_from(j, which):
        src, dst = tok_refs(which)
        place = pl.ds(j * quarter, quarter)
        return remote(src.at[0], dst.at[place], ts.at[which, j], tr.at[which, j], tok_move(j, which))

    def tok_local(j, which):
        src, dst = tok_refs(which)
        return pltpu.make_async_copy(src.at[j], dst.at[aligned(lax.rem(at.s, 2), quarter)], tl.at[which])

    def stays(j):
        return (2 * j + at.c == at.s) & (lax.div(at.s, 2) == at.c)

    def comes(j):
        return jnp.logical_not((2 * at.c + j == at.s) & (lax.rem(at.s, 2) == at.c))

    def tok_start(which):
        for j in range(2):
            @pl.when(stays(j))
            def _():
                tok_local(j, which).start()

            @pl.when(jnp.logical_not(stays(j)))
            def _():
                tok_to(j, which).start()

    def tok_finish(which):
        for j in range(2):
            @pl.when(stays(j))
            def _():
                tok_local(j, which).wait()

            @pl.when(jnp.logical_not(stays(j)))
            def _():
                tok_to(j, which).wait_send()

            @pl.when(comes(j))
            def _():
                tok_from(j, which).wait_recv()

    def own(k):
        return pltpu.make_async_copy(shard.at[k], bank.at[k, at.s, at.f, at.c], ls.at[k])

    def z_to(k, i):
        f = lax.rem(at.f + i, F)
        return remote(
            shard.at[k], bank.at[k, at.s, at.f, at.c], zs.at[k, i], zr.at[k, i], (at.s, f, at.g)
        )

    def z_from(k, i):
        f = lax.rem(at.f + F - i, F)
        return remote(shard.at[k], bank.at[k, at.s, f, at.c], zs.at[k, i], zr.at[k, i], (at.s, f, at.g))

    def a_copy(k, s):
        line = bank.at[k, s, :, at.c]
        return remote(line, line, as_.at[k], ar.at[k], (at.sa, at.f, at.g))

    def b_copy(k, s, n):
        line = bank.at[k, s, :, at.c]
        return remote(line, line, bs.at[k, n], br.at[k, n], (at.sb, at.f, at.g))

    sd = S - 1 - at.s

    def c_copy(k, s, n, core):
        line = bank.at[k, s, :, core]
        return remote(line, line, cs.at[k, n], cr.at[k, n], at.sibling())

    def z_start(k):
        own(k).start()
        for i in range(1, F):
            z_to(k, i).start()

    def step(t):
        if t + 2 < K:
            z_start(t + 2)
        if t < K:
            own(t).wait()
            for i in range(1, F):
                z_from(t, i).wait_recv()
            a_copy(t, at.s).start()
            c_copy(t, at.s, 0, at.c).start()
        if 1 <= t <= K:
            a_copy(t - 1, at.sa).wait_recv()
            b_copy(t - 1, at.s, 0).start()
            b_copy(t - 1, at.sa, 1).start()
            c_copy(t - 1, at.sa, 1, at.c).start()
        if t >= 2:
            b_copy(t - 2, at.sb, 0).wait_recv()
            c_copy(t - 2, at.sb, 2, at.c).start()
            b_copy(t - 2, sd, 1).wait_recv()
            c_copy(t - 2, sd, 3, at.c).start()

    def fetch(k):
        return pltpu.make_async_copy(bank.at[k], wbuf.at[k % 2], ws.at[k % 2])

    def arrive(k):
        for n, s in enumerate((at.s, at.sb, at.sa, sd)):
            c_copy(k, s, n, 1 - at.c).wait_recv()
        fetch(k).start()
        fetch(k).wait()

    def weights(k, cols):
        return wbuf[k % 2, :, :, :, :, cols].reshape(width, ROWS)

    saves = []

    def save(src, dst):
        copy = pltpu.make_async_copy(src, dst, save_sem.at[len(saves)])
        copy.start()
        saves.append(copy)
        return copy

    def prepare():
        mod_own.wait()
        loop(T - 1, lambda i: mod_from(i + 1).wait_recv())
        total = modr[0]
        for n in range(1, T):
            total = total + modr[n]
        mod[...] = total
        mod[0:6] = mod[0:6] + bias[8:14]
        save(mod, mod_o)
        tok_finish(0)
        save(xv, tok_o)

        def one(i):
            rows = aligned(i, CHUNK)
            scaled, _ = norm_rows(xv[rows].astype(F32))
            hid[rows] = (scaled * (1.0 + mod[1:2]) + mod[0:1]).astype(BF16)

        loop(tokens // CHUNK, one)
        save(hid, hid_o)

    def swap(n):
        return remote(
            stage.at[n], heads.at[n, aligned(at.c, tokens)], xs.at[n], xr.at[n], at.sibling()
        )

    def swap_from(n):
        return remote(
            stage.at[n], heads.at[n, aligned(1 - at.c, tokens)], xs.at[n], xr.at[n], at.sibling()
        )

    def project(n, bias_row):
        def one(i, core, dst):
            tile = core * (part // ROWS) + i
            cols = aligned(tile, ROWS)
            value = dot(hid[...], weights(n, cols))
            if bias_row is not None:
                value = value + bias[bias_row : bias_row + 1, cols]
            dst[:, aligned(i, ROWS)] = value.astype(BF16)

        loop(part // ROWS, lambda i: one(i, 1 - at.c, stage.at[n]))
        swap(n).start()
        loop(part // ROWS, lambda i: one(i, at.c, heads.at[n, aligned(at.c, tokens)]))

    def attend_part(pair):
        if pair == 0:
            for n in range(3):
                swap_from(n).wait_recv()
                save(heads.at[n], heads_o.at[n])
        attend_pair(heads.at[0], heads.at[1], heads.at[2], head_a, lse, pair)

    def give_out():
        return remote(
            head_a.at[aligned(1 - at.c, tokens)], att.at[:, aligned(at.c, part)], xs.at[3], xr.at[3], at.sibling()
        )

    def give_from():
        return remote(
            head_a.at[aligned(at.c, tokens)], att.at[:, aligned(1 - at.c, part)], xs.at[3], xr.at[3], at.sibling()
        )

    def send_attended():
        give_out().start()
        att[:, aligned(at.c, part)] = head_a[aligned(at.c, tokens)]
        save(head_a, head_a_o)
        save(lse, lse_o)

    def output_projection():
        give_from().wait_recv()
        save(att, att_o)

        def one(i):
            cols = aligned(i, ROWS)
            branch[:, cols] = dot(att[...], weights(3, cols)) + bias[2:3, cols]

        loop(tiles, one)
        save(branch, branch_o)

        def rest(i):
            rows = aligned(i, CHUNK)
            middle = xv[rows].astype(F32) + mod[2:3] * branch[rows]
            mid[rows] = middle
            scaled, _ = norm_rows(middle)
            hid2[rows] = (scaled * (1.0 + mod[4:5]) + mod[3:4]).astype(BF16)

        loop(tokens // CHUNK, rest)
        save(mid, mid_o)
        save(hid2, hid2_o)

    up_saves = []

    def upper(j):
        if j >= 2:
            up_saves[j - 2].wait()

        def one(i):
            cols = aligned(i, ROWS)
            value = dot(hid2[...], weights(4 + j, cols)) + bias[3 + j : 4 + j, cols]
            up[j % 2, :, cols] = value
            act[j, :, cols] = jax.nn.gelu(value, approximate=True).astype(BF16)

        loop(tiles, one)
        up_saves.append(save(up.at[j % 2], up_o.at[j]))
        save(act.at[j], act_o.at[j])

    def lower(j):
        def one(i):
            cols = aligned(i, ROWS)
            value = dot(act[j], weights(8 + j, cols))
            mlp[:, cols] = value + (bias[7:8, cols] if j == 0 else mlp[:, cols])

        loop(tiles, one)

    def finish_forward():
        save(mlp, mlp_o)

        def one(i):
            rows = aligned(i, CHUNK)
            res[rows] = (mid[rows] + mod[5:6] * mlp[rows]).astype(BF16)

        loop(tokens // CHUNK, one)
        save(res, res_o)

    loop(T - 1, lambda i: mod_to(i + 1).start())
    mod_own.start()
    tok_start(0)
    z_start(0)
    z_start(1)
    for t in range(K + 2):
        step(t)
        if t == 1:
            prepare()
        if t in (2, 3, 4):
            arrive(t - 2)
            project(t - 2, (0, None, 1)[t - 2])
        if 5 <= t <= 8:
            attend_part(t - 5)
        if t == 8:
            send_attended()
            arrive(3)
            arrive(4)
        if t == 9:
            output_projection()
            upper(0)
            arrive(5)
            upper(1)
        if t == 10:
            tok_start(1)
        if t in (10, 11):
            arrive(t - 4)
            upper(t - 8)
        if t in (12, 13):
            if t == 12:
                arrive(8)
                lower(0)
                arrive(9)
                lower(1)
            arrive(t - 2)
            lower(t - 10)
    finish_forward()

    def finish(k):
        for i in range(1, F):
            z_to(k, i).wait_send()
        a_copy(k, at.s).wait_send()
        b_copy(k, at.s, 0).wait_send()
        b_copy(k, at.sa, 1).wait_send()
        for n, s in enumerate((at.s, at.sa, at.sb, sd)):
            c_copy(k, s, n, at.c).wait_send()

    loop(K, finish)
    for n in range(3):
        swap(n).wait_send()
    give_out().wait_send()
    tok_finish(1)
    loop(T - 1, lambda i: mod_to(i + 1).wait_send())
    for copy in saves:
        if not any(copy is done for done in up_saves[:2]):
            copy.wait()


def forward(sizes, shard, modp, lat, cot, bias):
    S, F, G = sizes
    K, half, width = shard.shape
    T = 2 * S * F
    tokens = 2 * lat.shape[1]
    length, part = 2 * tokens, width // 2
    low = lambda *shape: (shape, BF16)
    high = lambda *shape: (shape, F32)
    outs = (
        low(K, S, F, 2, half, width),
        high(8, width),
        low(tokens, width),
        low(tokens, width),
        low(tokens, width),
        low(3, length, part),
        low(length, part),
        high(length, part),
        low(tokens, width),
        high(tokens, width),
        high(tokens, width),
        low(tokens, width),
        high(4, tokens, width),
        low(4, tokens, width),
        high(tokens, width),
        low(tokens, width),
    )
    scratch = (
        high(T, 8, width),
        high(8, width),
        low(tokens, width),
        low(tokens, width),
        low(3, tokens, part),
        low(3, length, part),
        low(length, part),
        high(length, part),
        low(tokens, width),
        high(tokens, width),
        high(tokens, width),
        low(tokens, width),
        high(2, tokens, width),
        low(4, tokens, width),
        high(tokens, width),
        low(tokens, width),
        low(2, S, F, 2, half, width),
    )
    return pl.pallas_call(
        functools.partial(forward_kernel, sizes),
        out_shape=tuple(jax.ShapeDtypeStruct(*o) for o in outs),
        in_specs=[ANY] * 4 + [VMEM],
        out_specs=(ANY,) * len(outs),
        scratch_shapes=[pltpu.VMEM(*s) for s in scratch]
        + [
            DMA((K,)),
            DMA((K, F)),
            DMA((K, F)),
            DMA((K,)),
            DMA((K,)),
            DMA((K, 2)),
            DMA((K, 2)),
            DMA((K, 4)),
            DMA((K, 4)),
            DMA((T,)),
            DMA((T,)),
            DMA((2, 2)),
            DMA((2, 2)),
            DMA((3,)),
            DMA((2,)),
            DMA((4,)),
            DMA((4,)),
            DMA((24,)),
        ],
        compiler_params=params(2, 60),
        name="forward",
    )(shard, modp, lat, cot, bias)


RING = 4
ORDER = (8, 4, 9, 5, 10, 6, 11, 7, 3, 0, 1, 2)


def gelu_slope(values):
    scale = 0.7978845608
    square = values * values
    bend = jnp.tanh(scale * values * (1.0 + 0.044715 * square))
    return 0.5 * (1.0 + bend) + 0.5 * values * (1.0 - bend * bend) * (
        scale * (1.0 + 3.0 * 0.044715 * square)
    )


def attend_pair_back(q, k, v, a, lse_ref, da_ref, pair, dq_ref, dk_ref, dv_ref):
    length = q.shape[0]
    factor = 1.0 / math.sqrt(HD)
    for h in range(2):
        cols = slice(h * HD, (h + 1) * HD)
        grad_cols = slice((2 * pair + h) * HD, (2 * pair + h + 1) * HD)
        key = k[:, cols]
        value = v[:, cols]
        dk = jnp.zeros((HD, length), F32)
        dv = jnp.zeros((HD, length), F32)
        for r in range(0, length, ROWS):
            rows = slice(r, r + ROWS)
            query = q[rows, cols]
            grad = da_ref[rows, grad_cols]
            lse = lse_ref[rows, h * HD : h * HD + 1]
            scores = dot(query, key, NT)
            probs = jnp.exp(scores * factor - lse)
            row_dot = jnp.sum(grad.astype(F32) * a[rows, cols].astype(F32), axis=1, keepdims=True)
            weight_grad = dot(grad, value, NT)
            score_grad = (probs * (weight_grad - row_dot)).astype(BF16)
            dq_ref[rows, cols] = (dot(score_grad, key, NN) * factor).astype(BF16)
            dk = dk + dot(query.T, score_grad, NN)
            dv = dv + dot(grad.T, probs.astype(BF16), NN)
        dk_ref[:, cols] = (dk * factor).T.astype(BF16)
        dv_ref[:, cols] = dv.T.astype(BF16)


def backward_kernel(sizes, *refs):
    (
        bank, mod, tok, ctok, hid, heads, head_a, lse, att, branch, mid, hid2, up, act, mlp, res,
        red, smalls, out_lat, in_lat,
        mine, give, r0, r1, r2, r3, total, wbuf,
        ebuf, dfb, f0, f1, a0, a1, dub, dh2, h2b, stage, dah, qkva, lsev, dpair, dqt, accs, small, sv, sw,
        cs, cr, bs, br, as_, ar, zs, zr, os_, free, vs, vr, ws, wr, wl, ts, tr, tl, loads, xs, xr, ps, pr,
    ) = refs
    at = Place(sizes)
    S, F, G = sizes
    K = mine.shape[0]
    half = mine.shape[3]
    tokens, width = ebuf.shape
    part = width // 2
    band = width // S
    count = S * F * G
    me = (at.s * F + at.f) * G + at.g
    quarter = out_lat.shape[1]
    sd = S - 1 - at.s
    chunks = tokens // CHUNK

    def device_of(i):
        n = lax.rem(me + i, count)
        return (lax.div(n, F * G), lax.rem(lax.div(n, G), F), lax.rem(n, G))

    meet_loop(count, device_of)

    def c_copy(r):
        return remote(give.at[r % 2], r0.at[r % RING], cs.at[r], cr.at[r], at.sibling())

    def b_copy(r, s, n):
        return remote(mine.at[r, s], r1.at[r, n], bs.at[r, n], br.at[r, n], (at.sb, at.f, at.g))

    def a_copy(r):
        return remote(mine.at[r, at.sa], r2.at[r], as_.at[r], ar.at[r], (at.sa, at.f, at.g))

    def z_to(r, i):
        f = lax.rem(at.f + i, F)
        return remote(mine.at[r, at.s, f], r3.at[r, i], zs.at[r, i], zr.at[r, i], (at.s, f, at.g))

    def out_copy(r):
        return pltpu.make_async_copy(total.at[r % 2], red.at[ORDER[r]], os_.at[r])

    def add_line(dst, src):
        def one(f):
            dst[f] = (dst[f].astype(F32) + src[f].astype(F32)).astype(BF16)

        loop(F, one)

    def hop0(r):
        c_copy(r).wait_recv()
        loop(S, lambda s: add_line(mine.at[r, s], r0.at[r % RING, s]))
        if r + RING < K:
            pl.semaphore_signal(free, inc=1, device_id=at.sibling(), device_id_type=MESH)
        b_copy(r, at.sb, 0).start()
        b_copy(r, sd, 1).start()

    def hop1(r):
        b_copy(r, at.sb, 0).wait_recv()
        b_copy(r, sd, 1).wait_recv()
        add_line(mine.at[r, at.sa], r1.at[r, 1])
        a_copy(r).start()
        add_line(mine.at[r, at.s], r1.at[r, 0])

    def hop2(r):
        a_copy(r).wait_recv()
        add_line(mine.at[r, at.s], r2.at[r])
        for i in range(1, F):
            z_to(r, i).start()

    def hop3(r):
        for i in range(1, F):
            z_to(r, i).wait_recv()
        if r >= 2:
            out_copy(r - 2).wait()
        value = mine[r, at.s, at.f].astype(F32)
        for i in range(1, F):
            value = value + r3[r, i].astype(F32)
        total[r % 2] = value
        out_copy(r).start()

    def produce(r, left, right):
        if r >= 2:
            c_copy(r - 2).wait_send()

        def one(n):
            s = lax.div(n, width // 512)
            cols = aligned(lax.rem(n, width // 512), 512)
            value = dot(left[:, aligned(s, band)], right[:, cols], TN)
            value = value.astype(BF16).reshape(F, 2, half, 512)
            first, second = value[:, 0], value[:, 1]
            mine[r, s, :, :, cols] = jnp.where(at.c == 0, first, second)
            give[r % 2, s, :, :, cols] = jnp.where(at.c == 0, second, first)

        loop(S * (width // 512), one)
        if r >= RING:
            pl.semaphore_wait(free, 1)
        c_copy(r).start()

    def back_device(j):
        return (2 * at.c + j, at.f, at.base + lax.rem(at.s, 2))

    def back_stays(j):
        return (2 * at.c + j == at.s) & (lax.rem(at.s, 2) == at.c)

    def back_comes(m):
        return jnp.logical_not((2 * m + at.c == at.s) & (lax.div(at.s, 2) == at.c))

    def back_refs(which):
        return ((res, out_lat), (dfb, in_lat))[which]

    def back_to(j, which):
        src, dst = back_refs(which)
        m = lax.div(at.s, 2)
        return remote(
            src.at[pl.ds(j * quarter, quarter)], dst.at[m], ts.at[which, j], tr.at[which, m], back_device(j)
        )

    def back_from(m, which):
        src, dst = back_refs(which)
        return remote(
            src.at[pl.ds(0, quarter)], dst.at[m], ts.at[which, m], tr.at[which, m], back_device(m)
        )

    def back_local(j, which):
        src, dst = back_refs(which)
        return pltpu.make_async_copy(
            src.at[pl.ds(j * quarter, quarter)], dst.at[lax.div(at.s, 2)], tl.at[which]
        )

    def back_start(which):
        for j in range(2):
            @pl.when(back_stays(j))
            def _():
                back_local(j, which).start()

            @pl.when(jnp.logical_not(back_stays(j)))
            def _():
                back_to(j, which).start()

    def back_finish(which):
        for j in range(2):
            @pl.when(back_stays(j))
            def _():
                back_local(j, which).wait()

            @pl.when(jnp.logical_not(back_stays(j)))
            def _():
                back_to(j, which).wait_send()

            @pl.when(back_comes(j))
            def _():
                back_from(j, which).wait_recv()

    def load(src, dst, n):
        return pltpu.make_async_copy(src, dst, loads.at[n])

    def load_weight(k, slot):
        return load(bank.at[k], wbuf.at[slot], slot)

    ups, acts = (f0, f1), (a0, a1)

    def load_up(j):
        return load(up.at[j], ups[j % 2], 2 + j % 2)

    def load_act(j):
        return load(act.at[j], acts[j % 2], 4 + j % 2)

    def load_pair(p):
        cols = pl.ds(p * 2 * HD, 2 * HD)
        slot = p % 2
        return [load(heads.at[n, :, cols], qkva.at[slot, n], 10 + 5 * slot + n) for n in range(3)] + [
            load(head_a.at[:, cols], qkva.at[slot, 3], 13 + 5 * slot),
            load(lse.at[:, cols], lsev.at[slot], 14 + 5 * slot),
        ]

    def rows_of(slot, n):
        return wbuf[slot, n].reshape(band, width)

    def add_rows(i, value, cols=slice(None)):
        accs[i, :, cols] += value.reshape(-1, 8, value.shape[-1]).sum(axis=0)

    back_start(0)
    load_e, load_mlp, load_h2 = load(ctok, ebuf, 6), load(mlp, dh2, 7), load(hid2, h2b, 8)
    for copy in (load_e, load_mlp):
        copy.start()
    load_weight(8, 0).start()
    load_act(0).start()
    load_up(0).start()
    load_h2.start()
    load_weight(4, 1).start()
    load_up(1).start()
    load_act(1).start()
    accs[...] = jnp.zeros_like(accs)
    load_e.wait()
    load_mlp.wait()

    def start_rows(i):
        rows = aligned(i, CHUNK)
        grad = ebuf[rows].astype(F32)
        add_rows(5, grad * dh2[rows])
        low = (mod[5:6] * grad).astype(BF16)
        dfb[rows] = low
        add_rows(13, low.astype(F32))

    loop(chunks, start_rows)

    def active_back(j):
        load_weight(8 + j, 0).wait()
        load_up(j).wait()

        def one(n):
            cols = aligned(n, band)
            value = dot(dfb[...], rows_of(0, n), NT) * gelu_slope(ups[j % 2][:, cols])
            low = value.astype(BF16)
            dub[:, cols] = low
            add_rows(9 + j, low.astype(F32), cols)

        loop(S, one)
        load_weight(9 + j if j < 3 else 3, 0).start()
        if j < 2:
            load_up(j + 2).start()

    def hidden_back(j):
        load_weight(4 + j, 1).wait()

        def one(n):
            cols = aligned(n, band)
            value = dot(dub[...], rows_of(1, n), NT)
            dh2[:, cols] = value if j == 0 else dh2[:, cols] + value

        loop(S, one)
        load_weight(5 + j if j < 3 else 0, 1).start()

    def product_eight(j):
        load_act(j).wait()
        produce(2 * j, acts[j % 2], dfb)
        if j < 2:
            load_act(j + 2).start()

    def product_four(j):
        if j == 0:
            load_h2.wait()
        produce(2 * j + 1, h2b, dub)

    load_mid, load_branch = load(mid, f0, 2), load(branch, f1, 3)
    load_att, load_hid, load_x = load(att, a0, 4), load(hid, h2b, 8), load(tok, ebuf, 6)

    def middle_back():
        load_mid.wait()
        load_branch.wait()

        def one(i):
            rows = aligned(i, CHUNK)
            scaled, inverse = norm_rows(f0[rows])
            grad = dh2[rows]
            inner = grad * (1.0 + mod[4:5])
            mean_inner = jnp.mean(inner, axis=-1, keepdims=True)
            mean_scaled = jnp.mean(inner * scaled, axis=-1, keepdims=True)
            value = ebuf[rows].astype(F32) + inverse * (inner - mean_inner - scaled * mean_scaled)
            add_rows(4, grad * scaled)
            add_rows(3, grad)
            dh2[rows] = value
            add_rows(2, value * f1[rows])
            low = (mod[2:3] * value).astype(BF16)
            dfb[rows] = low
            add_rows(8, low.astype(F32))

        loop(chunks, one)
        load_x.start()

    def swap_da(here):
        return remote(stage, dah.at[aligned(here, tokens)], xs, xr, at.sibling())

    def attended_back():
        load_weight(3, 0).wait()

        def one(i, core, dst):
            value = dot(dfb[...], rows_of(0, core * (S // 2) + i), NT)
            dst[:, aligned(i, band)] = value.astype(BF16)

        loop(S // 2, lambda i: one(i, 1 - at.c, stage))
        swap_da(at.c).start()
        loop(S // 2, lambda i: one(i, at.c, dah.at[aligned(at.c, tokens)]))
        load_weight(1, 0).start()

    def pair_to(p, n, core):
        rows = aligned(1 - at.c, tokens)
        cols = pl.ds(pl.multiple_of(core * part + p * 2 * HD, 2 * HD), 2 * HD)
        return remote(
            dpair.at[p % 2, n, rows], dqt.at[n, :, cols], ps.at[p, n], pr.at[p, n], at.sibling()
        )

    def attend_back_part(p):
        if p == 0:
            swap_da(1 - at.c).wait_recv()
        for copy in load_pair(p):
            copy.wait()
        if p >= 2:
            for n in range(3):
                pair_to(p - 2, n, at.c).wait_send()
        slot = p % 2
        attend_pair_back(
            qkva.at[slot, 0], qkva.at[slot, 1], qkva.at[slot, 2], qkva.at[slot, 3], lsev.at[slot], dah, p,
            dpair.at[slot, 0], dpair.at[slot, 1], dpair.at[slot, 2],
        )
        cols = pl.ds(pl.multiple_of(at.c * part + p * 2 * HD, 2 * HD), 2 * HD)
        for n in range(3):
            pair_to(p, n, at.c).start()
            dqt[n, :, cols] = dpair[slot, n, aligned(at.c, tokens)]
        if p + 2 < part // (2 * HD):
            for copy in load_pair(p + 2):
                copy.start()

    def pairs_arrive():
        for p in range(part // (2 * HD)):
            for n in range(3):
                pair_to(p, n, 1 - at.c).wait_recv()

        def one(i):
            rows = aligned(i, CHUNK)
            add_rows(6, dqt[0, rows].astype(F32))
            add_rows(7, dqt[2, rows].astype(F32))

        loop(chunks, one)

    def first_back(k, slot, start):
        load_weight(k, slot).wait()

        def one(n):
            cols = aligned(n, band)
            value = dot(dqt[k], rows_of(slot, n), NT)
            f0[:, cols] = value if start else f0[:, cols] + value

        loop(S, one)

    def input_back():
        load_x.wait()

        def one(i):
            rows = aligned(i, CHUNK)
            scaled, inverse = norm_rows(ebuf[rows].astype(F32))
            grad = f0[rows]
            inner = grad * (1.0 + mod[1:2])
            mean_inner = jnp.mean(inner, axis=-1, keepdims=True)
            mean_scaled = jnp.mean(inner * scaled, axis=-1, keepdims=True)
            value = dh2[rows] + inverse * (inner - mean_inner - scaled * mean_scaled)
            add_rows(1, grad * scaled)
            add_rows(0, grad)
            dfb[rows] = value.astype(BF16)

        loop(chunks, one)

    small_swap = remote(small, sv, vs, vr, at.sibling())
    chip = lax.div(me, 2)
    rows_each = small.shape[0] // 2
    sent = aligned(at.c, rows_each)

    def small_number(i):
        return lax.rem(me - at.c + 2 + i, count)

    def small_to(i):
        n = small_number(i)
        device = (lax.div(n, F * G), lax.rem(lax.div(n, G), F), lax.rem(n, G))
        return remote(sw.at[sent], smalls.at[chip, sent], ws.at[i], wr.at[chip, at.c], device)

    def small_from(i):
        n = small_number(i)
        there, core = lax.div(n, 2), lax.rem(n, 2)
        rows = aligned(core, rows_each)
        return remote(sw.at[rows], smalls.at[there, rows], ws.at[i], wr.at[there, core], at.sibling())

    small_own = pltpu.make_async_copy(sw, smalls.at[chip], wl)

    active_back(0)
    product_eight(0)
    hidden_back(0)
    hop0(0)
    product_four(0)
    active_back(1)
    hop0(1)
    product_eight(1)
    hidden_back(1)
    hop0(2)
    product_four(1)
    hop1(0)
    active_back(2)
    load_mid.start()
    hop0(3)
    product_eight(2)
    hidden_back(2)
    hop0(4)
    hop1(1)
    load_att.start()
    product_four(2)
    hop2(0)
    active_back(3)
    load_branch.start()
    hop0(5)
    product_eight(3)
    hidden_back(3)
    hop0(6)
    hop1(2)
    product_four(3)
    load_hid.start()
    hop2(1)
    middle_back()
    hop0(7)
    hop1(3)
    hop3(0)
    attended_back()
    for copy in load_pair(0) + load_pair(1):
        copy.start()
    load_att.wait()
    produce(8, a0, dfb)
    hop2(2)
    attend_back_part(0)
    hop0(8)
    hop1(4)
    hop3(1)
    attend_back_part(1)
    hop1(5)
    hop2(3)
    hop3(2)
    attend_back_part(2)
    hop1(6)
    hop2(4)
    hop3(3)
    attend_back_part(3)
    hop1(7)
    hop2(5)
    hop3(4)
    pairs_arrive()
    load_hid.wait()
    produce(9, h2b, dqt.at[0])
    hop2(6)
    hop1(8)
    produce(10, h2b, dqt.at[1])
    hop0(9)
    hop3(5)
    produce(11, h2b, dqt.at[2])
    hop0(10)
    hop2(7)
    first_back(0, 1, True)
    hop0(11)
    load_weight(2, 1).start()
    first_back(1, 0, False)
    hop1(9)
    hop2(8)
    hop3(6)
    first_back(2, 1, False)
    input_back()
    back_start(1)
    small[...] = jnp.zeros_like(small)
    small[0:14] = accs[...].sum(axis=1)
    small_swap.start()
    hop1(10)
    small_swap.wait()
    sw[...] = small[...] + sv[...]
    small_own.start()
    loop(count - 2, lambda i: small_to(i).start())
    hop2(9)
    hop3(7)
    hop1(11)
    hop2(10)
    hop3(8)
    hop3(9)
    hop2(11)
    hop3(10)
    hop3(11)

    swap_da(at.c).wait_send()
    for p in (2, 3):
        for n in range(3):
            pair_to(p, n, at.c).wait_send()
    for r in range(K):
        if r >= K - 2:
            c_copy(r).wait_send()
            out_copy(r).wait()
        b_copy(r, at.sb, 0).wait_send()
        b_copy(r, sd, 1).wait_send()
        a_copy(r).wait_send()
        for i in range(1, F):
            z_to(r, i).wait_send()
    back_finish(0)
    back_finish(1)
    small_own.wait()
    loop(count - 2, lambda i: small_to(i).wait_send())
    loop(count - 2, lambda i: small_from(i).wait_recv())


def backward(sizes, *arrays):
    S, F, G = sizes
    bank, tok = arrays[0], arrays[2]
    K, _, _, _, half, width = bank.shape
    tokens = tok.shape[0]
    quarter, part, length = tokens // 2, width // 2, 2 * tokens
    count = S * F * G
    low = lambda *shape: pltpu.VMEM(shape, BF16)
    high = lambda *shape: pltpu.VMEM(shape, F32)
    specs = [ANY] * len(arrays)
    specs[1] = VMEM
    return pl.pallas_call(
        functools.partial(backward_kernel, sizes),
        out_shape=(
            jax.ShapeDtypeStruct((K, half, width), F32),
            jax.ShapeDtypeStruct((count // 2, 16, width), F32),
            jax.ShapeDtypeStruct((2, quarter, width), BF16),
            jax.ShapeDtypeStruct((2, quarter, width), BF16),
        ),
        in_specs=specs,
        out_specs=(ANY,) * 4,
        scratch_shapes=[
            low(K, S, F, half, width),
            low(2, S, F, half, width),
            low(RING, S, F, half, width),
            low(K, 2, F, half, width),
            low(K, F, half, width),
            low(K, F, half, width),
            high(2, half, width),
            low(2, S, F, 2, half, width),
            low(tokens, width),
            low(tokens, width),
            high(tokens, width),
            high(tokens, width),
            low(tokens, width),
            low(tokens, width),
            low(tokens, width),
            high(tokens, width),
            low(tokens, width),
            low(tokens, part),
            low(length, part),
            low(2, 4, length, 2 * HD),
            high(2, length, 2 * HD),
            low(2, 3, length, 2 * HD),
            low(3, tokens, width),
            high(14, 8, width),
            high(16, width),
            high(16, width),
            high(16, width),
            DMA((K,)),
            DMA((K,)),
            DMA((K, 2)),
            DMA((K, 2)),
            DMA((K,)),
            DMA((K,)),
            DMA((K, F)),
            DMA((K, F)),
            DMA((K,)),
            pltpu.SemaphoreType.REGULAR,
            DMA,
            DMA,
            DMA((count,)),
            DMA((count // 2, 2)),
            DMA,
            DMA((2, 2)),
            DMA((2, 2)),
            DMA((2,)),
            DMA((20,)),
            DMA,
            DMA,
            DMA((4, 3)),
            DMA((4, 3)),
        ],
        compiler_params=params(3, 63),
        name="backward",
    )(*arrays)


def settle_kernel(sizes, red, cg, theirs, cgs, gs, gr, cs, cr, cl):
    at = Place(sizes)
    S, F, G = sizes
    T = 2 * S * F
    me = (at.s * F + at.f) * 2 + at.c
    others = [lax.rem(at.g + i, G) for i in range(1, G)]

    def device_of(i):
        n = lax.rem(me + i, T)
        return (lax.div(n, 2 * F), lax.rem(lax.div(n, 2), F), at.base + lax.rem(n, 2))

    bar = pltpu.get_barrier_semaphore()

    def greet(i, carry):
        pl.semaphore_signal(bar, inc=1, device_id=device_of(i), device_id_type=MESH)
        return carry

    lax.fori_loop(1, T, greet, 0)
    extra = 0
    if G > 2:
        for g in others:
            pl.semaphore_signal(bar, inc=1, device_id=(at.s, at.f, g), device_id_type=MESH)
        extra = G - 1
    pl.semaphore_wait(bar, T - 1 + extra)

    def to_group(i):
        return remote(
            red, theirs.at[G - 1 - i], gs.at[i], gr.at[G - 1 - i], (at.s, at.f, lax.rem(at.g + i, G))
        )

    for i in range(1, G):
        to_group(i).start()

    def cond_to(i):
        return remote(cg, cgs.at[me], cs.at[i], cr.at[me], device_of(i))

    def cond_from(i):
        n = lax.rem(me + T - i, T)
        return remote(cg, cgs.at[n], cs.at[i], cr.at[n], device_of(i))

    own = pltpu.make_async_copy(cg, cgs.at[me], cl)
    own.start()
    lax.fori_loop(1, T, lambda i, u: (cond_to(i).start(), u)[1], 0)
    own.wait()
    for i in range(1, G):
        to_group(i).wait()
    lax.fori_loop(1, T, lambda i, u: (cond_to(i).wait_send(), u)[1], 0)
    lax.fori_loop(1, T, lambda i, u: (cond_from(i).wait_recv(), u)[1], 0)


def settle(sizes, red, cg):
    S, F, G = sizes
    T = 2 * S * F
    return pl.pallas_call(
        functools.partial(settle_kernel, sizes),
        out_shape=(
            jax.ShapeDtypeStruct((G - 1,) + red.shape, F32),
            jax.ShapeDtypeStruct((T,) + cg.shape, F32),
        ),
        in_specs=[ANY, ANY],
        out_specs=(ANY, ANY),
        scratch_shapes=[DMA((G,)), DMA((G,)), DMA((T,)), DMA((T,)), DMA],
        compiler_params=params(4),
        name="settle_rows",
    )(red, cg)


def per_device(
    sizes,
    latents,
    conditioning,
    cotangent,
    owner_list,
    master,
    moment_one,
    moment_two,
    biases,
    bias_moment_one,
    bias_moment_two,
):
    S, F, G = sizes
    capacity, rows, width = master.shape
    half = rows // 2
    blocks = owner_list.shape[0]
    s, f, g = lax.axis_index("seq"), lax.axis_index("fsdp"), lax.axis_index("grp")
    core = g % 2
    pair = g // 2
    T = S * F

    block_slot, mine, slot_block, slot_live = slot_tables(owner_list, g, capacity)
    picked = pick_blocks(master, block_slot, mine)
    cond_pad = jnp.pad(conditioning[:, 0], ((0, 6), (0, 0)))
    theirs, conds = share(sizes, picked, cond_pad)
    shard = lax.dynamic_slice_in_dim(picked, core * half, half, 1)
    for i in range(G - 1):
        shard = shard + theirs[i]
    linear, modulation_rows = shard[:LINEAR], shard[LINEAR:]

    silu_all = jax.nn.silu(conds[:, :2]).astype(BF16).reshape(F, G // 2, 2, 2, width)
    silu_pair = lax.dynamic_index_in_dim(silu_all, pair, 1, keepdims=False)
    silu_pair = silu_pair.transpose(2, 1, 0, 3).reshape(T, width)
    first_row = (s * F + f) * rows + core * half
    silu_rows = lax.dynamic_slice_in_dim(silu_pair, first_row, half, 1)
    mod_part = jnp.einsum("tr,jre->tje", silu_rows, modulation_rows, preferred_element_type=F32)
    mod_part = jnp.pad(mod_part, ((0, 0), (0, 2), (0, 0)))

    bias_rows = jnp.pad(biases, ((0, 2), (0, 0)))
    saved = forward(sizes, linear, mod_part, latents[:, 0], cotangent[:, 0], bias_rows)
    reduced, smalls, out_lat, in_lat = backward(sizes, *saved)

    smalls = smalls.reshape(S, F, G // 2, 16, width)
    mod_grad = smalls[:, :, :, :6].astype(BF16)
    mod_grad_pair = lax.dynamic_index_in_dim(mod_grad, pair, 2, keepdims=False).reshape(T, 6, width)
    cond_rows = jnp.einsum("tje,jre->tr", mod_grad_pair, modulation_rows, preferred_element_type=F32)
    cond_rows = jnp.pad(cond_rows, ((0, 0), (0, 128 - half)))
    theirs_red, cond_all = settle(sizes, reduced, cond_rows)

    silu_every = silu_all.transpose(3, 2, 0, 1, 4).reshape(S * F * (G // 2), width)
    silu_mine = lax.dynamic_slice_in_dim(silu_every, (s * F + f) * rows, rows, 1)
    mod_weight_grads = jnp.einsum(
        "nr,nje->jre", silu_mine, mod_grad.reshape(-1, 6, width), preferred_element_type=F32
    )
    halves = [jnp.zeros_like(reduced), jnp.zeros_like(reduced)]
    for i in range(G):
        part = reduced if i == G - 1 else theirs_red[i]
        parity = (g + 1 + i) % 2
        halves = [halves[h] + jnp.where(parity == h, part, 0.0) for h in range(2)]
    linear_grads = jnp.concatenate(halves, axis=1)
    weight_grads = jnp.concatenate([linear_grads, mod_weight_grads], axis=0)

    new_master, new_one, new_two, new_copies = adam_slots(
        master, weight_grads, moment_one, moment_two, slot_block, slot_live
    )

    cond_full = cond_all[:, :, :half].reshape(S, F, 2, T, half)
    cond_full = cond_full.transpose(3, 0, 1, 2, 4).reshape(2, 2, F, width)
    cond_mine = lax.dynamic_index_in_dim(cond_full, core, 1, keepdims=False)
    cond_mine = lax.dynamic_index_in_dim(cond_mine, f, 1, keepdims=False)
    _, silu_pull = jax.vjp(jax.nn.silu, conditioning)
    cond_grad = silu_pull(cond_mine[:, None])[0]

    bias_sums = jnp.sum(smalls[:, :, :, 6:14], axis=(0, 1, 2))
    mod_sums = jnp.sum(mod_grad.astype(F32), axis=(0, 1, 2))
    bias_total = jnp.concatenate([bias_sums, mod_sums], axis=0)
    new_biases, new_bias_one, new_bias_two = adam_step(
        biases, bias_total, bias_moment_one, bias_moment_two, RATE_BIAS
    )
    return (
        out_lat[:, None],
        in_lat[:, None].astype(F32),
        cond_grad,
        new_master,
        new_one,
        new_two,
        new_copies,
        new_biases,
        new_bias_one,
        new_bias_two,
    )


def solution(mesh):
    sizes = (mesh.shape["seq"], mesh.shape["fsdp"], mesh.shape["grp"])
    tokens = P(None, ("fsdp", "grp"), "seq", None)
    vector = P(None, ("fsdp", "grp"), None)
    slots = P("grp", ("seq", "fsdp"), None)
    in_specs = (tokens, vector, tokens, P(), slots, slots, slots, P(), P(), P())
    out_specs = (tokens, tokens, vector, slots, slots, slots, slots, P(), P(), P())
    return jax.shard_map(
        functools.partial(per_device, sizes),
        mesh=mesh,
        in_specs=in_specs,
        out_specs=out_specs,
        check_vma=False,
    )
```

```python
import functools
import math

import jax
import jax.numpy as jnp
from jax import lax
from jax.experimental import pallas as pl
from jax.experimental.pallas import tpu as pltpu
from jax.sharding import PartitionSpec as P

HD = 64
STEP = 5
EPS_NORM = 1e-06
BETA_ONE = 0.5
BETA_TWO = 0.5
RATE_WEIGHT = 0.03
RATE_BIAS = 0.1
DECAY = 0.1
ADAM_EPS = 1e-08

MESH = pl.DeviceIdType.MESH
ANY = pl.BlockSpec(memory_space=pl.ANY)
VMEM = pl.BlockSpec(memory_space=pltpu.VMEM)
F32 = jnp.float32
BF16 = jnp.bfloat16
DMA = pltpu.SemaphoreType.DMA
LINEAR = 12


def params(cid, vmem=48):
    return pltpu.CompilerParams(
        collective_id=cid, has_side_effects=True, vmem_limit_bytes=vmem * 1024 * 1024
    )


def remote(src, dst, send_sem, recv_sem, device):
    return pltpu.make_async_remote_copy(
        src_ref=src,
        dst_ref=dst,
        send_sem=send_sem,
        recv_sem=recv_sem,
        device_id=device,
        device_id_type=MESH,
    )


class Place:
    def __init__(self, sizes):
        self.S, self.F, self.G = sizes
        self.s = lax.axis_index("seq")
        self.f = lax.axis_index("fsdp")
        self.g = lax.axis_index("grp")
        self.c = lax.rem(self.g, 2)
        self.base = self.g - self.c
        self.sib = self.base + 1 - self.c
        odd = lax.rem(self.s, 2)
        self.sx = self.s + 1 - 2 * odd
        self.sy = lax.rem(self.s + 2, 4)
        self.sa = self.sx + self.c * (self.sy - self.sx)
        self.sb = self.sy + self.c * (self.sx - self.sy)

    def sibling(self):
        return (self.s, self.f, self.sib)


def meet_loop(count, device_of):
    bar = pltpu.get_barrier_semaphore()

    def one(i, carry):
        pl.semaphore_signal(bar, inc=1, device_id=device_of(i), device_id_type=MESH)
        return carry

    lax.fori_loop(1, count, one, 0)
    pl.semaphore_wait(bar, count - 1)


def slot_tables(owner_list, group, capacity):
    blocks = owner_list.shape[0]
    position = jnp.arange(blocks, dtype=jnp.int32)
    same = owner_list[:, None] == owner_list[None, :]
    before = position[None, :] < position[:, None]
    ranks = jnp.sum(jnp.where(same & before, 1, 0), axis=1).astype(jnp.int32)
    mine = owner_list == group
    slots = jnp.arange(capacity, dtype=jnp.int32)
    holds = mine[None, :] & (ranks[None, :] == slots[:, None])
    slot_block = jnp.sum(jnp.where(holds, position[None, :], 0), axis=1).astype(jnp.int32)
    slot_live = jnp.any(holds, axis=1).astype(jnp.int32)
    block_slot = jnp.where(mine, ranks, 0).astype(jnp.int32)
    return block_slot, mine.astype(jnp.int32), slot_block, slot_live


def pick_kernel(slot_ref, mine_ref, master_ref, out_ref, buf, sems):
    blocks = out_ref.shape[0]

    def fetch(b):
        return pltpu.make_async_copy(master_ref.at[slot_ref[b]], buf.at[b], sems.at[b])

    for b in range(blocks):
        fetch(b).start()
    for b in range(blocks):
        fetch(b).wait()
        out_ref[b] = jnp.where(mine_ref[b] > 0, buf[b], 0.0).astype(BF16)


def pick_blocks(master, block_slot, mine):
    blocks = block_slot.shape[0]
    rows, width = master.shape[1:]
    scalars = pl.BlockSpec(memory_space=pltpu.SMEM)
    return pl.pallas_call(
        pick_kernel,
        out_shape=jax.ShapeDtypeStruct((blocks, rows, width), BF16),
        in_specs=[scalars, scalars, ANY],
        out_specs=VMEM,
        scratch_shapes=[pltpu.VMEM((blocks, rows, width), F32), DMA((blocks,))],
        compiler_params=pltpu.CompilerParams(vmem_limit_bytes=32 * 1024 * 1024),
        name="pick_blocks",
    )(block_slot, mine, master)


def adam_step(param, grad, one, two, rate):
    next_one = BETA_ONE * one + (1.0 - BETA_ONE) * grad
    next_two = BETA_TWO * two + (1.0 - BETA_TWO) * grad * grad
    fix_one = 1.0 - BETA_ONE**STEP
    fix_two = 1.0 - BETA_TWO**STEP
    update = next_one / fix_one / (jnp.sqrt(next_two / fix_two) + ADAM_EPS)
    return (param - rate * (update + DECAY * param), next_one, next_two)


def adam_kernel(
    block_ref, live_ref, master, linear, modulation, one, two,
    o_master, o_one, o_two, o_copy, params_v, grads_v, one_v, two_v, copy_v, in_sem, out_sem,
):
    slots, rows, _ = master.shape
    chunk = rows // 2

    def fetch(j):
        return [
            pltpu.make_async_copy(src.at[j], dst.at[j], in_sem.at[j, n])
            for n, (src, dst) in enumerate(((master, params_v), (one, one_v), (two, two_v)))
        ]

    def fetch_grad(j, src, first):
        block = jnp.clip(block_ref[j] - first, 0, src.shape[0] - 1)
        return pltpu.make_async_copy(src.at[block], grads_v.at[j], in_sem.at[j, 3])

    def put(j):
        return [
            pltpu.make_async_copy(src.at[j], dst.at[j], out_sem.at[j, n])
            for n, (src, dst) in enumerate(
                ((params_v, o_master), (one_v, o_one), (two_v, o_two), (copy_v, o_copy))
            )
        ]

    def start(j):
        for copy in fetch(j):
            copy.start()
        is_linear = block_ref[j] < LINEAR

        @pl.when(is_linear)
        def _():
            fetch_grad(j, linear, 0).start()

        @pl.when(jnp.logical_not(is_linear))
        def _():
            fetch_grad(j, modulation, LINEAR).start()

    def update(j):
        for copy in fetch(j):
            copy.wait()
        fetch_grad(j, linear, 0).wait()
        live = live_ref[j] > 0
        for n in range(2):
            at = (j, pl.ds(n * chunk, chunk))
            param, one_old, two_old = params_v[at], one_v[at], two_v[at]
            stepped, next_one, next_two = adam_step(
                param, grads_v[at], one_old, two_old, RATE_WEIGHT
            )
            new = jnp.where(live, stepped, param)
            params_v[at] = new
            one_v[at] = jnp.where(live, next_one, one_old)
            two_v[at] = jnp.where(live, next_two, two_old)
            copy_v[at] = new.astype(BF16)
        for copy in put(j):
            copy.start()

    def finish(j):
        for copy in put(j):
            copy.wait()

    for body in (start, update, finish):
        lax.fori_loop(0, slots, lambda j, u, body=body: (body(j), u)[1], 0)


def adam_slots(master, linear, modulation, one, two, slot_block, slot_live):
    shape = jax.ShapeDtypeStruct(master.shape, F32)
    scalars = pl.BlockSpec(memory_space=pltpu.SMEM)
    return pl.pallas_call(
        adam_kernel,
        out_shape=(shape, shape, shape, jax.ShapeDtypeStruct(master.shape, BF16)),
        in_specs=[scalars, scalars] + [ANY] * 5,
        out_specs=(ANY,) * 4,
        scratch_shapes=[pltpu.VMEM(master.shape, F32) for _ in range(4)]
        + [pltpu.VMEM(master.shape, BF16), DMA((master.shape[0], 4)), DMA((master.shape[0], 4))],
        compiler_params=pltpu.CompilerParams(vmem_limit_bytes=48 * 1024 * 1024),
        name="adam_slots",
    )(slot_block, slot_live, master, linear, modulation, one, two)


ROWS = 256
CHUNK = 128
NT = (((1,), (1,)), ((), ()))
NN = (((1,), (0,)), ((), ()))
TN = (((0,), (0,)), ((), ()))


def dot(left, right, dims=NN):
    return lax.dot_general(left, right, dims, preferred_element_type=F32)


def loop(count, body):
    def one(i, carry):
        body(i)
        return carry

    lax.fori_loop(0, count, one, 0)


def aligned(index, size):
    return pl.ds(pl.multiple_of(index * size, size), size)


def norm_rows(values):
    centre = jnp.mean(values, axis=-1, keepdims=True)
    centred = values - centre
    spread = jnp.mean(centred * centred, axis=-1, keepdims=True)
    inverse = lax.rsqrt(spread + EPS_NORM)
    return centred * inverse, inverse


def iota(shape, dim):
    return lax.broadcasted_iota(jnp.int32, shape, dim)


def attend_pair(q_ref, k_ref, v_ref, a_ref, lse_ref, pair):
    length = q_ref.shape[0]
    factor = 1.0 / math.sqrt(HD)
    for h in range(2):
        cols = slice((2 * pair + h) * HD, (2 * pair + h + 1) * HD)
        key = k_ref[:, cols]
        value = v_ref[:, cols]
        for r in range(0, length, ROWS):
            rows = slice(r, r + ROWS)
            scores = dot(q_ref[rows, cols], key, NT)
            high = jnp.max(scores, axis=1, keepdims=True)
            weights = jnp.exp((scores - high) * factor)
            total = jnp.sum(weights, axis=1, keepdims=True)
            out = dot(weights.astype(BF16), value, NN) / total
            a_ref[rows, cols] = out.astype(BF16)
            lse_ref[rows, cols] = jnp.broadcast_to(high * factor + jnp.log(total), (ROWS, HD))


def forward_kernel(sizes, *refs):
    (
        picked, cond, lat, cot, bias,
        bank_o, modw_o, mod_o, tok_o, ctok, hid_o, heads_o, head_a_o, lse_o, att_o, branch_o, mid_o, hid2_o, up_o, act_o, mlp_o, res_o,
        shard, theirs, conds, msg, modr, modh, mod, bank, xv, hid, stage, heads, head_a, lse, att, mid, hid2, up, act, mlp,
        gs, gr, gl, ds, dr, dl, zs, zr, as_, ar, bs, br, cs, cr, ms, mr, hs, hr, ts, tr, tl, xs, xr, save_sem,
    ) = refs
    at = Place(sizes)
    S, F, G = sizes
    K = bank.shape[0]
    half = shard.shape[1]
    blocks = picked.shape[0]
    T = 2 * S * F
    me = (at.s * F + at.f) * 2 + at.c
    quarter = lat.shape[1]
    tokens, width = xv.shape
    part = width // 2
    pieces = width // 128

    def device_of(i):
        n = lax.rem(me + i, T)
        return (lax.div(n, 2 * F), lax.rem(lax.div(n, 2), F), at.base + lax.rem(n, 2))

    bar = pltpu.get_barrier_semaphore()

    def greet(device):
        pl.semaphore_signal(bar, inc=1, device_id=device, device_id_type=MESH)

    loop(T - 1, lambda i: greet(device_of(i + 1)))
    for i in range(2, G):
        greet((at.s, at.f, lax.rem(at.base + i, G)))
    pl.semaphore_wait(bar, T - 1 + G - 2)

    def tok_move(j):
        return (2 * j + at.c, at.f, at.base + lax.div(at.s, 2))

    def tok_refs(which):
        return ((lat, xv), (cot, ctok))[which]

    def tok_to(j, which):
        src, dst = tok_refs(which)
        place = aligned(lax.rem(at.s, 2), quarter)
        return remote(
            src.at[j], dst.at[place], ts.at[which, j], tr.at[which, lax.rem(at.s, 2)], tok_move(j)
        )

    def tok_from(j, which):
        src, dst = tok_refs(which)
        place = pl.ds(j * quarter, quarter)
        return remote(src.at[0], dst.at[place], ts.at[which, j], tr.at[which, j], tok_move(j))

    def tok_local(j, which):
        src, dst = tok_refs(which)
        return pltpu.make_async_copy(src.at[j], dst.at[aligned(lax.rem(at.s, 2), quarter)], tl.at[which])

    def stays(j):
        return (2 * j + at.c == at.s) & (lax.div(at.s, 2) == at.c)

    def comes(j):
        return jnp.logical_not((2 * at.c + j == at.s) & (lax.rem(at.s, 2) == at.c))

    def tok_start(which):
        for j in range(2):
            @pl.when(stays(j))
            def _():
                tok_local(j, which).start()

            @pl.when(jnp.logical_not(stays(j)))
            def _():
                tok_to(j, which).start()

    def tok_finish(which):
        for j in range(2):
            @pl.when(stays(j))
            def _():
                tok_local(j, which).wait()

            @pl.when(jnp.logical_not(stays(j)))
            def _():
                tok_to(j, which).wait_send()

            @pl.when(comes(j))
            def _():
                tok_from(j, which).wait_recv()

    def rows_of(core):
        return picked.at[:, aligned(core, half)]

    def group_to(i):
        g = lax.rem(at.g + i, G)
        return remote(
            rows_of(lax.rem(g, 2)), theirs.at[G - 1 - i], gs.at[i], gr.at[G - 1 - i], (at.s, at.f, g)
        )

    def group_from(j):
        return remote(rows_of(0), theirs.at[j], gs.at[0], gr.at[j], at.sibling())

    group_own = pltpu.make_async_copy(rows_of(at.c), shard.at[0:blocks], gl)

    def cond_number(i):
        return lax.rem(at.f * 2 + at.c + i, 2 * F)

    def cond_to(i):
        n = cond_number(i)
        device = (at.s, lax.div(n, 2), at.base + lax.rem(n, 2))
        return remote(cond, conds.at[cond_number(0)], ds.at[i], dr.at[cond_number(0)], device)

    def cond_from(i):
        n = cond_number(i)
        return remote(cond, conds.at[n], ds.at[i], dr.at[n], at.sibling())

    cond_own = pltpu.make_async_copy(cond, conds.at[cond_number(0)], dl)

    here = at.s * F + at.f

    def mod_to(i):
        n = lax.rem(here + i, S * F)
        device = (lax.div(n, F), lax.rem(n, F), at.g)
        return remote(msg.at[n], modr.at[here], ms.at[i], mr.at[here], device)

    def mod_from(i):
        n = lax.rem(here + i, S * F)
        return remote(msg.at[n], modr.at[n], ms.at[i], mr.at[n], at.sibling())

    mod_swap = remote(modh.at[0], modh.at[1], hs, hr, at.sibling())

    def z_to(k, i):
        f = lax.rem(at.f + i, F)
        return remote(
            shard.at[k], bank.at[k, at.s, at.f, at.c], zs.at[k, i], zr.at[k, i], (at.s, f, at.g)
        )

    def z_from(k, i):
        f = lax.rem(at.f + F - i, F)
        return remote(shard.at[k], bank.at[k, at.s, f, at.c], zs.at[k, i], zr.at[k, i], (at.s, f, at.g))

    def a_copy(k, s):
        line = bank.at[k, s, :, at.c]
        return remote(line, line, as_.at[k], ar.at[k], (at.sa, at.f, at.g))

    def b_copy(k, s, n):
        line = bank.at[k, s, :, at.c]
        return remote(line, line, bs.at[k, n], br.at[k, n], (at.sb, at.f, at.g))

    sd = S - 1 - at.s

    def c_copy(k, s, n, core):
        line = bank.at[k, s, :, core]
        return remote(line, line, cs.at[k, n], cr.at[k, n], at.sibling())

    def z_start(k):
        for i in range(1, F):
            z_to(k, i).start()
        bank[k, at.s, at.f, at.c] = shard[k]

    def step(t):
        if t + 2 < K:
            z_start(t + 2)
        if t < K:
            for i in range(1, F):
                z_from(t, i).wait_recv()
            a_copy(t, at.s).start()
            c_copy(t, at.s, 0, at.c).start()
        if 1 <= t <= K:
            a_copy(t - 1, at.sa).wait_recv()
            b_copy(t - 1, at.s, 0).start()
            b_copy(t - 1, at.sa, 1).start()
            c_copy(t - 1, at.sa, 1, at.c).start()
        if t >= 2:
            b_copy(t - 2, at.sb, 0).wait_recv()
            c_copy(t - 2, at.sb, 2, at.c).start()
            b_copy(t - 2, sd, 1).wait_recv()
            c_copy(t - 2, sd, 3, at.c).start()

    saves = []

    def save(src, dst):
        copy = pltpu.make_async_copy(src, dst, save_sem.at[len(saves)])
        copy.start()
        saves.append(copy)
        return len(saves) - 1

    waited = set()

    def saved(n):
        if n not in waited:
            saves[n].wait()
            waited.add(n)

    def arrive(k):
        for n, s in enumerate((at.s, at.sb, at.sa, sd)):
            c_copy(k, s, n, 1 - at.c).wait_recv()
        save(bank.at[k], bank_o.at[k])

    def weights(k):
        return bank[k].reshape(width, width)

    def gather_rows():
        group_own.wait()
        for i in range(1, G):
            group_from(i - 1).wait_recv()

        def one(b):
            value = shard[b].astype(F32)
            for i in range(G - 1):
                value = value + theirs[i, b].astype(F32)
            shard[b] = value.astype(BF16)

        loop(blocks, one)
        shard[blocks:] = jnp.zeros_like(shard[blocks:])

    def modulation_parts():
        cond_own.wait()
        loop(2 * F - 1, lambda i: cond_from(i + 1).wait_recv())
        value = conds[...].reshape(2 * F * 2 * pieces, 128)
        silu = (value / (1.0 + jnp.exp(-value))).astype(BF16)
        parts = 8 * half
        first = here * 2 * half + at.c * half
        lane, column = iota((128, parts), 0), iota((128, parts), 1)
        select = jnp.where(lane == lax.rem(first, 128) + lax.rem(column, half), 1.0, 0.0)
        rows = dot(silu, select.astype(BF16)).astype(BF16)
        count = 8 * S * F
        line, source = iota((count, rows.shape[0]), 0), iota((count, rows.shape[0]), 1)
        latent = lax.div(line, 8)
        chip, depth = lax.div(latent, F), lax.rem(latent, F)
        wanted = ((depth * 2 + lax.rem(chip, 2)) * 2 + lax.div(chip, 2)) * pieces + lax.div(first, 128)
        spread = dot(jnp.where(source == wanted, 1.0, 0.0).astype(BF16), rows)
        line, column = iota((count, parts), 0), iota((count, parts), 1)
        spread = jnp.where(lax.rem(line, 8) == lax.div(column, half), spread, 0.0).astype(BF16)
        value = dot(spread, shard[K:].reshape(parts, width))
        for n in range(pieces):
            msg[:, n] = value[:, n * 128 : (n + 1) * 128].reshape(S * F, 8, 128)
        loop(S * F - 1, lambda i: mod_to(i + 1).start())

    def modulation_sum():
        def one(i):
            mod_from(i + 1).wait_recv()

        loop(S * F - 1, one)
        modr[here] = msg[here]
        total = modr[0]
        for n in range(1, S * F):
            total = total + modr[n]
        modh[0] = total
        mod_swap.start()
        mod_swap.wait()
        for n in range(pieces):
            cols = slice(n * 128, (n + 1) * 128)
            mod[:, cols] = modh[0, n] + modh[1, n]
        mod[0:6] = mod[0:6] + bias[8:14]
        save(mod, mod_o)

    def prepare():
        modulation_sum()
        tok_finish(0)
        save(xv, tok_o)

        def one(i):
            rows = aligned(i, CHUNK)
            scaled, _ = norm_rows(xv[rows].astype(F32))
            hid[rows] = (scaled * (1.0 + mod[1:2]) + mod[0:1]).astype(BF16)

        loop(tokens // CHUNK, one)
        hid_saved.append(save(hid, hid_o))

    hid_saved = []

    def swap(n):
        return remote(
            stage.at[n], heads.at[n, aligned(at.c, tokens)], xs.at[n], xr.at[n], at.sibling()
        )

    def swap_from(n):
        return remote(
            stage.at[n], heads.at[n, aligned(1 - at.c, tokens)], xs.at[n], xr.at[n], at.sibling()
        )

    def project(n, bias_row):
        value = dot(hid[...], weights(n))
        if bias_row is not None:
            value = value + bias[bias_row : bias_row + 1]
        value = value.astype(BF16)
        first, second = value[:, :part], value[:, part:]
        stage[n] = jnp.where(at.c == 0, second, first)
        swap(n).start()
        heads[n, aligned(at.c, tokens)] = jnp.where(at.c == 0, first, second)

    def attend_part(pair):
        if pair == 0:
            for n in range(3):
                swap_from(n).wait_recv()
                save(heads.at[n], heads_o.at[n])
        attend_pair(heads.at[0], heads.at[1], heads.at[2], head_a, lse, pair)

    def give_out():
        return remote(
            head_a.at[aligned(1 - at.c, tokens)], att.at[:, aligned(at.c, part)], xs.at[3], xr.at[3], at.sibling()
        )

    def give_from():
        return remote(
            head_a.at[aligned(at.c, tokens)], att.at[:, aligned(1 - at.c, part)], xs.at[3], xr.at[3], at.sibling()
        )

    def send_attended():
        give_out().start()
        att[:, aligned(at.c, part)] = head_a[aligned(at.c, tokens)]
        save(head_a, head_a_o)
        save(lse, lse_o)

    def output_projection():
        give_from().wait_recv()
        save(att, att_o)
        mlp[...] = dot(att[...], weights(3)) + bias[2:3]
        branch_saved = save(mlp, branch_o)

        def rest(i):
            rows = aligned(i, CHUNK)
            middle = xv[rows].astype(F32) + mod[2:3] * mlp[rows]
            mid[rows] = middle
            scaled, _ = norm_rows(middle)
            hid2[rows] = (scaled * (1.0 + mod[4:5]) + mod[3:4]).astype(BF16)

        loop(tokens // CHUNK, rest)
        save(mid, mid_o)
        save(hid2, hid2_o)
        return branch_saved

    up_saved = []

    def upper(j):
        if j >= 2:
            saved(up_saved[j - 2])
        value = dot(hid2[...], weights(4 + j)) + bias[3 + j : 4 + j]
        up[j % 2] = value
        act[j] = jax.nn.gelu(value, approximate=True).astype(BF16)
        up_saved.append(save(up.at[j % 2], up_o.at[j]))
        save(act.at[j], act_o.at[j])

    def lower(j):
        value = dot(act[j], weights(8 + j))
        mlp[...] = value + (bias[7:8] if j == 0 else mlp[...])

    def finish_forward():
        save(mlp, mlp_o)
        saved(hid_saved[0])

        def one(i):
            rows = aligned(i, CHUNK)
            hid[rows] = (mid[rows] + mod[5:6] * mlp[rows]).astype(BF16)

        loop(tokens // CHUNK, one)
        save(hid, res_o)

    tok_start(0)
    for i in range(1, G):
        group_to(i).start()
    group_own.start()
    cond_own.start()
    loop(2 * F - 1, lambda i: cond_to(i + 1).start())
    gather_rows()
    z_start(0)
    z_start(1)
    modulation_parts()
    save(shard.at[K:blocks], modw_o)
    for t in range(K + 2):
        step(t)
        if t == 1:
            prepare()
        if t >= 2:
            arrive(t - 2)
        if t in (2, 3, 4):
            project(t - 2, (0, None, 1)[t - 2])
        if 5 <= t <= 8:
            attend_part(t - 5)
        if t == 8:
            send_attended()
        if t == 9:
            branch_saved = output_projection()
            upper(0)
        if t == 10:
            upper(1)
            upper(2)
        if t == 11:
            upper(3)
            saved(branch_saved)
            lower(0)
            lower(1)
        if t == 12:
            tok_start(1)
            lower(2)
        if t == 13:
            lower(3)
    finish_forward()

    def finish(k):
        for i in range(1, F):
            z_to(k, i).wait_send()
        a_copy(k, at.s).wait_send()
        b_copy(k, at.s, 0).wait_send()
        b_copy(k, at.sa, 1).wait_send()
        for n, s in enumerate((at.s, at.sa, at.sb, sd)):
            c_copy(k, s, n, at.c).wait_send()

    loop(K, finish)
    for i in range(1, G):
        group_to(i).wait_send()
    loop(2 * F - 1, lambda i: cond_to(i + 1).wait_send())
    loop(S * F - 1, lambda i: mod_to(i + 1).wait_send())
    for n in range(3):
        swap(n).wait_send()
    give_out().wait_send()
    for n in range(len(saves)):
        saved(n)
    tok_finish(1)


def forward(sizes, picked, cond, lat, cot, bias):
    S, F, G = sizes
    blocks, rows, width = picked.shape
    K, half, T = LINEAR, rows // 2, 2 * S * F
    tokens = 2 * lat.shape[1]
    length, part = 2 * tokens, width // 2
    low = lambda *shape: (shape, BF16)
    high = lambda *shape: (shape, F32)
    outs = (
        low(K, S, F, 2, half, width),
        low(blocks - K, half, width),
        high(8, width),
        low(tokens, width),
        low(tokens, width),
        low(tokens, width),
        low(3, length, part),
        low(length, part),
        high(length, part),
        low(tokens, width),
        high(tokens, width),
        high(tokens, width),
        low(tokens, width),
        high(4, tokens, width),
        low(4, tokens, width),
        high(tokens, width),
        low(tokens, width),
    )
    scratch = (
        low(K + 8, half, width),
        low(G - 1, blocks, half, width),
        high(2 * F, 2 * width // 128, 128),
        high(S * F, width // 128, 8, 128),
        high(S * F, width // 128, 8, 128),
        high(2, width // 128, 8, 128),
        high(8, width),
        low(K, S, F, 2, half, width),
        low(tokens, width),
        low(tokens, width),
        low(3, tokens, part),
        low(3, length, part),
        low(length, part),
        high(length, part),
        low(tokens, width),
        high(tokens, width),
        low(tokens, width),
        high(2, tokens, width),
        low(4, tokens, width),
        high(tokens, width),
    )
    sems = (
        (G,), (G,), None, (2 * F,), (2 * F,), None, (K, F), (K, F), (K,), (K,), (K, 2), (K, 2), (K, 4), (K, 4),
        (S * F,), (S * F,), None, None, (2, 2), (2, 2), (2,), (4,), (4,), (40,),
    )
    return pl.pallas_call(
        functools.partial(forward_kernel, sizes),
        out_shape=tuple(jax.ShapeDtypeStruct(*o) for o in outs),
        in_specs=[ANY] * 4 + [VMEM],
        out_specs=(ANY,) * len(outs),
        scratch_shapes=[pltpu.VMEM(*s) for s in scratch] + [DMA if n is None else DMA(n) for n in sems],
        compiler_params=params(2, 63),
        name="forward",
    )(picked, cond, lat, cot, bias)


RING = 4
ORDER = (8, 4, 9, 5, 10, 6, 11, 7, 3, 0, 1, 2)


def gelu_slope(values):
    scale = 0.7978845608
    square = values * values
    bend = jnp.tanh(scale * values * (1.0 + 0.044715 * square))
    return 0.5 * (1.0 + bend) + 0.5 * values * (1.0 - bend * bend) * (
        scale * (1.0 + 3.0 * 0.044715 * square)
    )


def attend_pair_back(q, k, v, a, lse_ref, da_ref, pair, dq_ref, dk_ref, dv_ref):
    length = q.shape[0]
    factor = 1.0 / math.sqrt(HD)
    for h in range(2):
        cols = slice(h * HD, (h + 1) * HD)
        grad_cols = slice((2 * pair + h) * HD, (2 * pair + h + 1) * HD)
        key = k[:, cols]
        value = v[:, cols]
        dk = jnp.zeros((HD, length), F32)
        dv = jnp.zeros((HD, length), F32)
        for r in range(0, length, ROWS):
            rows = slice(r, r + ROWS)
            query = q[rows, cols]
            grad = da_ref[rows, grad_cols]
            lse = lse_ref[rows, h * HD : h * HD + 1]
            scores = dot(query, key, NT)
            probs = jnp.exp(scores * factor - lse)
            row_dot = jnp.sum(grad.astype(F32) * a[rows, cols].astype(F32), axis=1, keepdims=True)
            weight_grad = dot(grad, value, NT)
            score_grad = (probs * (weight_grad - row_dot)).astype(BF16)
            dq_ref[rows, cols] = (dot(score_grad, key, NN) * factor).astype(BF16)
            dk = dk + dot(query.T, score_grad, NN)
            dv = dv + dot(grad.T, probs.astype(BF16), NN)
        dk_ref[:, cols] = (dk * factor).T.astype(BF16)
        dv_ref[:, cols] = dv.T.astype(BF16)


def backward_kernel(sizes, *refs):
    (
        bank, modw, mod, tok, ctok, hid, heads, head_a, lse, att, branch, mid, hid2, up, act, mlp, res, silu,
        red, smalls, cgs, out_lat, in_lat,
        mine, give, r0, r1, r2, r3, total, wbuf,
        ebuf, dfb, f0, f1, a0, a1, dub, dh2, h2b, stage, dah, qkva, lsev, dpair, dqt, accs, small, sv, sw, swb, smv, cg,
        cs, cr, bs, br, as_, ar, zs, zr, os_, rs, rr, free, vs, vr, ws, wr, wl, us, ur, ds, dr, dl, ts, tr, tl, loads, xs, xr, ps, pr,
    ) = refs
    at = Place(sizes)
    S, F, G = sizes
    K = mine.shape[0]
    half = mine.shape[3]
    tokens, width = ebuf.shape
    part = width // 2
    band = width // S
    count = S * F * G
    me = (at.s * F + at.f) * G + at.g
    quarter = out_lat.shape[1]
    sd = S - 1 - at.s
    chunks = tokens // CHUNK

    def device_of(i):
        n = lax.rem(me + i, count)
        return (lax.div(n, F * G), lax.rem(lax.div(n, G), F), lax.rem(n, G))

    meet_loop(count, device_of)

    def c_copy(r):
        return remote(give.at[r % 2], r0.at[r % RING], cs.at[r], cr.at[r], at.sibling())

    def b_copy(r, s, n):
        return remote(mine.at[r, s], r1.at[r, n], bs.at[r, n], br.at[r, n], (at.sb, at.f, at.g))

    def a_copy(r):
        return remote(mine.at[r, at.sa], r2.at[r], as_.at[r], ar.at[r], (at.sa, at.f, at.g))

    def z_to(r, i):
        f = lax.rem(at.f + i, F)
        return remote(mine.at[r, at.s, f], r3.at[r, i], zs.at[r, i], zr.at[r, i], (at.s, f, at.g))

    pair = lax.div(at.g, 2)

    def out_copy(r):
        return pltpu.make_async_copy(total.at[r % 4], red.at[pair, ORDER[r], at.c], os_.at[r])

    def out_to(r, i):
        g = lax.rem(at.g + i, G)
        return remote(
            total.at[r % 4], red.at[pair, ORDER[r], at.c], rs.at[r, i], rr.at[r, i], (at.s, at.f, g)
        )

    def out_from(r, i):
        g = lax.rem(at.g + G - i, G)
        return remote(
            total.at[r % 4], red.at[lax.div(g, 2), ORDER[r], lax.rem(g, 2)], rs.at[r, i], rr.at[r, i], at.sibling()
        )

    def out_done(r):
        out_copy(r).wait()
        for i in range(1, G):
            out_to(r, i).wait_send()

    def add_line(dst, src):
        def one(f):
            dst[f] = (dst[f].astype(F32) + src[f].astype(F32)).astype(BF16)

        loop(F, one)

    def hop0(r):
        c_copy(r).wait_recv()
        loop(S, lambda s: add_line(mine.at[r, s], r0.at[r % RING, s]))
        if r + RING < K:
            pl.semaphore_signal(free, inc=1, device_id=at.sibling(), device_id_type=MESH)
        b_copy(r, at.sb, 0).start()
        b_copy(r, sd, 1).start()

    def hop1(r):
        b_copy(r, at.sb, 0).wait_recv()
        b_copy(r, sd, 1).wait_recv()
        add_line(mine.at[r, at.sa], r1.at[r, 1])
        a_copy(r).start()
        add_line(mine.at[r, at.s], r1.at[r, 0])

    def hop2(r):
        a_copy(r).wait_recv()
        add_line(mine.at[r, at.s], r2.at[r])
        for i in range(1, F):
            z_to(r, i).start()

    def hop3(r):
        for i in range(1, F):
            z_to(r, i).wait_recv()
        if r >= 4:
            out_done(r - 4)
        value = mine[r, at.s, at.f].astype(F32)
        for i in range(1, F):
            value = value + r3[r, i].astype(F32)
        total[r % 4] = value
        out_copy(r).start()
        for i in range(1, G):
            out_to(r, i).start()

    def produce(r, left, right):
        if r >= 2:
            c_copy(r - 2).wait_send()

        lines = S // 2

        def one(n):
            value = dot(left[:, aligned(n, lines * band)], right[...], TN)
            value = value.astype(BF16).reshape(lines, F, 2, half, width)
            first, second = value[:, :, 0], value[:, :, 1]
            mine[r, aligned(n, lines)] = jnp.where(at.c == 0, first, second)
            give[r % 2, aligned(n, lines)] = jnp.where(at.c == 0, second, first)

        loop(2, one)
        if r >= RING:
            pl.semaphore_wait(free, 1)
        c_copy(r).start()

    def back_device(j):
        return (2 * at.c + j, at.f, at.base + lax.rem(at.s, 2))

    def back_stays(j):
        return (2 * at.c + j == at.s) & (lax.rem(at.s, 2) == at.c)

    def back_comes(m):
        return jnp.logical_not((2 * m + at.c == at.s) & (lax.div(at.s, 2) == at.c))

    def back_refs(which):
        return ((res, out_lat), (dfb, in_lat))[which]

    def back_to(j, which):
        src, dst = back_refs(which)
        m = lax.div(at.s, 2)
        return remote(
            src.at[pl.ds(j * quarter, quarter)], dst.at[m], ts.at[which, j], tr.at[which, m], back_device(j)
        )

    def back_from(m, which):
        src, dst = back_refs(which)
        return remote(
            src.at[pl.ds(0, quarter)], dst.at[m], ts.at[which, m], tr.at[which, m], back_device(m)
        )

    def back_local(j, which):
        src, dst = back_refs(which)
        return pltpu.make_async_copy(
            src.at[pl.ds(j * quarter, quarter)], dst.at[lax.div(at.s, 2)], tl.at[which]
        )

    def back_start(which):
        for j in range(2):
            @pl.when(back_stays(j))
            def _():
                back_local(j, which).start()

            @pl.when(jnp.logical_not(back_stays(j)))
            def _():
                back_to(j, which).start()

    def back_finish(which):
        for j in range(2):
            @pl.when(back_stays(j))
            def _():
                back_local(j, which).wait()

            @pl.when(jnp.logical_not(back_stays(j)))
            def _():
                back_to(j, which).wait_send()

            @pl.when(back_comes(j))
            def _():
                back_from(j, which).wait_recv()

    def load(src, dst, n):
        return pltpu.make_async_copy(src, dst, loads.at[n])

    def load_weight(k, slot):
        return load(bank.at[k], wbuf.at[slot], slot)

    ups, acts = (f0, f1), (a0, a1)

    def load_up(j):
        return load(up.at[j], ups[j % 2], 2 + j % 2)

    def load_act(j):
        return load(act.at[j], acts[j % 2], 4 + j % 2)

    def load_pair(p):
        cols = pl.ds(p * 2 * HD, 2 * HD)
        slot = p % 2
        return [load(heads.at[n, :, cols], qkva.at[slot, n], 10 + 5 * slot + n) for n in range(3)] + [
            load(head_a.at[:, cols], qkva.at[slot, 3], 13 + 5 * slot),
            load(lse.at[:, cols], lsev.at[slot], 14 + 5 * slot),
        ]

    def weights(slot):
        return wbuf[slot].reshape(width, width)

    def add_rows(i, value, cols=slice(None)):
        accs[i, :, cols] += value.reshape(-1, 8, value.shape[-1]).sum(axis=0)

    back_start(0)
    load_e, load_mlp, load_h2 = load(ctok, ebuf, 6), load(mlp, dh2, 7), load(hid2, h2b, 8)
    for copy in (load_e, load_mlp):
        copy.start()
    load_weight(8, 0).start()
    load_act(0).start()
    load_up(0).start()
    load_h2.start()
    load_weight(4, 1).start()
    load_up(1).start()
    load_act(1).start()
    accs[...] = jnp.zeros_like(accs)
    load_e.wait()
    load_mlp.wait()

    def start_rows(i):
        rows = aligned(i, CHUNK)
        grad = ebuf[rows].astype(F32)
        add_rows(5, grad * dh2[rows])
        low = (mod[5:6] * grad).astype(BF16)
        dfb[rows] = low
        add_rows(13, low.astype(F32))

    loop(chunks, start_rows)

    def active_back(j):
        load_weight(8 + j, 0).wait()
        load_up(j).wait()

        value = dot(dfb[...], weights(0), NT) * gelu_slope(ups[j % 2][...])
        low = value.astype(BF16)
        dub[...] = low
        add_rows(9 + j, low.astype(F32))
        load_weight(9 + j if j < 3 else 3, 0).start()
        if j < 2:
            load_up(j + 2).start()

    def hidden_back(j):
        load_weight(4 + j, 1).wait()

        value = dot(dub[...], weights(1), NT)
        dh2[...] = value if j == 0 else dh2[...] + value
        load_weight(5 + j if j < 3 else 0, 1).start()

    def product_eight(j):
        load_act(j).wait()
        produce(2 * j, acts[j % 2], dfb)
        if j < 2:
            load_act(j + 2).start()

    def product_four(j):
        if j == 0:
            load_h2.wait()
        produce(2 * j + 1, h2b, dub)

    load_mid, load_branch = load(mid, f0, 2), load(branch, f1, 3)
    load_att, load_hid, load_x = load(att, a0, 4), load(hid, h2b, 8), load(tok, ebuf, 6)

    def middle_back():
        load_mid.wait()
        load_branch.wait()

        def one(i):
            rows = aligned(i, CHUNK)
            scaled, inverse = norm_rows(f0[rows])
            grad = dh2[rows]
            inner = grad * (1.0 + mod[4:5])
            mean_inner = jnp.mean(inner, axis=-1, keepdims=True)
            mean_scaled = jnp.mean(inner * scaled, axis=-1, keepdims=True)
            value = ebuf[rows].astype(F32) + inverse * (inner - mean_inner - scaled * mean_scaled)
            add_rows(4, grad * scaled)
            add_rows(3, grad)
            dh2[rows] = value
            add_rows(2, value * f1[rows])
            low = (mod[2:3] * value).astype(BF16)
            dfb[rows] = low
            add_rows(8, low.astype(F32))

        loop(chunks, one)
        load_x.start()

    def swap_da(here):
        return remote(stage, dah.at[aligned(here, tokens)], xs, xr, at.sibling())

    def attended_back():
        load_weight(3, 0).wait()

        value = dot(dfb[...], weights(0), NT).astype(BF16)
        first, second = value[:, :part], value[:, part:]
        stage[...] = jnp.where(at.c == 0, second, first)
        swap_da(at.c).start()
        dah[aligned(at.c, tokens)] = jnp.where(at.c == 0, first, second)
        load_weight(1, 0).start()

    def pair_to(p, n, core):
        rows = aligned(1 - at.c, tokens)
        cols = pl.ds(pl.multiple_of(core * part + p * 2 * HD, 2 * HD), 2 * HD)
        return remote(
            dpair.at[p % 2, n, rows], dqt.at[n, :, cols], ps.at[p, n], pr.at[p, n], at.sibling()
        )

    def attend_back_part(p):
        if p == 0:
            swap_da(1 - at.c).wait_recv()
        for copy in load_pair(p):
            copy.wait()
        if p >= 2:
            for n in range(3):
                pair_to(p - 2, n, at.c).wait_send()
        slot = p % 2
        attend_pair_back(
            qkva.at[slot, 0], qkva.at[slot, 1], qkva.at[slot, 2], qkva.at[slot, 3], lsev.at[slot], dah, p,
            dpair.at[slot, 0], dpair.at[slot, 1], dpair.at[slot, 2],
        )
        cols = pl.ds(pl.multiple_of(at.c * part + p * 2 * HD, 2 * HD), 2 * HD)
        for n in range(3):
            pair_to(p, n, at.c).start()
            dqt[n, :, cols] = dpair[slot, n, aligned(at.c, tokens)]
        if p + 2 < part // (2 * HD):
            for copy in load_pair(p + 2):
                copy.start()

    def pairs_arrive():
        for p in range(part // (2 * HD)):
            for n in range(3):
                pair_to(p, n, 1 - at.c).wait_recv()

        def one(i):
            rows = aligned(i, CHUNK)
            add_rows(6, dqt[0, rows].astype(F32))
            add_rows(7, dqt[2, rows].astype(F32))

        loop(chunks, one)

    def first_back(k, slot, start):
        load_weight(k, slot).wait()

        value = dot(dqt[k], weights(slot), NT)
        f0[...] = value if start else f0[...] + value

    def input_back():
        load_x.wait()

        def one(i):
            rows = aligned(i, CHUNK)
            scaled, inverse = norm_rows(ebuf[rows].astype(F32))
            grad = f0[rows]
            inner = grad * (1.0 + mod[1:2])
            mean_inner = jnp.mean(inner, axis=-1, keepdims=True)
            mean_scaled = jnp.mean(inner * scaled, axis=-1, keepdims=True)
            value = dh2[rows] + inverse * (inner - mean_inner - scaled * mean_scaled)
            add_rows(1, grad * scaled)
            add_rows(0, grad)
            dfb[rows] = value.astype(BF16)

        loop(chunks, one)

    small_swap = remote(small, sv, vs, vr, at.sibling())
    chips = S * F * G // 2
    chip = lax.div(me, 2)
    sent = aligned(at.c, part)

    def chip_rows(n, cols):
        return smalls.at[lax.div(n, G // 2), lax.rem(n, G // 2), :, cols]

    def small_to(i):
        n = lax.rem(chip + i, chips)
        row, group = lax.div(n, G // 2), lax.rem(n, G // 2)
        device = (lax.div(row, F), lax.rem(row, F), 2 * group + at.c)
        return remote(swb.at[:, sent], chip_rows(chip, sent), ws.at[i], wr.at[chip], device)

    def small_from(i):
        n = lax.rem(chip + i, chips)
        return remote(swb.at[:, sent], chip_rows(n, sent), ws.at[i], wr.at[n], at.sibling())

    small_own = pltpu.make_async_copy(swb.at[:, sent], chip_rows(chip, sent), wl)

    def small_share(core):
        region = smalls.at[:, :, :, aligned(core, part)]
        return remote(region, region, us, ur, at.sibling())

    def small_start():
        small[...] = jnp.zeros_like(small)
        small[0:14] = accs[...].sum(axis=1)
        small[14:15] = silu[0:1]
        small_swap.start()
        small_swap.wait()
        sw[...] = small[...] + sv[...]
        swb[...] = sw[...].astype(BF16)
        small_own.start()
        loop(chips - 1, lambda i: small_to(i + 1).start())

    load_modw = load(modw, dub.at[0 : 6 * half], 9)
    pair_smalls = pltpu.make_async_copy(smalls.at[:, pair], smv, dl)

    def cond_device(i):
        n = lax.rem((at.s * F + at.f) * 2 + at.c + i, 2 * S * F)
        return n, (lax.div(n, 2 * F), lax.rem(lax.div(n, 2), F), at.base + lax.rem(n, 2))

    def cond_to(i):
        n, device = cond_device(i)
        return remote(cg, cgs.at[cond_device(0)[0]], ds.at[i], dr.at[cond_device(0)[0]], device)

    def cond_from(i):
        n, device = cond_device(i)
        return remote(cg, cgs.at[n], ds.at[i], dr.at[n], at.sibling())

    cond_own = pltpu.make_async_copy(cg, cgs.at[cond_device(0)[0]], dl)

    def cond_start():
        small_own.wait()
        loop(chips - 1, lambda i: small_from(i + 1).wait_recv())
        small_share(at.c).start()
        small_share(1 - at.c).wait_recv()
        pair_smalls.start()
        load_modw.wait()
        dub[6 * half : 8 * half] = jnp.zeros((2 * half, width), BF16)
        pair_smalls.wait()
        value = dot(smv[...].reshape(S * F * 16, width), dub[0 : 8 * half], NT)
        line, column = iota(value.shape, 0), iota(value.shape, 1)
        value = jnp.where(lax.rem(line, 16) == lax.div(column, half), value, 0.0)
        value = value.reshape(S * F, 16, 8 * half).sum(axis=1)
        rows = value[:, 0:128]
        for n in range(1, 8 * half // 128):
            rows = rows + value[:, n * 128 : (n + 1) * 128]
        cg[...] = rows
        cond_own.start()
        loop(2 * S * F - 1, lambda i: cond_to(i + 1).start())

    active_back(0)
    product_eight(0)
    hidden_back(0)
    hop0(0)
    product_four(0)
    active_back(1)
    hop0(1)
    product_eight(1)
    hidden_back(1)
    hop0(2)
    product_four(1)
    hop1(0)
    active_back(2)
    load_mid.start()
    hop0(3)
    product_eight(2)
    hidden_back(2)
    hop0(4)
    hop1(1)
    load_att.start()
    product_four(2)
    hop2(0)
    active_back(3)
    load_branch.start()
    hop0(5)
    product_eight(3)
    hidden_back(3)
    hop0(6)
    hop1(2)
    product_four(3)
    load_hid.start()
    load_modw.start()
    hop2(1)
    middle_back()
    hop0(7)
    hop1(3)
    hop3(0)
    attended_back()
    for copy in load_pair(0) + load_pair(1):
        copy.start()
    load_att.wait()
    produce(8, a0, dfb)
    hop2(2)
    attend_back_part(0)
    hop0(8)
    hop1(4)
    hop3(1)
    attend_back_part(1)
    hop1(5)
    hop2(3)
    hop3(2)
    attend_back_part(2)
    hop1(6)
    hop2(4)
    hop3(3)
    attend_back_part(3)
    hop1(7)
    hop2(5)
    hop3(4)
    pairs_arrive()
    load_hid.wait()
    produce(9, h2b, dqt.at[0])
    hop2(6)
    hop1(8)
    produce(10, h2b, dqt.at[1])
    hop0(9)
    hop3(5)
    produce(11, h2b, dqt.at[2])
    hop0(10)
    hop2(7)
    first_back(0, 1, True)
    hop0(11)
    load_weight(2, 1).start()
    first_back(1, 0, False)
    hop1(9)
    hop2(8)
    hop3(6)
    first_back(2, 1, False)
    input_back()
    small_start()
    back_start(1)
    hop1(10)
    hop2(9)
    hop3(7)
    hop1(11)
    hop2(10)
    hop3(8)
    cond_start()
    hop3(9)
    hop2(11)
    hop3(10)
    hop3(11)

    swap_da(at.c).wait_send()
    for p in (2, 3):
        for n in range(3):
            pair_to(p, n, at.c).wait_send()
    for r in range(K):
        if r >= K - 2:
            c_copy(r).wait_send()
        if r >= K - 4:
            out_done(r)
        for i in range(1, G):
            out_from(r, i).wait_recv()
        b_copy(r, at.sb, 0).wait_send()
        b_copy(r, sd, 1).wait_send()
        a_copy(r).wait_send()
        for i in range(1, F):
            z_to(r, i).wait_send()
    back_finish(0)
    back_finish(1)
    loop(chips - 1, lambda i: small_to(i + 1).wait_send())
    small_share(at.c).wait_send()
    cond_own.wait()
    loop(2 * S * F - 1, lambda i: cond_to(i + 1).wait_send())
    loop(2 * S * F - 1, lambda i: cond_from(i + 1).wait_recv())


def backward(sizes, *arrays):
    S, F, G = sizes
    bank, tok = arrays[0], arrays[3]
    K, _, _, _, half, width = bank.shape
    tokens = tok.shape[0]
    quarter, part, length = tokens // 2, width // 2, 2 * tokens
    count = S * F * G
    low = lambda *shape: pltpu.VMEM(shape, BF16)
    high = lambda *shape: pltpu.VMEM(shape, F32)
    specs = [ANY] * len(arrays)
    specs[2] = specs[-1] = VMEM
    return pl.pallas_call(
        functools.partial(backward_kernel, sizes),
        out_shape=(
            jax.ShapeDtypeStruct((G // 2, K, 2, half, width), F32),
            jax.ShapeDtypeStruct((S * F, G // 2, 16, width), BF16),
            jax.ShapeDtypeStruct((2 * S * F, S * F, 128), F32),
            jax.ShapeDtypeStruct((2, quarter, width), BF16),
            jax.ShapeDtypeStruct((2, quarter, width), BF16),
        ),
        in_specs=specs,
        out_specs=(ANY,) * 5,
        scratch_shapes=[
            low(K, S, F, half, width),
            low(2, S, F, half, width),
            low(RING, S, F, half, width),
            low(K, 2, F, half, width),
            low(K, F, half, width),
            low(K, F, half, width),
            high(4, half, width),
            low(2, S, F, 2, half, width),
            low(tokens, width),
            low(tokens, width),
            high(tokens, width),
            high(tokens, width),
            low(tokens, width),
            low(tokens, width),
            low(tokens, width),
            high(tokens, width),
            low(tokens, width),
            low(tokens, part),
            low(length, part),
            low(2, 4, length, 2 * HD),
            high(2, length, 2 * HD),
            low(2, 3, length, 2 * HD),
            low(3, tokens, width),
            high(14, 8, width),
            high(16, width),
            high(16, width),
            high(16, width),
            low(16, width),
            low(S * F, 16, width),
            high(S * F, 128),
            DMA((K,)),
            DMA((K,)),
            DMA((K, 2)),
            DMA((K, 2)),
            DMA((K,)),
            DMA((K,)),
            DMA((K, F)),
            DMA((K, F)),
            DMA((K,)),
            DMA((K, G)),
            DMA((K, G)),
            pltpu.SemaphoreType.REGULAR,
            DMA,
            DMA,
            DMA((count // 2,)),
            DMA((count // 2,)),
            DMA,
            DMA,
            DMA,
            DMA((2 * S * F,)),
            DMA((2 * S * F,)),
            DMA,
            DMA((2, 2)),
            DMA((2, 2)),
            DMA((2,)),
            DMA((20,)),
            DMA,
            DMA,
            DMA((4, 3)),
            DMA((4, 3)),
        ],
        compiler_params=params(3, 63),
        name="backward",
    )(*arrays)


def per_device(
    sizes,
    latents,
    conditioning,
    cotangent,
    owner_list,
    master,
    moment_one,
    moment_two,
    biases,
    bias_moment_one,
    bias_moment_two,
):
    S, F, G = sizes
    capacity, rows, width = master.shape
    half = rows // 2
    blocks = owner_list.shape[0]
    s, f, g = lax.axis_index("seq"), lax.axis_index("fsdp"), lax.axis_index("grp")
    core = g % 2
    T = S * F

    block_slot, mine, slot_block, slot_live = slot_tables(owner_list, g, capacity)
    picked = pick_blocks(master, block_slot, mine)
    cond_rows = conditioning.reshape(2 * width // 128, 128)
    bias_rows = jnp.pad(biases, ((0, 2), (0, 0)))
    saved = forward(sizes, picked, cond_rows, latents[:, 0], cotangent[:, 0], bias_rows)
    saved = (saved[0], saved[1].reshape(-1, width)) + tuple(saved[2:])
    silu = jax.nn.silu(lax.dynamic_index_in_dim(conditioning, s // 2, 0, keepdims=False))
    silu = jnp.where(core == s % 2, silu.astype(BF16).astype(F32), 0.0)
    silu = jnp.pad(silu, ((0, 7), (0, 0)))
    reduced, smalls, cond_all, out_lat, in_lat = backward(sizes, *saved, silu)

    mod_grad = smalls[:, :, :6].reshape(-1, 6, width)
    silu_mine = lax.dynamic_slice_in_dim(smalls[:, :, 14], (s * F + f) * rows, rows, 2)
    mod_weight_grads = jnp.einsum(
        "nr,nje->jre", silu_mine.reshape(-1, rows), mod_grad, preferred_element_type=F32
    )
    linear_grads = jnp.sum(reduced, axis=0) if G > 2 else reduced[0]
    new_master, new_one, new_two, new_copies = adam_slots(
        master,
        linear_grads.reshape(LINEAR, rows, width),
        mod_weight_grads,
        moment_one,
        moment_two,
        slot_block,
        slot_live,
    )

    cond_full = cond_all.reshape(S, F, 2, T, 128 // half, half).sum(axis=4)
    cond_full = cond_full.transpose(3, 0, 1, 2, 4).reshape(2, 2, F, width)
    cond_mine = lax.dynamic_index_in_dim(cond_full, core, 1, keepdims=False)
    cond_mine = lax.dynamic_index_in_dim(cond_mine, f, 1, keepdims=False)
    _, silu_pull = jax.vjp(jax.nn.silu, conditioning)
    cond_grad = silu_pull(cond_mine[:, None])[0]

    sums = jnp.sum(smalls.astype(F32), axis=(0, 1))
    bias_total = jnp.concatenate([sums[6:14], sums[:6]], axis=0)
    new_biases, new_bias_one, new_bias_two = adam_step(
        biases, bias_total, bias_moment_one, bias_moment_two, RATE_BIAS
    )
    return (
        out_lat[:, None],
        in_lat[:, None].astype(F32),
        cond_grad,
        new_master,
        new_one,
        new_two,
        new_copies,
        new_biases,
        new_bias_one,
        new_bias_two,
    )


def solution(mesh):
    sizes = (mesh.shape["seq"], mesh.shape["fsdp"], mesh.shape["grp"])
    tokens = P(None, ("fsdp", "grp"), "seq", None)
    vector = P(None, ("fsdp", "grp"), None)
    slots = P("grp", ("seq", "fsdp"), None)
    in_specs = (tokens, vector, tokens, P(), slots, slots, slots, P(), P(), P())
    out_specs = (tokens, tokens, vector, slots, slots, slots, slots, P(), P(), P())
    return jax.shard_map(
        functools.partial(per_device, sizes),
        mesh=mesh,
        in_specs=in_specs,
        out_specs=out_specs,
        check_vma=False,
    )
```

```python
import functools
import math

import jax
import jax.numpy as jnp
from jax import lax
from jax.experimental import pallas as pl
from jax.experimental.pallas import tpu as pltpu
from jax.sharding import PartitionSpec as P

HD = 64
STEP = 5
EPS_NORM = 1e-06
BETA_ONE = 0.5
BETA_TWO = 0.5
RATE_WEIGHT = 0.03
RATE_BIAS = 0.1
DECAY = 0.1
ADAM_EPS = 1e-08

MESH = pl.DeviceIdType.MESH
ANY = pl.BlockSpec(memory_space=pl.ANY)
VMEM = pl.BlockSpec(memory_space=pltpu.VMEM)
F32 = jnp.float32
BF16 = jnp.bfloat16
DMA = pltpu.SemaphoreType.DMA
LINEAR = 12


def params(cid, vmem=48):
    return pltpu.CompilerParams(
        collective_id=cid, has_side_effects=True, vmem_limit_bytes=vmem * 1024 * 1024
    )


def remote(src, dst, send_sem, recv_sem, device):
    return pltpu.make_async_remote_copy(
        src_ref=src,
        dst_ref=dst,
        send_sem=send_sem,
        recv_sem=recv_sem,
        device_id=device,
        device_id_type=MESH,
    )


class Place:
    def __init__(self, sizes):
        self.S, self.F, self.G = sizes
        self.s = lax.axis_index("seq")
        self.f = lax.axis_index("fsdp")
        self.g = lax.axis_index("grp")
        self.c = lax.rem(self.g, 2)
        self.base = self.g - self.c
        self.sib = self.base + 1 - self.c
        odd = lax.rem(self.s, 2)
        self.sx = self.s + 1 - 2 * odd
        self.sy = lax.rem(self.s + 2, 4)
        self.sa = self.sx + self.c * (self.sy - self.sx)
        self.sb = self.sy + self.c * (self.sx - self.sy)

    def sibling(self):
        return (self.s, self.f, self.sib)


def meet_loop(count, device_of):
    bar = pltpu.get_barrier_semaphore()

    def one(i, carry):
        pl.semaphore_signal(bar, inc=1, device_id=device_of(i), device_id_type=MESH)
        return carry

    lax.fori_loop(1, count, one, 0)
    pl.semaphore_wait(bar, count - 1)


def slot_tables(owner_list, group, capacity):
    blocks = owner_list.shape[0]
    position = jnp.arange(blocks, dtype=jnp.int32)
    same = owner_list[:, None] == owner_list[None, :]
    before = position[None, :] < position[:, None]
    ranks = jnp.sum(jnp.where(same & before, 1, 0), axis=1).astype(jnp.int32)
    mine = owner_list == group
    slots = jnp.arange(capacity, dtype=jnp.int32)
    holds = mine[None, :] & (ranks[None, :] == slots[:, None])
    slot_block = jnp.sum(jnp.where(holds, position[None, :], 0), axis=1).astype(jnp.int32)
    slot_live = jnp.any(holds, axis=1).astype(jnp.int32)
    block_slot = jnp.where(mine, ranks, 0).astype(jnp.int32)
    return block_slot, mine.astype(jnp.int32), slot_block, slot_live


def pick_kernel(slot_ref, mine_ref, master_ref, out_ref, buf, sems):
    blocks = out_ref.shape[0]

    def fetch(b):
        return pltpu.make_async_copy(master_ref.at[slot_ref[b]], buf.at[b], sems.at[b])

    for b in range(blocks):
        fetch(b).start()
    for b in range(blocks):
        fetch(b).wait()
        out_ref[b] = jnp.where(mine_ref[b] > 0, buf[b], 0.0).astype(BF16)


def pick_blocks(master, block_slot, mine):
    blocks = block_slot.shape[0]
    rows, width = master.shape[1:]
    scalars = pl.BlockSpec(memory_space=pltpu.SMEM)
    return pl.pallas_call(
        pick_kernel,
        out_shape=jax.ShapeDtypeStruct((blocks, rows, width), BF16),
        in_specs=[scalars, scalars, ANY],
        out_specs=VMEM,
        scratch_shapes=[pltpu.VMEM((blocks, rows, width), F32), DMA((blocks,))],
        compiler_params=pltpu.CompilerParams(vmem_limit_bytes=32 * 1024 * 1024),
        name="pick_blocks",
    )(block_slot, mine, master)


def adam_step(param, grad, one, two, rate):
    next_one = BETA_ONE * one + (1.0 - BETA_ONE) * grad
    next_two = BETA_TWO * two + (1.0 - BETA_TWO) * grad * grad
    fix_one = 1.0 - BETA_ONE**STEP
    fix_two = 1.0 - BETA_TWO**STEP
    update = next_one / fix_one / (jnp.sqrt(next_two / fix_two) + ADAM_EPS)
    return (param - rate * (update + DECAY * param), next_one, next_two)


def adam_kernel(
    sizes, block_ref, live_ref, master, linear, smalls, one, two, bias, bias_one, bias_two,
    o_master, o_one, o_two, o_copy, o_bias, o_bias_one, o_bias_two,
    params_v, grads_v, one_v, two_v, copy_v, in_sem, out_sem,
):
    S, F, G = sizes
    slots, rows, width = master.shape
    half = rows // 2
    biases = bias.shape[0]

    def fetch(j):
        return [
            pltpu.make_async_copy(src.at[j], dst.at[j], in_sem.at[j, n])
            for n, (src, dst) in enumerate(((master, params_v), (one, one_v), (two, two_v)))
        ]

    def fetch_grad(j):
        block = jnp.minimum(block_ref[j], LINEAR - 1)
        return pltpu.make_async_copy(linear.at[0, block], grads_v.at[j], in_sem.at[j, 3])

    def put(j):
        return [
            pltpu.make_async_copy(src.at[j], dst.at[j], out_sem.at[j, n])
            for n, (src, dst) in enumerate(
                ((params_v, o_master), (one_v, o_one), (two_v, o_two), (copy_v, o_copy))
            )
        ]

    def start(j):
        for copy in fetch(j):
            copy.start()

        @pl.when(block_ref[j] < LINEAR)
        def _():
            fetch_grad(j).start()

    loop(slots, start)

    table = smalls[...]
    lines = table.shape[0]
    first = (lax.axis_index("seq") * F + lax.axis_index("fsdp")) * rows
    lane, column = iota((width, rows), 0), iota((width, rows), 1)
    picked = dot(table, jnp.where(lane == first + column, 1.0, 0.0).astype(BF16)).astype(BF16)
    line, source = iota((lines, lines), 0), iota((lines, lines), 1)
    silu = dot(jnp.where(source == line - lax.rem(line, 16) + 14, 1.0, 0.0).astype(BF16), picked)
    kind = lax.rem(iota((lines, rows), 0), 16)

    line, source = iota((16, lines), 0), lax.rem(iota((16, lines), 1), 16)
    wanted = jnp.where(line < biases - 6, line + 6, line - (biases - 6))
    total = dot(jnp.where(source == wanted, 1.0, 0.0).astype(BF16), table)[0:biases]
    o_bias[...], o_bias_one[...], o_bias_two[...] = adam_step(
        bias[...], total, bias_one[...], bias_two[...], RATE_BIAS
    )

    def update(j):
        for copy in fetch(j):
            copy.wait()
        block = block_ref[j]

        @pl.when(block < LINEAR)
        def _():
            fetch_grad(j).wait()

        @pl.when(block >= LINEAR)
        def _():
            chosen = jnp.where(kind == block - LINEAR, silu, 0.0).astype(BF16)
            grads_v[j] = dot(chosen, table, TN).reshape(2, half, width)

        live = live_ref[j] > 0
        for n in range(2):
            at = (j, pl.ds(n * half, half))
            param, one_old, two_old = params_v[at], one_v[at], two_v[at]
            stepped, next_one, next_two = adam_step(
                param, grads_v[j, n], one_old, two_old, RATE_WEIGHT
            )
            new = jnp.where(live, stepped, param)
            params_v[at] = new
            one_v[at] = jnp.where(live, next_one, one_old)
            two_v[at] = jnp.where(live, next_two, two_old)
            copy_v[at] = new.astype(BF16)
        for copy in put(j):
            copy.start()

    loop(slots, update)

    def finish(j):
        for copy in put(j):
            copy.wait()

    loop(slots, finish)


def adam_slots(sizes, master, linear, smalls, one, two, bias, bias_one, bias_two, slot_block, slot_live):
    slots, rows, width = master.shape
    shape = jax.ShapeDtypeStruct(master.shape, F32)
    bias_shape = jax.ShapeDtypeStruct(bias.shape, F32)
    scalars = pl.BlockSpec(memory_space=pltpu.SMEM)
    return pl.pallas_call(
        functools.partial(adam_kernel, sizes),
        out_shape=(shape, shape, shape, jax.ShapeDtypeStruct(master.shape, BF16)) + (bias_shape,) * 3,
        in_specs=[scalars, scalars, ANY, ANY, VMEM, ANY, ANY, VMEM, VMEM, VMEM],
        out_specs=(ANY,) * 4 + (VMEM,) * 3,
        scratch_shapes=[
            pltpu.VMEM(master.shape, F32),
            pltpu.VMEM((slots, 2, rows // 2, width), F32),
            pltpu.VMEM(master.shape, F32),
            pltpu.VMEM(master.shape, F32),
            pltpu.VMEM(master.shape, BF16),
            DMA((slots, 4)),
            DMA((slots, 4)),
        ],
        compiler_params=pltpu.CompilerParams(vmem_limit_bytes=48 * 1024 * 1024),
        name="adam_slots",
    )(slot_block, slot_live, master, linear, smalls, one, two, bias, bias_one, bias_two)


ROWS = 256
CHUNK = 128
NT = (((1,), (1,)), ((), ()))
NN = (((1,), (0,)), ((), ()))
TN = (((0,), (0,)), ((), ()))


def dot(left, right, dims=NN):
    return lax.dot_general(left, right, dims, preferred_element_type=F32)


def loop(count, body):
    def one(i, carry):
        body(i)
        return carry

    lax.fori_loop(0, count, one, 0)


def aligned(index, size):
    return pl.ds(pl.multiple_of(index * size, size), size)


def norm_rows(values):
    centre = jnp.mean(values, axis=-1, keepdims=True)
    centred = values - centre
    spread = jnp.mean(centred * centred, axis=-1, keepdims=True)
    inverse = lax.rsqrt(spread + EPS_NORM)
    return centred * inverse, inverse


def iota(shape, dim):
    return lax.broadcasted_iota(jnp.int32, shape, dim)


def attend_pair(q_ref, k_ref, v_ref, a_ref, lse_ref, pair):
    length = q_ref.shape[0]
    factor = 1.0 / math.sqrt(HD)
    for h in range(2):
        cols = slice((2 * pair + h) * HD, (2 * pair + h + 1) * HD)
        key = k_ref[:, cols]
        value = v_ref[:, cols]
        for r in range(0, length, ROWS):
            rows = slice(r, r + ROWS)
            scores = dot(q_ref[rows, cols], key, NT)
            high = jnp.max(scores, axis=1, keepdims=True)
            weights = jnp.exp((scores - high) * factor)
            total = jnp.sum(weights, axis=1, keepdims=True)
            out = dot(weights.astype(BF16), value, NN) / total
            a_ref[rows, cols] = out.astype(BF16)
            lse_ref[rows, cols] = jnp.broadcast_to(high * factor + jnp.log(total), (ROWS, HD))


def forward_kernel(sizes, *refs):
    (
        picked, cond, lat, cot, bias,
        bank_o, modw_o, mod_o, tok_o, ctok, hid_o, heads_o, head_a_o, lse_o, att_o, branch_o, mid_o, hid2_o, up_o, act_o, mlp_o, res_o,
        shard, theirs, conds, msg, modg, modr, modh, mod, bank, xv, hid, stage, heads, head_a, lse, att, mid, hid2, up, act, mlp,
        gs, gr, gl, ds, dr, dl, zs, zr, as_, ar, bs, br, cs, cr, ms, mr, hs, hr, ts, tr, tl, xs, xr, save_sem,
    ) = refs
    at = Place(sizes)
    S, F, G = sizes
    K = bank.shape[0]
    half = shard.shape[1]
    blocks = picked.shape[0]
    T = 2 * S * F
    me = (at.s * F + at.f) * 2 + at.c
    quarter = lat.shape[1]
    tokens, width = xv.shape
    part = width // 2
    pieces = width // 128

    def device_of(i):
        n = lax.rem(me + i, T)
        return (lax.div(n, 2 * F), lax.rem(lax.div(n, 2), F), at.base + lax.rem(n, 2))

    bar = pltpu.get_barrier_semaphore()

    def greet(device):
        pl.semaphore_signal(bar, inc=1, device_id=device, device_id_type=MESH)

    loop(T - 1, lambda i: greet(device_of(i + 1)))
    for i in range(2, G):
        greet((at.s, at.f, lax.rem(at.base + i, G)))
    pl.semaphore_wait(bar, T - 1 + G - 2)

    def tok_move(j):
        return (2 * j + at.c, at.f, at.base + lax.div(at.s, 2))

    def tok_refs(which):
        return ((lat, xv), (cot, ctok))[which]

    def tok_to(j, which):
        src, dst = tok_refs(which)
        place = aligned(lax.rem(at.s, 2), quarter)
        return remote(
            src.at[j], dst.at[place], ts.at[which, j], tr.at[which, lax.rem(at.s, 2)], tok_move(j)
        )

    def tok_from(j, which):
        src, dst = tok_refs(which)
        place = pl.ds(j * quarter, quarter)
        return remote(src.at[0], dst.at[place], ts.at[which, j], tr.at[which, j], tok_move(j))

    def tok_local(j, which):
        src, dst = tok_refs(which)
        return pltpu.make_async_copy(src.at[j], dst.at[aligned(lax.rem(at.s, 2), quarter)], tl.at[which])

    def stays(j):
        return (2 * j + at.c == at.s) & (lax.div(at.s, 2) == at.c)

    def comes(j):
        return jnp.logical_not((2 * at.c + j == at.s) & (lax.rem(at.s, 2) == at.c))

    def tok_start(which):
        for j in range(2):
            @pl.when(stays(j))
            def _():
                tok_local(j, which).start()

            @pl.when(jnp.logical_not(stays(j)))
            def _():
                tok_to(j, which).start()

    def tok_finish(which):
        for j in range(2):
            @pl.when(stays(j))
            def _():
                tok_local(j, which).wait()

            @pl.when(jnp.logical_not(stays(j)))
            def _():
                tok_to(j, which).wait_send()

            @pl.when(comes(j))
            def _():
                tok_from(j, which).wait_recv()

    def rows_of(core):
        return picked.at[:, aligned(core, half)]

    def group_to(i):
        g = lax.rem(at.g + i, G)
        return remote(
            rows_of(lax.rem(g, 2)), theirs.at[G - 1 - i], gs.at[i], gr.at[G - 1 - i], (at.s, at.f, g)
        )

    def group_from(j):
        return remote(rows_of(0), theirs.at[j], gs.at[0], gr.at[j], at.sibling())

    group_own = pltpu.make_async_copy(rows_of(at.c), shard.at[0:blocks], gl)

    def cond_number(i):
        return lax.rem(at.f * 2 + at.c + i, 2 * F)

    def cond_to(i):
        n = cond_number(i)
        device = (at.s, lax.div(n, 2), at.base + lax.rem(n, 2))
        return remote(cond, conds.at[cond_number(0)], ds.at[i], dr.at[cond_number(0)], device)

    def cond_from(i):
        n = cond_number(i)
        return remote(cond, conds.at[n], ds.at[i], dr.at[n], at.sibling())

    cond_own = pltpu.make_async_copy(cond, conds.at[cond_number(0)], dl)

    here = at.s * F + at.f
    takes = lax.rem(at.s, 2) == at.c

    mod_give = remote(msg.at[:, 1 - at.c, :, 0:6], modg, hs.at[0], hr.at[0], at.sibling())

    def mod_to(i):
        n = lax.rem(lax.div(at.s, 2) * F + at.f + i, 2 * F)
        m, f = lax.div(n, F), lax.rem(n, F)
        return remote(
            msg.at[m, at.c, f, 0:6], modr.at[here], ms.at[i], mr.at[here], (2 * m + at.c, f, at.g)
        )

    def mod_from(i):
        n = lax.rem(here + i, S * F)
        return remote(msg.at[0, 0, 0, 0:6], modr.at[n], ms.at[0], mr.at[n], at.sibling())

    mod_swap = remote(modh, modh, hs.at[1], hr.at[1], at.sibling())

    def z_to(k, i):
        f = lax.rem(at.f + i, F)
        return remote(
            shard.at[k], bank.at[k, at.s, at.f, at.c], zs.at[k, i], zr.at[k, i], (at.s, f, at.g)
        )

    def z_from(k, i):
        f = lax.rem(at.f + F - i, F)
        return remote(shard.at[k], bank.at[k, at.s, f, at.c], zs.at[k, i], zr.at[k, i], (at.s, f, at.g))

    def a_copy(k, s):
        line = bank.at[k, s, :, at.c]
        return remote(line, line, as_.at[k], ar.at[k], (at.sa, at.f, at.g))

    def b_copy(k, s, n):
        line = bank.at[k, s, :, at.c]
        return remote(line, line, bs.at[k, n], br.at[k, n], (at.sb, at.f, at.g))

    sd = S - 1 - at.s

    def c_copy(k, s, n, core):
        line = bank.at[k, s, :, core]
        return remote(line, line, cs.at[k, n], cr.at[k, n], at.sibling())

    def z_start(k):
        for i in range(1, F):
            z_to(k, i).start()
        bank[k, at.s, at.f, at.c] = shard[k]

    def step(t):
        if t + 2 < K:
            z_start(t + 2)
        if t < K:
            for i in range(1, F):
                z_from(t, i).wait_recv()
            a_copy(t, at.s).start()
            c_copy(t, at.s, 0, at.c).start()
        if 1 <= t <= K:
            a_copy(t - 1, at.sa).wait_recv()
            b_copy(t - 1, at.s, 0).start()
            b_copy(t - 1, at.sa, 1).start()
            c_copy(t - 1, at.sa, 1, at.c).start()
        if t >= 2:
            b_copy(t - 2, at.sb, 0).wait_recv()
            c_copy(t - 2, at.sb, 2, at.c).start()
            b_copy(t - 2, sd, 1).wait_recv()
            c_copy(t - 2, sd, 3, at.c).start()

    saves = []

    def save(src, dst):
        copy = pltpu.make_async_copy(src, dst, save_sem.at[len(saves)])
        copy.start()
        saves.append(copy)
        return len(saves) - 1

    waited = set()

    def saved(n):
        if n not in waited:
            saves[n].wait()
            waited.add(n)

    def arrive(k):
        for n, s in enumerate((at.s, at.sb, at.sa, sd)):
            c_copy(k, s, n, 1 - at.c).wait_recv()
        save(bank.at[k], bank_o.at[k])

    def weights(k):
        return bank[k].reshape(width, width)

    def gather_rows():
        group_own.wait()
        for i in range(1, G):
            group_from(i - 1).wait_recv()

        def one(b):
            value = shard[b].astype(F32)
            for i in range(G - 1):
                value = value + theirs[i, b].astype(F32)
            shard[b] = value.astype(BF16)

        loop(blocks, one)
        shard[blocks:] = jnp.zeros_like(shard[blocks:])

    def modulation_parts():
        cond_own.wait()
        loop(2 * F - 1, lambda i: cond_from(i + 1).wait_recv())
        value = conds[...].reshape(2 * F * 2 * pieces, 128)
        silu = (value / (1.0 + jnp.exp(-value))).astype(BF16)
        parts = 8 * half
        first = here * 2 * half + at.c * half
        lane, column = iota((128, parts), 0), iota((128, parts), 1)
        select = jnp.where(lane == lax.rem(first, 128) + lax.rem(column, half), 1.0, 0.0)
        rows = dot(silu, select.astype(BF16)).astype(BF16)
        count = 8 * S * F
        line, source = iota((count, rows.shape[0]), 0), iota((count, rows.shape[0]), 1)
        latent = lax.div(line, 8)
        chip, depth = lax.div(latent, F), lax.rem(latent, F)
        wanted = ((depth * 2 + lax.rem(chip, 2)) * 2 + lax.div(chip, 2)) * pieces + lax.div(first, 128)
        spread = dot(jnp.where(source == wanted, 1.0, 0.0).astype(BF16), rows)
        line, column = iota((count, parts), 0), iota((count, parts), 1)
        spread = jnp.where(lax.rem(line, 8) == lax.div(column, half), spread, 0.0).astype(BF16)
        value = dot(spread, shard[K:].reshape(parts, width))
        flat = msg.reshape(count * pieces, 128)
        for n in range(pieces):
            flat[pl.ds(n, count, stride=pieces)] = value[:, n * 128 : (n + 1) * 128]
        mod_give.start()

    def modulation_send():
        mod_give.wait()

        def add(n):
            m, f = lax.div(n, F), lax.rem(n, F)
            msg[m, at.c, f, 0:6] = msg[m, at.c, f, 0:6] + modg[m, f]

        loop(2 * F, add)

        @pl.when(jnp.logical_not(takes))
        def _():
            mod_to(0).start()

        loop(2 * F - 1, lambda i: mod_to(i + 1).start())

    def modulation_sum():
        @pl.when(takes)
        def _():
            loop(S * F - 1, lambda i: mod_from(i + 1).wait_recv())
            modr[here] = msg[lax.div(at.s, 2), at.c, at.f, 0:6]
            total = modr[0]
            for n in range(1, S * F):
                total = total + modr[n]
            modh[...] = total.reshape(6 * pieces, 128)
            mod_swap.start()

        @pl.when(jnp.logical_not(takes))
        def _():
            mod_swap.wait_recv()

        for n in range(pieces):
            cols = slice(n * 128, (n + 1) * 128)
            mod[0:6, cols] = modh[pl.ds(n, 6, stride=pieces)]
        mod[0:6] = mod[0:6] + bias[8:14]
        mod[6:8] = jnp.zeros((2, width), F32)
        save(mod, mod_o)

    def prepare():
        modulation_sum()
        tok_finish(0)
        save(xv, tok_o)

        def one(i):
            rows = aligned(i, CHUNK)
            scaled, _ = norm_rows(xv[rows].astype(F32))
            hid[rows] = (scaled * (1.0 + mod[1:2]) + mod[0:1]).astype(BF16)

        loop(tokens // CHUNK, one)
        hid_saved.append(save(hid, hid_o))

    hid_saved = []

    def swap(n):
        return remote(
            stage.at[n], heads.at[n, aligned(at.c, tokens)], xs.at[n], xr.at[n], at.sibling()
        )

    def swap_from(n):
        return remote(
            stage.at[n], heads.at[n, aligned(1 - at.c, tokens)], xs.at[n], xr.at[n], at.sibling()
        )

    def project(n, bias_row):
        value = dot(hid[...], weights(n))
        if bias_row is not None:
            value = value + bias[bias_row : bias_row + 1]
        value = value.astype(BF16)
        first, second = value[:, :part], value[:, part:]
        stage[n] = jnp.where(at.c == 0, second, first)
        swap(n).start()
        heads[n, aligned(at.c, tokens)] = jnp.where(at.c == 0, first, second)

    def attend_part(pair):
        if pair == 0:
            for n in range(3):
                swap_from(n).wait_recv()
                save(heads.at[n], heads_o.at[n])
        attend_pair(heads.at[0], heads.at[1], heads.at[2], head_a, lse, pair)

    def give_out():
        return remote(
            head_a.at[aligned(1 - at.c, tokens)], att.at[:, aligned(at.c, part)], xs.at[3], xr.at[3], at.sibling()
        )

    def give_from():
        return remote(
            head_a.at[aligned(at.c, tokens)], att.at[:, aligned(1 - at.c, part)], xs.at[3], xr.at[3], at.sibling()
        )

    def send_attended():
        give_out().start()
        att[:, aligned(at.c, part)] = head_a[aligned(at.c, tokens)]
        save(head_a, head_a_o)
        save(lse, lse_o)

    def output_projection():
        give_from().wait_recv()
        save(att, att_o)
        mlp[...] = dot(att[...], weights(3)) + bias[2:3]
        branch_saved = save(mlp, branch_o)

        def rest(i):
            rows = aligned(i, CHUNK)
            middle = xv[rows].astype(F32) + mod[2:3] * mlp[rows]
            mid[rows] = middle
            scaled, _ = norm_rows(middle)
            hid2[rows] = (scaled * (1.0 + mod[4:5]) + mod[3:4]).astype(BF16)

        loop(tokens // CHUNK, rest)
        save(mid, mid_o)
        save(hid2, hid2_o)
        return branch_saved

    up_saved = []

    def upper(j):
        if j >= 2:
            saved(up_saved[j - 2])
        value = dot(hid2[...], weights(4 + j)) + bias[3 + j : 4 + j]
        up[j % 2] = value
        act[j] = jax.nn.gelu(value, approximate=True).astype(BF16)
        up_saved.append(save(up.at[j % 2], up_o.at[j]))
        save(act.at[j], act_o.at[j])

    def lower(j):
        value = dot(act[j], weights(8 + j))
        mlp[...] = value + (bias[7:8] if j == 0 else mlp[...])

    def finish_forward():
        save(mlp, mlp_o)
        saved(hid_saved[0])

        def one(i):
            rows = aligned(i, CHUNK)
            hid[rows] = (mid[rows] + mod[5:6] * mlp[rows]).astype(BF16)

        loop(tokens // CHUNK, one)
        save(hid, res_o)

    tok_start(0)
    for i in range(1, G):
        group_to(i).start()
    group_own.start()
    cond_own.start()
    loop(2 * F - 1, lambda i: cond_to(i + 1).start())
    gather_rows()
    z_start(0)
    z_start(1)
    modulation_parts()
    save(shard.at[K:blocks], modw_o)
    modulation_send()
    for t in range(K + 2):
        step(t)
        if t == 1:
            prepare()
        if t >= 2:
            arrive(t - 2)
        if t in (2, 3, 4):
            project(t - 2, (0, None, 1)[t - 2])
        if 5 <= t <= 8:
            attend_part(t - 5)
        if t == 8:
            send_attended()
        if t == 9:
            branch_saved = output_projection()
            upper(0)
        if t == 10:
            upper(1)
            upper(2)
        if t == 11:
            upper(3)
            saved(branch_saved)
            lower(0)
            lower(1)
        if t == 12:
            tok_start(1)
            lower(2)
        if t == 13:
            lower(3)
    finish_forward()

    def finish(k):
        for i in range(1, F):
            z_to(k, i).wait_send()
        a_copy(k, at.s).wait_send()
        b_copy(k, at.s, 0).wait_send()
        b_copy(k, at.sa, 1).wait_send()
        for n, s in enumerate((at.s, at.sa, at.sb, sd)):
            c_copy(k, s, n, at.c).wait_send()

    loop(K, finish)
    for i in range(1, G):
        group_to(i).wait_send()
    loop(2 * F - 1, lambda i: cond_to(i + 1).wait_send())
    loop(2 * F - 1, lambda i: mod_to(i + 1).wait_send())

    @pl.when(takes)
    def _():
        mod_swap.wait_send()

    @pl.when(jnp.logical_not(takes))
    def _():
        mod_to(0).wait_send()

    for n in range(3):
        swap(n).wait_send()
    give_out().wait_send()
    for n in range(len(saves)):
        saved(n)
    tok_finish(1)


def forward(sizes, picked, cond, lat, cot, bias):
    S, F, G = sizes
    blocks, rows, width = picked.shape
    K, half, T = LINEAR, rows // 2, 2 * S * F
    tokens = 2 * lat.shape[1]
    length, part = 2 * tokens, width // 2
    low = lambda *shape: (shape, BF16)
    high = lambda *shape: (shape, F32)
    outs = (
        low(K, S, F, 2, half, width),
        low(blocks - K, half, width),
        high(8, width),
        low(tokens, width),
        low(tokens, width),
        low(tokens, width),
        low(3, length, part),
        low(length, part),
        high(length, part),
        low(tokens, width),
        high(tokens, width),
        high(tokens, width),
        low(tokens, width),
        high(4, tokens, width),
        low(4, tokens, width),
        high(tokens, width),
        low(tokens, width),
    )
    scratch = (
        low(K + 8, half, width),
        low(G - 1, blocks, half, width),
        high(2 * F, 2 * width // 128, 128),
        high(2, 2, F, 8, width // 128, 128),
        high(2, F, 6, width // 128, 128),
        high(S * F, 6, width // 128, 128),
        high(6 * width // 128, 128),
        high(8, width),
        low(K, S, F, 2, half, width),
        low(tokens, width),
        low(tokens, width),
        low(3, tokens, part),
        low(3, length, part),
        low(length, part),
        high(length, part),
        low(tokens, width),
        high(tokens, width),
        low(tokens, width),
        high(2, tokens, width),
        low(4, tokens, width),
        high(tokens, width),
    )
    sems = (
        (G,), (G,), None, (2 * F,), (2 * F,), None, (K, F), (K, F), (K,), (K,), (K, 2), (K, 2), (K, 4), (K, 4),
        (2 * F,), (S * F,), (2,), (2,), (2, 2), (2, 2), (2,), (4,), (4,), (40,),
    )
    return pl.pallas_call(
        functools.partial(forward_kernel, sizes),
        out_shape=tuple(jax.ShapeDtypeStruct(*o) for o in outs),
        in_specs=[ANY] * 4 + [VMEM],
        out_specs=(ANY,) * len(outs),
        scratch_shapes=[pltpu.VMEM(*s) for s in scratch] + [DMA if n is None else DMA(n) for n in sems],
        compiler_params=params(2, 63),
        name="forward",
    )(picked, cond, lat, cot, bias)


RING = 4
ORDER = (8, 4, 9, 5, 10, 6, 11, 7, 3, 0, 1, 2)


def gelu_slope(values):
    scale = 0.7978845608
    square = values * values
    bend = jnp.tanh(scale * values * (1.0 + 0.044715 * square))
    return 0.5 * (1.0 + bend) + 0.5 * values * (1.0 - bend * bend) * (
        scale * (1.0 + 3.0 * 0.044715 * square)
    )


def attend_pair_back(q, k, v, a, lse_ref, da_ref, pair, dq_ref, dk_ref, dv_ref):
    length = q.shape[0]
    factor = 1.0 / math.sqrt(HD)
    for h in range(2):
        cols = slice(h * HD, (h + 1) * HD)
        grad_cols = slice((2 * pair + h) * HD, (2 * pair + h + 1) * HD)
        key = k[:, cols]
        value = v[:, cols]
        dk = jnp.zeros((HD, length), F32)
        dv = jnp.zeros((HD, length), F32)
        for r in range(0, length, ROWS):
            rows = slice(r, r + ROWS)
            query = q[rows, cols]
            grad = da_ref[rows, grad_cols]
            lse = lse_ref[rows, h * HD : h * HD + 1]
            scores = dot(query, key, NT)
            probs = jnp.exp(scores * factor - lse)
            row_dot = jnp.sum(grad.astype(F32) * a[rows, cols].astype(F32), axis=1, keepdims=True)
            weight_grad = dot(grad, value, NT)
            score_grad = (probs * (weight_grad - row_dot)).astype(BF16)
            dq_ref[rows, cols] = (dot(score_grad, key, NN) * factor).astype(BF16)
            dk = dk + dot(query.T, score_grad, NN)
            dv = dv + dot(grad.T, probs.astype(BF16), NN)
        dk_ref[:, cols] = (dk * factor).T.astype(BF16)
        dv_ref[:, cols] = dv.T.astype(BF16)


def backward_kernel(sizes, *refs):
    (
        bank, modw, mod, tok, ctok, hid, heads, head_a, lse, att, branch, mid, hid2, up, act, mlp, res, silu,
        red, smalls, cgs, out_lat, in_lat,
        mine, give, r0, r1, r2, r3, total, wbuf,
        ebuf, dfb, f0, f1, a0, a1, dub, dh2, h2b, stage, dah, qkva, lsev, dpair, dqt, accs, small, sv, sw, swb, smv, cg,
        cs, cr, bs, br, as_, ar, zs, zr, os_, rs, rr, free, vs, vr, ws, wr, wl, us, ur, ds, dr, dl, ts, tr, tl, loads, xs, xr, ps, pr,
    ) = refs
    at = Place(sizes)
    S, F, G = sizes
    K = mine.shape[0]
    half = mine.shape[3]
    tokens, width = ebuf.shape
    part = width // 2
    band = width // S
    count = S * F * G
    me = (at.s * F + at.f) * G + at.g
    quarter = out_lat.shape[1]
    sd = S - 1 - at.s
    chunks = tokens // CHUNK

    def device_of(i):
        n = lax.rem(me + i, count)
        return (lax.div(n, F * G), lax.rem(lax.div(n, G), F), lax.rem(n, G))

    meet_loop(count, device_of)

    def c_copy(r):
        return remote(give.at[r % 2], r0.at[r % RING], cs.at[r], cr.at[r], at.sibling())

    def b_copy(r, s, n):
        return remote(mine.at[r, s], r1.at[r, n], bs.at[r, n], br.at[r, n], (at.sb, at.f, at.g))

    def a_copy(r):
        return remote(mine.at[r, at.sa], r2.at[r], as_.at[r], ar.at[r], (at.sa, at.f, at.g))

    def z_to(r, i):
        f = lax.rem(at.f + i, F)
        return remote(mine.at[r, at.s, f], r3.at[r, i], zs.at[r, i], zr.at[r, i], (at.s, f, at.g))

    pair = lax.div(at.g, 2)

    def out_copy(r):
        return pltpu.make_async_copy(total.at[r % 4], red.at[pair, ORDER[r], at.c], os_.at[r])

    def out_to(r, i):
        g = lax.rem(at.g + i, G)
        return remote(
            total.at[r % 4], red.at[pair, ORDER[r], at.c], rs.at[r, i], rr.at[r, i], (at.s, at.f, g)
        )

    def out_from(r, i):
        g = lax.rem(at.g + G - i, G)
        return remote(
            total.at[r % 4], red.at[lax.div(g, 2), ORDER[r], lax.rem(g, 2)], rs.at[r, i], rr.at[r, i], at.sibling()
        )

    def out_done(r):
        out_copy(r).wait()
        for i in range(1, G):
            out_to(r, i).wait_send()

    def add_line(dst, src):
        def one(f):
            dst[f] = (dst[f].astype(F32) + src[f].astype(F32)).astype(BF16)

        loop(F, one)

    def hop0(r):
        c_copy(r).wait_recv()
        loop(S, lambda s: add_line(mine.at[r, s], r0.at[r % RING, s]))
        if r + RING < K:
            pl.semaphore_signal(free, inc=1, device_id=at.sibling(), device_id_type=MESH)
        b_copy(r, at.sb, 0).start()
        b_copy(r, sd, 1).start()

    def hop1(r):
        b_copy(r, at.sb, 0).wait_recv()
        b_copy(r, sd, 1).wait_recv()
        add_line(mine.at[r, at.sa], r1.at[r, 1])
        a_copy(r).start()
        add_line(mine.at[r, at.s], r1.at[r, 0])

    def hop2(r):
        a_copy(r).wait_recv()
        add_line(mine.at[r, at.s], r2.at[r])
        for i in range(1, F):
            z_to(r, i).start()

    def hop3(r):
        for i in range(1, F):
            z_to(r, i).wait_recv()
        if r >= 4:
            out_done(r - 4)
        value = mine[r, at.s, at.f].astype(F32)
        for i in range(1, F):
            value = value + r3[r, i].astype(F32)
        total[r % 4] = value
        out_copy(r).start()
        for i in range(1, G):
            out_to(r, i).start()

    def produce(r, left, right):
        if r >= 2:
            c_copy(r - 2).wait_send()

        lines = S // 2

        def one(n):
            value = dot(left[:, aligned(n, lines * band)], right[...], TN)
            value = value.astype(BF16).reshape(lines, F, 2, half, width)
            first, second = value[:, :, 0], value[:, :, 1]
            mine[r, aligned(n, lines)] = jnp.where(at.c == 0, first, second)
            give[r % 2, aligned(n, lines)] = jnp.where(at.c == 0, second, first)

        loop(2, one)
        if r >= RING:
            pl.semaphore_wait(free, 1)
        c_copy(r).start()

    def back_device(j):
        return (2 * at.c + j, at.f, at.base + lax.rem(at.s, 2))

    def back_stays(j):
        return (2 * at.c + j == at.s) & (lax.rem(at.s, 2) == at.c)

    def back_comes(m):
        return jnp.logical_not((2 * m + at.c == at.s) & (lax.div(at.s, 2) == at.c))

    def back_refs(which):
        return ((res, out_lat), (dfb, in_lat))[which]

    def back_to(j, which):
        src, dst = back_refs(which)
        m = lax.div(at.s, 2)
        return remote(
            src.at[pl.ds(j * quarter, quarter)], dst.at[m], ts.at[which, j], tr.at[which, m], back_device(j)
        )

    def back_from(m, which):
        src, dst = back_refs(which)
        return remote(
            src.at[pl.ds(0, quarter)], dst.at[m], ts.at[which, m], tr.at[which, m], back_device(m)
        )

    def back_local(j, which):
        src, dst = back_refs(which)
        return pltpu.make_async_copy(
            src.at[pl.ds(j * quarter, quarter)], dst.at[lax.div(at.s, 2)], tl.at[which]
        )

    def back_start(which):
        for j in range(2):
            @pl.when(back_stays(j))
            def _():
                back_local(j, which).start()

            @pl.when(jnp.logical_not(back_stays(j)))
            def _():
                back_to(j, which).start()

    def back_finish(which):
        for j in range(2):
            @pl.when(back_stays(j))
            def _():
                back_local(j, which).wait()

            @pl.when(jnp.logical_not(back_stays(j)))
            def _():
                back_to(j, which).wait_send()

            @pl.when(back_comes(j))
            def _():
                back_from(j, which).wait_recv()

    def load(src, dst, n):
        return pltpu.make_async_copy(src, dst, loads.at[n])

    def load_weight(k, slot):
        return load(bank.at[k], wbuf.at[slot], slot)

    ups, acts = (f0, f1), (a0, a1)

    def load_up(j):
        return load(up.at[j], ups[j % 2], 2 + j % 2)

    def load_act(j):
        return load(act.at[j], acts[j % 2], 4 + j % 2)

    def load_pair(p):
        cols = pl.ds(p * 2 * HD, 2 * HD)
        slot = p % 2
        return [load(heads.at[n, :, cols], qkva.at[slot, n], 10 + 5 * slot + n) for n in range(3)] + [
            load(head_a.at[:, cols], qkva.at[slot, 3], 13 + 5 * slot),
            load(lse.at[:, cols], lsev.at[slot], 14 + 5 * slot),
        ]

    def weights(slot):
        return wbuf[slot].reshape(width, width)

    def add_rows(i, value, cols=slice(None)):
        accs[i, :, cols] += value.reshape(-1, 8, value.shape[-1]).sum(axis=0)

    back_start(0)
    load_e, load_mlp, load_h2 = load(ctok, ebuf, 6), load(mlp, dh2, 7), load(hid2, h2b, 8)
    for copy in (load_e, load_mlp):
        copy.start()
    load_weight(8, 0).start()
    load_act(0).start()
    load_up(0).start()
    load_h2.start()
    load_weight(4, 1).start()
    load_up(1).start()
    load_act(1).start()
    accs[...] = jnp.zeros_like(accs)
    load_e.wait()
    load_mlp.wait()

    def start_rows(i):
        rows = aligned(i, CHUNK)
        grad = ebuf[rows].astype(F32)
        add_rows(5, grad * dh2[rows])
        low = (mod[5:6] * grad).astype(BF16)
        dfb[rows] = low
        add_rows(13, low.astype(F32))

    loop(chunks, start_rows)

    def active_back(j):
        load_weight(8 + j, 0).wait()
        load_up(j).wait()

        value = dot(dfb[...], weights(0), NT) * gelu_slope(ups[j % 2][...])
        low = value.astype(BF16)
        dub[...] = low
        add_rows(9 + j, low.astype(F32))
        load_weight(9 + j if j < 3 else 3, 0).start()
        if j < 2:
            load_up(j + 2).start()

    def hidden_back(j):
        load_weight(4 + j, 1).wait()

        value = dot(dub[...], weights(1), NT)
        dh2[...] = value if j == 0 else dh2[...] + value
        load_weight(5 + j if j < 3 else 0, 1).start()

    def product_eight(j):
        load_act(j).wait()
        produce(2 * j, acts[j % 2], dfb)
        if j < 2:
            load_act(j + 2).start()

    def product_four(j):
        if j == 0:
            load_h2.wait()
        produce(2 * j + 1, h2b, dub)

    load_mid, load_branch = load(mid, f0, 2), load(branch, f1, 3)
    load_att, load_hid, load_x = load(att, a0, 4), load(hid, h2b, 8), load(tok, ebuf, 6)

    def middle_back():
        load_mid.wait()
        load_branch.wait()

        def one(i):
            rows = aligned(i, CHUNK)
            scaled, inverse = norm_rows(f0[rows])
            grad = dh2[rows]
            inner = grad * (1.0 + mod[4:5])
            mean_inner = jnp.mean(inner, axis=-1, keepdims=True)
            mean_scaled = jnp.mean(inner * scaled, axis=-1, keepdims=True)
            value = ebuf[rows].astype(F32) + inverse * (inner - mean_inner - scaled * mean_scaled)
            add_rows(4, grad * scaled)
            add_rows(3, grad)
            dh2[rows] = value
            add_rows(2, value * f1[rows])
            low = (mod[2:3] * value).astype(BF16)
            dfb[rows] = low
            add_rows(8, low.astype(F32))

        loop(chunks, one)
        load_x.start()

    def swap_da(here):
        return remote(stage, dah.at[aligned(here, tokens)], xs, xr, at.sibling())

    def attended_back():
        load_weight(3, 0).wait()

        value = dot(dfb[...], weights(0), NT).astype(BF16)
        first, second = value[:, :part], value[:, part:]
        stage[...] = jnp.where(at.c == 0, second, first)
        swap_da(at.c).start()
        dah[aligned(at.c, tokens)] = jnp.where(at.c == 0, first, second)
        load_weight(1, 0).start()

    def pair_to(p, n, core):
        rows = aligned(1 - at.c, tokens)
        cols = pl.ds(pl.multiple_of(core * part + p * 2 * HD, 2 * HD), 2 * HD)
        return remote(
            dpair.at[p % 2, n, rows], dqt.at[n, :, cols], ps.at[p, n], pr.at[p, n], at.sibling()
        )

    def attend_back_part(p):
        if p == 0:
            swap_da(1 - at.c).wait_recv()
        for copy in load_pair(p):
            copy.wait()
        if p >= 2:
            for n in range(3):
                pair_to(p - 2, n, at.c).wait_send()
        slot = p % 2
        attend_pair_back(
            qkva.at[slot, 0], qkva.at[slot, 1], qkva.at[slot, 2], qkva.at[slot, 3], lsev.at[slot], dah, p,
            dpair.at[slot, 0], dpair.at[slot, 1], dpair.at[slot, 2],
        )
        cols = pl.ds(pl.multiple_of(at.c * part + p * 2 * HD, 2 * HD), 2 * HD)
        for n in range(3):
            pair_to(p, n, at.c).start()
            dqt[n, :, cols] = dpair[slot, n, aligned(at.c, tokens)]
        if p + 2 < part // (2 * HD):
            for copy in load_pair(p + 2):
                copy.start()

    def pairs_arrive():
        for p in range(part // (2 * HD)):
            for n in range(3):
                pair_to(p, n, 1 - at.c).wait_recv()

        def one(i):
            rows = aligned(i, CHUNK)
            add_rows(6, dqt[0, rows].astype(F32))
            add_rows(7, dqt[2, rows].astype(F32))

        loop(chunks, one)

    def first_back(k, slot, start):
        load_weight(k, slot).wait()

        value = dot(dqt[k], weights(slot), NT)
        f0[...] = value if start else f0[...] + value

    def input_back():
        load_x.wait()

        def one(i):
            rows = aligned(i, CHUNK)
            scaled, inverse = norm_rows(ebuf[rows].astype(F32))
            grad = f0[rows]
            inner = grad * (1.0 + mod[1:2])
            mean_inner = jnp.mean(inner, axis=-1, keepdims=True)
            mean_scaled = jnp.mean(inner * scaled, axis=-1, keepdims=True)
            value = dh2[rows] + inverse * (inner - mean_inner - scaled * mean_scaled)
            add_rows(1, grad * scaled)
            add_rows(0, grad)
            dfb[rows] = value.astype(BF16)

        loop(chunks, one)

    small_swap = remote(small, sv, vs, vr, at.sibling())
    chips = S * F * G // 2
    chip = lax.div(me, 2)
    sent = aligned(at.c, part)

    def chip_rows(n, cols):
        return smalls.at[lax.div(n, G // 2), lax.rem(n, G // 2), :, cols]

    def small_to(i):
        n = lax.rem(chip + i, chips)
        row, group = lax.div(n, G // 2), lax.rem(n, G // 2)
        device = (lax.div(row, F), lax.rem(row, F), 2 * group + at.c)
        return remote(swb.at[:, sent], chip_rows(chip, sent), ws.at[i], wr.at[chip], device)

    def small_from(i):
        n = lax.rem(chip + i, chips)
        return remote(swb.at[:, sent], chip_rows(n, sent), ws.at[i], wr.at[n], at.sibling())

    small_own = pltpu.make_async_copy(swb.at[:, sent], chip_rows(chip, sent), wl)

    def small_share(core):
        region = smalls.at[:, :, :, aligned(core, part)]
        return remote(region, region, us, ur, at.sibling())

    def small_start():
        small[...] = jnp.zeros_like(small)
        small[0:14] = accs[...].sum(axis=1)
        small[14:15] = silu[0:1]
        small_swap.start()

    def small_send():
        small_swap.wait()
        sw[...] = small[...] + sv[...]
        swb[...] = sw[...].astype(BF16)
        small_own.start()
        loop(chips - 1, lambda i: small_to(i + 1).start())

    load_modw = load(modw, dub.at[0 : 6 * half], 9)
    pair_smalls = pltpu.make_async_copy(smalls.at[:, pair], smv, dl)

    def cond_device(i):
        n = lax.rem((at.s * F + at.f) * 2 + at.c + i, 2 * S * F)
        return n, (lax.div(n, 2 * F), lax.rem(lax.div(n, 2), F), at.base + lax.rem(n, 2))

    def cond_to(i):
        n, device = cond_device(i)
        return remote(cg, cgs.at[cond_device(0)[0]], ds.at[i], dr.at[cond_device(0)[0]], device)

    def cond_from(i):
        n, device = cond_device(i)
        return remote(cg, cgs.at[n], ds.at[i], dr.at[n], at.sibling())

    cond_own = pltpu.make_async_copy(cg, cgs.at[cond_device(0)[0]], dl)

    def small_share_start():
        small_own.wait()
        loop(chips - 1, lambda i: small_from(i + 1).wait_recv())
        small_share(at.c).start()

    def cond_start():
        small_share(1 - at.c).wait_recv()
        pair_smalls.start()
        load_modw.wait()
        dub[6 * half : 8 * half] = jnp.zeros((2 * half, width), BF16)
        pair_smalls.wait()
        value = dot(smv[...].reshape(S * F * 16, width), dub[0 : 8 * half], NT)
        line, column = iota(value.shape, 0), iota(value.shape, 1)
        value = jnp.where(lax.rem(line, 16) == lax.div(column, half), value, 0.0)
        value = value.reshape(S * F, 16, 8 * half).sum(axis=1)
        rows = value[:, 0:128]
        for n in range(1, 8 * half // 128):
            rows = rows + value[:, n * 128 : (n + 1) * 128]
        cg[...] = rows
        cond_own.start()
        loop(2 * S * F - 1, lambda i: cond_to(i + 1).start())

    active_back(0)
    product_eight(0)
    hidden_back(0)
    hop0(0)
    product_four(0)
    active_back(1)
    hop0(1)
    product_eight(1)
    hidden_back(1)
    hop0(2)
    product_four(1)
    hop1(0)
    active_back(2)
    load_mid.start()
    hop0(3)
    product_eight(2)
    hidden_back(2)
    hop0(4)
    hop1(1)
    load_att.start()
    product_four(2)
    hop2(0)
    active_back(3)
    load_branch.start()
    hop0(5)
    product_eight(3)
    hidden_back(3)
    hop0(6)
    hop1(2)
    product_four(3)
    load_hid.start()
    load_modw.start()
    hop2(1)
    middle_back()
    hop0(7)
    hop1(3)
    hop3(0)
    attended_back()
    for copy in load_pair(0) + load_pair(1):
        copy.start()
    load_att.wait()
    produce(8, a0, dfb)
    hop2(2)
    attend_back_part(0)
    hop0(8)
    hop1(4)
    hop3(1)
    attend_back_part(1)
    hop1(5)
    hop2(3)
    hop3(2)
    attend_back_part(2)
    hop1(6)
    hop2(4)
    hop3(3)
    attend_back_part(3)
    hop1(7)
    hop2(5)
    hop3(4)
    pairs_arrive()
    load_hid.wait()
    produce(9, h2b, dqt.at[0])
    hop2(6)
    hop1(8)
    produce(10, h2b, dqt.at[1])
    hop0(9)
    hop3(5)
    produce(11, h2b, dqt.at[2])
    hop0(10)
    hop2(7)
    first_back(0, 1, True)
    hop0(11)
    load_weight(2, 1).start()
    first_back(1, 0, False)
    hop1(9)
    hop2(8)
    hop3(6)
    first_back(2, 1, False)
    input_back()
    small_start()
    hop1(10)
    hop2(9)
    hop3(7)
    small_send()
    hop1(11)
    back_start(1)
    hop2(10)
    hop3(8)
    small_share_start()
    hop2(11)
    hop3(9)
    cond_start()
    hop3(10)
    hop3(11)

    swap_da(at.c).wait_send()
    for p in (2, 3):
        for n in range(3):
            pair_to(p, n, at.c).wait_send()
    for r in range(K):
        if r >= K - 2:
            c_copy(r).wait_send()
        if r >= K - 4:
            out_done(r)
        for i in range(1, G):
            out_from(r, i).wait_recv()
        b_copy(r, at.sb, 0).wait_send()
        b_copy(r, sd, 1).wait_send()
        a_copy(r).wait_send()
        for i in range(1, F):
            z_to(r, i).wait_send()
    back_finish(0)
    back_finish(1)
    loop(chips - 1, lambda i: small_to(i + 1).wait_send())
    small_share(at.c).wait_send()
    cond_own.wait()
    loop(2 * S * F - 1, lambda i: cond_to(i + 1).wait_send())
    loop(2 * S * F - 1, lambda i: cond_from(i + 1).wait_recv())


def backward(sizes, *arrays):
    S, F, G = sizes
    bank, tok = arrays[0], arrays[3]
    K, _, _, _, half, width = bank.shape
    tokens = tok.shape[0]
    quarter, part, length = tokens // 2, width // 2, 2 * tokens
    count = S * F * G
    low = lambda *shape: pltpu.VMEM(shape, BF16)
    high = lambda *shape: pltpu.VMEM(shape, F32)
    specs = [ANY] * len(arrays)
    specs[2] = specs[-1] = VMEM
    return pl.pallas_call(
        functools.partial(backward_kernel, sizes),
        out_shape=(
            jax.ShapeDtypeStruct((G // 2, K, 2, half, width), F32),
            jax.ShapeDtypeStruct((S * F, G // 2, 16, width), BF16),
            jax.ShapeDtypeStruct((2 * S * F, S * F, 128), F32),
            jax.ShapeDtypeStruct((2, quarter, width), BF16),
            jax.ShapeDtypeStruct((2, quarter, width), BF16),
        ),
        in_specs=specs,
        out_specs=(ANY,) * 5,
        scratch_shapes=[
            low(K, S, F, half, width),
            low(2, S, F, half, width),
            low(RING, S, F, half, width),
            low(K, 2, F, half, width),
            low(K, F, half, width),
            low(K, F, half, width),
            high(4, half, width),
            low(2, S, F, 2, half, width),
            low(tokens, width),
            low(tokens, width),
            high(tokens, width),
            high(tokens, width),
            low(tokens, width),
            low(tokens, width),
            low(tokens, width),
            high(tokens, width),
            low(tokens, width),
            low(tokens, part),
            low(length, part),
            low(2, 4, length, 2 * HD),
            high(2, length, 2 * HD),
            low(2, 3, length, 2 * HD),
            low(3, tokens, width),
            high(14, 8, width),
            high(16, width),
            high(16, width),
            high(16, width),
            low(16, width),
            low(S * F, 16, width),
            high(S * F, 128),
            DMA((K,)),
            DMA((K,)),
            DMA((K, 2)),
            DMA((K, 2)),
            DMA((K,)),
            DMA((K,)),
            DMA((K, F)),
            DMA((K, F)),
            DMA((K,)),
            DMA((K, G)),
            DMA((K, G)),
            pltpu.SemaphoreType.REGULAR,
            DMA,
            DMA,
            DMA((count // 2,)),
            DMA((count // 2,)),
            DMA,
            DMA,
            DMA,
            DMA((2 * S * F,)),
            DMA((2 * S * F,)),
            DMA,
            DMA((2, 2)),
            DMA((2, 2)),
            DMA((2,)),
            DMA((20,)),
            DMA,
            DMA,
            DMA((4, 3)),
            DMA((4, 3)),
        ],
        compiler_params=params(3, 63),
        name="backward",
    )(*arrays)


def per_device(
    sizes,
    latents,
    conditioning,
    cotangent,
    owner_list,
    master,
    moment_one,
    moment_two,
    biases,
    bias_moment_one,
    bias_moment_two,
):
    S, F, G = sizes
    capacity, rows, width = master.shape
    half = rows // 2
    blocks = owner_list.shape[0]
    s, f, g = lax.axis_index("seq"), lax.axis_index("fsdp"), lax.axis_index("grp")
    core = g % 2
    T = S * F

    block_slot, mine, slot_block, slot_live = slot_tables(owner_list, g, capacity)
    picked = pick_blocks(master, block_slot, mine)
    cond_rows = conditioning.reshape(2 * width // 128, 128)
    saved = forward(sizes, picked, cond_rows, latents[:, 0], cotangent[:, 0], biases)
    saved = (saved[0], saved[1].reshape(-1, width)) + tuple(saved[2:])
    silu = jax.nn.silu(lax.dynamic_index_in_dim(conditioning, s // 2, 0, keepdims=False))
    silu = jnp.where(core == s % 2, silu.astype(BF16).astype(F32), 0.0)
    silu = jnp.pad(silu, ((0, 7), (0, 0)))
    reduced, smalls, cond_all, out_lat, in_lat = backward(sizes, *saved, silu)

    linear_grads = jnp.sum(reduced, axis=0, keepdims=True) if G > 2 else reduced
    (
        new_master, new_one, new_two, new_copies, new_biases, new_bias_one, new_bias_two,
    ) = adam_slots(
        sizes, master, linear_grads, smalls.reshape(-1, width), moment_one, moment_two,
        biases, bias_moment_one, bias_moment_two, slot_block, slot_live,
    )

    cond_mine = cond_all.reshape(2 * T, 2, 2, F, 128)
    cond_mine = lax.dynamic_slice(cond_mine, (0, 0, core, f, 0), (2 * T, 2, 1, 1, 128))
    cond_mine = cond_mine.reshape(2 * T, 2, 128 // half, half).sum(axis=2)
    cond_mine = cond_mine.transpose(1, 0, 2).reshape(2, width)
    _, silu_pull = jax.vjp(jax.nn.silu, conditioning)
    cond_grad = silu_pull(cond_mine[:, None])[0]

    return (
        out_lat[:, None],
        in_lat[:, None].astype(F32),
        cond_grad,
        new_master,
        new_one,
        new_two,
        new_copies,
        new_biases,
        new_bias_one,
        new_bias_two,
    )


def solution(mesh):
    sizes = (mesh.shape["seq"], mesh.shape["fsdp"], mesh.shape["grp"])
    tokens = P(None, ("fsdp", "grp"), "seq", None)
    vector = P(None, ("fsdp", "grp"), None)
    slots = P("grp", ("seq", "fsdp"), None)
    in_specs = (tokens, vector, tokens, P(), slots, slots, slots, P(), P(), P())
    out_specs = (tokens, tokens, vector, slots, slots, slots, slots, P(), P(), P())
    return jax.shard_map(
        functools.partial(per_device, sizes),
        mesh=mesh,
        in_specs=in_specs,
        out_specs=out_specs,
        check_vma=False,
    )
```

```python
import functools
import math

import jax
import jax.numpy as jnp
from jax import lax
from jax.experimental import pallas as pl
from jax.experimental.pallas import tpu as pltpu
from jax.sharding import PartitionSpec as P

HD = 64
STEP = 5
EPS_NORM = 1e-06
BETA_ONE = 0.5
BETA_TWO = 0.5
RATE_WEIGHT = 0.03
RATE_BIAS = 0.1
DECAY = 0.1
ADAM_EPS = 1e-08

MESH = pl.DeviceIdType.MESH
ANY = pl.BlockSpec(memory_space=pl.ANY)
VMEM = pl.BlockSpec(memory_space=pltpu.VMEM)
F32 = jnp.float32
BF16 = jnp.bfloat16
DMA = pltpu.SemaphoreType.DMA
LINEAR = 12
LATE = 2


def params(cid, vmem=48):
    return pltpu.CompilerParams(
        collective_id=cid, has_side_effects=True, vmem_limit_bytes=vmem * 1024 * 1024
    )


def remote(src, dst, send_sem, recv_sem, device):
    return pltpu.make_async_remote_copy(
        src_ref=src,
        dst_ref=dst,
        send_sem=send_sem,
        recv_sem=recv_sem,
        device_id=device,
        device_id_type=MESH,
    )


class Place:
    def __init__(self, sizes):
        self.S, self.F, self.G = sizes
        self.s = lax.axis_index("seq")
        self.f = lax.axis_index("fsdp")
        self.g = lax.axis_index("grp")
        self.c = lax.rem(self.g, 2)
        self.base = self.g - self.c
        self.sib = self.base + 1 - self.c
        odd = lax.rem(self.s, 2)
        self.sx = self.s + 1 - 2 * odd
        self.sy = lax.rem(self.s + 2, 4)
        self.sa = self.sx + self.c * (self.sy - self.sx)
        self.sb = self.sy + self.c * (self.sx - self.sy)

    def sibling(self):
        return (self.s, self.f, self.sib)


def meet_loop(count, device_of):
    bar = pltpu.get_barrier_semaphore()

    def one(i, carry):
        pl.semaphore_signal(bar, inc=1, device_id=device_of(i), device_id_type=MESH)
        return carry

    lax.fori_loop(1, count, one, 0)
    pl.semaphore_wait(bar, count - 1)


def slot_tables(owner_list, group, capacity):
    blocks = owner_list.shape[0]
    position = jnp.arange(blocks, dtype=jnp.int32)
    same = owner_list[:, None] == owner_list[None, :]
    before = position[None, :] < position[:, None]
    ranks = jnp.sum(jnp.where(same & before, 1, 0), axis=1).astype(jnp.int32)
    mine = owner_list == group
    slots = jnp.arange(capacity, dtype=jnp.int32)
    holds = mine[None, :] & (ranks[None, :] == slots[:, None])
    slot_block = jnp.sum(jnp.where(holds, position[None, :], 0), axis=1).astype(jnp.int32)
    slot_live = jnp.any(holds, axis=1).astype(jnp.int32)
    block_slot = jnp.where(mine, ranks, 0).astype(jnp.int32)
    return block_slot, mine.astype(jnp.int32), slot_block, slot_live


def pick_kernel(slot_ref, mine_ref, master_ref, out_ref, buf, sems):
    blocks = out_ref.shape[0]

    def fetch(b):
        return pltpu.make_async_copy(master_ref.at[slot_ref[b]], buf.at[b], sems.at[b])

    for b in range(blocks):
        fetch(b).start()
    for b in range(blocks):
        fetch(b).wait()
        out_ref[b] = jnp.where(mine_ref[b] > 0, buf[b], 0.0).astype(BF16)


def pick_blocks(master, block_slot, mine):
    blocks = block_slot.shape[0]
    rows, width = master.shape[1:]
    scalars = pl.BlockSpec(memory_space=pltpu.SMEM)
    return pl.pallas_call(
        pick_kernel,
        out_shape=jax.ShapeDtypeStruct((blocks, rows, width), BF16),
        in_specs=[scalars, scalars, ANY],
        out_specs=VMEM,
        scratch_shapes=[pltpu.VMEM((blocks, rows, width), F32), DMA((blocks,))],
        compiler_params=pltpu.CompilerParams(vmem_limit_bytes=32 * 1024 * 1024),
        name="pick_blocks",
    )(block_slot, mine, master)


def adam_step(param, grad, one, two, rate):
    next_one = BETA_ONE * one + (1.0 - BETA_ONE) * grad
    next_two = BETA_TWO * two + (1.0 - BETA_TWO) * grad * grad
    fix_one = 1.0 - BETA_ONE**STEP
    fix_two = 1.0 - BETA_TWO**STEP
    update = next_one / fix_one / (jnp.sqrt(next_two / fix_two) + ADAM_EPS)
    return (param - rate * (update + DECAY * param), next_one, next_two)


def adam_kernel(
    sizes, block_ref, live_ref, master, linear, smalls, one, two, bias, bias_one, bias_two,
    o_master, o_one, o_two, o_copy, o_bias, o_bias_one, o_bias_two,
    params_v, grads_v, one_v, two_v, copy_v, in_sem, out_sem,
):
    S, F, G = sizes
    slots, rows, width = master.shape
    half = rows // 2
    biases = bias.shape[0]

    def fetch(j):
        return [
            pltpu.make_async_copy(src.at[j], dst.at[j], in_sem.at[j, n])
            for n, (src, dst) in enumerate(((master, params_v), (one, one_v), (two, two_v)))
        ]

    def fetch_grad(j):
        block = jnp.minimum(block_ref[j], LINEAR - 1)
        return pltpu.make_async_copy(linear.at[0, block], grads_v.at[j], in_sem.at[j, 3])

    def put(j):
        return [
            pltpu.make_async_copy(src.at[j], dst.at[j], out_sem.at[j, n])
            for n, (src, dst) in enumerate(
                ((params_v, o_master), (one_v, o_one), (two_v, o_two), (copy_v, o_copy))
            )
        ]

    def start(j):
        for copy in fetch(j):
            copy.start()

        @pl.when(block_ref[j] < LINEAR)
        def _():
            fetch_grad(j).start()

    loop(slots, start)

    table = smalls[...]
    lines = table.shape[0]
    first = (lax.axis_index("seq") * F + lax.axis_index("fsdp")) * rows
    lane, column = iota((width, rows), 0), iota((width, rows), 1)
    picked = dot(table, jnp.where(lane == first + column, 1.0, 0.0).astype(BF16)).astype(BF16)
    line, source = iota((lines, lines), 0), iota((lines, lines), 1)
    silu = dot(jnp.where(source == line - lax.rem(line, 16) + 14, 1.0, 0.0).astype(BF16), picked)
    kind = lax.rem(iota((lines, rows), 0), 16)

    line, source = iota((16, lines), 0), lax.rem(iota((16, lines), 1), 16)
    wanted = jnp.where(line < biases - 6, line + 6, line - (biases - 6))
    total = dot(jnp.where(source == wanted, 1.0, 0.0).astype(BF16), table)[0:biases]
    o_bias[...], o_bias_one[...], o_bias_two[...] = adam_step(
        bias[...], total, bias_one[...], bias_two[...], RATE_BIAS
    )

    def update(j):
        for copy in fetch(j):
            copy.wait()
        block = block_ref[j]

        @pl.when(block < LINEAR)
        def _():
            fetch_grad(j).wait()

        @pl.when(block >= LINEAR)
        def _():
            chosen = jnp.where(kind == block - LINEAR, silu, 0.0).astype(BF16)
            grads_v[j] = dot(chosen, table, TN).reshape(2, half, width)

        live = live_ref[j] > 0
        for n in range(2):
            at = (j, pl.ds(n * half, half))
            param, one_old, two_old = params_v[at], one_v[at], two_v[at]
            stepped, next_one, next_two = adam_step(
                param, grads_v[j, n], one_old, two_old, RATE_WEIGHT
            )
            new = jnp.where(live, stepped, param)
            params_v[at] = new
            one_v[at] = jnp.where(live, next_one, one_old)
            two_v[at] = jnp.where(live, next_two, two_old)
            copy_v[at] = new.astype(BF16)
        for copy in put(j):
            copy.start()

    loop(slots, update)

    def finish(j):
        for copy in put(j):
            copy.wait()

    loop(slots, finish)


def adam_slots(sizes, master, linear, smalls, one, two, bias, bias_one, bias_two, slot_block, slot_live):
    slots, rows, width = master.shape
    shape = jax.ShapeDtypeStruct(master.shape, F32)
    bias_shape = jax.ShapeDtypeStruct(bias.shape, F32)
    scalars = pl.BlockSpec(memory_space=pltpu.SMEM)
    return pl.pallas_call(
        functools.partial(adam_kernel, sizes),
        out_shape=(shape, shape, shape, jax.ShapeDtypeStruct(master.shape, BF16)) + (bias_shape,) * 3,
        in_specs=[scalars, scalars, ANY, ANY, VMEM, ANY, ANY, VMEM, VMEM, VMEM],
        out_specs=(ANY,) * 4 + (VMEM,) * 3,
        scratch_shapes=[
            pltpu.VMEM(master.shape, F32),
            pltpu.VMEM((slots, 2, rows // 2, width), F32),
            pltpu.VMEM(master.shape, F32),
            pltpu.VMEM(master.shape, F32),
            pltpu.VMEM(master.shape, BF16),
            DMA((slots, 4)),
            DMA((slots, 4)),
        ],
        compiler_params=pltpu.CompilerParams(vmem_limit_bytes=48 * 1024 * 1024),
        name="adam_slots",
    )(slot_block, slot_live, master, linear, smalls, one, two, bias, bias_one, bias_two)


ROWS = 256
LINES = (2, 4, 5, 6, 7, 8, 9, 10)
CHUNK = 128
NT = (((1,), (1,)), ((), ()))
NN = (((1,), (0,)), ((), ()))
TN = (((0,), (0,)), ((), ()))


def dot(left, right, dims=NN):
    return lax.dot_general(left, right, dims, preferred_element_type=F32)


def loop(count, body):
    def one(i, carry):
        body(i)
        return carry

    lax.fori_loop(0, count, one, 0)


def aligned(index, size):
    return pl.ds(pl.multiple_of(index * size, size), size)


def norm_rows(values):
    centre = jnp.mean(values, axis=-1, keepdims=True)
    centred = values - centre
    spread = jnp.mean(centred * centred, axis=-1, keepdims=True)
    inverse = lax.rsqrt(spread + EPS_NORM)
    return centred * inverse, inverse


def iota(shape, dim):
    return lax.broadcasted_iota(jnp.int32, shape, dim)


def attend_pair(q_ref, k_ref, v_ref, a_ref, lse_ref, pair):
    length = q_ref.shape[0]
    factor = 1.0 / math.sqrt(HD)
    for h in range(2):
        cols = slice((2 * pair + h) * HD, (2 * pair + h + 1) * HD)
        key = k_ref[:, cols]
        value = v_ref[:, cols]
        for r in range(0, length, ROWS):
            rows = slice(r, r + ROWS)
            scores = dot(q_ref[rows, cols], key, NT)
            high = jnp.max(scores, axis=1, keepdims=True)
            weights = jnp.exp((scores - high) * factor)
            total = jnp.sum(weights, axis=1, keepdims=True)
            out = dot(weights.astype(BF16), value, NN) / total
            a_ref[rows, cols] = out.astype(BF16)
            lse_ref[rows, cols] = jnp.broadcast_to(high * factor + jnp.log(total), (ROWS, HD))


def forward_kernel(sizes, *refs):
    (
        picked, cond, lat, cot, bias,
        bank_o, modw_o, mod_o, tok_o, ctok, hid_o, heads_o, head_a_o, lse_o, att_o, branch_o, mid_o, hid2_o, up_o, act_o, mlp_o, res_o,
        shard, theirs, conds, msg, modg, modr, modh, mod, bank, xv, hid, stage, heads, head_a, lse, att, mid, hid2, up, act, mlp,
        gs, gr, gl, ds, dr, dl, zs, zr, as_, ar, bs, br, cs, cr,
        las, lar, lbs, lbr, lzs, lzr, lcs, lcr, ms, mr, hs, hr, ts, tr, tl, xs, xr, save_sem,
    ) = refs
    at = Place(sizes)
    S, F, G = sizes
    K = bank.shape[0]
    half = shard.shape[1]
    blocks = picked.shape[0]
    T = 2 * S * F
    me = (at.s * F + at.f) * 2 + at.c
    quarter = lat.shape[1]
    tokens, width = xv.shape
    part = width // 2
    pieces = width // 128

    def device_of(i):
        n = lax.rem(me + i, T)
        return (lax.div(n, 2 * F), lax.rem(lax.div(n, 2), F), at.base + lax.rem(n, 2))

    bar = pltpu.get_barrier_semaphore()

    def greet(device):
        pl.semaphore_signal(bar, inc=1, device_id=device, device_id_type=MESH)

    loop(T - 1, lambda i: greet(device_of(i + 1)))
    for i in range(2, G):
        greet((at.s, at.f, lax.rem(at.base + i, G)))
    pl.semaphore_wait(bar, T - 1 + G - 2)

    def tok_move(j):
        return (2 * j + at.c, at.f, at.base + lax.div(at.s, 2))

    def tok_refs(which):
        return ((lat, xv), (cot, ctok))[which]

    def tok_to(j, which):
        src, dst = tok_refs(which)
        place = aligned(lax.rem(at.s, 2), quarter)
        return remote(
            src.at[j], dst.at[place], ts.at[which, j], tr.at[which, lax.rem(at.s, 2)], tok_move(j)
        )

    def tok_from(j, which):
        src, dst = tok_refs(which)
        place = pl.ds(j * quarter, quarter)
        return remote(src.at[0], dst.at[place], ts.at[which, j], tr.at[which, j], tok_move(j))

    def tok_local(j, which):
        src, dst = tok_refs(which)
        return pltpu.make_async_copy(src.at[j], dst.at[aligned(lax.rem(at.s, 2), quarter)], tl.at[which])

    def stays(j):
        return (2 * j + at.c == at.s) & (lax.div(at.s, 2) == at.c)

    def comes(j):
        return jnp.logical_not((2 * at.c + j == at.s) & (lax.rem(at.s, 2) == at.c))

    def tok_start(which):
        for j in range(2):
            @pl.when(stays(j))
            def _():
                tok_local(j, which).start()

            @pl.when(jnp.logical_not(stays(j)))
            def _():
                tok_to(j, which).start()

    def tok_finish(which):
        for j in range(2):
            @pl.when(stays(j))
            def _():
                tok_local(j, which).wait()

            @pl.when(jnp.logical_not(stays(j)))
            def _():
                tok_to(j, which).wait_send()

            @pl.when(comes(j))
            def _():
                tok_from(j, which).wait_recv()

    def rows_of(core):
        return picked.at[:, aligned(core, half)]

    def group_to(i):
        g = lax.rem(at.g + i, G)
        return remote(
            rows_of(lax.rem(g, 2)), theirs.at[G - 1 - i], gs.at[i], gr.at[G - 1 - i], (at.s, at.f, g)
        )

    def group_from(j):
        return remote(rows_of(0), theirs.at[j], gs.at[0], gr.at[j], at.sibling())

    group_own = pltpu.make_async_copy(rows_of(at.c), shard.at[0:blocks], gl)

    def cond_number(i):
        return lax.rem(at.f * 2 + at.c + i, 2 * F)

    def cond_to(i):
        n = cond_number(i)
        device = (at.s, lax.div(n, 2), at.base + lax.rem(n, 2))
        return remote(cond, conds.at[cond_number(0)], ds.at[i], dr.at[cond_number(0)], device)

    def cond_from(i):
        n = cond_number(i)
        return remote(cond, conds.at[n], ds.at[i], dr.at[n], at.sibling())

    cond_own = pltpu.make_async_copy(cond, conds.at[cond_number(0)], dl)

    here = at.s * F + at.f
    takes = lax.rem(at.s, 2) == at.c

    mod_give = remote(msg.at[:, 1 - at.c, :, 0:6], modg, hs.at[0], hr.at[0], at.sibling())

    def mod_to(i):
        n = lax.rem(lax.div(at.s, 2) * F + at.f + i, 2 * F)
        m, f = lax.div(n, F), lax.rem(n, F)
        return remote(
            msg.at[m, at.c, f, 0:6], modr.at[here], ms.at[i], mr.at[here], (2 * m + at.c, f, at.g)
        )

    def mod_from(i):
        n = lax.rem(here + i, S * F)
        return remote(msg.at[0, 0, 0, 0:6], modr.at[n], ms.at[0], mr.at[n], at.sibling())

    mod_swap = remote(modh, modh, hs.at[1], hr.at[1], at.sibling())

    def z_to(k, i):
        f = lax.rem(at.f + i, F)
        return remote(
            shard.at[k], bank.at[k, at.s, at.f, at.c], zs.at[k, i], zr.at[k, i], (at.s, f, at.g)
        )

    def z_from(k, i):
        f = lax.rem(at.f + F - i, F)
        return remote(shard.at[k], bank.at[k, at.s, f, at.c], zs.at[k, i], zr.at[k, i], (at.s, f, at.g))

    def a_copy(k, s):
        line = bank.at[k, s, :, at.c]
        return remote(line, line, as_.at[k], ar.at[k], (at.sa, at.f, at.g))

    def b_copy(k, s, n):
        line = bank.at[k, s, :, at.c]
        return remote(line, line, bs.at[k, n], br.at[k, n], (at.sb, at.f, at.g))

    sd = S - 1 - at.s

    def c_copy(k, s, n, core):
        line = bank.at[k, s, :, core]
        return remote(line, line, cs.at[k, n], cr.at[k, n], at.sibling())

    def z_start(k):
        for i in range(1, F):
            z_to(k, i).start()
        bank[k, at.s, at.f, at.c] = shard[k]

    late = K - LATE

    def late_a(n):
        piece = bank.at[late + n, at.s, at.f, at.c]
        return remote(piece, piece, las.at[n], lar.at[n], (at.sa, at.f, at.g))

    def late_a_from(n):
        piece = bank.at[late + n, at.sa, at.f, at.c]
        return remote(piece, piece, las.at[n], lar.at[n], (at.sa, at.f, at.g))

    def late_b(n, s, i):
        piece = bank.at[late + n, s, at.f, at.c]
        return remote(piece, piece, lbs.at[n, i], lbr.at[n, i], (at.sb, at.f, at.g))

    def late_line(n, way, j, f):
        line = bank.at[late + n, :, f, at.c]
        to = jnp.clip(at.f + 1 - 2 * way, 0, F - 1)
        return remote(line, line, lzs.at[n, way, j], lzr.at[n, way, j], (at.s, to, at.g))

    def late_c(n, f, core):
        line = bank.at[late + n, :, f, core]
        return remote(line, line, lcs.at[n, f], lcr.at[n, f], at.sibling())

    def late_first(n):
        bank[late + n, at.s, at.f, at.c] = shard[late + n]
        late_a(n).start()

    def late_second(n):
        late_a_from(n).wait_recv()
        late_b(n, at.s, 0).start()
        late_b(n, at.sa, 1).start()

    def late_sends(n, j, act):
        up, down = at.f - j, at.f + j

        @pl.when((up >= 0) & (at.f < F - 1))
        def _():
            act(late_line(n, 0, j, up))

        @pl.when((down < F) & (at.f > 0))
        def _():
            act(late_line(n, 1, j, down))

    def late_round(n, j):
        if j == 0:
            late_b(n, at.sb, 0).wait_recv()
            late_b(n, sd, 1).wait_recv()
            late_sends(n, 0, lambda copy: copy.start())
            late_c(n, at.f, at.c).start()
            return
        up, down = at.f - j, at.f + j

        @pl.when(up >= 0)
        def _():
            late_line(n, 0, j - 1, up).wait_recv()

        @pl.when(down < F)
        def _():
            late_line(n, 1, j - 1, down).wait_recv()

        if j < F - 1:
            late_sends(n, j, lambda copy: copy.start())

        @pl.when(up >= 0)
        def _():
            late_c(n, up, at.c).start()

        @pl.when(down < F)
        def _():
            late_c(n, down, at.c).start()

    def late_rounds(r):
        if r < LATE * F:
            late_round(r % LATE, r // LATE)

    def step(t):
        if t + 2 < late:
            z_start(t + 2)
        if t < late:
            for i in range(1, F):
                z_from(t, i).wait_recv()
            a_copy(t, at.s).start()
            c_copy(t, at.s, 0, at.c).start()
        if 1 <= t <= late:
            a_copy(t - 1, at.sa).wait_recv()
            b_copy(t - 1, at.s, 0).start()
            b_copy(t - 1, at.sa, 1).start()
            c_copy(t - 1, at.sa, 1, at.c).start()
        if t >= 2:
            b_copy(t - 2, at.sb, 0).wait_recv()
            c_copy(t - 2, at.sb, 2, at.c).start()
            b_copy(t - 2, sd, 1).wait_recv()
            c_copy(t - 2, sd, 3, at.c).start()

    saves = []

    def save(src, dst):
        copy = pltpu.make_async_copy(src, dst, save_sem.at[len(saves)])
        copy.start()
        saves.append(copy)
        return len(saves) - 1

    waited = set()

    def saved(n):
        if n not in waited:
            saves[n].wait()
            waited.add(n)

    def arrive(k):
        if k < late:
            for n, s in enumerate((at.s, at.sb, at.sa, sd)):
                c_copy(k, s, n, 1 - at.c).wait_recv()
        else:
            for f in range(F):
                late_c(k - late, f, 1 - at.c).wait_recv()
        save(bank.at[k], bank_o.at[k])

    def weights(k):
        return bank[k].reshape(width, width)

    def gather_rows():
        group_own.wait()
        for i in range(1, G):
            group_from(i - 1).wait_recv()

        def one(b):
            value = shard[b].astype(F32)
            for i in range(G - 1):
                value = value + theirs[i, b].astype(F32)
            shard[b] = value.astype(BF16)

        loop(blocks, one)
        shard[blocks:] = jnp.zeros_like(shard[blocks:])

    def modulation_parts():
        cond_own.wait()
        loop(2 * F - 1, lambda i: cond_from(i + 1).wait_recv())
        value = conds[...].reshape(2 * F * 2 * pieces, 128)
        silu = (value / (1.0 + jnp.exp(-value))).astype(BF16)
        parts = 8 * half
        first = here * 2 * half + at.c * half
        lane, column = iota((128, parts), 0), iota((128, parts), 1)
        select = jnp.where(lane == lax.rem(first, 128) + lax.rem(column, half), 1.0, 0.0)
        rows = dot(silu, select.astype(BF16)).astype(BF16)
        count = 8 * S * F
        line, source = iota((count, rows.shape[0]), 0), iota((count, rows.shape[0]), 1)
        latent = lax.div(line, 8)
        chip, depth = lax.div(latent, F), lax.rem(latent, F)
        wanted = ((depth * 2 + lax.rem(chip, 2)) * 2 + lax.div(chip, 2)) * pieces + lax.div(first, 128)
        spread = dot(jnp.where(source == wanted, 1.0, 0.0).astype(BF16), rows)
        line, column = iota((count, parts), 0), iota((count, parts), 1)
        spread = jnp.where(lax.rem(line, 8) == lax.div(column, half), spread, 0.0).astype(BF16)
        value = dot(spread, shard[K:].reshape(parts, width))
        flat = msg.reshape(count * pieces, 128)
        for n in range(pieces):
            flat[pl.ds(n, count, stride=pieces)] = value[:, n * 128 : (n + 1) * 128]
        mod_give.start()

    def modulation_send():
        mod_give.wait()

        def add(n):
            m, f = lax.div(n, F), lax.rem(n, F)
            msg[m, at.c, f, 0:6] = msg[m, at.c, f, 0:6] + modg[m, f]

        loop(2 * F, add)

        @pl.when(jnp.logical_not(takes))
        def _():
            mod_to(0).start()

        loop(2 * F - 1, lambda i: mod_to(i + 1).start())

    def modulation_sum():
        @pl.when(takes)
        def _():
            loop(S * F - 1, lambda i: mod_from(i + 1).wait_recv())
            modr[here] = msg[lax.div(at.s, 2), at.c, at.f, 0:6]
            total = modr[0]
            for n in range(1, S * F):
                total = total + modr[n]
            modh[...] = total.reshape(6 * pieces, 128)
            mod_swap.start()

        @pl.when(jnp.logical_not(takes))
        def _():
            mod_swap.wait_recv()

        for n in range(pieces):
            cols = slice(n * 128, (n + 1) * 128)
            mod[0:6, cols] = modh[pl.ds(n, 6, stride=pieces)]
        mod[0:6] = mod[0:6] + bias[8:14]
        mod[6:8] = jnp.zeros((2, width), F32)
        save(mod, mod_o)

    def prepare():
        modulation_sum()
        tok_finish(0)
        save(xv, tok_o)

        def one(i):
            rows = aligned(i, CHUNK)
            scaled, _ = norm_rows(xv[rows].astype(F32))
            hid[rows] = (scaled * (1.0 + mod[1:2]) + mod[0:1]).astype(BF16)

        loop(tokens // CHUNK, one)
        hid_saved.append(save(hid, hid_o))

    hid_saved = []

    def swap(n):
        return remote(
            stage.at[n], heads.at[n, aligned(at.c, tokens)], xs.at[n], xr.at[n], at.sibling()
        )

    def swap_from(n):
        return remote(
            stage.at[n], heads.at[n, aligned(1 - at.c, tokens)], xs.at[n], xr.at[n], at.sibling()
        )

    def project(n, bias_row):
        value = dot(hid[...], weights(n))
        if bias_row is not None:
            value = value + bias[bias_row : bias_row + 1]
        value = value.astype(BF16)
        first, second = value[:, :part], value[:, part:]
        stage[n] = jnp.where(at.c == 0, second, first)
        swap(n).start()
        heads[n, aligned(at.c, tokens)] = jnp.where(at.c == 0, first, second)

    def attend_part(pair):
        if pair == 0:
            for n in range(3):
                swap_from(n).wait_recv()
                save(heads.at[n], heads_o.at[n])
        attend_pair(heads.at[0], heads.at[1], heads.at[2], head_a, lse, pair)

    def give_out():
        return remote(
            head_a.at[aligned(1 - at.c, tokens)], att.at[:, aligned(at.c, part)], xs.at[3], xr.at[3], at.sibling()
        )

    def give_from():
        return remote(
            head_a.at[aligned(at.c, tokens)], att.at[:, aligned(1 - at.c, part)], xs.at[3], xr.at[3], at.sibling()
        )

    def send_attended():
        give_out().start()
        att[:, aligned(at.c, part)] = head_a[aligned(at.c, tokens)]
        save(head_a, head_a_o)
        save(lse, lse_o)

    def output_projection():
        give_from().wait_recv()
        save(att, att_o)
        mlp[...] = dot(att[...], weights(3)) + bias[2:3]
        branch_saved = save(mlp, branch_o)

        def rest(i):
            rows = aligned(i, CHUNK)
            middle = xv[rows].astype(F32) + mod[2:3] * mlp[rows]
            mid[rows] = middle
            scaled, _ = norm_rows(middle)
            hid2[rows] = (scaled * (1.0 + mod[4:5]) + mod[3:4]).astype(BF16)

        loop(tokens // CHUNK, rest)
        save(mid, mid_o)
        save(hid2, hid2_o)
        return branch_saved

    up_saved = []

    def upper(j):
        if j >= 2:
            saved(up_saved[j - 2])
        value = dot(hid2[...], weights(4 + j)) + bias[3 + j : 4 + j]
        up[j % 2] = value
        act[j] = jax.nn.gelu(value, approximate=True).astype(BF16)
        up_saved.append(save(up.at[j % 2], up_o.at[j]))
        save(act.at[j], act_o.at[j])

    def lower(j):
        value = dot(act[j], weights(8 + j))
        mlp[...] = value + (bias[7:8] if j == 0 else mlp[...])

    def finish_forward():
        save(mlp, mlp_o)
        saved(hid_saved[0])

        def one(i):
            rows = aligned(i, CHUNK)
            hid[rows] = (mid[rows] + mod[5:6] * mlp[rows]).astype(BF16)

        loop(tokens // CHUNK, one)
        save(hid, res_o)

    tok_start(0)
    for i in range(1, G):
        group_to(i).start()
    group_own.start()
    cond_own.start()
    loop(2 * F - 1, lambda i: cond_to(i + 1).start())
    gather_rows()
    z_start(0)
    z_start(1)
    modulation_parts()
    save(shard.at[K:blocks], modw_o)
    modulation_send()
    for t in range(late + 2):
        step(t)
        if t == 0:
            for n in range(LATE):
                late_first(n)
        if t == 1:
            for n in range(LATE):
                late_second(n)
            prepare()
        if t in LINES:
            late_rounds(LINES.index(t))
        if t >= 2:
            arrive(t - 2)
        if t in (2, 3, 4):
            project(t - 2, (0, None, 1)[t - 2])
        if 5 <= t <= 8:
            attend_part(t - 5)
        if t == 8:
            send_attended()
        if t == 9:
            branch_saved = output_projection()
            upper(0)
        if t == 10:
            tok_start(1)
            upper(1)
            upper(2)
        if t == 11:
            upper(3)
            saved(branch_saved)
            lower(0)
    for r in range(len(LINES), LATE * F):
        late_rounds(r)
    lower(1)
    for n in range(LATE):
        arrive(late + n)
        lower(4 - LATE + n)
    finish_forward()

    def finish(k):
        for i in range(1, F):
            z_to(k, i).wait_send()
        a_copy(k, at.s).wait_send()
        b_copy(k, at.s, 0).wait_send()
        b_copy(k, at.sa, 1).wait_send()
        for n, s in enumerate((at.s, at.sa, at.sb, sd)):
            c_copy(k, s, n, at.c).wait_send()

    loop(late, finish)
    for n in range(LATE):
        late_a(n).wait_send()
        late_b(n, at.s, 0).wait_send()
        late_b(n, at.sa, 1).wait_send()
        for j in range(F - 1):
            late_sends(n, j, lambda copy: copy.wait_send())
        for f in range(F):
            late_c(n, f, at.c).wait_send()
    for i in range(1, G):
        group_to(i).wait_send()
    loop(2 * F - 1, lambda i: cond_to(i + 1).wait_send())
    loop(2 * F - 1, lambda i: mod_to(i + 1).wait_send())

    @pl.when(takes)
    def _():
        mod_swap.wait_send()

    @pl.when(jnp.logical_not(takes))
    def _():
        mod_to(0).wait_send()

    for n in range(3):
        swap(n).wait_send()
    give_out().wait_send()
    for n in range(len(saves)):
        saved(n)
    tok_finish(1)


def forward(sizes, picked, cond, lat, cot, bias):
    S, F, G = sizes
    blocks, rows, width = picked.shape
    K, half, T = LINEAR, rows // 2, 2 * S * F
    tokens = 2 * lat.shape[1]
    length, part = 2 * tokens, width // 2
    low = lambda *shape: (shape, BF16)
    high = lambda *shape: (shape, F32)
    outs = (
        low(K, S, F, 2, half, width),
        low(blocks - K, half, width),
        high(8, width),
        low(tokens, width),
        low(tokens, width),
        low(tokens, width),
        low(3, length, part),
        low(length, part),
        high(length, part),
        low(tokens, width),
        high(tokens, width),
        high(tokens, width),
        low(tokens, width),
        high(4, tokens, width),
        low(4, tokens, width),
        high(tokens, width),
        low(tokens, width),
    )
    scratch = (
        low(K + 8, half, width),
        low(G - 1, blocks, half, width),
        high(2 * F, 2 * width // 128, 128),
        high(2, 2, F, 8, width // 128, 128),
        high(2, F, 6, width // 128, 128),
        high(S * F, 6, width // 128, 128),
        high(6 * width // 128, 128),
        high(8, width),
        low(K, S, F, 2, half, width),
        low(tokens, width),
        low(tokens, width),
        low(3, tokens, part),
        low(3, length, part),
        low(length, part),
        high(length, part),
        low(tokens, width),
        high(tokens, width),
        low(tokens, width),
        high(2, tokens, width),
        low(4, tokens, width),
        high(tokens, width),
    )
    sems = (
        (G,), (G,), None, (2 * F,), (2 * F,), None, (K, F), (K, F), (K,), (K,), (K, 2), (K, 2), (K, 4), (K, 4),
        (LATE,), (LATE,), (LATE, 2), (LATE, 2), (LATE, 2, F), (LATE, 2, F), (LATE, F), (LATE, F),
        (2 * F,), (S * F,), (2,), (2,), (2, 2), (2, 2), (2,), (4,), (4,), (40,),
    )
    return pl.pallas_call(
        functools.partial(forward_kernel, sizes),
        out_shape=tuple(jax.ShapeDtypeStruct(*o) for o in outs),
        in_specs=[ANY] * 4 + [VMEM],
        out_specs=(ANY,) * len(outs),
        scratch_shapes=[pltpu.VMEM(*s) for s in scratch] + [DMA if n is None else DMA(n) for n in sems],
        compiler_params=params(2, 63),
        name="forward",
    )(picked, cond, lat, cot, bias)


RING = 4
ORDER = (8, 4, 9, 5, 10, 6, 11, 7, 3, 0, 1, 2)
LINED = (2, 7)
PLAIN = tuple(r for r in range(LINEAR) if r not in LINED)


def gelu_slope(values):
    scale = 0.7978845608
    square = values * values
    bend = jnp.tanh(scale * values * (1.0 + 0.044715 * square))
    return 0.5 * (1.0 + bend) + 0.5 * values * (1.0 - bend * bend) * (
        scale * (1.0 + 3.0 * 0.044715 * square)
    )


def attend_pair_back(q, k, v, a, lse_ref, da_ref, pair, dq_ref, dk_ref, dv_ref):
    length = q.shape[0]
    factor = 1.0 / math.sqrt(HD)
    for h in range(2):
        cols = slice(h * HD, (h + 1) * HD)
        grad_cols = slice((2 * pair + h) * HD, (2 * pair + h + 1) * HD)
        key = k[:, cols]
        value = v[:, cols]
        dk = jnp.zeros((HD, length), F32)
        dv = jnp.zeros((HD, length), F32)
        for r in range(0, length, ROWS):
            rows = slice(r, r + ROWS)
            query = q[rows, cols]
            grad = da_ref[rows, grad_cols]
            lse = lse_ref[rows, h * HD : h * HD + 1]
            scores = dot(query, key, NT)
            probs = jnp.exp(scores * factor - lse)
            row_dot = jnp.sum(grad.astype(F32) * a[rows, cols].astype(F32), axis=1, keepdims=True)
            weight_grad = dot(grad, value, NT)
            score_grad = (probs * (weight_grad - row_dot)).astype(BF16)
            dq_ref[rows, cols] = (dot(score_grad, key, NN) * factor).astype(BF16)
            dk = dk + dot(query.T, score_grad, NN)
            dv = dv + dot(grad.T, probs.astype(BF16), NN)
        dk_ref[:, cols] = (dk * factor).T.astype(BF16)
        dv_ref[:, cols] = dv.T.astype(BF16)


def backward_kernel(sizes, *refs):
    (
        bank, modw, mod, tok, ctok, hid, heads, head_a, lse, att, branch, mid, hid2, up, act, mlp, res, silu,
        red, smalls, cgs, out_lat, in_lat,
        mine, give, r0, r1, r2, r3, lz, l1, l2, total, wbuf,
        ebuf, dfb, f0, f1, a0, a1, dub, dh2, h2b, stage, dah, qkva, lsev, dpair, dqt, accs, small, sv, sw, swb, smv, cg,
        cs, cr, bs, br, as_, ar, zs, zr, lzs, lzr, os_, rs, rr, free, vs, vr, ws, wr, wl, us, ur, ds, dr, dl, ts, tr, tl, loads, xs, xr, ps, pr,
    ) = refs
    at = Place(sizes)
    S, F, G = sizes
    K = mine.shape[0]
    half = mine.shape[3]
    tokens, width = ebuf.shape
    part = width // 2
    band = width // S
    count = S * F * G
    me = (at.s * F + at.f) * G + at.g
    quarter = out_lat.shape[1]
    sd = S - 1 - at.s
    chunks = tokens // CHUNK

    def device_of(i):
        n = lax.rem(me + i, count)
        return (lax.div(n, F * G), lax.rem(lax.div(n, G), F), lax.rem(n, G))

    meet_loop(count, device_of)

    def c_copy(r):
        return remote(give.at[r % 2], r0.at[r % RING], cs.at[r], cr.at[r], at.sibling())

    def b_copy(r, s, n):
        if r in LINED:
            src, dst = mine.at[r, s, at.f], l1.at[LINED.index(r), n]
        else:
            src, dst = mine.at[r, s], r1.at[PLAIN.index(r), n]
        return remote(src, dst, bs.at[r, n], br.at[r, n], (at.sb, at.f, at.g))

    def a_copy(r):
        if r in LINED:
            src, dst = mine.at[r, at.sa, at.f], l2.at[LINED.index(r)]
        else:
            src, dst = mine.at[r, at.sa], r2.at[PLAIN.index(r)]
        return remote(src, dst, as_.at[r], ar.at[r], (at.sa, at.f, at.g))

    def z_to(r, i):
        f = lax.rem(at.f + i, F)
        return remote(
            mine.at[r, at.s, f], r3.at[PLAIN.index(r), i - 1], zs.at[r, i], zr.at[r, i], (at.s, f, at.g)
        )

    def up_line(r, i):
        tau = F - 1 - i + at.f
        to = jnp.clip(at.f + 1, 0, F - 1)
        tau_in = jnp.clip(tau, 0, F - 1)
        return tau_in, remote(
            mine.at[r, :, tau_in], lz.at[LINED.index(r), tau_in], lzs.at[LINED.index(r), 0, i], lzr.at[LINED.index(r), 0, i], (at.s, to, at.g)
        )

    def down_line(r, i):
        tau = jnp.clip(i + at.f - F + 1, 0, F - 1)
        to = jnp.clip(at.f - 1, 0, F - 1)
        place = F if i == F - 2 else tau
        return remote(
            mine.at[r, :, tau], lz.at[LINED.index(r), place], lzs.at[LINED.index(r), 1, i], lzr.at[LINED.index(r), 1, i], (at.s, to, at.g)
        )

    def line_sends(r, i, act):
        @pl.when((at.f <= i) & (at.f < F - 1))
        def _():
            act(up_line(r, i)[1])

        @pl.when((F - 1 - at.f <= i) & (at.f > 0))
        def _():
            act(down_line(r, i))

    def add_set(r, tau, place):
        def one(s):
            mine[r, s, tau] = mine[r, s, tau] + lz[LINED.index(r), place, s]

        loop(S, one)

    def line(r, i):
        if i > 0:
            @pl.when((at.f >= 1) & (at.f <= i))
            def _():
                tau = jnp.clip(F - 1 - i + at.f, 0, F - 1)
                remote(
                    mine.at[r, :, tau], lz.at[LINED.index(r), tau], lzs.at[LINED.index(r), 0, i - 1], lzr.at[LINED.index(r), 0, i - 1], at.sibling()
                ).wait_recv()
                add_set(r, tau, tau)

            @pl.when((at.f <= F - 2) & (F - 1 - at.f <= i))
            def _():
                tau = jnp.clip(i + at.f - F + 1, 0, F - 1)
                place = F if i == F - 1 else tau
                remote(
                    mine.at[r, :, tau], lz.at[LINED.index(r), place], lzs.at[LINED.index(r), 1, i - 1], lzr.at[LINED.index(r), 1, i - 1], at.sibling()
                ).wait_recv()
                add_set(r, tau, place)

        if i < F - 1:
            line_sends(r, i, lambda copy: copy.start())
        else:
            b_copy(r, at.sb, 0).start()
            b_copy(r, sd, 1).start()

    def add_piece(r, s, src):
        mine[r, s, at.f] = mine[r, s, at.f] + src

    pair = lax.div(at.g, 2)
    finals = []

    def out_copy(r):
        return pltpu.make_async_copy(total.at[finals.index(r) % 4], red.at[pair, ORDER[r], at.c], os_.at[r])

    def out_to(r, i):
        g = lax.rem(at.g + i, G)
        return remote(
            total.at[finals.index(r) % 4], red.at[pair, ORDER[r], at.c], rs.at[r, i], rr.at[r, i], (at.s, at.f, g)
        )

    def out_from(r, i):
        g = lax.rem(at.g + G - i, G)
        return remote(
            total.at[finals.index(r) % 4], red.at[lax.div(g, 2), ORDER[r], lax.rem(g, 2)], rs.at[r, i], rr.at[r, i], at.sibling()
        )

    def out_done(r):
        out_copy(r).wait()
        for i in range(1, G):
            out_to(r, i).wait_send()

    def add_line(dst, src):
        dst[...] = dst[...] + src[...]

    def hop0(r):
        c_copy(r).wait_recv()
        loop(S, lambda s: add_line(mine.at[r, s], r0.at[r % RING, s]))
        if r + RING < K:
            pl.semaphore_signal(free, inc=1, device_id=at.sibling(), device_id_type=MESH)
        if r in LINED:
            line(r, 0)
            return
        b_copy(r, at.sb, 0).start()
        b_copy(r, sd, 1).start()

    def hop1(r):
        b_copy(r, at.sb, 0).wait_recv()
        b_copy(r, sd, 1).wait_recv()
        if r in LINED:
            add_piece(r, at.sa, l1[LINED.index(r), 1])
            a_copy(r).start()
            add_piece(r, at.s, l1[LINED.index(r), 0])
            return
        add_line(mine.at[r, at.sa], r1.at[PLAIN.index(r), 1])
        a_copy(r).start()
        add_line(mine.at[r, at.s], r1.at[PLAIN.index(r), 0])

    def hop2(r):
        if r in LINED:
            return
        a_copy(r).wait_recv()
        add_line(mine.at[r, at.s], r2.at[PLAIN.index(r)])
        for i in range(1, F):
            z_to(r, i).start()

    def hop3(r):
        if r in LINED:
            a_copy(r).wait_recv()
            others = [l2.at[LINED.index(r)]]
        else:
            for i in range(1, F):
                z_to(r, i).wait_recv()
            others = [r3.at[PLAIN.index(r), i] for i in range(F - 1)]
        finals.append(r)
        if len(finals) > 4:
            out_done(finals[-5])
        value = mine[r, at.s, at.f].astype(F32)
        for other in others:
            value = value + other[...].astype(F32)
        total[finals.index(r) % 4] = value
        out_copy(r).start()
        for i in range(1, G):
            out_to(r, i).start()

    def produce(r, left, right):
        if r >= 2:
            c_copy(r - 2).wait_send()

        lines = S // 2

        def one(n):
            value = dot(left[:, aligned(n, lines * band)], right[...], TN)
            value = value.astype(BF16).reshape(lines, F, 2, half, width)
            first, second = value[:, :, 0], value[:, :, 1]
            mine[r, aligned(n, lines)] = jnp.where(at.c == 0, first, second)
            give[r % 2, aligned(n, lines)] = jnp.where(at.c == 0, second, first)

        loop(2, one)
        if r >= RING:
            pl.semaphore_wait(free, 1)
        c_copy(r).start()

    def back_device(j):
        return (2 * at.c + j, at.f, at.base + lax.rem(at.s, 2))

    def back_stays(j):
        return (2 * at.c + j == at.s) & (lax.rem(at.s, 2) == at.c)

    def back_comes(m):
        return jnp.logical_not((2 * m + at.c == at.s) & (lax.div(at.s, 2) == at.c))

    def back_refs(which):
        return ((res, out_lat), (dfb, in_lat))[which]

    def back_to(j, which):
        src, dst = back_refs(which)
        m = lax.div(at.s, 2)
        return remote(
            src.at[pl.ds(j * quarter, quarter)], dst.at[m], ts.at[which, j], tr.at[which, m], back_device(j)
        )

    def back_from(m, which):
        src, dst = back_refs(which)
        return remote(
            src.at[pl.ds(0, quarter)], dst.at[m], ts.at[which, m], tr.at[which, m], back_device(m)
        )

    def back_local(j, which):
        src, dst = back_refs(which)
        return pltpu.make_async_copy(
            src.at[pl.ds(j * quarter, quarter)], dst.at[lax.div(at.s, 2)], tl.at[which]
        )

    def back_start(which):
        for j in range(2):
            @pl.when(back_stays(j))
            def _():
                back_local(j, which).start()

            @pl.when(jnp.logical_not(back_stays(j)))
            def _():
                back_to(j, which).start()

    def back_finish(which):
        for j in range(2):
            @pl.when(back_stays(j))
            def _():
                back_local(j, which).wait()

            @pl.when(jnp.logical_not(back_stays(j)))
            def _():
                back_to(j, which).wait_send()

            @pl.when(back_comes(j))
            def _():
                back_from(j, which).wait_recv()

    def load(src, dst, n):
        return pltpu.make_async_copy(src, dst, loads.at[n])

    def load_weight(k, slot):
        return load(bank.at[k], wbuf.at[slot], slot)

    ups, acts = (f0, f1), (a0, a1)

    def load_up(j):
        return load(up.at[j], ups[j % 2], 2 + j % 2)

    def load_act(j):
        return load(act.at[j], acts[j % 2], 4 + j % 2)

    def load_pair(p):
        cols = pl.ds(p * 2 * HD, 2 * HD)
        slot = p % 2
        return [load(heads.at[n, :, cols], qkva.at[slot, n], 10 + 5 * slot + n) for n in range(3)] + [
            load(head_a.at[:, cols], qkva.at[slot, 3], 13 + 5 * slot),
            load(lse.at[:, cols], lsev.at[slot], 14 + 5 * slot),
        ]

    def weights(slot):
        return wbuf[slot].reshape(width, width)

    def add_rows(i, value, cols=slice(None)):
        accs[i, :, cols] += value.reshape(-1, 8, value.shape[-1]).sum(axis=0)

    back_start(0)
    load_e, load_mlp, load_h2 = load(ctok, ebuf, 6), load(mlp, dh2, 7), load(hid2, h2b, 8)
    for copy in (load_e, load_mlp):
        copy.start()
    load_weight(8, 0).start()
    load_act(0).start()
    load_up(0).start()
    load_h2.start()
    load_weight(4, 1).start()
    load_up(1).start()
    load_act(1).start()
    accs[...] = jnp.zeros_like(accs)
    load_e.wait()
    load_mlp.wait()

    def start_rows(i):
        rows = aligned(i, CHUNK)
        grad = ebuf[rows].astype(F32)
        add_rows(5, grad * dh2[rows])
        low = (mod[5:6] * grad).astype(BF16)
        dfb[rows] = low
        add_rows(13, low.astype(F32))

    loop(chunks, start_rows)

    def active_back(j):
        load_weight(8 + j, 0).wait()
        load_up(j).wait()

        value = dot(dfb[...], weights(0), NT) * gelu_slope(ups[j % 2][...])
        low = value.astype(BF16)
        dub[...] = low
        add_rows(9 + j, low.astype(F32))
        load_weight(9 + j if j < 3 else 3, 0).start()
        if j < 2:
            load_up(j + 2).start()
        else:
            (load_mid, load_branch)[j - 2].start()

    def hidden_back(j):
        load_weight(4 + j, 1).wait()

        value = dot(dub[...], weights(1), NT)
        dh2[...] = value if j == 0 else dh2[...] + value
        load_weight(5 + j if j < 3 else 0, 1).start()

    def product_eight(j):
        load_act(j).wait()
        produce(2 * j, acts[j % 2], dfb)
        if j < 2:
            load_act(j + 2).start()
        if j == 2:
            load_att.start()

    def product_four(j):
        if j == 0:
            load_h2.wait()
        produce(2 * j + 1, h2b, dub)
        if j == 3:
            load_hid.start()
            load_modw.start()

    def product_three():
        load_att.wait()
        produce(8, a0, dfb)

    def product_first(n):
        if n == 0:
            load_hid.wait()
        produce(9 + n, h2b, dqt.at[n])

    load_mid, load_branch = load(mid, f0, 2), load(branch, f1, 3)
    load_att, load_hid, load_x = load(att, a0, 4), load(hid, h2b, 8), load(tok, ebuf, 6)

    def middle_back():
        load_mid.wait()
        load_branch.wait()

        def one(i):
            rows = aligned(i, CHUNK)
            scaled, inverse = norm_rows(f0[rows])
            grad = dh2[rows]
            inner = grad * (1.0 + mod[4:5])
            mean_inner = jnp.mean(inner, axis=-1, keepdims=True)
            mean_scaled = jnp.mean(inner * scaled, axis=-1, keepdims=True)
            value = ebuf[rows].astype(F32) + inverse * (inner - mean_inner - scaled * mean_scaled)
            add_rows(4, grad * scaled)
            add_rows(3, grad)
            dh2[rows] = value
            add_rows(2, value * f1[rows])
            low = (mod[2:3] * value).astype(BF16)
            dfb[rows] = low
            add_rows(8, low.astype(F32))

        loop(chunks, one)
        load_x.start()

    def swap_da(here):
        return remote(stage, dah.at[aligned(here, tokens)], xs, xr, at.sibling())

    def attended_back():
        load_weight(3, 0).wait()

        value = dot(dfb[...], weights(0), NT).astype(BF16)
        first, second = value[:, :part], value[:, part:]
        stage[...] = jnp.where(at.c == 0, second, first)
        swap_da(at.c).start()
        dah[aligned(at.c, tokens)] = jnp.where(at.c == 0, first, second)
        load_weight(1, 0).start()
        for copy in load_pair(0) + load_pair(1):
            copy.start()

    def pair_to(p, n, core):
        rows = aligned(1 - at.c, tokens)
        cols = pl.ds(pl.multiple_of(core * part + p * 2 * HD, 2 * HD), 2 * HD)
        return remote(
            dpair.at[p % 2, n, rows], dqt.at[n, :, cols], ps.at[p, n], pr.at[p, n], at.sibling()
        )

    def attend_back_part(p):
        if p == 0:
            swap_da(1 - at.c).wait_recv()
        for copy in load_pair(p):
            copy.wait()
        if p >= 2:
            for n in range(3):
                pair_to(p - 2, n, at.c).wait_send()
        slot = p % 2
        attend_pair_back(
            qkva.at[slot, 0], qkva.at[slot, 1], qkva.at[slot, 2], qkva.at[slot, 3], lsev.at[slot], dah, p,
            dpair.at[slot, 0], dpair.at[slot, 1], dpair.at[slot, 2],
        )
        cols = pl.ds(pl.multiple_of(at.c * part + p * 2 * HD, 2 * HD), 2 * HD)
        for n in range(3):
            pair_to(p, n, at.c).start()
            dqt[n, :, cols] = dpair[slot, n, aligned(at.c, tokens)]
        if p + 2 < part // (2 * HD):
            for copy in load_pair(p + 2):
                copy.start()

    def pairs_arrive():
        for p in range(part // (2 * HD)):
            for n in range(3):
                pair_to(p, n, 1 - at.c).wait_recv()

        def one(i):
            rows = aligned(i, CHUNK)
            add_rows(6, dqt[0, rows].astype(F32))
            add_rows(7, dqt[2, rows].astype(F32))

        loop(chunks, one)

    def first_back(k):
        slot = (1, 0, 1)[k]
        load_weight(k, slot).wait()
        value = dot(dqt[k], weights(slot), NT)
        f0[...] = value if k == 0 else f0[...] + value
        if k == 0:
            load_weight(2, 1).start()

    def input_back():
        load_x.wait()

        def one(i):
            rows = aligned(i, CHUNK)
            scaled, inverse = norm_rows(ebuf[rows].astype(F32))
            grad = f0[rows]
            inner = grad * (1.0 + mod[1:2])
            mean_inner = jnp.mean(inner, axis=-1, keepdims=True)
            mean_scaled = jnp.mean(inner * scaled, axis=-1, keepdims=True)
            value = dh2[rows] + inverse * (inner - mean_inner - scaled * mean_scaled)
            add_rows(1, grad * scaled)
            add_rows(0, grad)
            dfb[rows] = value.astype(BF16)

        loop(chunks, one)

    small_swap = remote(small, sv, vs, vr, at.sibling())
    chips = S * F * G // 2
    chip = lax.div(me, 2)
    sent = aligned(at.c, part)

    def chip_rows(n, cols):
        return smalls.at[lax.div(n, G // 2), lax.rem(n, G // 2), :, cols]

    def small_to(i):
        n = lax.rem(chip + i, chips)
        row, group = lax.div(n, G // 2), lax.rem(n, G // 2)
        device = (lax.div(row, F), lax.rem(row, F), 2 * group + at.c)
        return remote(swb.at[:, sent], chip_rows(chip, sent), ws.at[i], wr.at[chip], device)

    def small_from(i):
        n = lax.rem(chip + i, chips)
        return remote(swb.at[:, sent], chip_rows(n, sent), ws.at[i], wr.at[n], at.sibling())

    small_own = pltpu.make_async_copy(swb.at[:, sent], chip_rows(chip, sent), wl)

    def small_share(core):
        region = smalls.at[:, :, :, aligned(core, part)]
        return remote(region, region, us, ur, at.sibling())

    def small_start():
        small[...] = jnp.zeros_like(small)
        small[0:14] = accs[...].sum(axis=1)
        small[14:15] = silu[0:1]
        small_swap.start()

    def small_send():
        small_swap.wait()
        sw[...] = small[...] + sv[...]
        swb[...] = sw[...].astype(BF16)
        small_own.start()
        loop(chips - 1, lambda i: small_to(i + 1).start())

    load_modw = load(modw, dub.at[0 : 6 * half], 9)
    pair_smalls = pltpu.make_async_copy(smalls.at[:, pair], smv, dl)

    def cond_device(i):
        n = lax.rem((at.s * F + at.f) * 2 + at.c + i, 2 * S * F)
        return n, (lax.div(n, 2 * F), lax.rem(lax.div(n, 2), F), at.base + lax.rem(n, 2))

    def cond_to(i):
        n, device = cond_device(i)
        return remote(cg, cgs.at[cond_device(0)[0]], ds.at[i], dr.at[cond_device(0)[0]], device)

    def cond_from(i):
        n, device = cond_device(i)
        return remote(cg, cgs.at[n], ds.at[i], dr.at[n], at.sibling())

    cond_own = pltpu.make_async_copy(cg, cgs.at[cond_device(0)[0]], dl)

    def small_share_start():
        small_own.wait()
        loop(chips - 1, lambda i: small_from(i + 1).wait_recv())
        small_share(at.c).start()

    def cond_start():
        small_share(1 - at.c).wait_recv()
        pair_smalls.start()
        load_modw.wait()
        dub[6 * half : 8 * half] = jnp.zeros((2 * half, width), BF16)
        pair_smalls.wait()
        value = dot(smv[...].reshape(S * F * 16, width), dub[0 : 8 * half], NT)
        line, column = iota(value.shape, 0), iota(value.shape, 1)
        value = jnp.where(lax.rem(line, 16) == lax.div(column, half), value, 0.0)
        value = value.reshape(S * F, 16, 8 * half).sum(axis=1)
        rows = value[:, 0:128]
        for n in range(1, 8 * half // 128):
            rows = rows + value[:, n * 128 : (n + 1) * 128]
        cg[...] = rows
        cond_own.start()
        loop(2 * S * F - 1, lambda i: cond_to(i + 1).start())

    active_back(0)
    product_eight(0)
    hidden_back(0)
    product_four(0)
    hop0(0)
    active_back(1)
    product_eight(1)
    hidden_back(1)
    hop0(1)
    product_four(1)
    hop0(2)
    active_back(2)
    hop0(3)
    product_eight(2)
    hidden_back(2)
    product_four(2)
    line(2, 1)
    active_back(3)
    hop1(0)
    product_eight(3)
    hop0(4)
    hop0(5)
    hop1(3)
    hidden_back(3)
    product_four(3)
    line(2, 2)
    hop1(1)
    middle_back()
    hop0(6)
    hop0(7)
    attended_back()
    product_three()
    hop2(3)
    attend_back_part(0)
    hop0(8)
    hop1(4)
    line(7, 1)
    hop2(0)
    attend_back_part(1)
    attend_back_part(2)
    hop1(6)
    line(7, 2)
    for i in range(3, F):
        line(2, i)
    hop1(5)
    attend_back_part(3)
    hop2(1)
    hop1(8)
    pairs_arrive()
    product_first(0)
    for i in range(3, F):
        line(7, i)
    hop1(2)
    product_first(1)
    hop2(6)
    hop0(9)
    product_first(2)
    first_back(0)
    hop2(8)
    hop3(2)
    hop0(10)
    hop1(7)
    hop3(0)
    first_back(1)
    hop0(11)
    first_back(2)
    hop2(4)
    input_back()
    hop3(8)
    hop1(9)
    hop3(6)
    hop1(10)
    hop2(5)
    hop3(3)
    small_start()
    hop3(1)
    hop2(9)
    small_send()
    hop1(11)
    hop2(10)
    hop3(7)
    back_start(1)
    hop2(11)
    small_share_start()
    hop3(9)
    hop3(4)
    cond_start()
    hop3(11)
    hop3(5)
    hop3(10)

    swap_da(at.c).wait_send()
    for p in (2, 3):
        for n in range(3):
            pair_to(p, n, at.c).wait_send()
    for r in range(K):
        if r >= K - 2:
            c_copy(r).wait_send()
        if r in finals[-4:]:
            out_done(r)
        for i in range(1, G):
            out_from(r, i).wait_recv()
        b_copy(r, at.sb, 0).wait_send()
        b_copy(r, sd, 1).wait_send()
        a_copy(r).wait_send()
        for i in range(F - 1 if r in LINED else 0):
            line_sends(r, i, lambda copy: copy.wait_send())
        for i in range(1, 0 if r in LINED else F):
            z_to(r, i).wait_send()
    back_finish(0)
    back_finish(1)
    loop(chips - 1, lambda i: small_to(i + 1).wait_send())
    small_share(at.c).wait_send()
    cond_own.wait()
    loop(2 * S * F - 1, lambda i: cond_to(i + 1).wait_send())
    loop(2 * S * F - 1, lambda i: cond_from(i + 1).wait_recv())


def backward(sizes, *arrays):
    S, F, G = sizes
    bank, tok = arrays[0], arrays[3]
    K, _, _, _, half, width = bank.shape
    tokens = tok.shape[0]
    quarter, part, length = tokens // 2, width // 2, 2 * tokens
    count = S * F * G
    low = lambda *shape: pltpu.VMEM(shape, BF16)
    high = lambda *shape: pltpu.VMEM(shape, F32)
    specs = [ANY] * len(arrays)
    specs[2] = specs[-1] = VMEM
    return pl.pallas_call(
        functools.partial(backward_kernel, sizes),
        out_shape=(
            jax.ShapeDtypeStruct((G // 2, K, 2, half, width), F32),
            jax.ShapeDtypeStruct((S * F, G // 2, 16, width), BF16),
            jax.ShapeDtypeStruct((2 * S * F, S * F, 128), F32),
            jax.ShapeDtypeStruct((2, quarter, width), BF16),
            jax.ShapeDtypeStruct((2, quarter, width), BF16),
        ),
        in_specs=specs,
        out_specs=(ANY,) * 5,
        scratch_shapes=[
            low(K, S, F, half, width),
            low(2, S, F, half, width),
            low(RING, S, F, half, width),
            low(K - LATE, 2, F, half, width),
            low(K - LATE, F, half, width),
            low(K - LATE, F - 1, half, width),
            low(LATE, F + 1, S, half, width),
            low(LATE, 2, half, width),
            low(LATE, half, width),
            high(4, half, width),
            low(2, S, F, 2, half, width),
            low(tokens, width),
            low(tokens, width),
            high(tokens, width),
            high(tokens, width),
            low(tokens, width),
            low(tokens, width),
            low(tokens, width),
            high(tokens, width),
            low(tokens, width),
            low(tokens, part),
            low(length, part),
            low(2, 4, length, 2 * HD),
            high(2, length, 2 * HD),
            low(2, 3, length, 2 * HD),
            low(3, tokens, width),
            high(14, 8, width),
            high(16, width),
            high(16, width),
            high(16, width),
            low(16, width),
            low(S * F, 16, width),
            high(S * F, 128),
            DMA((K,)),
            DMA((K,)),
            DMA((K, 2)),
            DMA((K, 2)),
            DMA((K,)),
            DMA((K,)),
            DMA((K, F)),
            DMA((K, F)),
            DMA((LATE, 2, F)),
            DMA((LATE, 2, F)),
            DMA((K,)),
            DMA((K, G)),
            DMA((K, G)),
            pltpu.SemaphoreType.REGULAR,
            DMA,
            DMA,
            DMA((count // 2,)),
            DMA((count // 2,)),
            DMA,
            DMA,
            DMA,
            DMA((2 * S * F,)),
            DMA((2 * S * F,)),
            DMA,
            DMA((2, 2)),
            DMA((2, 2)),
            DMA((2,)),
            DMA((20,)),
            DMA,
            DMA,
            DMA((4, 3)),
            DMA((4, 3)),
        ],
        compiler_params=params(3, 63),
        name="backward",
    )(*arrays)


def per_device(
    sizes,
    latents,
    conditioning,
    cotangent,
    owner_list,
    master,
    moment_one,
    moment_two,
    biases,
    bias_moment_one,
    bias_moment_two,
):
    S, F, G = sizes
    capacity, rows, width = master.shape
    half = rows // 2
    blocks = owner_list.shape[0]
    s, f, g = lax.axis_index("seq"), lax.axis_index("fsdp"), lax.axis_index("grp")
    core = g % 2
    T = S * F

    block_slot, mine, slot_block, slot_live = slot_tables(owner_list, g, capacity)
    picked = pick_blocks(master, block_slot, mine)
    cond_rows = conditioning.reshape(2 * width // 128, 128)
    saved = forward(sizes, picked, cond_rows, latents[:, 0], cotangent[:, 0], biases)
    saved = (saved[0], saved[1].reshape(-1, width)) + tuple(saved[2:])
    silu = jax.nn.silu(lax.dynamic_index_in_dim(conditioning, s // 2, 0, keepdims=False))
    silu = jnp.where(core == s % 2, silu.astype(BF16).astype(F32), 0.0)
    silu = jnp.pad(silu, ((0, 7), (0, 0)))
    reduced, smalls, cond_all, out_lat, in_lat = backward(sizes, *saved, silu)

    linear_grads = jnp.sum(reduced, axis=0, keepdims=True) if G > 2 else reduced
    (
        new_master, new_one, new_two, new_copies, new_biases, new_bias_one, new_bias_two,
    ) = adam_slots(
        sizes, master, linear_grads, smalls.reshape(-1, width), moment_one, moment_two,
        biases, bias_moment_one, bias_moment_two, slot_block, slot_live,
    )

    cond_mine = cond_all.reshape(2 * T, 2, 2, F, 128)
    cond_mine = lax.dynamic_slice(cond_mine, (0, 0, core, f, 0), (2 * T, 2, 1, 1, 128))
    cond_mine = cond_mine.reshape(2 * T, 2, 128 // half, half).sum(axis=2)
    cond_mine = cond_mine.transpose(1, 0, 2).reshape(2, width)
    _, silu_pull = jax.vjp(jax.nn.silu, conditioning)
    cond_grad = silu_pull(cond_mine[:, None])[0]

    return (
        out_lat[:, None],
        in_lat[:, None].astype(F32),
        cond_grad,
        new_master,
        new_one,
        new_two,
        new_copies,
        new_biases,
        new_bias_one,
        new_bias_two,
    )


def solution(mesh):
    sizes = (mesh.shape["seq"], mesh.shape["fsdp"], mesh.shape["grp"])
    tokens = P(None, ("fsdp", "grp"), "seq", None)
    vector = P(None, ("fsdp", "grp"), None)
    slots = P("grp", ("seq", "fsdp"), None)
    in_specs = (tokens, vector, tokens, P(), slots, slots, slots, P(), P(), P())
    out_specs = (tokens, tokens, vector, slots, slots, slots, slots, P(), P(), P())
    return jax.shard_map(
        functools.partial(per_device, sizes),
        mesh=mesh,
        in_specs=in_specs,
        out_specs=out_specs,
        check_vma=False,
    )
```

```python
import functools
import math

import jax
import jax.numpy as jnp
from jax import lax
from jax.experimental import pallas as pl
from jax.experimental.pallas import tpu as pltpu
from jax.sharding import PartitionSpec as P

HD = 64
STEP = 5
EPS_NORM = 1e-06
BETA_ONE = 0.5
BETA_TWO = 0.5
RATE_WEIGHT = 0.03
RATE_BIAS = 0.1
DECAY = 0.1
ADAM_EPS = 1e-08

MESH = pl.DeviceIdType.MESH
ANY = pl.BlockSpec(memory_space=pl.ANY)
VMEM = pl.BlockSpec(memory_space=pltpu.VMEM)
F32 = jnp.float32
BF16 = jnp.bfloat16
DMA = pltpu.SemaphoreType.DMA
LINEAR = 12
LATE = 2


def params(cid, vmem=48):
    return pltpu.CompilerParams(
        collective_id=cid, has_side_effects=True, vmem_limit_bytes=vmem * 1024 * 1024
    )


def remote(src, dst, send_sem, recv_sem, device):
    return pltpu.make_async_remote_copy(
        src_ref=src,
        dst_ref=dst,
        send_sem=send_sem,
        recv_sem=recv_sem,
        device_id=device,
        device_id_type=MESH,
    )


class Place:
    def __init__(self, sizes):
        self.S, self.F, self.G = sizes
        self.s = lax.axis_index("seq")
        self.f = lax.axis_index("fsdp")
        self.g = lax.axis_index("grp")
        self.c = lax.rem(self.g, 2)
        self.base = self.g - self.c
        self.sib = self.base + 1 - self.c
        odd = lax.rem(self.s, 2)
        self.sx = self.s + 1 - 2 * odd
        self.sy = lax.rem(self.s + 2, 4)
        self.sa = self.sx + self.c * (self.sy - self.sx)
        self.sb = self.sy + self.c * (self.sx - self.sy)

    def sibling(self):
        return (self.s, self.f, self.sib)


def pick_kernel(owner_ref, master_ref, out_ref, buf, low, sems, out_sems):
    blocks = out_ref.shape[0]
    group = lax.axis_index("grp")
    slots, mine, before = [], [], jnp.int32(0)
    for b in range(blocks):
        own = owner_ref[b] == group
        mine.append(own)
        slots.append(jnp.where(own, before, 0))
        before = before + jnp.where(own, 1, 0)

    def fetch(b):
        return pltpu.make_async_copy(master_ref.at[slots[b]], buf.at[b], sems.at[b])

    for b in range(blocks):
        fetch(b).start()
    for b in range(blocks):
        fetch(b).wait()
        low[b] = jnp.where(mine[b], buf[b], 0.0).astype(BF16)
        pltpu.make_async_copy(low.at[b], out_ref.at[b], out_sems.at[b]).start()
    for b in range(blocks):
        pltpu.make_async_copy(low.at[b], out_ref.at[b], out_sems.at[b]).wait()


def pick_blocks(master, owner_list):
    blocks = owner_list.shape[0]
    rows, width = master.shape[1:]
    return pl.pallas_call(
        pick_kernel,
        out_shape=jax.ShapeDtypeStruct((blocks, rows, width), BF16),
        in_specs=[pl.BlockSpec(memory_space=pltpu.SMEM), ANY],
        out_specs=ANY,
        scratch_shapes=[
            pltpu.VMEM((blocks, rows, width), F32),
            pltpu.VMEM((blocks, rows, width), BF16),
            DMA((blocks,)),
            DMA((blocks,)),
        ],
        compiler_params=pltpu.CompilerParams(vmem_limit_bytes=62 * 1024 * 1024),
        name="pick_blocks",
    )(owner_list, master)


def adam_step(param, grad, one, two, rate):
    next_one = BETA_ONE * one + (1.0 - BETA_ONE) * grad
    next_two = BETA_TWO * two + (1.0 - BETA_TWO) * grad * grad
    fix_one = 1.0 - BETA_ONE**STEP
    fix_two = 1.0 - BETA_TWO**STEP
    update = next_one / fix_one / (jnp.sqrt(next_two / fix_two) + ADAM_EPS)
    return (param - rate * (update + DECAY * param), next_one, next_two)


def adam_kernel(
    sizes, owner_ref, master, linear, smalls, one, two, bias, bias_one, bias_two, out_lat, in_lat,
    o_master, o_one, o_two, o_copy, o_bias, o_bias_one, o_bias_two, o_out, o_in,
    block_ref, params_v, grads_v, one_v, two_v, copy_v, out_v, low_v, high_v, in_sem, out_sem, lat_sem,
):
    S, F, G = sizes
    slots, rows, width = master.shape
    half = rows // 2
    biases = bias.shape[0]
    out_copy = pltpu.make_async_copy(out_lat, out_v, lat_sem.at[0])
    out_put = pltpu.make_async_copy(out_v, o_out, lat_sem.at[3])
    low_copy = pltpu.make_async_copy(in_lat, low_v, lat_sem.at[1])
    high_copy = pltpu.make_async_copy(high_v, o_in, lat_sem.at[2])

    group = lax.axis_index("grp")
    for j in range(slots):
        block_ref[j] = 0
    held = jnp.int32(0)
    for b in range(owner_ref.shape[0]):
        own = owner_ref[b] == group

        @pl.when(own)
        def _(b=b, held=held):
            block_ref[held] = b

        held = held + jnp.where(own, 1, 0)

    def fetch(j):
        return [
            pltpu.make_async_copy(src.at[j], dst.at[j], in_sem.at[j, n])
            for n, (src, dst) in enumerate(((master, params_v), (one, one_v), (two, two_v)))
        ]

    def fetch_grad(j):
        block = jnp.minimum(block_ref[j], LINEAR - 1)
        return pltpu.make_async_copy(linear.at[0, block], grads_v.at[j], in_sem.at[j, 3])

    def put(j):
        return [
            pltpu.make_async_copy(src.at[j], dst.at[j], out_sem.at[j, n])
            for n, (src, dst) in enumerate(
                ((params_v, o_master), (one_v, o_one), (two_v, o_two), (copy_v, o_copy))
            )
        ]

    def start(j):
        for copy in fetch(j):
            copy.start()

        @pl.when(block_ref[j] < LINEAR)
        def _():
            fetch_grad(j).start()

    loop(slots, start)
    low_copy.start()
    out_copy.start()

    table = smalls[...]
    lines = table.shape[0]
    first = (lax.axis_index("seq") * F + lax.axis_index("fsdp")) * rows
    lane, column = iota((width, rows), 0), iota((width, rows), 1)
    picked = dot(table, jnp.where(lane == first + column, 1.0, 0.0).astype(BF16)).astype(BF16)
    line, source = iota((lines, lines), 0), iota((lines, lines), 1)
    silu = dot(jnp.where(source == line - lax.rem(line, 16) + 14, 1.0, 0.0).astype(BF16), picked)
    kind = lax.rem(iota((lines, rows), 0), 16)

    line, source = iota((16, lines), 0), lax.rem(iota((16, lines), 1), 16)
    wanted = jnp.where(line < biases - 6, line + 6, line - (biases - 6))
    total = dot(jnp.where(source == wanted, 1.0, 0.0).astype(BF16), table)[0:biases]
    o_bias[...], o_bias_one[...], o_bias_two[...] = adam_step(
        bias[...], total, bias_one[...], bias_two[...], RATE_BIAS
    )

    def update(j):
        for copy in fetch(j):
            copy.wait()
        block = block_ref[j]

        @pl.when(block < LINEAR)
        def _():
            fetch_grad(j).wait()

        @pl.when(block >= LINEAR)
        def _():
            chosen = jnp.where(kind == block - LINEAR, silu, 0.0).astype(BF16)
            grads_v[j] = dot(chosen, table, TN).reshape(2, half, width)

        live = j < held
        for n in range(2):
            at = (j, pl.ds(n * half, half))
            param, one_old, two_old = params_v[at], one_v[at], two_v[at]
            stepped, next_one, next_two = adam_step(
                param, grads_v[j, n], one_old, two_old, RATE_WEIGHT
            )
            new = jnp.where(live, stepped, param)
            params_v[at] = new
            one_v[at] = jnp.where(live, next_one, one_old)
            two_v[at] = jnp.where(live, next_two, two_old)
            copy_v[at] = new.astype(BF16)
        for copy in put(j):
            copy.start()

    loop(slots, update)

    out_copy.wait()
    out_put.start()
    low_copy.wait()
    high_v[...] = low_v[...].astype(F32)
    high_copy.start()

    def finish(j):
        for copy in put(j):
            copy.wait()

    loop(slots, finish)
    out_put.wait()
    high_copy.wait()


def adam_slots(
    sizes, owner_list, master, linear, smalls, one, two, bias, bias_one, bias_two, out_lat, in_lat
):
    slots, rows, width = master.shape
    shape = jax.ShapeDtypeStruct(master.shape, F32)
    bias_shape = jax.ShapeDtypeStruct(bias.shape, F32)
    return pl.pallas_call(
        functools.partial(adam_kernel, sizes),
        out_shape=(shape, shape, shape, jax.ShapeDtypeStruct(master.shape, BF16))
        + (bias_shape,) * 3
        + (jax.ShapeDtypeStruct(out_lat.shape, BF16), jax.ShapeDtypeStruct(in_lat.shape, F32)),
        in_specs=[pl.BlockSpec(memory_space=pltpu.SMEM), ANY, ANY, VMEM, ANY, ANY]
        + [VMEM] * 3
        + [ANY] * 2,
        out_specs=(ANY,) * 4 + (VMEM,) * 3 + (ANY,) * 2,
        scratch_shapes=[
            pltpu.SMEM((slots,), jnp.int32),
            pltpu.VMEM(master.shape, F32),
            pltpu.VMEM((slots, 2, rows // 2, width), F32),
            pltpu.VMEM(master.shape, F32),
            pltpu.VMEM(master.shape, F32),
            pltpu.VMEM(master.shape, BF16),
            pltpu.VMEM(out_lat.shape, BF16),
            pltpu.VMEM(in_lat.shape, BF16),
            pltpu.VMEM(in_lat.shape, F32),
            DMA((slots, 4)),
            DMA((slots, 4)),
            DMA((4,)),
        ],
        compiler_params=pltpu.CompilerParams(vmem_limit_bytes=62 * 1024 * 1024),
        name="adam_slots",
    )(owner_list, master, linear, smalls, one, two, bias, bias_one, bias_two, out_lat, in_lat)


ROWS = 256
CHUNK = 128
NT = (((1,), (1,)), ((), ()))
NN = (((1,), (0,)), ((), ()))
TN = (((0,), (0,)), ((), ()))


def dot(left, right, dims=NN):
    return lax.dot_general(left, right, dims, preferred_element_type=F32)


def loop(count, body):
    def one(i, carry):
        body(i)
        return carry

    lax.fori_loop(0, count, one, 0)


def aligned(index, size):
    return pl.ds(pl.multiple_of(index * size, size), size)


def norm_rows(values):
    centre = jnp.mean(values, axis=-1, keepdims=True)
    centred = values - centre
    spread = jnp.mean(centred * centred, axis=-1, keepdims=True)
    inverse = lax.rsqrt(spread + EPS_NORM)
    return centred * inverse, inverse


def iota(shape, dim):
    return lax.broadcasted_iota(jnp.int32, shape, dim)


def attend_pair(q_ref, k_ref, v_ref, a_ref, lse_ref, pair):
    length = q_ref.shape[0]
    factor = 1.0 / math.sqrt(HD)
    for h in range(2):
        cols = slice((2 * pair + h) * HD, (2 * pair + h + 1) * HD)
        key = k_ref[:, cols]
        value = v_ref[:, cols]
        for r in range(0, length, ROWS):
            rows = slice(r, r + ROWS)
            scores = dot(q_ref[rows, cols], key, NT)
            high = jnp.max(scores, axis=1, keepdims=True)
            weights = jnp.exp((scores - high) * factor)
            total = jnp.sum(weights, axis=1, keepdims=True)
            out = dot(weights.astype(BF16), value, NN) / total
            a_ref[rows, cols] = out.astype(BF16)
            lse_ref[rows, cols] = jnp.broadcast_to(high * factor + jnp.log(total), (ROWS, HD))


def forward_kernel(sizes, *refs):
    (
        picked, cond, lat, cot, bias,
        bank_o, modw_o, mod_o, tok_o, ctok, hid_o, heads_o, head_a_o, lse_o, att_o, branch_o, mid_o, hid2_o, up_o, act_o, mlp_o, res_o,
        shard, theirs, conds, msg, modg, modr, modh, mod, bank, xv, hid, stage, heads, head_a, lse, att, mid, hid2, up, act, mlp,
        gs, gr, gl, ds, dr, dl, zs, zr, as_, ar, bs, br, cs, cr,
        las, lar, lbs, lbr, lzs, lzr, lcs, lcr, ms, mr, hs, hr, ts, tr, tl, xs, xr, save_sem,
    ) = refs
    at = Place(sizes)
    S, F, G = sizes
    K = bank.shape[0]
    half = shard.shape[1]
    blocks = picked.shape[0]
    T = 2 * S * F
    me = (at.s * F + at.f) * 2 + at.c
    quarter = lat.shape[1]
    tokens, width = xv.shape
    part = width // 2
    pieces = width // 128

    def device_of(i):
        n = lax.rem(me + i, T)
        return (lax.div(n, 2 * F), lax.rem(lax.div(n, 2), F), at.base + lax.rem(n, 2))

    bar = pltpu.get_barrier_semaphore()

    def greet(device):
        pl.semaphore_signal(bar, inc=1, device_id=device, device_id_type=MESH)

    loop(T - 1, lambda i: greet(device_of(i + 1)))
    for i in range(2, G):
        greet((at.s, at.f, lax.rem(at.base + i, G)))
    pl.semaphore_wait(bar, T - 1 + G - 2)

    def tok_move(j):
        return (2 * j + at.c, at.f, at.base + lax.div(at.s, 2))

    def tok_refs(which):
        return ((lat, xv), (cot, ctok))[which]

    def tok_to(j, which):
        src, dst = tok_refs(which)
        place = aligned(lax.rem(at.s, 2), quarter)
        return remote(
            src.at[j], dst.at[place], ts.at[which, j], tr.at[which, lax.rem(at.s, 2)], tok_move(j)
        )

    def tok_from(j, which):
        src, dst = tok_refs(which)
        place = pl.ds(j * quarter, quarter)
        return remote(src.at[0], dst.at[place], ts.at[which, j], tr.at[which, j], tok_move(j))

    def tok_local(j, which):
        src, dst = tok_refs(which)
        return pltpu.make_async_copy(src.at[j], dst.at[aligned(lax.rem(at.s, 2), quarter)], tl.at[which])

    def stays(j):
        return (2 * j + at.c == at.s) & (lax.div(at.s, 2) == at.c)

    def comes(j):
        return jnp.logical_not((2 * at.c + j == at.s) & (lax.rem(at.s, 2) == at.c))

    def tok_start(which):
        for j in range(2):
            @pl.when(stays(j))
            def _():
                tok_local(j, which).start()

            @pl.when(jnp.logical_not(stays(j)))
            def _():
                tok_to(j, which).start()

    def tok_finish(which):
        for j in range(2):
            @pl.when(stays(j))
            def _():
                tok_local(j, which).wait()

            @pl.when(jnp.logical_not(stays(j)))
            def _():
                tok_to(j, which).wait_send()

            @pl.when(comes(j))
            def _():
                tok_from(j, which).wait_recv()

    def rows_of(core):
        return picked.at[:, aligned(core, half)]

    def group_to(i):
        g = lax.rem(at.g + i, G)
        return remote(
            rows_of(lax.rem(g, 2)), theirs.at[G - 1 - i], gs.at[i], gr.at[G - 1 - i], (at.s, at.f, g)
        )

    def group_from(j):
        return remote(rows_of(0), theirs.at[j], gs.at[0], gr.at[j], at.sibling())

    group_own = pltpu.make_async_copy(rows_of(at.c), shard.at[0:blocks], gl)

    def cond_number(i):
        return lax.rem(at.f * 2 + at.c + i, 2 * F)

    def cond_to(i):
        n = cond_number(i)
        device = (at.s, lax.div(n, 2), at.base + lax.rem(n, 2))
        return remote(cond, conds.at[cond_number(0)], ds.at[i], dr.at[cond_number(0)], device)

    def cond_from(i):
        n = cond_number(i)
        return remote(cond, conds.at[n], ds.at[i], dr.at[n], at.sibling())

    cond_own = pltpu.make_async_copy(cond, conds.at[cond_number(0)], dl)

    here = at.s * F + at.f
    takes = lax.rem(at.s, 2) == at.c

    mod_give = remote(msg.at[:, 1 - at.c, :, 0:6], modg, hs.at[0], hr.at[0], at.sibling())

    def mod_to(i):
        n = lax.rem(lax.div(at.s, 2) * F + at.f + i, 2 * F)
        m, f = lax.div(n, F), lax.rem(n, F)
        return remote(
            msg.at[m, at.c, f, 0:6], modr.at[here], ms.at[i], mr.at[here], (2 * m + at.c, f, at.g)
        )

    def mod_from(i):
        n = lax.rem(here + i, S * F)
        return remote(msg.at[0, 0, 0, 0:6], modr.at[n], ms.at[0], mr.at[n], at.sibling())

    mod_swap = remote(modh, modh, hs.at[1], hr.at[1], at.sibling())

    def z_to(k, i):
        f = lax.rem(at.f + i, F)
        return remote(
            shard.at[k], bank.at[k, at.s, at.f, at.c], zs.at[k, i], zr.at[k, i], (at.s, f, at.g)
        )

    def z_from(k, i):
        f = lax.rem(at.f + F - i, F)
        return remote(shard.at[k], bank.at[k, at.s, f, at.c], zs.at[k, i], zr.at[k, i], (at.s, f, at.g))

    def a_copy(k, s):
        line = bank.at[k, s, :, at.c]
        return remote(line, line, as_.at[k], ar.at[k], (at.sa, at.f, at.g))

    def b_copy(k, s, n):
        line = bank.at[k, s, :, at.c]
        return remote(line, line, bs.at[k, n], br.at[k, n], (at.sb, at.f, at.g))

    sd = S - 1 - at.s

    def c_copy(k, s, n, core):
        line = bank.at[k, s, :, core]
        return remote(line, line, cs.at[k, n], cr.at[k, n], at.sibling())

    def z_start(k):
        for i in range(1, F):
            z_to(k, i).start()
        bank[k, at.s, at.f, at.c] = shard[k]

    late = K - LATE

    def late_a(n):
        piece = bank.at[late + n, at.s, at.f, at.c]
        return remote(piece, piece, las.at[n], lar.at[n], (at.sa, at.f, at.g))

    def late_a_from(n):
        piece = bank.at[late + n, at.sa, at.f, at.c]
        return remote(piece, piece, las.at[n], lar.at[n], (at.sa, at.f, at.g))

    def late_b(n, s, i):
        piece = bank.at[late + n, s, at.f, at.c]
        return remote(piece, piece, lbs.at[n, i], lbr.at[n, i], (at.sb, at.f, at.g))

    def late_line(n, way, j, f):
        line = bank.at[late + n, :, f, at.c]
        to = jnp.clip(at.f + 1 - 2 * way, 0, F - 1)
        return remote(line, line, lzs.at[n, way, j], lzr.at[n, way, j], (at.s, to, at.g))

    def late_c(n, f, core):
        line = bank.at[late + n, :, f, core]
        return remote(line, line, lcs.at[n, f], lcr.at[n, f], at.sibling())

    def late_first(n):
        bank[late + n, at.s, at.f, at.c] = shard[late + n]
        late_a(n).start()

    def late_second(n):
        late_a_from(n).wait_recv()
        late_b(n, at.s, 0).start()
        late_b(n, at.sa, 1).start()

    def late_sends(n, j, act):
        up, down = at.f - j, at.f + j

        @pl.when((up >= 0) & (at.f < F - 1))
        def _():
            act(late_line(n, 0, j, up))

        @pl.when((down < F) & (at.f > 0))
        def _():
            act(late_line(n, 1, j, down))

    def late_round(n, j):
        if j == 0:
            late_b(n, at.sb, 0).wait_recv()
            late_b(n, sd, 1).wait_recv()
            late_sends(n, 0, lambda copy: copy.start())
            late_c(n, at.f, at.c).start()
            return
        up, down = at.f - j, at.f + j

        @pl.when(up >= 0)
        def _():
            late_line(n, 0, j - 1, up).wait_recv()

        @pl.when(down < F)
        def _():
            late_line(n, 1, j - 1, down).wait_recv()

        if j < F - 1:
            late_sends(n, j, lambda copy: copy.start())

        @pl.when(up >= 0)
        def _():
            late_c(n, up, at.c).start()

        @pl.when(down < F)
        def _():
            late_c(n, down, at.c).start()

    def step_a(k):
        for i in range(1, F):
            z_from(k, i).wait_recv()
        a_copy(k, at.s).start()
        c_copy(k, at.s, 0, at.c).start()

    def step_b(k):
        a_copy(k, at.sa).wait_recv()
        b_copy(k, at.s, 0).start()
        b_copy(k, at.sa, 1).start()
        c_copy(k, at.sa, 1, at.c).start()

    def step_c(k):
        b_copy(k, at.sb, 0).wait_recv()
        c_copy(k, at.sb, 2, at.c).start()
        b_copy(k, sd, 1).wait_recv()
        c_copy(k, sd, 3, at.c).start()

    saves = []

    def save(src, dst):
        copy = pltpu.make_async_copy(src, dst, save_sem.at[len(saves)])
        copy.start()
        saves.append(copy)
        return len(saves) - 1

    waited = set()

    def saved(n):
        if n not in waited:
            saves[n].wait()
            waited.add(n)

    def arrive(k):
        if k < late:
            for n, s in enumerate((at.s, at.sb, at.sa, sd)):
                c_copy(k, s, n, 1 - at.c).wait_recv()
        else:
            for f in range(F):
                late_c(k - late, f, 1 - at.c).wait_recv()
        save(bank.at[k], bank_o.at[k])

    def weights(k):
        return bank[k].reshape(width, width)

    def gather_rows():
        group_own.wait()
        for i in range(1, G):
            group_from(i - 1).wait_recv()

        def one(b):
            value = shard[b].astype(F32)
            for i in range(G - 1):
                value = value + theirs[i, b].astype(F32)
            shard[b] = value.astype(BF16)

        loop(blocks, one)
        shard[blocks:] = jnp.zeros_like(shard[blocks:])

    def modulation_parts():
        cond_own.wait()
        loop(2 * F - 1, lambda i: cond_from(i + 1).wait_recv())
        value = conds[...].reshape(2 * F * 2 * pieces, 128)
        silu = (value / (1.0 + jnp.exp(-value))).astype(BF16)
        parts = 8 * half
        first = here * 2 * half + at.c * half
        lane, column = iota((128, parts), 0), iota((128, parts), 1)
        select = jnp.where(lane == lax.rem(first, 128) + lax.rem(column, half), 1.0, 0.0)
        rows = dot(silu, select.astype(BF16)).astype(BF16)
        count = 8 * S * F
        line, source = iota((count, rows.shape[0]), 0), iota((count, rows.shape[0]), 1)
        latent = lax.div(line, 8)
        chip, depth = lax.div(latent, F), lax.rem(latent, F)
        wanted = ((depth * 2 + lax.rem(chip, 2)) * 2 + lax.div(chip, 2)) * pieces + lax.div(first, 128)
        spread = dot(jnp.where(source == wanted, 1.0, 0.0).astype(BF16), rows)
        line, column = iota((count, parts), 0), iota((count, parts), 1)
        spread = jnp.where(lax.rem(line, 8) == lax.div(column, half), spread, 0.0).astype(BF16)
        value = dot(spread, shard[K:].reshape(parts, width))
        flat = msg.reshape(count * pieces, 128)
        for n in range(pieces):
            flat[pl.ds(n, count, stride=pieces)] = value[:, n * 128 : (n + 1) * 128]
        mod_give.start()

    def modulation_send():
        mod_give.wait()

        def add(n):
            m, f = lax.div(n, F), lax.rem(n, F)
            msg[m, at.c, f, 0:6] = msg[m, at.c, f, 0:6] + modg[m, f]

        loop(2 * F, add)

        @pl.when(jnp.logical_not(takes))
        def _():
            mod_to(0).start()

        loop(2 * F - 1, lambda i: mod_to(i + 1).start())

    def modulation():
        modulation_parts()
        save(shard.at[K:blocks], modw_o)
        modulation_send()

    def modulation_sum():
        @pl.when(takes)
        def _():
            loop(S * F - 1, lambda i: mod_from(i + 1).wait_recv())
            modr[here] = msg[lax.div(at.s, 2), at.c, at.f, 0:6]
            total = modr[0]
            for n in range(1, S * F):
                total = total + modr[n]
            modh[...] = total.reshape(6 * pieces, 128)
            mod_swap.start()

        @pl.when(jnp.logical_not(takes))
        def _():
            mod_swap.wait_recv()

        for n in range(pieces):
            cols = slice(n * 128, (n + 1) * 128)
            mod[0:6, cols] = modh[pl.ds(n, 6, stride=pieces)]
        mod[0:6] = mod[0:6] + bias[8:14]
        mod[6:8] = jnp.zeros((2, width), F32)
        save(mod, mod_o)

    def prepare():
        modulation_sum()
        tok_finish(0)
        save(xv, tok_o)

        def one(i):
            rows = aligned(i, CHUNK)
            scaled, _ = norm_rows(xv[rows].astype(F32))
            hid[rows] = (scaled * (1.0 + mod[1:2]) + mod[0:1]).astype(BF16)

        loop(tokens // CHUNK, one)
        hid_saved.append(save(hid, hid_o))

    hid_saved = []

    def swap(n):
        return remote(
            stage.at[n], heads.at[n, aligned(at.c, tokens)], xs.at[n], xr.at[n], at.sibling()
        )

    def swap_from(n):
        return remote(
            stage.at[n], heads.at[n, aligned(1 - at.c, tokens)], xs.at[n], xr.at[n], at.sibling()
        )

    def project(n):
        value = dot(hid[...], weights(n))
        if n != 1:
            row = n // 2
            value = value + bias[row : row + 1]
        value = value.astype(BF16)
        first, second = value[:, :part], value[:, part:]
        stage[n] = jnp.where(at.c == 0, second, first)
        swap(n).start()
        heads[n, aligned(at.c, tokens)] = jnp.where(at.c == 0, first, second)

    def attend_part(pair):
        if pair == 0:
            for n in range(3):
                swap_from(n).wait_recv()
                save(heads.at[n], heads_o.at[n])
        attend_pair(heads.at[0], heads.at[1], heads.at[2], head_a, lse, pair)

    def give_out():
        return remote(
            head_a.at[aligned(1 - at.c, tokens)], att.at[:, aligned(at.c, part)], xs.at[3], xr.at[3], at.sibling()
        )

    def give_from():
        return remote(
            head_a.at[aligned(at.c, tokens)], att.at[:, aligned(1 - at.c, part)], xs.at[3], xr.at[3], at.sibling()
        )

    def send_attended():
        give_out().start()
        att[:, aligned(at.c, part)] = head_a[aligned(at.c, tokens)]
        save(head_a, head_a_o)
        save(lse, lse_o)

    branch_saved = []

    def output_projection():
        give_from().wait_recv()
        save(att, att_o)
        mlp[...] = dot(att[...], weights(3)) + bias[2:3]
        branch_saved.append(save(mlp, branch_o))

        def rest(i):
            rows = aligned(i, CHUNK)
            middle = xv[rows].astype(F32) + mod[2:3] * mlp[rows]
            mid[rows] = middle
            scaled, _ = norm_rows(middle)
            hid2[rows] = (scaled * (1.0 + mod[4:5]) + mod[3:4]).astype(BF16)

        loop(tokens // CHUNK, rest)
        save(mid, mid_o)
        save(hid2, hid2_o)

    up_saved = []

    def upper(j):
        if j >= 2:
            saved(up_saved[j - 2])
        value = dot(hid2[...], weights(4 + j)) + bias[3 + j : 4 + j]
        up[j % 2] = value
        act[j] = jax.nn.gelu(value, approximate=True).astype(BF16)
        up_saved.append(save(up.at[j % 2], up_o.at[j]))
        save(act.at[j], act_o.at[j])

    def lower(j):
        if j == 0:
            saved(branch_saved[0])
        value = dot(act[j], weights(8 + j))
        mlp[...] = value + (bias[7:8] if j == 0 else mlp[...])

    def finish_forward():
        save(mlp, mlp_o)
        saved(hid_saved[0])

        def one(i):
            rows = aligned(i, CHUNK)
            hid[rows] = (mid[rows] + mod[5:6] * mlp[rows]).astype(BF16)

        loop(tokens // CHUNK, one)
        save(hid, res_o)

    tok_start(0)
    for i in range(1, G):
        group_to(i).start()
    group_own.start()
    cond_own.start()
    loop(2 * F - 1, lambda i: cond_to(i + 1).start())
    gather_rows()
    z_start(0)
    z_start(1)
    step_a(0)
    z_start(2)
    modulation()
    step_b(0)
    z_start(3)
    late_first(0)
    z_start(4)
    z_start(5)
    step_a(1)
    step_a(2)
    z_start(6)
    step_b(1)
    late_first(1)
    step_c(0)
    step_b(2)
    late_second(0)
    step_c(1)
    step_a(3)
    step_a(4)
    arrive(1)
    prepare()
    step_c(2)
    arrive(0)
    step_a(5)
    step_b(3)
    project(0)
    z_start(7)
    step_a(6)
    late_round(0, 0)
    late_second(1)
    step_b(4)
    z_start(8)
    step_c(3)
    z_start(9)
    arrive(2)
    project(1)
    step_a(7)
    step_b(5)
    late_round(1, 0)
    project(2)
    step_a(8)
    step_b(6)
    arrive(3)
    late_round(0, 1)
    attend_part(0)
    step_c(4)
    step_a(9)
    attend_part(1)
    step_b(7)
    late_round(1, 1)
    step_c(5)
    attend_part(2)
    step_b(8)
    attend_part(3)
    arrive(5)
    late_round(0, 2)
    step_c(6)
    send_attended()
    step_b(9)
    late_round(1, 2)
    step_c(7)
    arrive(4)
    output_projection()
    upper(0)
    arrive(6)
    step_c(8)
    for j in range(3, F):
        late_round(0, j)
    upper(1)
    tok_start(1)
    arrive(7)
    upper(2)
    for j in range(3, F):
        late_round(1, j)
    upper(3)
    arrive(8)
    step_c(9)
    arrive(11)
    arrive(10)
    lower(0)
    arrive(9)
    lower(1)
    lower(2)
    lower(3)
    finish_forward()

    def finish(k):
        for i in range(1, F):
            z_to(k, i).wait_send()
        a_copy(k, at.s).wait_send()
        b_copy(k, at.s, 0).wait_send()
        b_copy(k, at.sa, 1).wait_send()
        for n, s in enumerate((at.s, at.sa, at.sb, sd)):
            c_copy(k, s, n, at.c).wait_send()

    loop(late, finish)
    for n in range(LATE):
        late_a(n).wait_send()
        late_b(n, at.s, 0).wait_send()
        late_b(n, at.sa, 1).wait_send()
        for j in range(F - 1):
            late_sends(n, j, lambda copy: copy.wait_send())
        for f in range(F):
            late_c(n, f, at.c).wait_send()
    for i in range(1, G):
        group_to(i).wait_send()
    loop(2 * F - 1, lambda i: cond_to(i + 1).wait_send())
    loop(2 * F - 1, lambda i: mod_to(i + 1).wait_send())

    @pl.when(takes)
    def _():
        mod_swap.wait_send()

    @pl.when(jnp.logical_not(takes))
    def _():
        mod_to(0).wait_send()

    for n in range(3):
        swap(n).wait_send()
    give_out().wait_send()
    for n in range(len(saves)):
        saved(n)
    tok_finish(1)


def forward(sizes, picked, cond, lat, cot, bias):
    S, F, G = sizes
    blocks, rows, width = picked.shape
    K, half, T = LINEAR, rows // 2, 2 * S * F
    tokens = 2 * lat.shape[1]
    length, part = 2 * tokens, width // 2
    low = lambda *shape: (shape, BF16)
    high = lambda *shape: (shape, F32)
    outs = (
        low(K, S, F, 2, half, width),
        low(blocks - K, half, width),
        high(8, width),
        low(tokens, width),
        low(tokens, width),
        low(tokens, width),
        low(3, length, part),
        low(length, part),
        high(length, part),
        low(tokens, width),
        high(tokens, width),
        high(tokens, width),
        low(tokens, width),
        high(4, tokens, width),
        low(4, tokens, width),
        high(tokens, width),
        low(tokens, width),
    )
    scratch = (
        low(K + 8, half, width),
        low(G - 1, blocks, half, width),
        high(2 * F, 2 * width // 128, 128),
        high(2, 2, F, 8, width // 128, 128),
        high(2, F, 6, width // 128, 128),
        high(S * F, 6, width // 128, 128),
        high(6 * width // 128, 128),
        high(8, width),
        low(K, S, F, 2, half, width),
        low(tokens, width),
        low(tokens, width),
        low(3, tokens, part),
        low(3, length, part),
        low(length, part),
        high(length, part),
        low(tokens, width),
        high(tokens, width),
        low(tokens, width),
        high(2, tokens, width),
        low(4, tokens, width),
        high(tokens, width),
    )
    sems = (
        (G,), (G,), None, (2 * F,), (2 * F,), None, (K, F), (K, F), (K,), (K,), (K, 2), (K, 2), (K, 4), (K, 4),
        (LATE,), (LATE,), (LATE, 2), (LATE, 2), (LATE, 2, F), (LATE, 2, F), (LATE, F), (LATE, F),
        (2 * F,), (S * F,), (2,), (2,), (2, 2), (2, 2), (2,), (4,), (4,), (40,),
    )
    return pl.pallas_call(
        functools.partial(forward_kernel, sizes),
        out_shape=tuple(jax.ShapeDtypeStruct(*o) for o in outs),
        in_specs=[ANY] * 4 + [VMEM],
        out_specs=(ANY,) * len(outs),
        scratch_shapes=[pltpu.VMEM(*s) for s in scratch] + [DMA if n is None else DMA(n) for n in sems],
        compiler_params=params(2, 63),
        name="forward",
    )(picked, cond, lat, cot, bias)


RING = 4
ORDER = (8, 4, 9, 5, 10, 6, 11, 7, 3, 0, 1, 2)
LINED = (0, 5)
PLAIN = tuple(r for r in range(LINEAR) if r not in LINED)


def gelu_slope(values):
    scale = 0.7978845608
    square = values * values
    bend = jnp.tanh(scale * values * (1.0 + 0.044715 * square))
    return 0.5 * (1.0 + bend) + 0.5 * values * (1.0 - bend * bend) * (
        scale * (1.0 + 3.0 * 0.044715 * square)
    )


def attend_pair_back(q, k, v, a, lse_ref, da_ref, pair, dq_ref, dk_ref, dv_ref):
    length = q.shape[0]
    factor = 1.0 / math.sqrt(HD)
    for h in range(2):
        cols = slice(h * HD, (h + 1) * HD)
        grad_cols = slice((2 * pair + h) * HD, (2 * pair + h + 1) * HD)
        key = k[:, cols]
        value = v[:, cols]
        dk = jnp.zeros((HD, length), F32)
        dv = jnp.zeros((HD, length), F32)
        for r in range(0, length, ROWS):
            rows = slice(r, r + ROWS)
            query = q[rows, cols]
            grad = da_ref[rows, grad_cols]
            lse = lse_ref[rows, h * HD : h * HD + 1]
            scores = dot(query, key, NT)
            probs = jnp.exp(scores * factor - lse)
            row_dot = jnp.sum(grad.astype(F32) * a[rows, cols].astype(F32), axis=1, keepdims=True)
            weight_grad = dot(grad, value, NT)
            score_grad = (probs * (weight_grad - row_dot)).astype(BF16)
            dq_ref[rows, cols] = (dot(score_grad, key, NN) * factor).astype(BF16)
            dk = dk + dot(query.T, score_grad, NN)
            dv = dv + dot(grad.T, probs.astype(BF16), NN)
        dk_ref[:, cols] = (dk * factor).T.astype(BF16)
        dv_ref[:, cols] = dv.T.astype(BF16)


def backward_kernel(sizes, *refs):
    (
        bank, modw, mod, tok, ctok, hid, heads, head_a, lse, att, branch, mid, hid2, up, act, mlp, res, silu,
        red, smalls, cgs, out_lat, in_lat,
        mine, give, r0, r1, r2, r3, lz, l1, l2, total, wbuf,
        ebuf, dfb, f0, f1, a0, a1, dub, dh2, h2b, stage, dah, qkva, lsev, dpair, dqt, accs, small, sv, sw, swb, smv, cg, cgl,
        cs, cr, bs, br, as_, ar, zs, zr, lzs, lzr, os_, rs, rr, free, vs, vr, ws, wr, wl, qs, qr, us, ur, ds, dr, dl, es, er, ts, tr, tl, loads, xs, xr, ps, pr,
    ) = refs
    at = Place(sizes)
    S, F, G = sizes
    K = mine.shape[0]
    half = mine.shape[3]
    tokens, width = ebuf.shape
    part = width // 2
    band = width // S
    count = S * F * G
    me = (at.s * F + at.f) * G + at.g
    quarter = out_lat.shape[1]
    sd = S - 1 - at.s
    chunks = tokens // CHUNK

    def device_of(i):
        n = lax.rem(me + i, count)
        return (lax.div(n, F * G), lax.rem(lax.div(n, G), F), lax.rem(n, G))

    bar = pltpu.get_barrier_semaphore()

    def greet(i):
        pl.semaphore_signal(bar, inc=1, device_id=device_of(i + 1), device_id_type=MESH)

    loop(count - 1, greet)

    def c_copy(r):
        return remote(give.at[r % 2], r0.at[r % RING], cs.at[r], cr.at[r], at.sibling())

    def b_copy(r, s, n):
        if r in LINED:
            src, dst = mine.at[r, s, at.f], l1.at[LINED.index(r), n]
        else:
            src, dst = mine.at[r, s], r1.at[PLAIN.index(r), n]
        return remote(src, dst, bs.at[r, n], br.at[r, n], (at.sb, at.f, at.g))

    def a_copy(r):
        if r in LINED:
            src, dst = mine.at[r, at.sa, at.f], l2.at[LINED.index(r)]
        else:
            src, dst = mine.at[r, at.sa], r2.at[PLAIN.index(r)]
        return remote(src, dst, as_.at[r], ar.at[r], (at.sa, at.f, at.g))

    def z_to(r, i):
        f = lax.rem(at.f + i, F)
        return remote(
            mine.at[r, at.s, f], r3.at[PLAIN.index(r), i - 1], zs.at[r, i], zr.at[r, i], (at.s, f, at.g)
        )

    def up_line(r, i):
        tau = F - 1 - i + at.f
        to = jnp.clip(at.f + 1, 0, F - 1)
        tau_in = jnp.clip(tau, 0, F - 1)
        return tau_in, remote(
            mine.at[r, :, tau_in], lz.at[LINED.index(r), tau_in], lzs.at[LINED.index(r), 0, i], lzr.at[LINED.index(r), 0, i], (at.s, to, at.g)
        )

    def down_line(r, i):
        tau = jnp.clip(i + at.f - F + 1, 0, F - 1)
        to = jnp.clip(at.f - 1, 0, F - 1)
        place = F if i == F - 2 else tau
        return remote(
            mine.at[r, :, tau], lz.at[LINED.index(r), place], lzs.at[LINED.index(r), 1, i], lzr.at[LINED.index(r), 1, i], (at.s, to, at.g)
        )

    def line_sends(r, i, act):
        @pl.when((at.f <= i) & (at.f < F - 1))
        def _():
            act(up_line(r, i)[1])

        @pl.when((F - 1 - at.f <= i) & (at.f > 0))
        def _():
            act(down_line(r, i))

    def add_set(r, tau, place):
        def one(s):
            mine[r, s, tau] = mine[r, s, tau] + lz[LINED.index(r), place, s]

        loop(S, one)

    def line(r, i):
        if i > 0:
            @pl.when((at.f >= 1) & (at.f <= i))
            def _():
                tau = jnp.clip(F - 1 - i + at.f, 0, F - 1)
                remote(
                    mine.at[r, :, tau], lz.at[LINED.index(r), tau], lzs.at[LINED.index(r), 0, i - 1], lzr.at[LINED.index(r), 0, i - 1], at.sibling()
                ).wait_recv()
                add_set(r, tau, tau)

            @pl.when((at.f <= F - 2) & (F - 1 - at.f <= i))
            def _():
                tau = jnp.clip(i + at.f - F + 1, 0, F - 1)
                place = F if i == F - 1 else tau
                remote(
                    mine.at[r, :, tau], lz.at[LINED.index(r), place], lzs.at[LINED.index(r), 1, i - 1], lzr.at[LINED.index(r), 1, i - 1], at.sibling()
                ).wait_recv()
                add_set(r, tau, place)

        if i < F - 1:
            line_sends(r, i, lambda copy: copy.start())
        else:
            b_copy(r, at.sb, 0).start()
            b_copy(r, sd, 1).start()

    def add_piece(r, s, src):
        mine[r, s, at.f] = mine[r, s, at.f] + src

    pair = lax.div(at.g, 2)
    finals = []

    def out_copy(r):
        return pltpu.make_async_copy(total.at[finals.index(r) % 4], red.at[pair, ORDER[r], at.c], os_.at[r])

    def out_to(r, i):
        g = lax.rem(at.g + i, G)
        return remote(
            total.at[finals.index(r) % 4], red.at[pair, ORDER[r], at.c], rs.at[r, i], rr.at[r, i], (at.s, at.f, g)
        )

    def out_from(r, i):
        g = lax.rem(at.g + G - i, G)
        return remote(
            total.at[finals.index(r) % 4], red.at[lax.div(g, 2), ORDER[r], lax.rem(g, 2)], rs.at[r, i], rr.at[r, i], at.sibling()
        )

    def out_done(r):
        out_copy(r).wait()
        for i in range(1, G):
            out_to(r, i).wait_send()

    def add_line(dst, src):
        dst[...] = dst[...] + src[...]

    def hop0(r):
        c_copy(r).wait_recv()
        loop(S, lambda s: add_line(mine.at[r, s], r0.at[r % RING, s]))
        if r + RING < K:
            pl.semaphore_signal(free, inc=1, device_id=at.sibling(), device_id_type=MESH)
        if r in LINED:
            line(r, 0)
            return
        b_copy(r, at.sb, 0).start()
        b_copy(r, sd, 1).start()

    def hop1(r):
        b_copy(r, at.sb, 0).wait_recv()
        b_copy(r, sd, 1).wait_recv()
        if r in LINED:
            add_piece(r, at.sa, l1[LINED.index(r), 1])
            a_copy(r).start()
            add_piece(r, at.s, l1[LINED.index(r), 0])
            return
        add_line(mine.at[r, at.sa], r1.at[PLAIN.index(r), 1])
        a_copy(r).start()
        add_line(mine.at[r, at.s], r1.at[PLAIN.index(r), 0])

    def hop2(r):
        if r in LINED:
            return
        a_copy(r).wait_recv()
        add_line(mine.at[r, at.s], r2.at[PLAIN.index(r)])
        for i in range(1, F):
            z_to(r, i).start()

    def hop3(r):
        if r in LINED:
            a_copy(r).wait_recv()
            others = [l2.at[LINED.index(r)]]
        else:
            for i in range(1, F):
                z_to(r, i).wait_recv()
            others = [r3.at[PLAIN.index(r), i] for i in range(F - 1)]
        finals.append(r)
        if len(finals) > 4:
            out_done(finals[-5])
        value = mine[r, at.s, at.f].astype(F32)
        for other in others:
            value = value + other[...].astype(F32)
        total[finals.index(r) % 4] = value
        out_copy(r).start()
        for i in range(1, G):
            out_to(r, i).start()

    def produce(r, left, right):
        if r >= 2:
            c_copy(r - 2).wait_send()

        lines = S // 2

        def one(n):
            value = dot(left[:, aligned(n, lines * band)], right[...], TN)
            value = value.astype(BF16).reshape(lines, F, 2, half, width)
            first, second = value[:, :, 0], value[:, :, 1]
            mine[r, aligned(n, lines)] = jnp.where(at.c == 0, first, second)
            give[r % 2, aligned(n, lines)] = jnp.where(at.c == 0, second, first)

        loop(2, one)
        if r >= RING:
            pl.semaphore_wait(free, 1)
        c_copy(r).start()

    def back_device(j):
        return (2 * at.c + j, at.f, at.base + lax.rem(at.s, 2))

    def back_stays(j):
        return (2 * at.c + j == at.s) & (lax.rem(at.s, 2) == at.c)

    def back_comes(m):
        return jnp.logical_not((2 * m + at.c == at.s) & (lax.div(at.s, 2) == at.c))

    def back_refs(which):
        return ((res, out_lat), (dfb, in_lat))[which]

    def back_to(j, which):
        src, dst = back_refs(which)
        m = lax.div(at.s, 2)
        return remote(
            src.at[pl.ds(j * quarter, quarter)], dst.at[m], ts.at[which, j], tr.at[which, m], back_device(j)
        )

    def back_from(m, which):
        src, dst = back_refs(which)
        return remote(
            src.at[pl.ds(0, quarter)], dst.at[m], ts.at[which, m], tr.at[which, m], back_device(m)
        )

    def back_local(j, which):
        src, dst = back_refs(which)
        return pltpu.make_async_copy(
            src.at[pl.ds(j * quarter, quarter)], dst.at[lax.div(at.s, 2)], tl.at[which]
        )

    def back_start(which):
        for j in range(2):
            @pl.when(back_stays(j))
            def _():
                back_local(j, which).start()

            @pl.when(jnp.logical_not(back_stays(j)))
            def _():
                back_to(j, which).start()

    def back_finish(which):
        for j in range(2):
            @pl.when(back_stays(j))
            def _():
                back_local(j, which).wait()

            @pl.when(jnp.logical_not(back_stays(j)))
            def _():
                back_to(j, which).wait_send()

            @pl.when(back_comes(j))
            def _():
                back_from(j, which).wait_recv()

    def load(src, dst, n):
        return pltpu.make_async_copy(src, dst, loads.at[n])

    def load_weight(k, slot):
        return load(bank.at[k], wbuf.at[slot], slot)

    ups, acts = (f0, f1), (a0, a1)

    def load_up(j):
        return load(up.at[j], ups[j % 2], 2 + j % 2)

    def load_act(j):
        return load(act.at[j], acts[j % 2], 4 + j % 2)

    def load_pair(p):
        cols = pl.ds(p * 2 * HD, 2 * HD)
        slot = p % 2
        return [load(heads.at[n, :, cols], qkva.at[slot, n], 10 + 5 * slot + n) for n in range(3)] + [
            load(head_a.at[:, cols], qkva.at[slot, 3], 13 + 5 * slot),
            load(lse.at[:, cols], lsev.at[slot], 14 + 5 * slot),
        ]

    def weights(slot):
        return wbuf[slot].reshape(width, width)

    def add_rows(i, value, cols=slice(None)):
        accs[i, :, cols] += value.reshape(-1, 8, value.shape[-1]).sum(axis=0)

    load_e, load_mlp, load_h2 = load(ctok, ebuf, 6), load(mlp, dh2, 7), load(hid2, h2b, 8)
    for copy in (load_e, load_mlp):
        copy.start()
    load_weight(8, 0).start()
    load_act(0).start()
    load_up(0).start()
    load_h2.start()
    load_weight(4, 1).start()
    load_up(1).start()
    load_act(1).start()
    pl.semaphore_wait(bar, count - 1)
    back_start(0)
    accs[...] = jnp.zeros_like(accs)
    load_e.wait()
    load_mlp.wait()

    def start_rows(i):
        rows = aligned(i, CHUNK)
        grad = ebuf[rows].astype(F32)
        add_rows(5, grad * dh2[rows])
        low = (mod[5:6] * grad).astype(BF16)
        dfb[rows] = low
        add_rows(13, low.astype(F32))

    loop(chunks, start_rows)

    def active_back(j):
        load_weight(8 + j, 0).wait()
        load_up(j).wait()

        value = dot(dfb[...], weights(0), NT) * gelu_slope(ups[j % 2][...])
        low = value.astype(BF16)
        dub[...] = low
        add_rows(9 + j, low.astype(F32))
        load_weight(9 + j if j < 3 else 3, 0).start()
        if j < 2:
            load_up(j + 2).start()
        else:
            (load_mid, load_branch)[j - 2].start()

    def hidden_back(j):
        load_weight(4 + j, 1).wait()

        value = dot(dub[...], weights(1), NT)
        dh2[...] = value if j == 0 else dh2[...] + value
        load_weight(5 + j if j < 3 else 0, 1).start()

    def product_eight(j):
        load_act(j).wait()
        produce(2 * j, acts[j % 2], dfb)
        if j < 2:
            load_act(j + 2).start()
        if j == 2:
            load_att.start()

    def product_four(j):
        if j == 0:
            load_h2.wait()
        produce(2 * j + 1, h2b, dub)
        if j == 3:
            load_hid.start()
            load_modw.start()

    def product_three():
        load_att.wait()
        produce(8, a0, dfb)

    def product_first(n):
        if n == 0:
            load_hid.wait()
        produce(9 + n, h2b, dqt.at[n])

    load_mid, load_branch = load(mid, f0, 2), load(branch, f1, 3)
    load_att, load_hid, load_x = load(att, a0, 4), load(hid, h2b, 8), load(tok, ebuf, 6)

    def middle_back():
        load_mid.wait()
        load_branch.wait()

        def one(i):
            rows = aligned(i, CHUNK)
            scaled, inverse = norm_rows(f0[rows])
            grad = dh2[rows]
            inner = grad * (1.0 + mod[4:5])
            mean_inner = jnp.mean(inner, axis=-1, keepdims=True)
            mean_scaled = jnp.mean(inner * scaled, axis=-1, keepdims=True)
            value = ebuf[rows].astype(F32) + inverse * (inner - mean_inner - scaled * mean_scaled)
            add_rows(4, grad * scaled)
            add_rows(3, grad)
            dh2[rows] = value
            add_rows(2, value * f1[rows])
            low = (mod[2:3] * value).astype(BF16)
            dfb[rows] = low
            add_rows(8, low.astype(F32))

        loop(chunks, one)
        load_x.start()

    def swap_da(here):
        return remote(stage, dah.at[aligned(here, tokens)], xs, xr, at.sibling())

    def attended_back():
        load_weight(3, 0).wait()

        value = dot(dfb[...], weights(0), NT).astype(BF16)
        first, second = value[:, :part], value[:, part:]
        stage[...] = jnp.where(at.c == 0, second, first)
        swap_da(at.c).start()
        dah[aligned(at.c, tokens)] = jnp.where(at.c == 0, first, second)
        load_weight(1, 0).start()
        for copy in load_pair(0) + load_pair(1):
            copy.start()

    def pair_to(p, n, core):
        rows = aligned(1 - at.c, tokens)
        cols = pl.ds(pl.multiple_of(core * part + p * 2 * HD, 2 * HD), 2 * HD)
        return remote(
            dpair.at[p % 2, n, rows], dqt.at[n, :, cols], ps.at[p, n], pr.at[p, n], at.sibling()
        )

    def attend_back_part(p):
        if p == 0:
            swap_da(1 - at.c).wait_recv()
        for copy in load_pair(p):
            copy.wait()
        if p >= 2:
            for n in range(3):
                pair_to(p - 2, n, at.c).wait_send()
        slot = p % 2
        attend_pair_back(
            qkva.at[slot, 0], qkva.at[slot, 1], qkva.at[slot, 2], qkva.at[slot, 3], lsev.at[slot], dah, p,
            dpair.at[slot, 0], dpair.at[slot, 1], dpair.at[slot, 2],
        )
        cols = pl.ds(pl.multiple_of(at.c * part + p * 2 * HD, 2 * HD), 2 * HD)
        for n in range(3):
            pair_to(p, n, at.c).start()
            dqt[n, :, cols] = dpair[slot, n, aligned(at.c, tokens)]
        if p + 2 < part // (2 * HD):
            for copy in load_pair(p + 2):
                copy.start()

    def pairs_arrive():
        for p in range(part // (2 * HD)):
            for n in range(3):
                pair_to(p, n, 1 - at.c).wait_recv()

        def one(i):
            rows = aligned(i, CHUNK)
            add_rows(6, dqt[0, rows].astype(F32))
            add_rows(7, dqt[2, rows].astype(F32))

        loop(chunks, one)

    def first_back(k):
        slot = (1, 0, 1)[k]
        load_weight(k, slot).wait()
        value = dot(dqt[k], weights(slot), NT)
        f0[...] = value if k == 0 else f0[...] + value
        if k == 0:
            load_weight(2, 1).start()

    def input_back():
        load_x.wait()

        def one(i):
            rows = aligned(i, CHUNK)
            scaled, inverse = norm_rows(ebuf[rows].astype(F32))
            grad = f0[rows]
            inner = grad * (1.0 + mod[1:2])
            mean_inner = jnp.mean(inner, axis=-1, keepdims=True)
            mean_scaled = jnp.mean(inner * scaled, axis=-1, keepdims=True)
            value = dh2[rows] + inverse * (inner - mean_inner - scaled * mean_scaled)
            add_rows(1, grad * scaled)
            add_rows(0, grad)
            dfb[rows] = value.astype(BF16)

        loop(chunks, one)

    small_swap = remote(small, sv, vs, vr, at.sibling())
    lines = F * G // 2
    mark = at.f * (G // 2) + pair
    sent = aligned(at.c, part)

    def small_region(s, n):
        return smalls.at[s, lax.div(n, G // 2), lax.rem(n, G // 2), :, sent]

    def small_to(i):
        n = lax.rem(mark + i, lines)
        device = (at.s, lax.div(n, G // 2), 2 * lax.rem(n, G // 2) + at.c)
        return remote(swb.at[:, sent], small_region(at.s, mark), ws.at[i], wr.at[mark], device)

    def small_from(i):
        n = lax.rem(mark + i, lines)
        return remote(swb.at[:, sent], small_region(at.s, n), ws.at[i], wr.at[n], at.sibling())

    small_own = pltpu.make_async_copy(swb.at[:, sent], small_region(at.s, mark), wl)
    plane = (at.sx, at.sy, sd)

    def small_across(n, s, to):
        region = smalls.at[s, :, :, :, sent]
        return remote(region, region, qs.at[n], qr.at[n], (to, at.f, at.g))

    def small_share(core):
        region = smalls.at[:, :, :, :, aligned(core, part)]
        return remote(region, region, us, ur, at.sibling())

    def small_start():
        small[...] = jnp.zeros_like(small)
        small[0:14] = accs[...].sum(axis=1)
        small[14:15] = silu[0:1]
        small_swap.start()

    def small_send():
        small_swap.wait()
        sw[...] = small[...] + sv[...]
        swb[...] = sw[...].astype(BF16)
        small_own.start()
        for i in range(1, lines):
            small_to(i).start()

    def small_plane():
        small_own.wait()
        for i in range(1, lines):
            small_from(i).wait_recv()
        for n, s in enumerate(plane):
            small_across(n, at.s, s).start()

    def small_share_start():
        for n, s in enumerate(plane):
            small_across(n, s, s).wait_recv()
        small_share(at.c).start()

    load_modw = load(modw, dub.at[0 : 6 * half], 9)
    pair_smalls = pltpu.make_async_copy(smalls.at[:, :, pair], smv, dl.at[0])
    spot = at.f * 2 + at.c

    def cond_number(i):
        return lax.rem(spot + i, 2 * F)

    def cond_to(i):
        n = cond_number(i)
        device = (at.s, lax.div(n, 2), at.base + lax.rem(n, 2))
        return remote(cg.at[aligned(lax.div(n, 4), 8)], cgl.at[spot], ds.at[i], dr.at[spot], device)

    def cond_from(i):
        n = cond_number(i)
        return remote(cg.at[0:8], cgl.at[n], ds.at[i], dr.at[n], at.sibling())

    cond_own = pltpu.make_async_copy(cgl, cgs.at[at.s], dl.at[1])

    def cond_across(n, s, to):
        return remote(cgl, cgs.at[s], es.at[n], er.at[n], (to, at.f, at.g))

    def cond_start():
        small_share(1 - at.c).wait_recv()
        pair_smalls.start()
        load_modw.wait()
        dub[6 * half : 8 * half] = jnp.zeros((2 * half, width), BF16)
        pair_smalls.wait()
        value = dot(smv[...].reshape(S * F * 16, width), dub[0 : 8 * half], NT)
        line, column = iota(value.shape, 0), iota(value.shape, 1)
        value = jnp.where(lax.rem(line, 16) == lax.div(column, half), value, 0.0)
        value = value.reshape(S * F, 16, 8 * half).sum(axis=1)
        rows = value[:, 0:128]
        for n in range(1, 8 * half // 128):
            rows = rows + value[:, n * 128 : (n + 1) * 128]
        for s in range(S):
            for f in range(F):
                to = (f * 2 + s % 2) * 2 + s // 2
                cg[to : to + 1] = rows[s * F + f : s * F + f + 1]
        cgl[spot] = cg[aligned(lax.div(spot, 4), 8)]
        loop(2 * F - 1, lambda i: cond_to(i + 1).start())

    def cond_plane():
        loop(2 * F - 1, lambda i: cond_from(i + 1).wait_recv())
        cond_own.start()
        for n, s in enumerate(plane):
            cond_across(n, at.s, s).start()

    active_back(0)
    product_eight(0)
    hidden_back(0)
    product_four(0)
    active_back(1)
    hop0(0)
    hop0(1)
    product_eight(1)
    hidden_back(1)
    product_four(1)
    hop0(2)
    active_back(2)
    product_eight(2)
    line(0, 1)
    hop0(3)
    hop1(1)
    hidden_back(2)
    product_four(2)
    hop0(4)
    active_back(3)
    hop0(5)
    product_eight(3)
    hidden_back(3)
    middle_back()
    hop1(3)
    product_four(3)
    hop0(6)
    line(0, 2)
    hop1(2)
    attended_back()
    line(5, 1)
    attend_back_part(0)
    hop2(1)
    product_three()
    hop1(4)
    hop2(2)
    hop0(7)
    hop1(6)
    attend_back_part(1)
    line(5, 2)
    hop0(8)
    attend_back_part(2)
    hop2(6)
    hop1(7)
    hop2(3)
    for i in range(3, F):
        line(0, i)
    attend_back_part(3)
    hop1(8)
    pairs_arrive()
    product_first(0)
    hop1(0)
    hop2(7)
    hop3(2)
    for i in range(3, F):
        line(5, i)
    hop0(9)
    product_first(1)
    product_first(2)
    hop2(8)
    hop0(10)
    first_back(0)
    first_back(1)
    hop2(4)
    first_back(2)
    hop1(9)
    input_back()
    hop3(1)
    hop0(11)
    hop1(5)
    small_start()
    hop3(5)
    small_send()
    hop1(10)
    hop2(9)
    small_plane()
    hop3(0)
    hop3(3)
    hop1(11)
    hop3(7)
    hop2(10)
    hop3(4)
    back_start(1)
    small_share_start()
    hop3(6)
    cond_start()
    hop2(11)
    hop3(9)
    cond_plane()
    hop3(10)
    hop3(8)
    hop3(11)

    swap_da(at.c).wait_send()
    for p in (2, 3):
        for n in range(3):
            pair_to(p, n, at.c).wait_send()
    for r in range(K):
        if r >= K - 2:
            c_copy(r).wait_send()
        if r in finals[-4:]:
            out_done(r)
        for i in range(1, G):
            out_from(r, i).wait_recv()
        b_copy(r, at.sb, 0).wait_send()
        b_copy(r, sd, 1).wait_send()
        a_copy(r).wait_send()
        for i in range(F - 1 if r in LINED else 0):
            line_sends(r, i, lambda copy: copy.wait_send())
        for i in range(1, 0 if r in LINED else F):
            z_to(r, i).wait_send()
    back_finish(0)
    back_finish(1)
    for i in range(1, lines):
        small_to(i).wait_send()
    for n, s in enumerate(plane):
        small_across(n, at.s, s).wait_send()
    small_share(at.c).wait_send()
    loop(2 * F - 1, lambda i: cond_to(i + 1).wait_send())
    for n, s in enumerate(plane):
        cond_across(n, at.s, s).wait_send()
        cond_across(n, s, s).wait_recv()
    cond_own.wait()


def backward(sizes, *arrays):
    S, F, G = sizes
    bank, tok = arrays[0], arrays[3]
    K, _, _, _, half, width = bank.shape
    tokens = tok.shape[0]
    quarter, part, length = tokens // 2, width // 2, 2 * tokens
    count = S * F * G
    low = lambda *shape: pltpu.VMEM(shape, BF16)
    high = lambda *shape: pltpu.VMEM(shape, F32)
    specs = [ANY] * len(arrays)
    specs[2] = specs[-1] = VMEM
    return pl.pallas_call(
        functools.partial(backward_kernel, sizes),
        out_shape=(
            jax.ShapeDtypeStruct((G // 2, K, 2, half, width), F32),
            jax.ShapeDtypeStruct((S, F, G // 2, 16, width), BF16),
            jax.ShapeDtypeStruct((S, 2 * F, 8, 128), F32),
            jax.ShapeDtypeStruct((2, quarter, width), BF16),
            jax.ShapeDtypeStruct((2, quarter, width), BF16),
        ),
        in_specs=specs,
        out_specs=(ANY,) * 5,
        scratch_shapes=[
            low(K, S, F, half, width),
            low(2, S, F, half, width),
            low(RING, S, F, half, width),
            low(K - LATE, 2, F, half, width),
            low(K - LATE, F, half, width),
            low(K - LATE, F - 1, half, width),
            low(LATE, F + 1, S, half, width),
            low(LATE, 2, half, width),
            low(LATE, half, width),
            high(4, half, width),
            low(2, S, F, 2, half, width),
            low(tokens, width),
            low(tokens, width),
            high(tokens, width),
            high(tokens, width),
            low(tokens, width),
            low(tokens, width),
            low(tokens, width),
            high(tokens, width),
            low(tokens, width),
            low(tokens, part),
            low(length, part),
            low(2, 4, length, 2 * HD),
            high(2, length, 2 * HD),
            low(2, 3, length, 2 * HD),
            low(3, tokens, width),
            high(14, 8, width),
            high(16, width),
            high(16, width),
            high(16, width),
            low(16, width),
            low(S, F, 16, width),
            high(S * F, 128),
            high(2 * F, 8, 128),
            DMA((K,)),
            DMA((K,)),
            DMA((K, 2)),
            DMA((K, 2)),
            DMA((K,)),
            DMA((K,)),
            DMA((K, F)),
            DMA((K, F)),
            DMA((LATE, 2, F)),
            DMA((LATE, 2, F)),
            DMA((K,)),
            DMA((K, G)),
            DMA((K, G)),
            pltpu.SemaphoreType.REGULAR,
            DMA,
            DMA,
            DMA((count // 2,)),
            DMA((count // 2,)),
            DMA,
            DMA((3,)),
            DMA((3,)),
            DMA,
            DMA,
            DMA((2 * F,)),
            DMA((2 * F,)),
            DMA((2,)),
            DMA((3,)),
            DMA((3,)),
            DMA((2, 2)),
            DMA((2, 2)),
            DMA((2,)),
            DMA((20,)),
            DMA,
            DMA,
            DMA((4, 3)),
            DMA((4, 3)),
        ],
        compiler_params=params(3, 63),
        name="backward",
    )(*arrays)


def per_device(
    sizes,
    latents,
    conditioning,
    cotangent,
    owner_list,
    master,
    moment_one,
    moment_two,
    biases,
    bias_moment_one,
    bias_moment_two,
):
    S, F, G = sizes
    rows, width = master.shape[1:]
    half = rows // 2
    s, f, g = lax.axis_index("seq"), lax.axis_index("fsdp"), lax.axis_index("grp")
    core = g % 2

    picked = pick_blocks(master, owner_list)
    cond_rows = conditioning.reshape(2 * width // 128, 128)
    saved = forward(sizes, picked, cond_rows, latents[:, 0], cotangent[:, 0], biases)
    saved = (saved[0], saved[1].reshape(-1, width)) + tuple(saved[2:])
    silu = jax.nn.silu(lax.dynamic_index_in_dim(conditioning, s // 2, 0, keepdims=False))
    silu = jnp.where(core == s % 2, silu.astype(BF16).astype(F32), 0.0)
    silu = jnp.pad(silu, ((0, 7), (0, 0)))
    reduced, smalls, cond_all, out_lat, in_lat = backward(sizes, *saved, silu)

    linear_grads = jnp.sum(reduced, axis=0, keepdims=True) if G > 2 else reduced
    (
        new_master, new_one, new_two, new_copies, new_biases, new_bias_one, new_bias_two, output, input_grad,
    ) = adam_slots(
        sizes, owner_list, master, linear_grads, smalls.reshape(-1, width), moment_one, moment_two,
        biases, bias_moment_one, bias_moment_two, out_lat, in_lat,
    )

    first = (f % 2) * 4 + core * 2
    cond_mine = lax.dynamic_slice_in_dim(cond_all, first, 2, 2).reshape(S * F * 2, 2, 128)
    cond_mine = cond_mine.reshape(S * F * 2, 2, 128 // half, half).sum(axis=2)
    cond_mine = cond_mine.transpose(1, 0, 2).reshape(2, width)
    _, silu_pull = jax.vjp(jax.nn.silu, conditioning)
    cond_grad = silu_pull(cond_mine[:, None])[0]

    return (
        output[:, None],
        input_grad[:, None],
        cond_grad,
        new_master,
        new_one,
        new_two,
        new_copies,
        new_biases,
        new_bias_one,
        new_bias_two,
    )


def solution(mesh):
    sizes = (mesh.shape["seq"], mesh.shape["fsdp"], mesh.shape["grp"])
    tokens = P(None, ("fsdp", "grp"), "seq", None)
    vector = P(None, ("fsdp", "grp"), None)
    slots = P("grp", ("seq", "fsdp"), None)
    in_specs = (tokens, vector, tokens, P(), slots, slots, slots, P(), P(), P())
    out_specs = (tokens, tokens, vector, slots, slots, slots, slots, P(), P(), P())
    return jax.shard_map(
        functools.partial(per_device, sizes),
        mesh=mesh,
        in_specs=in_specs,
        out_specs=out_specs,
        check_vma=False,
    )
```

```python
import functools
import math

import jax
import jax.numpy as jnp
from jax import lax
from jax.experimental import pallas as pl
from jax.experimental.pallas import tpu as pltpu
from jax.sharding import PartitionSpec as P

HD = 64
STEP = 5
EPS_NORM = 1e-06
BETA_ONE = 0.5
BETA_TWO = 0.5
RATE_WEIGHT = 0.03
RATE_BIAS = 0.1
DECAY = 0.1
ADAM_EPS = 1e-08

MESH = pl.DeviceIdType.MESH
ANY = pl.BlockSpec(memory_space=pl.ANY)
VMEM = pl.BlockSpec(memory_space=pltpu.VMEM)
F32 = jnp.float32
BF16 = jnp.bfloat16
DMA = pltpu.SemaphoreType.DMA
LINEAR = 12
LATE = 2


def params(cid, vmem=48):
    return pltpu.CompilerParams(
        collective_id=cid, has_side_effects=True, vmem_limit_bytes=vmem * 1024 * 1024
    )


def remote(src, dst, send_sem, recv_sem, device):
    return pltpu.make_async_remote_copy(
        src_ref=src,
        dst_ref=dst,
        send_sem=send_sem,
        recv_sem=recv_sem,
        device_id=device,
        device_id_type=MESH,
    )


class Place:
    def __init__(self, sizes):
        self.S, self.F, self.G = sizes
        self.s = lax.axis_index("seq")
        self.f = lax.axis_index("fsdp")
        self.g = lax.axis_index("grp")
        self.c = lax.rem(self.g, 2)
        self.base = self.g - self.c
        self.sib = self.base + 1 - self.c
        odd = lax.rem(self.s, 2)
        self.sx = self.s + 1 - 2 * odd
        self.sy = lax.rem(self.s + 2, 4)
        self.sa = self.sx + self.c * (self.sy - self.sx)
        self.sb = self.sy + self.c * (self.sx - self.sy)

    def sibling(self):
        return (self.s, self.f, self.sib)


def pick_kernel(owner_ref, master_ref, out_ref, buf, low, sems, out_sems):
    blocks = out_ref.shape[0]
    group = lax.axis_index("grp")
    slots, mine, before = [], [], jnp.int32(0)
    for b in range(blocks):
        own = owner_ref[b] == group
        mine.append(own)
        slots.append(jnp.where(own, before, 0))
        before = before + jnp.where(own, 1, 0)

    def fetch(b):
        return pltpu.make_async_copy(master_ref.at[slots[b]], buf.at[b], sems.at[b])

    for b in range(blocks):
        fetch(b).start()
    for b in range(blocks):
        fetch(b).wait()
        low[b] = jnp.where(mine[b], buf[b], 0.0).astype(BF16)
        pltpu.make_async_copy(low.at[b], out_ref.at[b], out_sems.at[b]).start()
    for b in range(blocks):
        pltpu.make_async_copy(low.at[b], out_ref.at[b], out_sems.at[b]).wait()


def pick_blocks(master, owner_list):
    blocks = owner_list.shape[0]
    rows, width = master.shape[1:]
    return pl.pallas_call(
        pick_kernel,
        out_shape=jax.ShapeDtypeStruct((blocks, rows, width), BF16),
        in_specs=[pl.BlockSpec(memory_space=pltpu.SMEM), ANY],
        out_specs=ANY,
        scratch_shapes=[
            pltpu.VMEM((blocks, rows, width), F32),
            pltpu.VMEM((blocks, rows, width), BF16),
            DMA((blocks,)),
            DMA((blocks,)),
        ],
        compiler_params=pltpu.CompilerParams(vmem_limit_bytes=62 * 1024 * 1024),
        name="pick_blocks",
    )(owner_list, master)


def adam_step(param, grad, one, two, rate):
    next_one = BETA_ONE * one + (1.0 - BETA_ONE) * grad
    next_two = BETA_TWO * two + (1.0 - BETA_TWO) * grad * grad
    fix_one = 1.0 - BETA_ONE**STEP
    fix_two = 1.0 - BETA_TWO**STEP
    update = next_one * (1.0 / fix_one) / (jnp.sqrt(next_two * (1.0 / fix_two)) + ADAM_EPS)
    return (param - rate * (update + DECAY * param), next_one, next_two)


def adam_kernel(
    sizes, owner_ref, master, linear, smalls, one, two, bias, bias_one, bias_two, out_lat, in_lat,
    o_master, o_one, o_two, o_copy, o_bias, o_bias_one, o_bias_two, o_out, o_in,
    block_ref, params_v, grads_v, one_v, two_v, copy_v, out_v, low_v, high_v, in_sem, out_sem, lat_sem,
):
    S, F, G = sizes
    slots, rows, width = master.shape
    half = rows // 2
    biases = bias.shape[0]
    out_copy = pltpu.make_async_copy(out_lat, out_v, lat_sem.at[0])
    out_put = pltpu.make_async_copy(out_v, o_out, lat_sem.at[3])
    low_copy = pltpu.make_async_copy(in_lat, low_v, lat_sem.at[1])
    high_copy = pltpu.make_async_copy(high_v, o_in, lat_sem.at[2])

    group = lax.axis_index("grp")
    for j in range(slots):
        block_ref[j] = 0
    held = jnp.int32(0)
    for b in range(owner_ref.shape[0]):
        own = owner_ref[b] == group

        @pl.when(own)
        def _(b=b, held=held):
            block_ref[held] = b

        held = held + jnp.where(own, 1, 0)

    def fetch(j):
        return [
            pltpu.make_async_copy(src.at[j], dst.at[j], in_sem.at[j, n])
            for n, (src, dst) in enumerate(((master, params_v), (one, one_v), (two, two_v)))
        ]

    def fetch_grad(j):
        block = jnp.minimum(block_ref[j], LINEAR - 1)
        return pltpu.make_async_copy(linear.at[0, block], grads_v.at[j], in_sem.at[j, 3])

    def put(j):
        return [
            pltpu.make_async_copy(src.at[j], dst.at[j], out_sem.at[j, n])
            for n, (src, dst) in enumerate(
                ((params_v, o_master), (one_v, o_one), (two_v, o_two), (copy_v, o_copy))
            )
        ]

    def start(j):
        for copy in fetch(j):
            copy.start()

        @pl.when(block_ref[j] < LINEAR)
        def _():
            fetch_grad(j).start()

    loop(slots, start)
    low_copy.start()
    out_copy.start()

    table = smalls[...]
    lines = table.shape[0]
    first = (lax.axis_index("seq") * F + lax.axis_index("fsdp")) * rows
    lane, column = iota((width, rows), 0), iota((width, rows), 1)
    picked = dot(table, jnp.where(lane == first + column, 1.0, 0.0).astype(BF16)).astype(BF16)
    line, source = iota((lines, lines), 0), iota((lines, lines), 1)
    silu = dot(jnp.where(source == line - lax.rem(line, 16) + 14, 1.0, 0.0).astype(BF16), picked)
    kind = lax.rem(iota((lines, rows), 0), 16)

    line, source = iota((16, lines), 0), lax.rem(iota((16, lines), 1), 16)
    wanted = jnp.where(line < biases - 6, line + 6, line - (biases - 6))
    total = dot(jnp.where(source == wanted, 1.0, 0.0).astype(BF16), table)[0:biases]
    o_bias[...], o_bias_one[...], o_bias_two[...] = adam_step(
        bias[...], total, bias_one[...], bias_two[...], RATE_BIAS
    )

    def update(j):
        for copy in fetch(j):
            copy.wait()
        block = block_ref[j]

        @pl.when(block < LINEAR)
        def _():
            fetch_grad(j).wait()

        @pl.when(block >= LINEAR)
        def _():
            chosen = jnp.where(kind == block - LINEAR, silu, 0.0).astype(BF16)
            grads_v[j] = dot(chosen, table, TN).reshape(2, half, width)

        live = j < held
        for n in range(2):
            at = (j, pl.ds(n * half, half))
            param, one_old, two_old = params_v[at], one_v[at], two_v[at]
            stepped, next_one, next_two = adam_step(
                param, grads_v[j, n], one_old, two_old, RATE_WEIGHT
            )
            new = jnp.where(live, stepped, param)
            params_v[at] = new
            one_v[at] = jnp.where(live, next_one, one_old)
            two_v[at] = jnp.where(live, next_two, two_old)
            copy_v[at] = new.astype(BF16)
        for copy in put(j):
            copy.start()

    loop(slots, update)

    out_copy.wait()
    out_put.start()
    low_copy.wait()
    high_v[...] = low_v[...].astype(F32)
    high_copy.start()

    def finish(j):
        for copy in put(j):
            copy.wait()

    loop(slots, finish)
    out_put.wait()
    high_copy.wait()


def adam_slots(
    sizes, owner_list, master, linear, smalls, one, two, bias, bias_one, bias_two, out_lat, in_lat
):
    slots, rows, width = master.shape
    shape = jax.ShapeDtypeStruct(master.shape, F32)
    bias_shape = jax.ShapeDtypeStruct(bias.shape, F32)
    return pl.pallas_call(
        functools.partial(adam_kernel, sizes),
        out_shape=(shape, shape, shape, jax.ShapeDtypeStruct(master.shape, BF16))
        + (bias_shape,) * 3
        + (jax.ShapeDtypeStruct(out_lat.shape, BF16), jax.ShapeDtypeStruct(in_lat.shape, F32)),
        in_specs=[pl.BlockSpec(memory_space=pltpu.SMEM), ANY, ANY, VMEM, ANY, ANY]
        + [VMEM] * 3
        + [ANY] * 2,
        out_specs=(ANY,) * 4 + (VMEM,) * 3 + (ANY,) * 2,
        scratch_shapes=[
            pltpu.SMEM((slots,), jnp.int32),
            pltpu.VMEM(master.shape, F32),
            pltpu.VMEM((slots, 2, rows // 2, width), F32),
            pltpu.VMEM(master.shape, F32),
            pltpu.VMEM(master.shape, F32),
            pltpu.VMEM(master.shape, BF16),
            pltpu.VMEM(out_lat.shape, BF16),
            pltpu.VMEM(in_lat.shape, BF16),
            pltpu.VMEM(in_lat.shape, F32),
            DMA((slots, 4)),
            DMA((slots, 4)),
            DMA((4,)),
        ],
        compiler_params=pltpu.CompilerParams(vmem_limit_bytes=62 * 1024 * 1024),
        name="adam_slots",
    )(owner_list, master, linear, smalls, one, two, bias, bias_one, bias_two, out_lat, in_lat)


ROWS = 256
CHUNK = 128
NT = (((1,), (1,)), ((), ()))
NN = (((1,), (0,)), ((), ()))
TN = (((0,), (0,)), ((), ()))


def dot(left, right, dims=NN):
    return lax.dot_general(left, right, dims, preferred_element_type=F32)


def loop(count, body):
    def one(i, carry):
        body(i)
        return carry

    lax.fori_loop(0, count, one, 0)


def aligned(index, size):
    return pl.ds(pl.multiple_of(index * size, size), size)


def norm_rows(values):
    centre = jnp.mean(values, axis=-1, keepdims=True)
    centred = values - centre
    spread = jnp.mean(centred * centred, axis=-1, keepdims=True)
    inverse = lax.rsqrt(spread + EPS_NORM)
    return centred * inverse, inverse


def iota(shape, dim):
    return lax.broadcasted_iota(jnp.int32, shape, dim)


def attend_pair(q_ref, k_ref, v_ref, a_ref, lse_ref, pair):
    length = q_ref.shape[0]
    factor = 1.0 / math.sqrt(HD)
    for h in range(2):
        cols = slice((2 * pair + h) * HD, (2 * pair + h + 1) * HD)
        key = k_ref[:, cols]
        value = v_ref[:, cols]
        for r in range(0, length, ROWS):
            rows = slice(r, r + ROWS)
            scores = dot(q_ref[rows, cols], key, NT)
            high = jnp.max(scores, axis=1, keepdims=True)
            weights = jnp.exp((scores - high) * factor)
            total = jnp.sum(weights, axis=1, keepdims=True)
            out = dot(weights.astype(BF16), value, NN) / total
            a_ref[rows, cols] = out.astype(BF16)
            lse_ref[rows, cols] = jnp.broadcast_to(high * factor + jnp.log(total), (ROWS, HD))


def forward_kernel(sizes, *refs):
    (
        picked, cond, lat, cot, bias,
        bank_o, modw_o, mod_o, tok_o, ctok, hid_o, heads_o, head_a_o, lse_o, att_o, branch_o, mid_o, hid2_o, up_o, act_o, mlp_o, res_o,
        shard, theirs, conds, msg, modg, modr, modh, mod, bank, xv, hid, stage, heads, head_a, lse, att, mid, hid2, up, act, mlp,
        gs, gr, gl, ds, dr, dl, zs, zr, as_, ar, bs, br, cs, cr,
        las, lar, lbs, lbr, lzs, lzr, lcs, lcr, ms, mr, hs, hr, ts, tr, tl, xs, xr, save_sem,
    ) = refs
    at = Place(sizes)
    S, F, G = sizes
    K = bank.shape[0]
    half = shard.shape[1]
    blocks = picked.shape[0]
    T = 2 * S * F
    me = (at.s * F + at.f) * 2 + at.c
    quarter = lat.shape[1]
    tokens, width = xv.shape
    part = width // 2
    pieces = width // 128

    def device_of(i):
        n = lax.rem(me + i, T)
        return (lax.div(n, 2 * F), lax.rem(lax.div(n, 2), F), at.base + lax.rem(n, 2))

    bar = pltpu.get_barrier_semaphore()

    def greet(device):
        pl.semaphore_signal(bar, inc=1, device_id=device, device_id_type=MESH)

    loop(T - 1, lambda i: greet(device_of(i + 1)))
    for i in range(2, G):
        greet((at.s, at.f, lax.rem(at.base + i, G)))
    pl.semaphore_wait(bar, T - 1 + G - 2)

    def tok_move(j):
        return (2 * j + at.c, at.f, at.base + lax.div(at.s, 2))

    def tok_refs(which):
        return ((lat, xv), (cot, ctok))[which]

    def tok_to(j, which):
        src, dst = tok_refs(which)
        place = aligned(lax.rem(at.s, 2), quarter)
        return remote(
            src.at[j], dst.at[place], ts.at[which, j], tr.at[which, lax.rem(at.s, 2)], tok_move(j)
        )

    def tok_from(j, which):
        src, dst = tok_refs(which)
        place = pl.ds(j * quarter, quarter)
        return remote(src.at[0], dst.at[place], ts.at[which, j], tr.at[which, j], tok_move(j))

    def tok_local(j, which):
        src, dst = tok_refs(which)
        return pltpu.make_async_copy(src.at[j], dst.at[aligned(lax.rem(at.s, 2), quarter)], tl.at[which])

    def stays(j):
        return (2 * j + at.c == at.s) & (lax.div(at.s, 2) == at.c)

    def comes(j):
        return jnp.logical_not((2 * at.c + j == at.s) & (lax.rem(at.s, 2) == at.c))

    def tok_start(which):
        for j in range(2):
            @pl.when(stays(j))
            def _():
                tok_local(j, which).start()

            @pl.when(jnp.logical_not(stays(j)))
            def _():
                tok_to(j, which).start()

    def tok_finish(which):
        for j in range(2):
            @pl.when(stays(j))
            def _():
                tok_local(j, which).wait()

            @pl.when(jnp.logical_not(stays(j)))
            def _():
                tok_to(j, which).wait_send()

            @pl.when(comes(j))
            def _():
                tok_from(j, which).wait_recv()

    def rows_of(core):
        return picked.at[:, aligned(core, half)]

    def group_to(i):
        g = lax.rem(at.g + i, G)
        return remote(
            rows_of(lax.rem(g, 2)), theirs.at[G - 1 - i], gs.at[i], gr.at[G - 1 - i], (at.s, at.f, g)
        )

    def group_from(j):
        return remote(rows_of(0), theirs.at[j], gs.at[0], gr.at[j], at.sibling())

    group_own = pltpu.make_async_copy(rows_of(at.c), shard.at[0:blocks], gl)

    def cond_number(i):
        return lax.rem(at.f * 2 + at.c + i, 2 * F)

    def cond_to(i):
        n = cond_number(i)
        device = (at.s, lax.div(n, 2), at.base + lax.rem(n, 2))
        return remote(cond, conds.at[cond_number(0)], ds.at[i], dr.at[cond_number(0)], device)

    def cond_from(i):
        n = cond_number(i)
        return remote(cond, conds.at[n], ds.at[i], dr.at[n], at.sibling())

    cond_own = pltpu.make_async_copy(cond, conds.at[cond_number(0)], dl)

    here = at.s * F + at.f
    takes = lax.rem(at.s, 2) == at.c

    mod_give = remote(msg.at[:, 1 - at.c, :, 0:6], modg, hs.at[0], hr.at[0], at.sibling())

    def mod_to(i):
        n = lax.rem(lax.div(at.s, 2) * F + at.f + i, 2 * F)
        m, f = lax.div(n, F), lax.rem(n, F)
        return remote(
            msg.at[m, at.c, f, 0:6], modr.at[here], ms.at[i], mr.at[here], (2 * m + at.c, f, at.g)
        )

    def mod_from(i):
        n = lax.rem(here + i, S * F)
        return remote(msg.at[0, 0, 0, 0:6], modr.at[n], ms.at[0], mr.at[n], at.sibling())

    mod_swap = remote(modh, modh, hs.at[1], hr.at[1], at.sibling())

    def z_to(k, i):
        f = lax.rem(at.f + i, F)
        return remote(
            shard.at[k], bank.at[k, at.s, at.f, at.c], zs.at[k, i], zr.at[k, i], (at.s, f, at.g)
        )

    def z_from(k, i):
        f = lax.rem(at.f + F - i, F)
        return remote(shard.at[k], bank.at[k, at.s, f, at.c], zs.at[k, i], zr.at[k, i], (at.s, f, at.g))

    def a_copy(k, s):
        line = bank.at[k, s, :, at.c]
        return remote(line, line, as_.at[k], ar.at[k], (at.sa, at.f, at.g))

    def b_copy(k, s, n):
        line = bank.at[k, s, :, at.c]
        return remote(line, line, bs.at[k, n], br.at[k, n], (at.sb, at.f, at.g))

    sd = S - 1 - at.s

    def c_copy(k, s, n, core):
        line = bank.at[k, s, :, core]
        return remote(line, line, cs.at[k, n], cr.at[k, n], at.sibling())

    def z_start(k):
        for i in range(1, F):
            z_to(k, i).start()
        bank[k, at.s, at.f, at.c] = shard[k]

    late = K - LATE

    def late_a(n):
        piece = bank.at[late + n, at.s, at.f, at.c]
        return remote(piece, piece, las.at[n], lar.at[n], (at.sa, at.f, at.g))

    def late_a_from(n):
        piece = bank.at[late + n, at.sa, at.f, at.c]
        return remote(piece, piece, las.at[n], lar.at[n], (at.sa, at.f, at.g))

    def late_b(n, s, i):
        piece = bank.at[late + n, s, at.f, at.c]
        return remote(piece, piece, lbs.at[n, i], lbr.at[n, i], (at.sb, at.f, at.g))

    def late_line(n, way, j, f):
        line = bank.at[late + n, :, f, at.c]
        to = jnp.clip(at.f + 1 - 2 * way, 0, F - 1)
        return remote(line, line, lzs.at[n, way, j], lzr.at[n, way, j], (at.s, to, at.g))

    def late_c(n, f, core):
        line = bank.at[late + n, :, f, core]
        return remote(line, line, lcs.at[n, f], lcr.at[n, f], at.sibling())

    def late_first(n):
        bank[late + n, at.s, at.f, at.c] = shard[late + n]
        late_a(n).start()

    def late_second(n):
        late_a_from(n).wait_recv()
        late_b(n, at.s, 0).start()
        late_b(n, at.sa, 1).start()

    def late_sends(n, j, act):
        up, down = at.f - j, at.f + j

        @pl.when((up >= 0) & (at.f < F - 1))
        def _():
            act(late_line(n, 0, j, up))

        @pl.when((down < F) & (at.f > 0))
        def _():
            act(late_line(n, 1, j, down))

    def late_round(n, j):
        if j == 0:
            late_b(n, at.sb, 0).wait_recv()
            late_b(n, sd, 1).wait_recv()
            late_sends(n, 0, lambda copy: copy.start())
            late_c(n, at.f, at.c).start()
            return
        up, down = at.f - j, at.f + j

        @pl.when(up >= 0)
        def _():
            late_line(n, 0, j - 1, up).wait_recv()

        @pl.when(down < F)
        def _():
            late_line(n, 1, j - 1, down).wait_recv()

        if j < F - 1:
            late_sends(n, j, lambda copy: copy.start())

        @pl.when(up >= 0)
        def _():
            late_c(n, up, at.c).start()

        @pl.when(down < F)
        def _():
            late_c(n, down, at.c).start()

    def step_a(k):
        for i in range(1, F):
            z_from(k, i).wait_recv()
        a_copy(k, at.s).start()
        c_copy(k, at.s, 0, at.c).start()

    def step_b(k):
        a_copy(k, at.sa).wait_recv()
        b_copy(k, at.s, 0).start()
        b_copy(k, at.sa, 1).start()
        c_copy(k, at.sa, 1, at.c).start()

    def step_c(k):
        b_copy(k, at.sb, 0).wait_recv()
        c_copy(k, at.sb, 2, at.c).start()
        b_copy(k, sd, 1).wait_recv()
        c_copy(k, sd, 3, at.c).start()

    saves = []

    def save(src, dst):
        copy = pltpu.make_async_copy(src, dst, save_sem.at[len(saves)])
        copy.start()
        saves.append(copy)
        return len(saves) - 1

    waited = set()

    def saved(n):
        if n not in waited:
            saves[n].wait()
            waited.add(n)

    def arrive(k):
        if k < late:
            for n, s in enumerate((at.s, at.sb, at.sa, sd)):
                c_copy(k, s, n, 1 - at.c).wait_recv()
        else:
            for f in range(F):
                late_c(k - late, f, 1 - at.c).wait_recv()
        save(bank.at[k], bank_o.at[k])

    def weights(k):
        return bank[k].reshape(width, width)

    def gather_rows():
        group_own.wait()
        for i in range(1, G):
            group_from(i - 1).wait_recv()

        def one(b):
            value = shard[b].astype(F32)
            for i in range(G - 1):
                value = value + theirs[i, b].astype(F32)
            shard[b] = value.astype(BF16)

        loop(blocks, one)
        shard[blocks:] = jnp.zeros_like(shard[blocks:])

    def modulation_parts():
        cond_own.wait()
        loop(2 * F - 1, lambda i: cond_from(i + 1).wait_recv())
        value = conds[...].reshape(2 * F * 2 * pieces, 128)
        silu = (value / (1.0 + jnp.exp(-value))).astype(BF16)
        parts = 8 * half
        first = here * 2 * half + at.c * half
        lane, column = iota((128, parts), 0), iota((128, parts), 1)
        select = jnp.where(lane == lax.rem(first, 128) + lax.rem(column, half), 1.0, 0.0)
        rows = dot(silu, select.astype(BF16)).astype(BF16)
        count = 8 * S * F
        line, source = iota((count, rows.shape[0]), 0), iota((count, rows.shape[0]), 1)
        latent = lax.div(line, 8)
        chip, depth = lax.div(latent, F), lax.rem(latent, F)
        wanted = ((depth * 2 + lax.rem(chip, 2)) * 2 + lax.div(chip, 2)) * pieces + lax.div(first, 128)
        spread = dot(jnp.where(source == wanted, 1.0, 0.0).astype(BF16), rows)
        line, column = iota((count, parts), 0), iota((count, parts), 1)
        spread = jnp.where(lax.rem(line, 8) == lax.div(column, half), spread, 0.0).astype(BF16)
        value = dot(spread, shard[K:].reshape(parts, width))
        flat = msg.reshape(count * pieces, 128)
        for n in range(pieces):
            flat[pl.ds(n, count, stride=pieces)] = value[:, n * 128 : (n + 1) * 128]
        mod_give.start()

    def modulation_send():
        mod_give.wait()

        def add(n):
            m, f = lax.div(n, F), lax.rem(n, F)
            msg[m, at.c, f, 0:6] = msg[m, at.c, f, 0:6] + modg[m, f]

        loop(2 * F, add)

        @pl.when(jnp.logical_not(takes))
        def _():
            mod_to(0).start()

        loop(2 * F - 1, lambda i: mod_to(i + 1).start())

    def modulation():
        modulation_parts()
        save(shard.at[K:blocks], modw_o)
        modulation_send()

    def modulation_sum():
        @pl.when(takes)
        def _():
            loop(S * F - 1, lambda i: mod_from(i + 1).wait_recv())
            modr[here] = msg[lax.div(at.s, 2), at.c, at.f, 0:6]
            total = modr[0]
            for n in range(1, S * F):
                total = total + modr[n]
            modh[...] = total.reshape(6 * pieces, 128)
            mod_swap.start()

        @pl.when(jnp.logical_not(takes))
        def _():
            mod_swap.wait_recv()

        for n in range(pieces):
            cols = slice(n * 128, (n + 1) * 128)
            mod[0:6, cols] = modh[pl.ds(n, 6, stride=pieces)]
        mod[0:6] = mod[0:6] + bias[8:14]
        mod[6:8] = jnp.zeros((2, width), F32)
        save(mod, mod_o)

    def prepare():
        modulation_sum()
        tok_finish(0)
        save(xv, tok_o)

        def one(i):
            rows = aligned(i, CHUNK)
            scaled, _ = norm_rows(xv[rows].astype(F32))
            hid[rows] = (scaled * (1.0 + mod[1:2]) + mod[0:1]).astype(BF16)

        loop(tokens // CHUNK, one)
        hid_saved.append(save(hid, hid_o))

    hid_saved = []

    def swap(n):
        return remote(
            stage.at[n], heads.at[n, aligned(at.c, tokens)], xs.at[n], xr.at[n], at.sibling()
        )

    def swap_from(n):
        return remote(
            stage.at[n], heads.at[n, aligned(1 - at.c, tokens)], xs.at[n], xr.at[n], at.sibling()
        )

    def project(n):
        value = dot(hid[...], weights(n))
        if n != 1:
            row = n // 2
            value = value + bias[row : row + 1]
        value = value.astype(BF16)
        first, second = value[:, :part], value[:, part:]
        stage[n] = jnp.where(at.c == 0, second, first)
        swap(n).start()
        heads[n, aligned(at.c, tokens)] = jnp.where(at.c == 0, first, second)

    def attend_part(pair):
        if pair == 0:
            for n in range(3):
                swap_from(n).wait_recv()
                save(heads.at[n], heads_o.at[n])
        attend_pair(heads.at[0], heads.at[1], heads.at[2], head_a, lse, pair)

    def give_out():
        return remote(
            head_a.at[aligned(1 - at.c, tokens)], att.at[:, aligned(at.c, part)], xs.at[3], xr.at[3], at.sibling()
        )

    def give_from():
        return remote(
            head_a.at[aligned(at.c, tokens)], att.at[:, aligned(1 - at.c, part)], xs.at[3], xr.at[3], at.sibling()
        )

    def send_attended():
        give_out().start()
        att[:, aligned(at.c, part)] = head_a[aligned(at.c, tokens)]
        save(head_a, head_a_o)
        save(lse, lse_o)

    branch_saved = []

    def output_projection():
        give_from().wait_recv()
        save(att, att_o)
        mlp[...] = dot(att[...], weights(3)) + bias[2:3]
        branch_saved.append(save(mlp, branch_o))

        def rest(i):
            rows = aligned(i, CHUNK)
            middle = xv[rows].astype(F32) + mod[2:3] * mlp[rows]
            mid[rows] = middle
            scaled, _ = norm_rows(middle)
            hid2[rows] = (scaled * (1.0 + mod[4:5]) + mod[3:4]).astype(BF16)

        loop(tokens // CHUNK, rest)
        save(mid, mid_o)
        save(hid2, hid2_o)

    up_saved = []

    def upper(j):
        if j >= 2:
            saved(up_saved[j - 2])
        value = dot(hid2[...], weights(4 + j)) + bias[3 + j : 4 + j]
        up[j % 2] = value
        act[j] = jax.nn.gelu(value, approximate=True).astype(BF16)
        up_saved.append(save(up.at[j % 2], up_o.at[j]))
        save(act.at[j], act_o.at[j])

    def lower(j):
        if j == 0:
            saved(branch_saved[0])
        value = dot(act[j], weights(8 + j))
        mlp[...] = value + (bias[7:8] if j == 0 else mlp[...])

    def finish_forward():
        save(mlp, mlp_o)
        saved(hid_saved[0])

        def one(i):
            rows = aligned(i, CHUNK)
            hid[rows] = (mid[rows] + mod[5:6] * mlp[rows]).astype(BF16)

        loop(tokens // CHUNK, one)
        save(hid, res_o)

    tok_start(0)
    for i in range(1, G):
        group_to(i).start()
    group_own.start()
    cond_own.start()
    loop(2 * F - 1, lambda i: cond_to(i + 1).start())
    gather_rows()
    z_start(0)
    z_start(1)
    step_a(0)
    z_start(2)
    modulation()
    step_b(0)
    z_start(3)
    late_first(0)
    z_start(4)
    z_start(5)
    step_a(1)
    step_a(2)
    z_start(6)
    step_b(1)
    late_first(1)
    step_c(0)
    step_b(2)
    late_second(0)
    step_c(1)
    step_a(3)
    step_a(4)
    arrive(1)
    prepare()
    step_c(2)
    arrive(0)
    step_a(5)
    step_b(3)
    project(0)
    z_start(7)
    step_a(6)
    late_round(0, 0)
    late_second(1)
    step_b(4)
    z_start(8)
    step_c(3)
    z_start(9)
    arrive(2)
    project(1)
    step_a(7)
    step_b(5)
    late_round(1, 0)
    project(2)
    step_a(8)
    step_b(6)
    arrive(3)
    late_round(0, 1)
    attend_part(0)
    step_c(4)
    step_a(9)
    attend_part(1)
    step_b(7)
    late_round(1, 1)
    step_c(5)
    attend_part(2)
    step_b(8)
    attend_part(3)
    arrive(5)
    late_round(0, 2)
    step_c(6)
    send_attended()
    step_b(9)
    late_round(1, 2)
    step_c(7)
    arrive(4)
    output_projection()
    upper(0)
    arrive(6)
    step_c(8)
    for j in range(3, F):
        late_round(0, j)
    upper(1)
    tok_start(1)
    arrive(7)
    upper(2)
    for j in range(3, F):
        late_round(1, j)
    upper(3)
    arrive(8)
    step_c(9)
    arrive(11)
    arrive(10)
    lower(0)
    arrive(9)
    lower(1)
    lower(2)
    lower(3)
    finish_forward()

    def finish(k):
        for i in range(1, F):
            z_to(k, i).wait_send()
        a_copy(k, at.s).wait_send()
        b_copy(k, at.s, 0).wait_send()
        b_copy(k, at.sa, 1).wait_send()
        for n, s in enumerate((at.s, at.sa, at.sb, sd)):
            c_copy(k, s, n, at.c).wait_send()

    loop(late, finish)
    for n in range(LATE):
        late_a(n).wait_send()
        late_b(n, at.s, 0).wait_send()
        late_b(n, at.sa, 1).wait_send()
        for j in range(F - 1):
            late_sends(n, j, lambda copy: copy.wait_send())
        for f in range(F):
            late_c(n, f, at.c).wait_send()
    for i in range(1, G):
        group_to(i).wait_send()
    loop(2 * F - 1, lambda i: cond_to(i + 1).wait_send())
    loop(2 * F - 1, lambda i: mod_to(i + 1).wait_send())

    @pl.when(takes)
    def _():
        mod_swap.wait_send()

    @pl.when(jnp.logical_not(takes))
    def _():
        mod_to(0).wait_send()

    for n in range(3):
        swap(n).wait_send()
    give_out().wait_send()
    for n in range(len(saves)):
        saved(n)
    tok_finish(1)


def forward(sizes, picked, cond, lat, cot, bias):
    S, F, G = sizes
    blocks, rows, width = picked.shape
    K, half, T = LINEAR, rows // 2, 2 * S * F
    tokens = 2 * lat.shape[1]
    length, part = 2 * tokens, width // 2
    low = lambda *shape: (shape, BF16)
    high = lambda *shape: (shape, F32)
    outs = (
        low(K, S, F, 2, half, width),
        low(blocks - K, half, width),
        high(8, width),
        low(tokens, width),
        low(tokens, width),
        low(tokens, width),
        low(3, length, part),
        low(length, part),
        high(length, part),
        low(tokens, width),
        high(tokens, width),
        high(tokens, width),
        low(tokens, width),
        high(4, tokens, width),
        low(4, tokens, width),
        high(tokens, width),
        low(tokens, width),
    )
    scratch = (
        low(K + 8, half, width),
        low(G - 1, blocks, half, width),
        high(2 * F, 2 * width // 128, 128),
        high(2, 2, F, 8, width // 128, 128),
        high(2, F, 6, width // 128, 128),
        high(S * F, 6, width // 128, 128),
        high(6 * width // 128, 128),
        high(8, width),
        low(K, S, F, 2, half, width),
        low(tokens, width),
        low(tokens, width),
        low(3, tokens, part),
        low(3, length, part),
        low(length, part),
        high(length, part),
        low(tokens, width),
        high(tokens, width),
        low(tokens, width),
        high(2, tokens, width),
        low(4, tokens, width),
        high(tokens, width),
    )
    sems = (
        (G,), (G,), None, (2 * F,), (2 * F,), None, (K, F), (K, F), (K,), (K,), (K, 2), (K, 2), (K, 4), (K, 4),
        (LATE,), (LATE,), (LATE, 2), (LATE, 2), (LATE, 2, F), (LATE, 2, F), (LATE, F), (LATE, F),
        (2 * F,), (S * F,), (2,), (2,), (2, 2), (2, 2), (2,), (4,), (4,), (40,),
    )
    return pl.pallas_call(
        functools.partial(forward_kernel, sizes),
        out_shape=tuple(jax.ShapeDtypeStruct(*o) for o in outs),
        in_specs=[ANY] * 4 + [VMEM],
        out_specs=(ANY,) * len(outs),
        scratch_shapes=[pltpu.VMEM(*s) for s in scratch] + [DMA if n is None else DMA(n) for n in sems],
        compiler_params=params(2, 63),
        name="forward",
    )(picked, cond, lat, cot, bias)


RING = 4
ORDER = (8, 4, 9, 5, 10, 6, 11, 7, 3, 0, 1, 2)
LINED = (0, 3, 7)
PLAIN = tuple(r for r in range(LINEAR) if r not in LINED)


def gelu_slope(values):
    scale = 0.7978845608
    square = values * values
    bend = jnp.tanh(scale * values * (1.0 + 0.044715 * square))
    return 0.5 * (1.0 + bend) + 0.5 * values * (1.0 - bend * bend) * (
        scale * (1.0 + 3.0 * 0.044715 * square)
    )


def attend_pair_back(q, k, v, a, lse_ref, da_ref, pair, dq_ref, dk_ref, dv_ref):
    length = q.shape[0]
    factor = 1.0 / math.sqrt(HD)
    for h in range(2):
        cols = slice(h * HD, (h + 1) * HD)
        grad_cols = slice((2 * pair + h) * HD, (2 * pair + h + 1) * HD)
        key = k[:, cols]
        value = v[:, cols]
        dk = jnp.zeros((HD, length), F32)
        dv = jnp.zeros((HD, length), F32)
        for r in range(0, length, ROWS):
            rows = slice(r, r + ROWS)
            query = q[rows, cols]
            grad = da_ref[rows, grad_cols]
            lse = lse_ref[rows, h * HD : h * HD + 1]
            scores = dot(query, key, NT)
            probs = jnp.exp(scores * factor - lse)
            row_dot = jnp.sum(grad.astype(F32) * a[rows, cols].astype(F32), axis=1, keepdims=True)
            weight_grad = dot(grad, value, NT)
            score_grad = (probs * (weight_grad - row_dot)).astype(BF16)
            dq_ref[rows, cols] = (dot(score_grad, key, NN) * factor).astype(BF16)
            dk = dk + dot(query.T, score_grad, NN)
            dv = dv + dot(grad.T, probs.astype(BF16), NN)
        dk_ref[:, cols] = (dk * factor).T.astype(BF16)
        dv_ref[:, cols] = dv.T.astype(BF16)


def backward_kernel(sizes, *refs):
    (
        bank, modw, mod, tok, ctok, hid, heads, head_a, lse, att, branch, mid, hid2, up, act, mlp, res, silu,
        red, smalls, cgs, out_lat, in_lat,
        mine, give, r0, r1, r2, r3, lz, l1, l2, total, wbuf,
        ebuf, dfb, f0, f1, a0, a1, dub, dh2, h2b, stage, dah, qkva, lsev, dpair, dqt, accs, small, sv, sw, swb, smv, cg, cgl,
        cs, cr, bs, br, as_, ar, zs, zr, lzs, lzr, os_, rs, rr, free, vs, vr, ws, wr, wl, qs, qr, us, ur, ds, dr, dl, es, er, ts, tr, tl, loads, xs, xr, ps, pr,
    ) = refs
    at = Place(sizes)
    S, F, G = sizes
    K = mine.shape[0]
    half = mine.shape[3]
    tokens, width = ebuf.shape
    part = width // 2
    band = width // S
    count = S * F * G
    me = (at.s * F + at.f) * G + at.g
    quarter = out_lat.shape[1]
    sd = S - 1 - at.s
    chunks = tokens // CHUNK

    def device_of(i):
        n = lax.rem(me + i, count)
        return (lax.div(n, F * G), lax.rem(lax.div(n, G), F), lax.rem(n, G))

    bar = pltpu.get_barrier_semaphore()

    def greet(i):
        pl.semaphore_signal(bar, inc=1, device_id=device_of(i + 1), device_id_type=MESH)

    loop(count - 1, greet)

    def c_copy(r):
        return remote(give.at[r % 2], r0.at[r % RING], cs.at[r], cr.at[r], at.sibling())

    def b_copy(r, s, n):
        if r in LINED:
            src, dst = mine.at[r, s, at.f], l1.at[LINED.index(r), n]
        else:
            src, dst = mine.at[r, s], r1.at[PLAIN.index(r), n]
        return remote(src, dst, bs.at[r, n], br.at[r, n], (at.sb, at.f, at.g))

    def a_copy(r):
        if r in LINED:
            src, dst = mine.at[r, at.sa, at.f], l2.at[LINED.index(r)]
        else:
            src, dst = mine.at[r, at.sa], r2.at[PLAIN.index(r)]
        return remote(src, dst, as_.at[r], ar.at[r], (at.sa, at.f, at.g))

    def z_to(r, i):
        f = lax.rem(at.f + i, F)
        return remote(
            mine.at[r, at.s, f], r3.at[PLAIN.index(r), i - 1], zs.at[r, i], zr.at[r, i], (at.s, f, at.g)
        )

    def up_line(r, i):
        tau = F - 1 - i + at.f
        to = jnp.clip(at.f + 1, 0, F - 1)
        tau_in = jnp.clip(tau, 0, F - 1)
        return tau_in, remote(
            mine.at[r, :, tau_in], lz.at[LINED.index(r), tau_in], lzs.at[LINED.index(r), 0, i], lzr.at[LINED.index(r), 0, i], (at.s, to, at.g)
        )

    def down_line(r, i):
        tau = jnp.clip(i + at.f - F + 1, 0, F - 1)
        to = jnp.clip(at.f - 1, 0, F - 1)
        place = F if i == F - 2 else tau
        return remote(
            mine.at[r, :, tau], lz.at[LINED.index(r), place], lzs.at[LINED.index(r), 1, i], lzr.at[LINED.index(r), 1, i], (at.s, to, at.g)
        )

    def line_sends(r, i, act):
        @pl.when((at.f <= i) & (at.f < F - 1))
        def _():
            act(up_line(r, i)[1])

        @pl.when((F - 1 - at.f <= i) & (at.f > 0))
        def _():
            act(down_line(r, i))

    def add_set(r, tau, place):
        def one(s):
            mine[r, s, tau] = mine[r, s, tau] + lz[LINED.index(r), place, s]

        loop(S, one)

    def line(r, i):
        if i > 0:
            @pl.when((at.f >= 1) & (at.f <= i))
            def _():
                tau = jnp.clip(F - 1 - i + at.f, 0, F - 1)
                remote(
                    mine.at[r, :, tau], lz.at[LINED.index(r), tau], lzs.at[LINED.index(r), 0, i - 1], lzr.at[LINED.index(r), 0, i - 1], at.sibling()
                ).wait_recv()
                add_set(r, tau, tau)

            @pl.when((at.f <= F - 2) & (F - 1 - at.f <= i))
            def _():
                tau = jnp.clip(i + at.f - F + 1, 0, F - 1)
                place = F if i == F - 1 else tau
                remote(
                    mine.at[r, :, tau], lz.at[LINED.index(r), place], lzs.at[LINED.index(r), 1, i - 1], lzr.at[LINED.index(r), 1, i - 1], at.sibling()
                ).wait_recv()
                add_set(r, tau, place)

        if i < F - 1:
            line_sends(r, i, lambda copy: copy.start())
        else:
            b_copy(r, at.sb, 0).start()
            b_copy(r, sd, 1).start()

    def add_piece(r, s, src):
        mine[r, s, at.f] = mine[r, s, at.f] + src

    pair = lax.div(at.g, 2)
    finals = []

    def out_copy(r):
        return pltpu.make_async_copy(total.at[finals.index(r) % 2], red.at[pair, ORDER[r], at.c], os_.at[r])

    def out_to(r, i):
        g = lax.rem(at.g + i, G)
        return remote(
            total.at[finals.index(r) % 2], red.at[pair, ORDER[r], at.c], rs.at[r, i], rr.at[r, i], (at.s, at.f, g)
        )

    def out_from(r, i):
        g = lax.rem(at.g + G - i, G)
        return remote(
            total.at[finals.index(r) % 2], red.at[lax.div(g, 2), ORDER[r], lax.rem(g, 2)], rs.at[r, i], rr.at[r, i], at.sibling()
        )

    def out_done(r):
        out_copy(r).wait()
        for i in range(1, G):
            out_to(r, i).wait_send()

    def add_line(dst, src):
        dst[...] = dst[...] + src[...]

    def hop0(r):
        c_copy(r).wait_recv()
        loop(S, lambda s: add_line(mine.at[r, s], r0.at[r % RING, s]))
        if r + RING < K:
            pl.semaphore_signal(free, inc=1, device_id=at.sibling(), device_id_type=MESH)
        if r in LINED:
            line(r, 0)
            return
        b_copy(r, at.sb, 0).start()
        b_copy(r, sd, 1).start()

    def hop1(r):
        b_copy(r, at.sb, 0).wait_recv()
        b_copy(r, sd, 1).wait_recv()
        if r in LINED:
            add_piece(r, at.sa, l1[LINED.index(r), 1])
            a_copy(r).start()
            add_piece(r, at.s, l1[LINED.index(r), 0])
            return
        add_line(mine.at[r, at.sa], r1.at[PLAIN.index(r), 1])
        a_copy(r).start()
        add_line(mine.at[r, at.s], r1.at[PLAIN.index(r), 0])

    def hop2(r):
        if r in LINED:
            return
        a_copy(r).wait_recv()
        add_line(mine.at[r, at.s], r2.at[PLAIN.index(r)])
        for i in range(1, F):
            z_to(r, i).start()

    def hop3(r):
        if r in LINED:
            a_copy(r).wait_recv()
            others = [l2.at[LINED.index(r)]]
        else:
            for i in range(1, F):
                z_to(r, i).wait_recv()
            others = [r3.at[PLAIN.index(r), i] for i in range(F - 1)]
        finals.append(r)
        if len(finals) > 2:
            out_done(finals[-3])
        value = mine[r, at.s, at.f].astype(F32)
        for other in others:
            value = value + other[...].astype(F32)
        total[finals.index(r) % 2] = value
        out_copy(r).start()
        for i in range(1, G):
            out_to(r, i).start()

    def produce(r, left, right):
        if r >= 2:
            c_copy(r - 2).wait_send()

        lines = S // 2

        def one(n):
            value = dot(left[:, aligned(n, lines * band)], right[...], TN)
            value = value.astype(BF16).reshape(lines, F, 2, half, width)
            first, second = value[:, :, 0], value[:, :, 1]
            mine[r, aligned(n, lines)] = jnp.where(at.c == 0, first, second)
            give[r % 2, aligned(n, lines)] = jnp.where(at.c == 0, second, first)

        loop(2, one)
        if r >= RING:
            pl.semaphore_wait(free, 1)
        c_copy(r).start()

    def back_device(j):
        return (2 * at.c + j, at.f, at.base + lax.rem(at.s, 2))

    def back_stays(j):
        return (2 * at.c + j == at.s) & (lax.rem(at.s, 2) == at.c)

    def back_comes(m):
        return jnp.logical_not((2 * m + at.c == at.s) & (lax.div(at.s, 2) == at.c))

    def back_refs(which):
        return ((res, out_lat), (dfb, in_lat))[which]

    def back_to(j, which):
        src, dst = back_refs(which)
        m = lax.div(at.s, 2)
        return remote(
            src.at[pl.ds(j * quarter, quarter)], dst.at[m], ts.at[which, j], tr.at[which, m], back_device(j)
        )

    def back_from(m, which):
        src, dst = back_refs(which)
        return remote(
            src.at[pl.ds(0, quarter)], dst.at[m], ts.at[which, m], tr.at[which, m], back_device(m)
        )

    def back_local(j, which):
        src, dst = back_refs(which)
        return pltpu.make_async_copy(
            src.at[pl.ds(j * quarter, quarter)], dst.at[lax.div(at.s, 2)], tl.at[which]
        )

    def back_start(which):
        for j in range(2):
            @pl.when(back_stays(j))
            def _():
                back_local(j, which).start()

            @pl.when(jnp.logical_not(back_stays(j)))
            def _():
                back_to(j, which).start()

    def back_finish(which):
        for j in range(2):
            @pl.when(back_stays(j))
            def _():
                back_local(j, which).wait()

            @pl.when(jnp.logical_not(back_stays(j)))
            def _():
                back_to(j, which).wait_send()

            @pl.when(back_comes(j))
            def _():
                back_from(j, which).wait_recv()

    def load(src, dst, n):
        return pltpu.make_async_copy(src, dst, loads.at[n])

    def load_weight(k, slot):
        return load(bank.at[k], wbuf.at[slot], slot)

    ups, acts = (f0, f1), (a0, a1)

    def load_up(j):
        return load(up.at[j], ups[j % 2], 2 + j % 2)

    def load_act(j):
        return load(act.at[j], acts[j % 2], 4 + j % 2)

    def load_pair(p):
        cols = pl.ds(p * 2 * HD, 2 * HD)
        slot = p % 2
        return [load(heads.at[n, :, cols], qkva.at[slot, n], 10 + 5 * slot + n) for n in range(3)] + [
            load(head_a.at[:, cols], qkva.at[slot, 3], 13 + 5 * slot),
            load(lse.at[:, cols], lsev.at[slot], 14 + 5 * slot),
        ]

    def weights(slot):
        return wbuf[slot].reshape(width, width)

    def add_rows(i, value, cols=slice(None)):
        accs[i, :, cols] += value.reshape(-1, 8, value.shape[-1]).sum(axis=0)

    load_e, load_mlp, load_h2 = load(ctok, ebuf, 6), load(mlp, dh2, 7), load(hid2, h2b, 8)
    for copy in (load_e, load_mlp):
        copy.start()
    load_weight(8, 0).start()
    load_act(0).start()
    load_up(0).start()
    load_h2.start()
    load_weight(4, 1).start()
    load_up(1).start()
    load_act(1).start()
    pl.semaphore_wait(bar, count - 1)
    back_start(0)
    accs[...] = jnp.zeros_like(accs)
    load_e.wait()
    load_mlp.wait()

    def start_rows(i):
        rows = aligned(i, CHUNK)
        grad = ebuf[rows].astype(F32)
        add_rows(5, grad * dh2[rows])
        low = (mod[5:6] * grad).astype(BF16)
        dfb[rows] = low
        add_rows(13, low.astype(F32))

    loop(chunks, start_rows)

    def active_back(j):
        load_weight(8 + j, 0).wait()
        load_up(j).wait()

        value = dot(dfb[...], weights(0), NT) * gelu_slope(ups[j % 2][...])
        low = value.astype(BF16)
        dub[...] = low
        add_rows(9 + j, low.astype(F32))
        load_weight(9 + j if j < 3 else 3, 0).start()
        if j < 2:
            load_up(j + 2).start()
        else:
            (load_mid, load_branch)[j - 2].start()

    def hidden_back(j):
        load_weight(4 + j, 1).wait()

        value = dot(dub[...], weights(1), NT)
        dh2[...] = value if j == 0 else dh2[...] + value
        load_weight(5 + j if j < 3 else 0, 1).start()

    def product_eight(j):
        load_act(j).wait()
        produce(2 * j, acts[j % 2], dfb)
        if j < 2:
            load_act(j + 2).start()
        if j == 2:
            load_att.start()

    def product_four(j):
        if j == 0:
            load_h2.wait()
        produce(2 * j + 1, h2b, dub)
        if j == 3:
            load_hid.start()
            load_modw.start()

    def product_three():
        load_att.wait()
        produce(8, a0, dfb)

    def product_first(n):
        if n == 0:
            load_hid.wait()
        produce(9 + n, h2b, dqt.at[n])

    load_mid, load_branch = load(mid, f0, 2), load(branch, f1, 3)
    load_att, load_hid, load_x = load(att, a0, 4), load(hid, h2b, 8), load(tok, ebuf, 6)

    def middle_back():
        load_mid.wait()
        load_branch.wait()

        def one(i):
            rows = aligned(i, CHUNK)
            scaled, inverse = norm_rows(f0[rows])
            grad = dh2[rows]
            inner = grad * (1.0 + mod[4:5])
            mean_inner = jnp.mean(inner, axis=-1, keepdims=True)
            mean_scaled = jnp.mean(inner * scaled, axis=-1, keepdims=True)
            value = ebuf[rows].astype(F32) + inverse * (inner - mean_inner - scaled * mean_scaled)
            add_rows(4, grad * scaled)
            add_rows(3, grad)
            dh2[rows] = value
            add_rows(2, value * f1[rows])
            low = (mod[2:3] * value).astype(BF16)
            dfb[rows] = low
            add_rows(8, low.astype(F32))

        loop(chunks, one)
        load_x.start()

    def swap_da(here):
        return remote(stage, dah.at[aligned(here, tokens)], xs, xr, at.sibling())

    def attended_back():
        load_weight(3, 0).wait()

        value = dot(dfb[...], weights(0), NT).astype(BF16)
        first, second = value[:, :part], value[:, part:]
        stage[...] = jnp.where(at.c == 0, second, first)
        swap_da(at.c).start()
        dah[aligned(at.c, tokens)] = jnp.where(at.c == 0, first, second)
        load_weight(1, 0).start()
        for copy in load_pair(0) + load_pair(1):
            copy.start()

    def pair_to(p, n, core):
        rows = aligned(1 - at.c, tokens)
        cols = pl.ds(pl.multiple_of(core * part + p * 2 * HD, 2 * HD), 2 * HD)
        return remote(
            dpair.at[p % 2, n, rows], dqt.at[n, :, cols], ps.at[p, n], pr.at[p, n], at.sibling()
        )

    def attend_back_part(p):
        if p == 0:
            swap_da(1 - at.c).wait_recv()
        for copy in load_pair(p):
            copy.wait()
        if p >= 2:
            for n in range(3):
                pair_to(p - 2, n, at.c).wait_send()
        slot = p % 2
        attend_pair_back(
            qkva.at[slot, 0], qkva.at[slot, 1], qkva.at[slot, 2], qkva.at[slot, 3], lsev.at[slot], dah, p,
            dpair.at[slot, 0], dpair.at[slot, 1], dpair.at[slot, 2],
        )
        cols = pl.ds(pl.multiple_of(at.c * part + p * 2 * HD, 2 * HD), 2 * HD)
        for n in range(3):
            pair_to(p, n, at.c).start()
            dqt[n, :, cols] = dpair[slot, n, aligned(at.c, tokens)]
        if p + 2 < part // (2 * HD):
            for copy in load_pair(p + 2):
                copy.start()

    def pairs_arrive():
        for p in range(part // (2 * HD)):
            for n in range(3):
                pair_to(p, n, 1 - at.c).wait_recv()

        def one(i):
            rows = aligned(i, CHUNK)
            add_rows(6, dqt[0, rows].astype(F32))
            add_rows(7, dqt[2, rows].astype(F32))

        loop(chunks, one)

    def first_back(k):
        slot = (1, 0, 1)[k]
        load_weight(k, slot).wait()
        value = dot(dqt[k], weights(slot), NT)
        f0[...] = value if k == 0 else f0[...] + value
        if k == 0:
            load_weight(2, 1).start()

    def input_back():
        load_x.wait()

        def one(i):
            rows = aligned(i, CHUNK)
            scaled, inverse = norm_rows(ebuf[rows].astype(F32))
            grad = f0[rows]
            inner = grad * (1.0 + mod[1:2])
            mean_inner = jnp.mean(inner, axis=-1, keepdims=True)
            mean_scaled = jnp.mean(inner * scaled, axis=-1, keepdims=True)
            value = dh2[rows] + inverse * (inner - mean_inner - scaled * mean_scaled)
            add_rows(1, grad * scaled)
            add_rows(0, grad)
            dfb[rows] = value.astype(BF16)

        loop(chunks, one)

    small_swap = remote(small, sv, vs, vr, at.sibling())
    lines = F * G // 2
    mark = at.f * (G // 2) + pair
    sent = aligned(at.c, part)

    def small_region(s, n):
        return smalls.at[s, lax.div(n, G // 2), lax.rem(n, G // 2), :, sent]

    def small_to(i):
        n = lax.rem(mark + i, lines)
        device = (at.s, lax.div(n, G // 2), 2 * lax.rem(n, G // 2) + at.c)
        return remote(swb.at[:, sent], small_region(at.s, mark), ws.at[i], wr.at[mark], device)

    def small_from(i):
        n = lax.rem(mark + i, lines)
        return remote(swb.at[:, sent], small_region(at.s, n), ws.at[i], wr.at[n], at.sibling())

    small_own = pltpu.make_async_copy(swb.at[:, sent], small_region(at.s, mark), wl)
    plane = (at.sx, at.sy, sd)

    def small_across(n, s, to):
        region = smalls.at[s, :, :, :, sent]
        return remote(region, region, qs.at[n], qr.at[n], (to, at.f, at.g))

    def small_share(core):
        region = smalls.at[:, :, :, :, aligned(core, part)]
        return remote(region, region, us, ur, at.sibling())

    def small_start():
        small[...] = jnp.zeros_like(small)
        small[0:14] = accs[...].sum(axis=1)
        small[14:15] = silu[0:1]
        small_swap.start()

    def small_send():
        small_swap.wait()
        sw[...] = small[...] + sv[...]
        swb[...] = sw[...].astype(BF16)
        small_own.start()
        for i in range(1, lines):
            small_to(i).start()

    def small_plane():
        small_own.wait()
        for i in range(1, lines):
            small_from(i).wait_recv()
        for n, s in enumerate(plane):
            small_across(n, at.s, s).start()

    def small_share_start():
        for n, s in enumerate(plane):
            small_across(n, s, s).wait_recv()
        small_share(at.c).start()

    load_modw = load(modw, dub.at[0 : 6 * half], 9)
    pair_smalls = pltpu.make_async_copy(smalls.at[:, :, pair], smv, dl.at[0])
    spot = at.f * 2 + at.c

    def cond_number(i):
        return lax.rem(spot + i, 2 * F)

    def cond_to(i):
        n = cond_number(i)
        device = (at.s, lax.div(n, 2), at.base + lax.rem(n, 2))
        return remote(cg.at[aligned(lax.div(n, 4), 8)], cgl.at[spot], ds.at[i], dr.at[spot], device)

    def cond_from(i):
        n = cond_number(i)
        return remote(cg.at[0:8], cgl.at[n], ds.at[i], dr.at[n], at.sibling())

    cond_own = pltpu.make_async_copy(cgl, cgs.at[at.s], dl.at[1])

    def cond_across(n, s, to):
        return remote(cgl, cgs.at[s], es.at[n], er.at[n], (to, at.f, at.g))

    def cond_start():
        small_share(1 - at.c).wait_recv()
        pair_smalls.start()
        load_modw.wait()
        dub[6 * half : 8 * half] = jnp.zeros((2 * half, width), BF16)
        pair_smalls.wait()
        value = dot(smv[...].reshape(S * F * 16, width), dub[0 : 8 * half], NT)
        line, column = iota(value.shape, 0), iota(value.shape, 1)
        value = jnp.where(lax.rem(line, 16) == lax.div(column, half), value, 0.0)
        value = value.reshape(S * F, 16, 8 * half).sum(axis=1)
        rows = value[:, 0:128]
        for n in range(1, 8 * half // 128):
            rows = rows + value[:, n * 128 : (n + 1) * 128]
        for s in range(S):
            for f in range(F):
                to = (f * 2 + s % 2) * 2 + s // 2
                cg[to : to + 1] = rows[s * F + f : s * F + f + 1]
        cgl[spot] = cg[aligned(lax.div(spot, 4), 8)]
        loop(2 * F - 1, lambda i: cond_to(i + 1).start())

    def cond_plane():
        loop(2 * F - 1, lambda i: cond_from(i + 1).wait_recv())
        cond_own.start()
        for n, s in enumerate(plane):
            cond_across(n, at.s, s).start()

    active_back(0)
    product_eight(0)
    hidden_back(0)
    product_four(0)
    hop0(0)
    active_back(1)
    hop0(1)
    product_eight(1)
    hidden_back(1)
    product_four(1)
    line(0, 1)
    active_back(2)
    hop0(2)
    hop0(3)
    product_eight(2)
    hidden_back(2)
    line(0, 2)
    product_four(2)
    active_back(3)
    hop0(4)
    hop0(5)
    product_eight(3)
    line(3, 1)
    hidden_back(3)
    hop1(2)
    product_four(3)
    middle_back()
    hop0(6)
    hop0(7)
    attended_back()
    product_three()
    hop1(4)
    line(3, 2)
    attend_back_part(0)
    line(7, 1)
    hop1(1)
    hop2(2)
    attend_back_part(1)
    hop0(8)
    for i in range(3, F):
        line(0, i)
    hop2(1)
    attend_back_part(2)
    hop1(5)
    hop1(6)
    for i in range(3, F):
        line(3, i)
    line(7, 2)
    hop1(8)
    attend_back_part(3)
    pairs_arrive()
    hop2(5)
    product_first(0)
    hop1(0)
    for i in range(3, F):
        line(7, i)
    hop1(3)
    hop2(4)
    hop0(9)
    product_first(1)
    hop3(5)
    hop0(10)
    hop3(1)
    hop2(8)
    product_first(2)
    first_back(0)
    hop1(9)
    first_back(1)
    first_back(2)
    hop2(6)
    hop0(11)
    input_back()
    hop1(10)
    small_start()
    small_send()
    hop3(2)
    hop2(9)
    small_plane()
    hop3(6)
    hop3(4)
    hop2(10)
    hop1(11)
    hop1(7)
    small_share_start()
    back_start(1)
    hop3(3)
    hop3(9)
    cond_start()
    hop3(0)
    hop2(11)
    cond_plane()
    hop3(7)
    hop3(8)
    hop3(10)
    hop3(11)

    swap_da(at.c).wait_send()
    for p in (2, 3):
        for n in range(3):
            pair_to(p, n, at.c).wait_send()
    for r in range(K):
        if r >= K - 2:
            c_copy(r).wait_send()
        if r in finals[-2:]:
            out_done(r)
        for i in range(1, G):
            out_from(r, i).wait_recv()
        b_copy(r, at.sb, 0).wait_send()
        b_copy(r, sd, 1).wait_send()
        a_copy(r).wait_send()
        for i in range(F - 1 if r in LINED else 0):
            line_sends(r, i, lambda copy: copy.wait_send())
        for i in range(1, 0 if r in LINED else F):
            z_to(r, i).wait_send()
    back_finish(0)
    back_finish(1)
    for i in range(1, lines):
        small_to(i).wait_send()
    for n, s in enumerate(plane):
        small_across(n, at.s, s).wait_send()
    small_share(at.c).wait_send()
    loop(2 * F - 1, lambda i: cond_to(i + 1).wait_send())
    for n, s in enumerate(plane):
        cond_across(n, at.s, s).wait_send()
        cond_across(n, s, s).wait_recv()
    cond_own.wait()


def backward(sizes, *arrays):
    S, F, G = sizes
    bank, tok = arrays[0], arrays[3]
    K, _, _, _, half, width = bank.shape
    tokens = tok.shape[0]
    quarter, part, length = tokens // 2, width // 2, 2 * tokens
    count = S * F * G
    low = lambda *shape: pltpu.VMEM(shape, BF16)
    high = lambda *shape: pltpu.VMEM(shape, F32)
    specs = [ANY] * len(arrays)
    specs[2] = specs[-1] = VMEM
    return pl.pallas_call(
        functools.partial(backward_kernel, sizes),
        out_shape=(
            jax.ShapeDtypeStruct((G // 2, K, 2, half, width), F32),
            jax.ShapeDtypeStruct((S, F, G // 2, 16, width), BF16),
            jax.ShapeDtypeStruct((S, 2 * F, 8, 128), F32),
            jax.ShapeDtypeStruct((2, quarter, width), BF16),
            jax.ShapeDtypeStruct((2, quarter, width), BF16),
        ),
        in_specs=specs,
        out_specs=(ANY,) * 5,
        scratch_shapes=[
            low(K, S, F, half, width),
            low(2, S, F, half, width),
            low(RING, S, F, half, width),
            low(K - len(LINED), 2, F, half, width),
            low(K - len(LINED), F, half, width),
            low(K - len(LINED), F - 1, half, width),
            low(len(LINED), F + 1, S, half, width),
            low(len(LINED), 2, half, width),
            low(len(LINED), half, width),
            high(2, half, width),
            low(2, S, F, 2, half, width),
            low(tokens, width),
            low(tokens, width),
            high(tokens, width),
            high(tokens, width),
            low(tokens, width),
            low(tokens, width),
            low(tokens, width),
            high(tokens, width),
            low(tokens, width),
            low(tokens, part),
            low(length, part),
            low(2, 4, length, 2 * HD),
            high(2, length, 2 * HD),
            low(2, 3, length, 2 * HD),
            low(3, tokens, width),
            high(14, 8, width),
            high(16, width),
            high(16, width),
            high(16, width),
            low(16, width),
            low(S, F, 16, width),
            high(S * F, 128),
            high(2 * F, 8, 128),
            DMA((K,)),
            DMA((K,)),
            DMA((K, 2)),
            DMA((K, 2)),
            DMA((K,)),
            DMA((K,)),
            DMA((K, F)),
            DMA((K, F)),
            DMA((len(LINED), 2, F)),
            DMA((len(LINED), 2, F)),
            DMA((K,)),
            DMA((K, G)),
            DMA((K, G)),
            pltpu.SemaphoreType.REGULAR,
            DMA,
            DMA,
            DMA((count // 2,)),
            DMA((count // 2,)),
            DMA,
            DMA((3,)),
            DMA((3,)),
            DMA,
            DMA,
            DMA((2 * F,)),
            DMA((2 * F,)),
            DMA((2,)),
            DMA((3,)),
            DMA((3,)),
            DMA((2, 2)),
            DMA((2, 2)),
            DMA((2,)),
            DMA((20,)),
            DMA,
            DMA,
            DMA((4, 3)),
            DMA((4, 3)),
        ],
        compiler_params=params(3, 63),
        name="backward",
    )(*arrays)


def per_device(
    sizes,
    latents,
    conditioning,
    cotangent,
    owner_list,
    master,
    moment_one,
    moment_two,
    biases,
    bias_moment_one,
    bias_moment_two,
):
    S, F, G = sizes
    rows, width = master.shape[1:]
    half = rows // 2
    s, f, g = lax.axis_index("seq"), lax.axis_index("fsdp"), lax.axis_index("grp")
    core = g % 2

    picked = pick_blocks(master, owner_list)
    cond_rows = conditioning.reshape(2 * width // 128, 128)
    saved = forward(sizes, picked, cond_rows, latents[:, 0], cotangent[:, 0], biases)
    saved = (saved[0], saved[1].reshape(-1, width)) + tuple(saved[2:])
    silu = jax.nn.silu(lax.dynamic_index_in_dim(conditioning, s // 2, 0, keepdims=False))
    silu = jnp.where(core == s % 2, silu.astype(BF16).astype(F32), 0.0)
    silu = jnp.pad(silu, ((0, 7), (0, 0)))
    reduced, smalls, cond_all, out_lat, in_lat = backward(sizes, *saved, silu)

    linear_grads = jnp.sum(reduced, axis=0, keepdims=True) if G > 2 else reduced
    (
        new_master, new_one, new_two, new_copies, new_biases, new_bias_one, new_bias_two, output, input_grad,
    ) = adam_slots(
        sizes, owner_list, master, linear_grads, smalls.reshape(-1, width), moment_one, moment_two,
        biases, bias_moment_one, bias_moment_two, out_lat, in_lat,
    )

    first = (f % 2) * 4 + core * 2
    cond_mine = lax.dynamic_slice_in_dim(cond_all, first, 2, 2).reshape(S * F * 2, 2, 128)
    cond_mine = cond_mine.reshape(S * F * 2, 2, 128 // half, half).sum(axis=2)
    cond_mine = cond_mine.transpose(1, 0, 2).reshape(2, width)
    _, silu_pull = jax.vjp(jax.nn.silu, conditioning)
    cond_grad = silu_pull(cond_mine[:, None])[0]

    return (
        output[:, None],
        input_grad[:, None],
        cond_grad,
        new_master,
        new_one,
        new_two,
        new_copies,
        new_biases,
        new_bias_one,
        new_bias_two,
    )


def solution(mesh):
    sizes = (mesh.shape["seq"], mesh.shape["fsdp"], mesh.shape["grp"])
    tokens = P(None, ("fsdp", "grp"), "seq", None)
    vector = P(None, ("fsdp", "grp"), None)
    slots = P("grp", ("seq", "fsdp"), None)
    in_specs = (tokens, vector, tokens, P(), slots, slots, slots, P(), P(), P())
    out_specs = (tokens, tokens, vector, slots, slots, slots, slots, P(), P(), P())
    return jax.shard_map(
        functools.partial(per_device, sizes),
        mesh=mesh,
        in_specs=in_specs,
        out_specs=out_specs,
        check_vma=False,
    )
```

```python
import functools
import math

import jax
import jax.numpy as jnp
from jax import lax
from jax.experimental import pallas as pl
from jax.experimental.pallas import tpu as pltpu
from jax.sharding import PartitionSpec as P

HD = 64
STEP = 5
EPS_NORM = 1e-06
BETA_ONE = 0.5
BETA_TWO = 0.5
RATE_WEIGHT = 0.03
RATE_BIAS = 0.1
DECAY = 0.1
ADAM_EPS = 1e-08

MESH = pl.DeviceIdType.MESH
ANY = pl.BlockSpec(memory_space=pl.ANY)
VMEM = pl.BlockSpec(memory_space=pltpu.VMEM)
F32 = jnp.float32
BF16 = jnp.bfloat16
DMA = pltpu.SemaphoreType.DMA
LINEAR = 12
LATE = 2


def params(cid, vmem=48):
    return pltpu.CompilerParams(
        collective_id=cid, has_side_effects=True, vmem_limit_bytes=vmem * 1024 * 1024
    )


def remote(src, dst, send_sem, recv_sem, device):
    return pltpu.make_async_remote_copy(
        src_ref=src,
        dst_ref=dst,
        send_sem=send_sem,
        recv_sem=recv_sem,
        device_id=device,
        device_id_type=MESH,
    )


class Place:
    def __init__(self, sizes):
        self.S, self.F, self.G = sizes
        self.s = lax.axis_index("seq")
        self.f = lax.axis_index("fsdp")
        self.g = lax.axis_index("grp")
        self.c = lax.rem(self.g, 2)
        self.base = self.g - self.c
        self.sib = self.base + 1 - self.c
        odd = lax.rem(self.s, 2)
        self.sx = self.s + 1 - 2 * odd
        self.sy = lax.rem(self.s + 2, 4)
        self.sa = self.sx + self.c * (self.sy - self.sx)
        self.sb = self.sy + self.c * (self.sx - self.sy)

    def sibling(self):
        return (self.s, self.f, self.sib)


def pick_kernel(owner_ref, master_ref, out_ref, buf, low, sems, out_sems):
    blocks = out_ref.shape[0]
    group = lax.axis_index("grp")
    slots, mine, before = [], [], jnp.int32(0)
    for b in range(blocks):
        own = owner_ref[b] == group
        mine.append(own)
        slots.append(jnp.where(own, before, 0))
        before = before + jnp.where(own, 1, 0)

    def fetch(b):
        return pltpu.make_async_copy(master_ref.at[slots[b]], buf.at[b], sems.at[b])

    for b in range(blocks):
        fetch(b).start()
    for b in range(blocks):
        fetch(b).wait()
        low[b] = jnp.where(mine[b], buf[b], 0.0).astype(BF16)
        pltpu.make_async_copy(low.at[b], out_ref.at[b], out_sems.at[b]).start()
    for b in range(blocks):
        pltpu.make_async_copy(low.at[b], out_ref.at[b], out_sems.at[b]).wait()


def pick_blocks(master, owner_list):
    blocks = owner_list.shape[0]
    rows, width = master.shape[1:]
    return pl.pallas_call(
        pick_kernel,
        out_shape=jax.ShapeDtypeStruct((blocks, rows, width), BF16),
        in_specs=[pl.BlockSpec(memory_space=pltpu.SMEM), ANY],
        out_specs=ANY,
        scratch_shapes=[
            pltpu.VMEM((blocks, rows, width), F32),
            pltpu.VMEM((blocks, rows, width), BF16),
            DMA((blocks,)),
            DMA((blocks,)),
        ],
        compiler_params=pltpu.CompilerParams(vmem_limit_bytes=62 * 1024 * 1024),
        name="pick_blocks",
    )(owner_list, master)


def adam_step(param, grad, one, two, rate):
    next_one = BETA_ONE * one + (1.0 - BETA_ONE) * grad
    next_two = BETA_TWO * two + (1.0 - BETA_TWO) * grad * grad
    fix_one = 1.0 - BETA_ONE**STEP
    fix_two = 1.0 - BETA_TWO**STEP
    update = next_one * (1.0 / fix_one) / (jnp.sqrt(next_two * (1.0 / fix_two)) + ADAM_EPS)
    return (param - rate * (update + DECAY * param), next_one, next_two)


def adam_kernel(
    sizes, owner_ref, master, linear, smalls, one, two, bias, bias_one, bias_two, out_lat, in_lat,
    o_master, o_one, o_two, o_copy, o_bias, o_bias_one, o_bias_two, o_out, o_in,
    block_ref, params_v, grads_v, one_v, two_v, copy_v, out_v, low_v, high_v, in_sem, out_sem, lat_sem,
):
    S, F, G = sizes
    slots, rows, width = master.shape
    half = rows // 2
    biases = bias.shape[0]
    out_copy = pltpu.make_async_copy(out_lat, out_v, lat_sem.at[0])
    out_put = pltpu.make_async_copy(out_v, o_out, lat_sem.at[3])
    low_copy = pltpu.make_async_copy(in_lat, low_v, lat_sem.at[1])
    high_copy = pltpu.make_async_copy(high_v, o_in, lat_sem.at[2])

    group = lax.axis_index("grp")
    for j in range(slots):
        block_ref[j] = 0
    held = jnp.int32(0)
    for b in range(owner_ref.shape[0]):
        own = owner_ref[b] == group

        @pl.when(own)
        def _(b=b, held=held):
            block_ref[held] = b

        held = held + jnp.where(own, 1, 0)

    def fetch(j):
        return [
            pltpu.make_async_copy(src.at[j], dst.at[j], in_sem.at[j, n])
            for n, (src, dst) in enumerate(((master, params_v), (one, one_v), (two, two_v)))
        ]

    def fetch_grad(j):
        block = jnp.minimum(block_ref[j], LINEAR - 1)
        return pltpu.make_async_copy(linear.at[0, block], grads_v.at[j], in_sem.at[j, 3])

    def put(j):
        return [
            pltpu.make_async_copy(src.at[j], dst.at[j], out_sem.at[j, n])
            for n, (src, dst) in enumerate(
                ((params_v, o_master), (one_v, o_one), (two_v, o_two), (copy_v, o_copy))
            )
        ]

    def start(j):
        for copy in fetch(j):
            copy.start()

        @pl.when(block_ref[j] < LINEAR)
        def _():
            fetch_grad(j).start()

    loop(slots, start)
    low_copy.start()
    out_copy.start()

    table = smalls[...]
    lines = table.shape[0]
    first = (lax.axis_index("seq") * F + lax.axis_index("fsdp")) * rows
    lane, column = iota((width, rows), 0), iota((width, rows), 1)
    picked = dot(table, jnp.where(lane == first + column, 1.0, 0.0).astype(BF16)).astype(BF16)
    line, source = iota((lines, lines), 0), iota((lines, lines), 1)
    silu = dot(jnp.where(source == line - lax.rem(line, 16) + 14, 1.0, 0.0).astype(BF16), picked)
    kind = lax.rem(iota((lines, rows), 0), 16)

    line, source = iota((16, lines), 0), lax.rem(iota((16, lines), 1), 16)
    wanted = jnp.where(line < biases - 6, line + 6, line - (biases - 6))
    total = dot(jnp.where(source == wanted, 1.0, 0.0).astype(BF16), table)[0:biases]
    o_bias[...], o_bias_one[...], o_bias_two[...] = adam_step(
        bias[...], total, bias_one[...], bias_two[...], RATE_BIAS
    )

    def update(j):
        for copy in fetch(j):
            copy.wait()
        block = block_ref[j]

        @pl.when(block < LINEAR)
        def _():
            fetch_grad(j).wait()

        @pl.when(block >= LINEAR)
        def _():
            chosen = jnp.where(kind == block - LINEAR, silu, 0.0).astype(BF16)
            grads_v[j] = dot(chosen, table, TN).reshape(2, half, width)

        live = j < held
        for n in range(2):
            at = (j, pl.ds(n * half, half))
            param, one_old, two_old = params_v[at], one_v[at], two_v[at]
            stepped, next_one, next_two = adam_step(
                param, grads_v[j, n], one_old, two_old, RATE_WEIGHT
            )
            new = jnp.where(live, stepped, param)
            params_v[at] = new
            one_v[at] = jnp.where(live, next_one, one_old)
            two_v[at] = jnp.where(live, next_two, two_old)
            copy_v[at] = new.astype(BF16)
        for copy in put(j):
            copy.start()

    loop(slots, update)

    out_copy.wait()
    out_put.start()
    low_copy.wait()
    high_v[...] = low_v[...].astype(F32)
    high_copy.start()

    def finish(j):
        for copy in put(j):
            copy.wait()

    loop(slots, finish)
    out_put.wait()
    high_copy.wait()


def adam_slots(
    sizes, owner_list, master, linear, smalls, one, two, bias, bias_one, bias_two, out_lat, in_lat
):
    slots, rows, width = master.shape
    shape = jax.ShapeDtypeStruct(master.shape, F32)
    bias_shape = jax.ShapeDtypeStruct(bias.shape, F32)
    return pl.pallas_call(
        functools.partial(adam_kernel, sizes),
        out_shape=(shape, shape, shape, jax.ShapeDtypeStruct(master.shape, BF16))
        + (bias_shape,) * 3
        + (jax.ShapeDtypeStruct(out_lat.shape, BF16), jax.ShapeDtypeStruct(in_lat.shape, F32)),
        in_specs=[pl.BlockSpec(memory_space=pltpu.SMEM), ANY, ANY, VMEM, ANY, ANY]
        + [VMEM] * 3
        + [ANY] * 2,
        out_specs=(ANY,) * 4 + (VMEM,) * 3 + (ANY,) * 2,
        scratch_shapes=[
            pltpu.SMEM((slots,), jnp.int32),
            pltpu.VMEM(master.shape, F32),
            pltpu.VMEM((slots, 2, rows // 2, width), F32),
            pltpu.VMEM(master.shape, F32),
            pltpu.VMEM(master.shape, F32),
            pltpu.VMEM(master.shape, BF16),
            pltpu.VMEM(out_lat.shape, BF16),
            pltpu.VMEM(in_lat.shape, BF16),
            pltpu.VMEM(in_lat.shape, F32),
            DMA((slots, 4)),
            DMA((slots, 4)),
            DMA((4,)),
        ],
        compiler_params=pltpu.CompilerParams(vmem_limit_bytes=62 * 1024 * 1024),
        name="adam_slots",
    )(owner_list, master, linear, smalls, one, two, bias, bias_one, bias_two, out_lat, in_lat)


ROWS = 256
CHUNK = 128
NT = (((1,), (1,)), ((), ()))
NN = (((1,), (0,)), ((), ()))
TN = (((0,), (0,)), ((), ()))


def dot(left, right, dims=NN):
    return lax.dot_general(left, right, dims, preferred_element_type=F32)


def loop(count, body):
    def one(i, carry):
        body(i)
        return carry

    lax.fori_loop(0, count, one, 0)


def aligned(index, size):
    return pl.ds(pl.multiple_of(index * size, size), size)


def norm_rows(values):
    centre = jnp.mean(values, axis=-1, keepdims=True)
    centred = values - centre
    spread = jnp.mean(centred * centred, axis=-1, keepdims=True)
    inverse = lax.rsqrt(spread + EPS_NORM)
    return centred * inverse, inverse


def iota(shape, dim):
    return lax.broadcasted_iota(jnp.int32, shape, dim)


def attend_pair(q_ref, k_ref, v_ref, a_ref, lse_ref, pair):
    length = q_ref.shape[0]
    factor = 1.0 / math.sqrt(HD)
    for h in range(2):
        cols = slice((2 * pair + h) * HD, (2 * pair + h + 1) * HD)
        key = k_ref[:, cols]
        value = v_ref[:, cols]
        for r in range(0, length, ROWS):
            rows = slice(r, r + ROWS)
            scores = dot(q_ref[rows, cols], key, NT)
            high = jnp.max(scores, axis=1, keepdims=True)
            weights = jnp.exp((scores - high) * factor)
            total = jnp.sum(weights, axis=1, keepdims=True)
            out = dot(weights.astype(BF16), value, NN) / total
            a_ref[rows, cols] = out.astype(BF16)
            lse_ref[rows, cols] = jnp.broadcast_to(high * factor + jnp.log(total), (ROWS, HD))


def forward_kernel(sizes, *refs):
    (
        picked, cond, lat, cot, bias,
        bank_o, modw_o, mod_o, tok_o, ctok, hid_o, heads_o, head_a_o, lse_o, att_o, branch_o, mid_o, hid2_o, up_o, act_o, mlp_o, res_o,
        shard, theirs, conds, msg, modg, modr, modh, mod, bank, xv, hid, stage, heads, head_a, lse, att, mid, hid2, up, act, mlp,
        gs, gr, gl, ds, dr, dl, zs, zr, as_, ar, bs, br, cs, cr,
        las, lar, lbs, lbr, lzs, lzr, lcs, lcr, ms, mr, hs, hr, ts, tr, tl, xs, xr, save_sem,
    ) = refs
    at = Place(sizes)
    S, F, G = sizes
    K = bank.shape[0]
    half = shard.shape[1]
    blocks = picked.shape[0]
    T = 2 * S * F
    me = (at.s * F + at.f) * 2 + at.c
    quarter = lat.shape[1]
    tokens, width = xv.shape
    part = width // 2
    pieces = width // 128

    def device_of(i):
        n = lax.rem(me + i, T)
        return (lax.div(n, 2 * F), lax.rem(lax.div(n, 2), F), at.base + lax.rem(n, 2))

    bar = pltpu.get_barrier_semaphore()

    def greet(device):
        pl.semaphore_signal(bar, inc=1, device_id=device, device_id_type=MESH)

    loop(T - 1, lambda i: greet(device_of(i + 1)))
    for i in range(2, G):
        greet((at.s, at.f, lax.rem(at.base + i, G)))
    pl.semaphore_wait(bar, T - 1 + G - 2)

    def tok_move(j):
        return (2 * j + at.c, at.f, at.base + lax.div(at.s, 2))

    def tok_refs(which):
        return ((lat, xv), (cot, ctok))[which]

    def tok_to(j, which):
        src, dst = tok_refs(which)
        place = aligned(lax.rem(at.s, 2), quarter)
        return remote(
            src.at[j], dst.at[place], ts.at[which, j], tr.at[which, lax.rem(at.s, 2)], tok_move(j)
        )

    def tok_from(j, which):
        src, dst = tok_refs(which)
        place = pl.ds(j * quarter, quarter)
        return remote(src.at[0], dst.at[place], ts.at[which, j], tr.at[which, j], tok_move(j))

    def tok_local(j, which):
        src, dst = tok_refs(which)
        return pltpu.make_async_copy(src.at[j], dst.at[aligned(lax.rem(at.s, 2), quarter)], tl.at[which])

    def stays(j):
        return (2 * j + at.c == at.s) & (lax.div(at.s, 2) == at.c)

    def comes(j):
        return jnp.logical_not((2 * at.c + j == at.s) & (lax.rem(at.s, 2) == at.c))

    def tok_start(which):
        for j in range(2):
            if which == 0:
                @pl.when(stays(j))
                def _():
                    tok_local(j, 0).start()
                    tok_local(j, 1).start()

            @pl.when(jnp.logical_not(stays(j)))
            def _():
                tok_to(j, which).start()

    def tok_finish(which):
        for j in range(2):
            @pl.when(stays(j))
            def _():
                tok_local(j, which).wait()

            @pl.when(jnp.logical_not(stays(j)))
            def _():
                tok_to(j, which).wait_send()

            @pl.when(comes(j))
            def _():
                tok_from(j, which).wait_recv()

    def rows_of(core):
        return picked.at[:, aligned(core, half)]

    def group_to(i):
        g = lax.rem(at.g + i, G)
        return remote(
            rows_of(lax.rem(g, 2)), theirs.at[G - 1 - i], gs.at[i], gr.at[G - 1 - i], (at.s, at.f, g)
        )

    def group_from(j):
        return remote(rows_of(0), theirs.at[j], gs.at[0], gr.at[j], at.sibling())

    group_own = pltpu.make_async_copy(rows_of(at.c), shard.at[0:blocks], gl)

    def cond_number(i):
        return lax.rem(at.f * 2 + at.c + i, 2 * F)

    def cond_to(i):
        n = cond_number(i)
        device = (at.s, lax.div(n, 2), at.base + lax.rem(n, 2))
        return remote(cond, conds.at[cond_number(0)], ds.at[i], dr.at[cond_number(0)], device)

    def cond_from(i):
        n = cond_number(i)
        return remote(cond, conds.at[n], ds.at[i], dr.at[n], at.sibling())

    cond_own = pltpu.make_async_copy(cond, conds.at[cond_number(0)], dl)

    here = at.s * F + at.f
    takes = lax.rem(at.s, 2) == at.c

    mod_give = remote(msg.at[:, 1 - at.c, :, 0:6], modg, hs.at[0], hr.at[0], at.sibling())

    def mod_to(i):
        n = lax.rem(lax.div(at.s, 2) * F + at.f + i, 2 * F)
        m, f = lax.div(n, F), lax.rem(n, F)
        return remote(
            msg.at[m, at.c, f, 0:6], modr.at[here], ms.at[i], mr.at[here], (2 * m + at.c, f, at.g)
        )

    def mod_from(i):
        n = lax.rem(here + i, S * F)
        return remote(msg.at[0, 0, 0, 0:6], modr.at[n], ms.at[0], mr.at[n], at.sibling())

    mod_swap = remote(modh, modh, hs.at[1], hr.at[1], at.sibling())

    def z_to(k, i):
        f = lax.rem(at.f + i, F)
        return remote(
            shard.at[k], bank.at[k, at.s, at.f, at.c], zs.at[k, i], zr.at[k, i], (at.s, f, at.g)
        )

    def z_from(k, i):
        f = lax.rem(at.f + F - i, F)
        return remote(shard.at[k], bank.at[k, at.s, f, at.c], zs.at[k, i], zr.at[k, i], (at.s, f, at.g))

    def a_copy(k, s):
        line = bank.at[k, s, :, at.c]
        return remote(line, line, as_.at[k], ar.at[k], (at.sa, at.f, at.g))

    def b_copy(k, s, n):
        line = bank.at[k, s, :, at.c]
        return remote(line, line, bs.at[k, n], br.at[k, n], (at.sb, at.f, at.g))

    sd = S - 1 - at.s

    def c_copy(k, s, n, core):
        line = bank.at[k, s, :, core]
        return remote(line, line, cs.at[k, n], cr.at[k, n], at.sibling())

    def z_start(k):
        for i in range(1, F):
            z_to(k, i).start()
        bank[k, at.s, at.f, at.c] = shard[k]

    late = K - LATE

    def late_a(n):
        piece = bank.at[late + n, at.s, at.f, at.c]
        return remote(piece, piece, las.at[n], lar.at[n], (at.sa, at.f, at.g))

    def late_a_from(n):
        piece = bank.at[late + n, at.sa, at.f, at.c]
        return remote(piece, piece, las.at[n], lar.at[n], (at.sa, at.f, at.g))

    def late_b(n, s, i):
        piece = bank.at[late + n, s, at.f, at.c]
        return remote(piece, piece, lbs.at[n, i], lbr.at[n, i], (at.sb, at.f, at.g))

    def late_line(n, way, j, f):
        line = bank.at[late + n, :, f, at.c]
        to = jnp.clip(at.f + 1 - 2 * way, 0, F - 1)
        return remote(line, line, lzs.at[n, way, j], lzr.at[n, way, j], (at.s, to, at.g))

    def late_c(n, f, core):
        line = bank.at[late + n, :, f, core]
        return remote(line, line, lcs.at[n, f], lcr.at[n, f], at.sibling())

    def late_first(n):
        bank[late + n, at.s, at.f, at.c] = shard[late + n]
        late_a(n).start()

    def late_second(n):
        late_a_from(n).wait_recv()
        late_b(n, at.s, 0).start()
        late_b(n, at.sa, 1).start()

    def late_sends(n, j, act):
        up, down = at.f - j, at.f + j

        @pl.when((up >= 0) & (at.f < F - 1))
        def _():
            act(late_line(n, 0, j, up))

        @pl.when((down < F) & (at.f > 0))
        def _():
            act(late_line(n, 1, j, down))

    def late_round(n, j):
        if j == 0:
            late_b(n, at.sb, 0).wait_recv()
            late_b(n, sd, 1).wait_recv()
            late_sends(n, 0, lambda copy: copy.start())
            late_c(n, at.f, at.c).start()
            return
        up, down = at.f - j, at.f + j

        @pl.when(up >= 0)
        def _():
            late_line(n, 0, j - 1, up).wait_recv()

        @pl.when(down < F)
        def _():
            late_line(n, 1, j - 1, down).wait_recv()

        if j < F - 1:
            late_sends(n, j, lambda copy: copy.start())

        @pl.when(up >= 0)
        def _():
            late_c(n, up, at.c).start()

        @pl.when(down < F)
        def _():
            late_c(n, down, at.c).start()

    def step_a(k):
        for i in range(1, F):
            z_from(k, i).wait_recv()
        a_copy(k, at.s).start()
        c_copy(k, at.s, 0, at.c).start()

    def step_b(k):
        a_copy(k, at.sa).wait_recv()
        b_copy(k, at.s, 0).start()
        b_copy(k, at.sa, 1).start()
        c_copy(k, at.sa, 1, at.c).start()

    def step_c(k):
        b_copy(k, at.sb, 0).wait_recv()
        c_copy(k, at.sb, 2, at.c).start()
        b_copy(k, sd, 1).wait_recv()
        c_copy(k, sd, 3, at.c).start()

    saves = []

    def save(src, dst):
        copy = pltpu.make_async_copy(src, dst, save_sem.at[len(saves)])
        copy.start()
        saves.append(copy)
        return len(saves) - 1

    waited = set()

    def saved(n):
        if n not in waited:
            saves[n].wait()
            waited.add(n)

    def arrive(k):
        if k < late:
            for n, s in enumerate((at.s, at.sb, at.sa, sd)):
                c_copy(k, s, n, 1 - at.c).wait_recv()
        else:
            for f in range(F):
                late_c(k - late, f, 1 - at.c).wait_recv()
        save(bank.at[k], bank_o.at[k])

    def weights(k):
        return bank[k].reshape(width, width)

    def gather_rows():
        group_own.wait()
        for i in range(1, G):
            group_from(i - 1).wait_recv()

        def one(b):
            value = shard[b].astype(F32)
            for i in range(G - 1):
                value = value + theirs[i, b].astype(F32)
            shard[b] = value.astype(BF16)

        loop(blocks, one)
        shard[blocks:] = jnp.zeros_like(shard[blocks:])

    def modulation_parts():
        cond_own.wait()
        loop(2 * F - 1, lambda i: cond_from(i + 1).wait_recv())
        value = conds[...].reshape(2 * F * 2 * pieces, 128)
        silu = (value / (1.0 + jnp.exp(-value))).astype(BF16)
        parts = 8 * half
        first = here * 2 * half + at.c * half
        lane, column = iota((128, parts), 0), iota((128, parts), 1)
        select = jnp.where(lane == lax.rem(first, 128) + lax.rem(column, half), 1.0, 0.0)
        rows = dot(silu, select.astype(BF16)).astype(BF16)
        count = 8 * S * F
        line, source = iota((count, rows.shape[0]), 0), iota((count, rows.shape[0]), 1)
        latent = lax.div(line, 8)
        chip, depth = lax.div(latent, F), lax.rem(latent, F)
        wanted = ((depth * 2 + lax.rem(chip, 2)) * 2 + lax.div(chip, 2)) * pieces + lax.div(first, 128)
        spread = dot(jnp.where(source == wanted, 1.0, 0.0).astype(BF16), rows)
        line, column = iota((count, parts), 0), iota((count, parts), 1)
        spread = jnp.where(lax.rem(line, 8) == lax.div(column, half), spread, 0.0).astype(BF16)
        value = dot(spread, shard[K:].reshape(parts, width))
        flat = msg.reshape(count * pieces, 128)
        for n in range(pieces):
            flat[pl.ds(n, count, stride=pieces)] = value[:, n * 128 : (n + 1) * 128]
        mod_give.start()

    def modulation_send():
        mod_give.wait()

        def add(n):
            m, f = lax.div(n, F), lax.rem(n, F)
            msg[m, at.c, f, 0:6] = msg[m, at.c, f, 0:6] + modg[m, f]

        loop(2 * F, add)

        @pl.when(jnp.logical_not(takes))
        def _():
            mod_to(0).start()

        loop(2 * F - 1, lambda i: mod_to(i + 1).start())

    def modulation():
        modulation_parts()
        save(shard.at[K:blocks], modw_o)
        modulation_send()

    def modulation_sum():
        @pl.when(takes)
        def _():
            loop(S * F - 1, lambda i: mod_from(i + 1).wait_recv())
            modr[here] = msg[lax.div(at.s, 2), at.c, at.f, 0:6]
            total = modr[0]
            for n in range(1, S * F):
                total = total + modr[n]
            modh[...] = total.reshape(6 * pieces, 128)
            mod_swap.start()

        @pl.when(jnp.logical_not(takes))
        def _():
            mod_swap.wait_recv()

        for n in range(pieces):
            cols = slice(n * 128, (n + 1) * 128)
            mod[0:6, cols] = modh[pl.ds(n, 6, stride=pieces)]
        mod[0:6] = mod[0:6] + bias[8:14]
        mod[6:8] = jnp.zeros((2, width), F32)
        save(mod, mod_o)

    def prepare():
        modulation_sum()
        tok_finish(0)
        save(xv, tok_o)

        def one(i):
            rows = aligned(i, CHUNK)
            scaled, _ = norm_rows(xv[rows].astype(F32))
            hid[rows] = (scaled * (1.0 + mod[1:2]) + mod[0:1]).astype(BF16)

        loop(tokens // CHUNK, one)
        hid_saved.append(save(hid, hid_o))

    hid_saved = []

    def swap(n):
        return remote(
            stage.at[n], heads.at[n, aligned(at.c, tokens)], xs.at[n], xr.at[n], at.sibling()
        )

    def swap_from(n):
        return remote(
            stage.at[n], heads.at[n, aligned(1 - at.c, tokens)], xs.at[n], xr.at[n], at.sibling()
        )

    def project(n):
        value = dot(hid[...], weights(n))
        if n != 1:
            row = n // 2
            value = value + bias[row : row + 1]
        value = value.astype(BF16)
        first, second = value[:, :part], value[:, part:]
        stage[n] = jnp.where(at.c == 0, second, first)
        swap(n).start()
        heads[n, aligned(at.c, tokens)] = jnp.where(at.c == 0, first, second)

    def attend_part(pair):
        if pair == 0:
            for n in range(3):
                swap_from(n).wait_recv()
                save(heads.at[n], heads_o.at[n])
        attend_pair(heads.at[0], heads.at[1], heads.at[2], head_a, lse, pair)

    def give_out():
        return remote(
            head_a.at[aligned(1 - at.c, tokens)], att.at[:, aligned(at.c, part)], xs.at[3], xr.at[3], at.sibling()
        )

    def give_from():
        return remote(
            head_a.at[aligned(at.c, tokens)], att.at[:, aligned(1 - at.c, part)], xs.at[3], xr.at[3], at.sibling()
        )

    def send_attended():
        give_out().start()
        att[:, aligned(at.c, part)] = head_a[aligned(at.c, tokens)]
        save(head_a, head_a_o)
        save(lse, lse_o)

    branch_saved = []

    def output_projection():
        give_from().wait_recv()
        save(att, att_o)
        mlp[...] = dot(att[...], weights(3)) + bias[2:3]
        branch_saved.append(save(mlp, branch_o))

        def rest(i):
            rows = aligned(i, CHUNK)
            middle = xv[rows].astype(F32) + mod[2:3] * mlp[rows]
            mid[rows] = middle
            scaled, _ = norm_rows(middle)
            hid2[rows] = (scaled * (1.0 + mod[4:5]) + mod[3:4]).astype(BF16)

        loop(tokens // CHUNK, rest)
        save(mid, mid_o)
        save(hid2, hid2_o)

    up_saved = []

    def upper(j):
        if j >= 2:
            saved(up_saved[j - 2])
        value = dot(hid2[...], weights(4 + j)) + bias[3 + j : 4 + j]
        up[j % 2] = value
        act[j] = jax.nn.gelu(value, approximate=True).astype(BF16)
        up_saved.append(save(up.at[j % 2], up_o.at[j]))
        save(act.at[j], act_o.at[j])

    def lower(j):
        if j == 0:
            saved(branch_saved[0])
        value = dot(act[j], weights(8 + j))
        mlp[...] = value + (bias[7:8] if j == 0 else mlp[...])

    def finish_forward():
        save(mlp, mlp_o)
        saved(hid_saved[0])

        def one(i):
            rows = aligned(i, CHUNK)
            hid[rows] = (mid[rows] + mod[5:6] * mlp[rows]).astype(BF16)

        loop(tokens // CHUNK, one)
        save(hid, res_o)

    tok_start(0)
    for i in range(1, G):
        group_to(i).start()
    group_own.start()
    cond_own.start()
    loop(2 * F - 1, lambda i: cond_to(i + 1).start())
    gather_rows()
    z_start(0)
    z_start(1)
    step_a(0)
    z_start(2)
    modulation()
    step_b(0)
    z_start(3)
    late_first(0)
    z_start(4)
    z_start(5)
    step_a(1)
    step_a(2)
    z_start(6)
    step_b(1)
    late_first(1)
    step_c(0)
    step_b(2)
    late_second(0)
    step_c(1)
    step_a(3)
    step_a(4)
    arrive(1)
    prepare()
    step_c(2)
    arrive(0)
    step_a(5)
    step_b(3)
    project(0)
    z_start(7)
    step_a(6)
    late_round(0, 0)
    late_second(1)
    step_b(4)
    z_start(8)
    step_c(3)
    z_start(9)
    arrive(2)
    project(1)
    step_a(7)
    step_b(5)
    late_round(1, 0)
    project(2)
    step_a(8)
    step_b(6)
    arrive(3)
    late_round(0, 1)
    attend_part(0)
    step_c(4)
    step_a(9)
    attend_part(1)
    step_b(7)
    late_round(1, 1)
    step_c(5)
    attend_part(2)
    step_b(8)
    attend_part(3)
    arrive(5)
    late_round(0, 2)
    step_c(6)
    send_attended()
    step_b(9)
    late_round(1, 2)
    step_c(7)
    arrive(4)
    output_projection()
    upper(0)
    arrive(6)
    step_c(8)
    for j in range(3, F):
        late_round(0, j)
    upper(1)
    tok_start(1)
    arrive(7)
    upper(2)
    for j in range(3, F):
        late_round(1, j)
    upper(3)
    arrive(8)
    step_c(9)
    arrive(11)
    arrive(10)
    lower(0)
    arrive(9)
    lower(1)
    lower(2)
    lower(3)
    finish_forward()

    def finish(k):
        for i in range(1, F):
            z_to(k, i).wait_send()
        a_copy(k, at.s).wait_send()
        b_copy(k, at.s, 0).wait_send()
        b_copy(k, at.sa, 1).wait_send()
        for n, s in enumerate((at.s, at.sa, at.sb, sd)):
            c_copy(k, s, n, at.c).wait_send()

    loop(late, finish)
    for n in range(LATE):
        late_a(n).wait_send()
        late_b(n, at.s, 0).wait_send()
        late_b(n, at.sa, 1).wait_send()
        for j in range(F - 1):
            late_sends(n, j, lambda copy: copy.wait_send())
        for f in range(F):
            late_c(n, f, at.c).wait_send()
    for i in range(1, G):
        group_to(i).wait_send()
    loop(2 * F - 1, lambda i: cond_to(i + 1).wait_send())
    loop(2 * F - 1, lambda i: mod_to(i + 1).wait_send())

    @pl.when(takes)
    def _():
        mod_swap.wait_send()

    @pl.when(jnp.logical_not(takes))
    def _():
        mod_to(0).wait_send()

    for n in range(3):
        swap(n).wait_send()
    give_out().wait_send()
    for n in range(len(saves)):
        saved(n)
    tok_finish(1)


def forward(sizes, picked, cond, lat, cot, bias):
    S, F, G = sizes
    blocks, rows, width = picked.shape
    K, half, T = LINEAR, rows // 2, 2 * S * F
    tokens = 2 * lat.shape[1]
    length, part = 2 * tokens, width // 2
    low = lambda *shape: (shape, BF16)
    high = lambda *shape: (shape, F32)
    outs = (
        low(K, S, F, 2, half, width),
        low(blocks - K, half, width),
        high(8, width),
        low(tokens, width),
        low(tokens, width),
        low(tokens, width),
        low(3, length, part),
        low(length, part),
        high(length, part),
        low(tokens, width),
        high(tokens, width),
        high(tokens, width),
        low(tokens, width),
        high(4, tokens, width),
        low(4, tokens, width),
        high(tokens, width),
        low(tokens, width),
    )
    scratch = (
        low(K + 8, half, width),
        low(G - 1, blocks, half, width),
        high(2 * F, 2 * width // 128, 128),
        high(2, 2, F, 8, width // 128, 128),
        high(2, F, 6, width // 128, 128),
        high(S * F, 6, width // 128, 128),
        high(6 * width // 128, 128),
        high(8, width),
        low(K, S, F, 2, half, width),
        low(tokens, width),
        low(tokens, width),
        low(3, tokens, part),
        low(3, length, part),
        low(length, part),
        high(length, part),
        low(tokens, width),
        high(tokens, width),
        low(tokens, width),
        high(2, tokens, width),
        low(4, tokens, width),
        high(tokens, width),
    )
    sems = (
        (G,), (G,), None, (2 * F,), (2 * F,), None, (K, F), (K, F), (K,), (K,), (K, 2), (K, 2), (K, 4), (K, 4),
        (LATE,), (LATE,), (LATE, 2), (LATE, 2), (LATE, 2, F), (LATE, 2, F), (LATE, F), (LATE, F),
        (2 * F,), (S * F,), (2,), (2,), (2, 2), (2, 2), (2,), (4,), (4,), (40,),
    )
    return pl.pallas_call(
        functools.partial(forward_kernel, sizes),
        out_shape=tuple(jax.ShapeDtypeStruct(*o) for o in outs),
        in_specs=[ANY] * 4 + [VMEM],
        out_specs=(ANY,) * len(outs),
        scratch_shapes=[pltpu.VMEM(*s) for s in scratch] + [DMA if n is None else DMA(n) for n in sems],
        compiler_params=params(2, 63),
        name="forward",
    )(picked, cond, lat, cot, bias)


RING = 4
ORDER = (8, 4, 9, 5, 10, 6, 11, 7, 3, 0, 1, 2)
LINED = (0, 3, 7)
PLAIN = tuple(r for r in range(LINEAR) if r not in LINED)


def gelu_slope(values):
    scale = 0.7978845608
    square = values * values
    bend = jnp.tanh(scale * values * (1.0 + 0.044715 * square))
    return 0.5 * (1.0 + bend) + 0.5 * values * (1.0 - bend * bend) * (
        scale * (1.0 + 3.0 * 0.044715 * square)
    )


def attend_pair_back(q, k, v, a, lse_ref, da_ref, pair, dq_ref, dk_ref, dv_ref):
    length = q.shape[0]
    factor = 1.0 / math.sqrt(HD)
    for h in range(2):
        cols = slice(h * HD, (h + 1) * HD)
        grad_cols = slice((2 * pair + h) * HD, (2 * pair + h + 1) * HD)
        key = k[:, cols]
        value = v[:, cols]
        dk = jnp.zeros((HD, length), F32)
        dv = jnp.zeros((HD, length), F32)
        for r in range(0, length, ROWS):
            rows = slice(r, r + ROWS)
            query = q[rows, cols]
            grad = da_ref[rows, grad_cols]
            lse = lse_ref[rows, h * HD : h * HD + 1]
            scores = dot(query, key, NT)
            probs = jnp.exp(scores * factor - lse)
            row_dot = jnp.sum(grad.astype(F32) * a[rows, cols].astype(F32), axis=1, keepdims=True)
            weight_grad = dot(grad, value, NT)
            score_grad = (probs * (weight_grad - row_dot)).astype(BF16)
            dq_ref[rows, cols] = (dot(score_grad, key, NN) * factor).astype(BF16)
            dk = dk + dot(query.T, score_grad, NN)
            dv = dv + dot(grad.T, probs.astype(BF16), NN)
        dk_ref[:, cols] = (dk * factor).T.astype(BF16)
        dv_ref[:, cols] = dv.T.astype(BF16)


def backward_kernel(sizes, *refs):
    (
        bank, modw, mod, tok, ctok, hid, heads, head_a, lse, att, branch, mid, hid2, up, act, mlp, res, silu,
        red, smalls, cgs, out_lat, in_lat,
        mine, give, r0, r1, r2, r3, lz, l1, l2, total, wbuf,
        ebuf, dfb, f0, f1, a0, a1, dub, dh2, h2b, stage, dah, qkva, lsev, dpair, dqt, accs, small, sv, sw, swb, smv, cg, cgl,
        cs, cr, bs, br, as_, ar, zs, zr, lzs, lzr, os_, rs, rr, free, vs, vr, ws, wr, wl, qs, qr, us, ur, ds, dr, dl, es, er, ts, tr, tl, loads, xs, xr, ps, pr,
    ) = refs
    at = Place(sizes)
    S, F, G = sizes
    K = mine.shape[0]
    half = mine.shape[3]
    tokens, width = ebuf.shape
    part = width // 2
    band = width // S
    count = S * F * G
    me = (at.s * F + at.f) * G + at.g
    quarter = out_lat.shape[1]
    sd = S - 1 - at.s
    chunks = tokens // CHUNK

    def device_of(i):
        n = lax.rem(me + i, count)
        return (lax.div(n, F * G), lax.rem(lax.div(n, G), F), lax.rem(n, G))

    bar = pltpu.get_barrier_semaphore()

    def greet(i):
        pl.semaphore_signal(bar, inc=1, device_id=device_of(i + 1), device_id_type=MESH)

    loop(count - 1, greet)

    def c_copy(r):
        return remote(give.at[r % 2], r0.at[r % RING], cs.at[r], cr.at[r], at.sibling())

    def b_copy(r, s, n):
        if r in LINED:
            src, dst = mine.at[r, s, at.f], l1.at[LINED.index(r), n]
        else:
            src, dst = mine.at[r, s], r1.at[PLAIN.index(r), n]
        return remote(src, dst, bs.at[r, n], br.at[r, n], (at.sb, at.f, at.g))

    def a_copy(r):
        if r in LINED:
            src, dst = mine.at[r, at.sa, at.f], l2.at[LINED.index(r)]
        else:
            src, dst = mine.at[r, at.sa], r2.at[PLAIN.index(r)]
        return remote(src, dst, as_.at[r], ar.at[r], (at.sa, at.f, at.g))

    def z_to(r, i):
        f = lax.rem(at.f + i, F)
        return remote(
            mine.at[r, at.s, f], r3.at[PLAIN.index(r), i - 1], zs.at[r, i], zr.at[r, i], (at.s, f, at.g)
        )

    def up_line(r, i):
        tau = F - 1 - i + at.f
        to = jnp.clip(at.f + 1, 0, F - 1)
        tau_in = jnp.clip(tau, 0, F - 1)
        return tau_in, remote(
            mine.at[r, :, tau_in], lz.at[LINED.index(r), tau_in], lzs.at[LINED.index(r), 0, i], lzr.at[LINED.index(r), 0, i], (at.s, to, at.g)
        )

    def down_line(r, i):
        tau = jnp.clip(i + at.f - F + 1, 0, F - 1)
        to = jnp.clip(at.f - 1, 0, F - 1)
        place = F if i == F - 2 else tau
        return remote(
            mine.at[r, :, tau], lz.at[LINED.index(r), place], lzs.at[LINED.index(r), 1, i], lzr.at[LINED.index(r), 1, i], (at.s, to, at.g)
        )

    def line_sends(r, i, act):
        @pl.when((at.f <= i) & (at.f < F - 1))
        def _():
            act(up_line(r, i)[1])

        @pl.when((F - 1 - at.f <= i) & (at.f > 0))
        def _():
            act(down_line(r, i))

    def add_set(r, tau, place):
        def one(s):
            mine[r, s, tau] = mine[r, s, tau] + lz[LINED.index(r), place, s]

        loop(S, one)

    def line(r, i):
        if i > 0:
            @pl.when((at.f >= 1) & (at.f <= i))
            def _():
                tau = jnp.clip(F - 1 - i + at.f, 0, F - 1)
                remote(
                    mine.at[r, :, tau], lz.at[LINED.index(r), tau], lzs.at[LINED.index(r), 0, i - 1], lzr.at[LINED.index(r), 0, i - 1], at.sibling()
                ).wait_recv()
                add_set(r, tau, tau)

            @pl.when((at.f <= F - 2) & (F - 1 - at.f <= i))
            def _():
                tau = jnp.clip(i + at.f - F + 1, 0, F - 1)
                place = F if i == F - 1 else tau
                remote(
                    mine.at[r, :, tau], lz.at[LINED.index(r), place], lzs.at[LINED.index(r), 1, i - 1], lzr.at[LINED.index(r), 1, i - 1], at.sibling()
                ).wait_recv()
                add_set(r, tau, place)

        if i < F - 1:
            line_sends(r, i, lambda copy: copy.start())
        else:
            b_copy(r, at.sb, 0).start()
            b_copy(r, sd, 1).start()

    def add_piece(r, s, src):
        mine[r, s, at.f] = mine[r, s, at.f] + src

    pair = lax.div(at.g, 2)
    finals = []

    def out_copy(r):
        return pltpu.make_async_copy(total.at[finals.index(r) % 2], red.at[pair, ORDER[r], at.c], os_.at[r])

    def out_to(r, i):
        g = lax.rem(at.g + i, G)
        return remote(
            total.at[finals.index(r) % 2], red.at[pair, ORDER[r], at.c], rs.at[r, i], rr.at[r, i], (at.s, at.f, g)
        )

    def out_from(r, i):
        g = lax.rem(at.g + G - i, G)
        return remote(
            total.at[finals.index(r) % 2], red.at[lax.div(g, 2), ORDER[r], lax.rem(g, 2)], rs.at[r, i], rr.at[r, i], at.sibling()
        )

    def out_done(r):
        out_copy(r).wait()
        for i in range(1, G):
            out_to(r, i).wait_send()

    def add_line(dst, src):
        dst[...] = dst[...] + src[...]

    def hop0(r):
        c_copy(r).wait_recv()
        loop(S, lambda s: add_line(mine.at[r, s], r0.at[r % RING, s]))
        if r + RING < K:
            pl.semaphore_signal(free, inc=1, device_id=at.sibling(), device_id_type=MESH)
        if r in LINED:
            line(r, 0)
            return
        b_copy(r, at.sb, 0).start()
        b_copy(r, sd, 1).start()

    def hop1(r):
        b_copy(r, at.sb, 0).wait_recv()
        b_copy(r, sd, 1).wait_recv()
        if r in LINED:
            add_piece(r, at.sa, l1[LINED.index(r), 1])
            a_copy(r).start()
            add_piece(r, at.s, l1[LINED.index(r), 0])
            return
        add_line(mine.at[r, at.sa], r1.at[PLAIN.index(r), 1])
        a_copy(r).start()
        add_line(mine.at[r, at.s], r1.at[PLAIN.index(r), 0])

    def hop2(r):
        if r in LINED:
            return
        a_copy(r).wait_recv()
        add_line(mine.at[r, at.s], r2.at[PLAIN.index(r)])
        for i in range(1, F):
            z_to(r, i).start()

    def hop3(r):
        if r in LINED:
            a_copy(r).wait_recv()
            others = [l2.at[LINED.index(r)]]
        else:
            for i in range(1, F):
                z_to(r, i).wait_recv()
            others = [r3.at[PLAIN.index(r), i] for i in range(F - 1)]
        finals.append(r)
        if len(finals) > 2:
            out_done(finals[-3])
        value = mine[r, at.s, at.f].astype(F32)
        for other in others:
            value = value + other[...].astype(F32)
        total[finals.index(r) % 2] = value
        out_copy(r).start()
        for i in range(1, G):
            out_to(r, i).start()

    def produce(r, left, right):
        if r >= 2:
            c_copy(r - 2).wait_send()

        lines = S // 2

        def one(n):
            value = dot(left[:, aligned(n, lines * band)], right[...], TN)
            value = value.astype(BF16).reshape(lines, F, 2, half, width)
            first, second = value[:, :, 0], value[:, :, 1]
            mine[r, aligned(n, lines)] = jnp.where(at.c == 0, first, second)
            give[r % 2, aligned(n, lines)] = jnp.where(at.c == 0, second, first)

        loop(2, one)
        if r >= RING:
            pl.semaphore_wait(free, 1)
        c_copy(r).start()

    def back_device(j):
        return (2 * at.c + j, at.f, at.base + lax.rem(at.s, 2))

    def back_stays(j):
        return (2 * at.c + j == at.s) & (lax.rem(at.s, 2) == at.c)

    def back_comes(m):
        return jnp.logical_not((2 * m + at.c == at.s) & (lax.div(at.s, 2) == at.c))

    def back_refs(which):
        return ((res, out_lat), (dfb, in_lat))[which]

    def back_to(j, which):
        src, dst = back_refs(which)
        m = lax.div(at.s, 2)
        return remote(
            src.at[pl.ds(j * quarter, quarter)], dst.at[m], ts.at[which, j], tr.at[which, m], back_device(j)
        )

    def back_from(m, which):
        src, dst = back_refs(which)
        return remote(
            src.at[pl.ds(0, quarter)], dst.at[m], ts.at[which, m], tr.at[which, m], back_device(m)
        )

    def back_local(j, which):
        src, dst = back_refs(which)
        return pltpu.make_async_copy(
            src.at[pl.ds(j * quarter, quarter)], dst.at[lax.div(at.s, 2)], tl.at[which]
        )

    def back_start(which):
        for j in range(2):
            @pl.when(back_stays(j))
            def _():
                back_local(j, which).start()

            @pl.when(jnp.logical_not(back_stays(j)))
            def _():
                back_to(j, which).start()

    def back_finish(which):
        for j in range(2):
            @pl.when(back_stays(j))
            def _():
                back_local(j, which).wait()

            @pl.when(jnp.logical_not(back_stays(j)))
            def _():
                back_to(j, which).wait_send()

            @pl.when(back_comes(j))
            def _():
                back_from(j, which).wait_recv()

    def load(src, dst, n):
        return pltpu.make_async_copy(src, dst, loads.at[n])

    def load_weight(k, slot):
        return load(bank.at[k], wbuf.at[slot], slot)

    ups, acts = (f0, f1), (a0, a1)

    def load_up(j):
        return load(up.at[j], ups[j % 2], 2 + j % 2)

    def load_act(j):
        return load(act.at[j], acts[j % 2], 4 + j % 2)

    def load_pair(p):
        cols = pl.ds(p * 2 * HD, 2 * HD)
        slot = p % 2
        return [load(heads.at[n, :, cols], qkva.at[slot, n], 10 + 5 * slot + n) for n in range(3)] + [
            load(head_a.at[:, cols], qkva.at[slot, 3], 13 + 5 * slot),
            load(lse.at[:, cols], lsev.at[slot], 14 + 5 * slot),
        ]

    def weights(slot):
        return wbuf[slot].reshape(width, width)

    def add_rows(i, value, cols=slice(None)):
        accs[i, :, cols] += value.reshape(-1, 8, value.shape[-1]).sum(axis=0)

    load_e, load_mlp, load_h2 = load(ctok, ebuf, 6), load(mlp, dh2, 7), load(hid2, h2b, 8)
    for copy in (load_e, load_mlp):
        copy.start()
    load_weight(8, 0).start()
    load_act(0).start()
    load_up(0).start()
    load_h2.start()
    load_weight(4, 1).start()
    load_up(1).start()
    load_act(1).start()
    pl.semaphore_wait(bar, count - 1)
    back_start(0)
    accs[...] = jnp.zeros_like(accs)
    load_e.wait()
    load_mlp.wait()

    def start_rows(i):
        rows = aligned(i, CHUNK)
        grad = ebuf[rows].astype(F32)
        add_rows(5, grad * dh2[rows])
        low = (mod[5:6] * grad).astype(BF16)
        dfb[rows] = low
        add_rows(13, low.astype(F32))

    loop(chunks, start_rows)

    def active_back(j):
        load_weight(8 + j, 0).wait()
        load_up(j).wait()

        value = dot(dfb[...], weights(0), NT) * gelu_slope(ups[j % 2][...])
        low = value.astype(BF16)
        dub[...] = low
        add_rows(9 + j, low.astype(F32))
        load_weight(9 + j if j < 3 else 3, 0).start()
        if j < 2:
            load_up(j + 2).start()
        else:
            (load_mid, load_branch)[j - 2].start()

    def hidden_back(j):
        load_weight(4 + j, 1).wait()

        value = dot(dub[...], weights(1), NT)
        dh2[...] = value if j == 0 else dh2[...] + value
        load_weight(5 + j if j < 3 else 0, 1).start()

    def product_eight(j):
        load_act(j).wait()
        produce(2 * j, acts[j % 2], dfb)
        if j < 2:
            load_act(j + 2).start()
        if j == 2:
            load_att.start()

    def product_four(j):
        if j == 0:
            load_h2.wait()
        produce(2 * j + 1, h2b, dub)
        if j == 3:
            load_hid.start()
            load_modw.start()

    def product_three():
        load_att.wait()
        produce(8, a0, dfb)

    def product_first(n):
        if n == 0:
            load_hid.wait()
        produce(9 + n, h2b, dqt.at[n])

    load_mid, load_branch = load(mid, f0, 2), load(branch, f1, 3)
    load_att, load_hid, load_x = load(att, a0, 4), load(hid, h2b, 8), load(tok, ebuf, 6)

    def middle_back():
        load_mid.wait()
        load_branch.wait()

        def one(i):
            rows = aligned(i, CHUNK)
            scaled, inverse = norm_rows(f0[rows])
            grad = dh2[rows]
            inner = grad * (1.0 + mod[4:5])
            mean_inner = jnp.mean(inner, axis=-1, keepdims=True)
            mean_scaled = jnp.mean(inner * scaled, axis=-1, keepdims=True)
            value = ebuf[rows].astype(F32) + inverse * (inner - mean_inner - scaled * mean_scaled)
            add_rows(4, grad * scaled)
            add_rows(3, grad)
            dh2[rows] = value
            add_rows(2, value * f1[rows])
            low = (mod[2:3] * value).astype(BF16)
            dfb[rows] = low
            add_rows(8, low.astype(F32))

        loop(chunks, one)
        load_x.start()

    def swap_da(here):
        return remote(stage, dah.at[aligned(here, tokens)], xs, xr, at.sibling())

    def attended_back():
        load_weight(3, 0).wait()

        value = dot(dfb[...], weights(0), NT).astype(BF16)
        first, second = value[:, :part], value[:, part:]
        stage[...] = jnp.where(at.c == 0, second, first)
        swap_da(at.c).start()
        dah[aligned(at.c, tokens)] = jnp.where(at.c == 0, first, second)
        load_weight(1, 0).start()
        for copy in load_pair(0) + load_pair(1):
            copy.start()

    def pair_to(p, n, core):
        rows = aligned(1 - at.c, tokens)
        cols = pl.ds(pl.multiple_of(core * part + p * 2 * HD, 2 * HD), 2 * HD)
        return remote(
            dpair.at[p % 2, n, rows], dqt.at[n, :, cols], ps.at[p, n], pr.at[p, n], at.sibling()
        )

    def attend_back_part(p):
        if p == 0:
            swap_da(1 - at.c).wait_recv()
        for copy in load_pair(p):
            copy.wait()
        if p >= 2:
            for n in range(3):
                pair_to(p - 2, n, at.c).wait_send()
        slot = p % 2
        attend_pair_back(
            qkva.at[slot, 0], qkva.at[slot, 1], qkva.at[slot, 2], qkva.at[slot, 3], lsev.at[slot], dah, p,
            dpair.at[slot, 0], dpair.at[slot, 1], dpair.at[slot, 2],
        )
        cols = pl.ds(pl.multiple_of(at.c * part + p * 2 * HD, 2 * HD), 2 * HD)
        for n in range(3):
            pair_to(p, n, at.c).start()
            dqt[n, :, cols] = dpair[slot, n, aligned(at.c, tokens)]
        if p + 2 < part // (2 * HD):
            for copy in load_pair(p + 2):
                copy.start()

    def pairs_arrive():
        for p in range(part // (2 * HD)):
            for n in range(3):
                pair_to(p, n, 1 - at.c).wait_recv()

        def one(i):
            rows = aligned(i, CHUNK)
            add_rows(6, dqt[0, rows].astype(F32))
            add_rows(7, dqt[2, rows].astype(F32))

        loop(chunks, one)

    def first_back(k):
        slot = (1, 0, 1)[k]
        load_weight(k, slot).wait()
        value = dot(dqt[k], weights(slot), NT)
        f0[...] = value if k == 0 else f0[...] + value
        if k == 0:
            load_weight(2, 1).start()

    def input_back():
        load_x.wait()

        def one(i):
            rows = aligned(i, CHUNK)
            scaled, inverse = norm_rows(ebuf[rows].astype(F32))
            grad = f0[rows]
            inner = grad * (1.0 + mod[1:2])
            mean_inner = jnp.mean(inner, axis=-1, keepdims=True)
            mean_scaled = jnp.mean(inner * scaled, axis=-1, keepdims=True)
            value = dh2[rows] + inverse * (inner - mean_inner - scaled * mean_scaled)
            add_rows(1, grad * scaled)
            add_rows(0, grad)
            dfb[rows] = value.astype(BF16)

        loop(chunks, one)

    small_swap = remote(small, sv, vs, vr, at.sibling())
    lines = F * G // 2
    mark = at.f * (G // 2) + pair
    sent = aligned(at.c, part)

    def small_region(s, n):
        return smalls.at[s, lax.div(n, G // 2), lax.rem(n, G // 2), :, sent]

    def small_to(i):
        n = lax.rem(mark + i, lines)
        device = (at.s, lax.div(n, G // 2), 2 * lax.rem(n, G // 2) + at.c)
        return remote(swb.at[:, sent], small_region(at.s, mark), ws.at[i], wr.at[mark], device)

    def small_from(i):
        n = lax.rem(mark + i, lines)
        return remote(swb.at[:, sent], small_region(at.s, n), ws.at[i], wr.at[n], at.sibling())

    small_own = pltpu.make_async_copy(swb.at[:, sent], small_region(at.s, mark), wl)
    plane = (at.sx, at.sy, sd)

    def small_across(n, s, to):
        region = smalls.at[s, :, :, :, sent]
        return remote(region, region, qs.at[n], qr.at[n], (to, at.f, at.g))

    def small_share(core):
        region = smalls.at[:, :, :, :, aligned(core, part)]
        return remote(region, region, us, ur, at.sibling())

    def small_start():
        small[...] = jnp.zeros_like(small)
        small[0:14] = accs[...].sum(axis=1)
        small[14:15] = silu[0:1]
        small_swap.start()

    def small_send():
        small_swap.wait()
        sw[...] = small[...] + sv[...]
        swb[...] = sw[...].astype(BF16)
        small_own.start()
        for i in range(1, lines):
            small_to(i).start()

    def small_plane():
        small_own.wait()
        for i in range(1, lines):
            small_from(i).wait_recv()
        for n, s in enumerate(plane):
            small_across(n, at.s, s).start()

    def small_share_start():
        for n, s in enumerate(plane):
            small_across(n, s, s).wait_recv()
        small_share(at.c).start()

    load_modw = load(modw, dub.at[0 : 6 * half], 9)
    pair_smalls = pltpu.make_async_copy(smalls.at[:, :, pair], smv, dl.at[0])
    spot = at.f * 2 + at.c

    def cond_number(i):
        return lax.rem(spot + i, 2 * F)

    def cond_to(i):
        n = cond_number(i)
        device = (at.s, lax.div(n, 2), at.base + lax.rem(n, 2))
        return remote(cg.at[aligned(lax.div(n, 4), 8)], cgl.at[spot], ds.at[i], dr.at[spot], device)

    def cond_from(i):
        n = cond_number(i)
        return remote(cg.at[0:8], cgl.at[n], ds.at[i], dr.at[n], at.sibling())

    cond_own = pltpu.make_async_copy(cgl, cgs.at[at.s], dl.at[1])

    def cond_across(n, s, to):
        return remote(cgl, cgs.at[s], es.at[n], er.at[n], (to, at.f, at.g))

    def cond_start():
        small_share(1 - at.c).wait_recv()
        pair_smalls.start()
        load_modw.wait()
        dub[6 * half : 8 * half] = jnp.zeros((2 * half, width), BF16)
        pair_smalls.wait()
        value = dot(smv[...].reshape(S * F * 16, width), dub[0 : 8 * half], NT)
        line, column = iota(value.shape, 0), iota(value.shape, 1)
        value = jnp.where(lax.rem(line, 16) == lax.div(column, half), value, 0.0)
        value = value.reshape(S * F, 16, 8 * half).sum(axis=1)
        rows = value[:, 0:128]
        for n in range(1, 8 * half // 128):
            rows = rows + value[:, n * 128 : (n + 1) * 128]
        for s in range(S):
            for f in range(F):
                to = (f * 2 + s % 2) * 2 + s // 2
                cg[to : to + 1] = rows[s * F + f : s * F + f + 1]
        cgl[spot] = cg[aligned(lax.div(spot, 4), 8)]
        loop(2 * F - 1, lambda i: cond_to(i + 1).start())

    def cond_plane():
        loop(2 * F - 1, lambda i: cond_from(i + 1).wait_recv())
        cond_own.start()
        for n, s in enumerate(plane):
            cond_across(n, at.s, s).start()

    active_back(0)
    product_eight(0)
    hidden_back(0)
    product_four(0)
    hop0(0)
    active_back(1)
    hop0(1)
    product_eight(1)
    hidden_back(1)
    product_four(1)
    line(0, 1)
    active_back(2)
    hop0(2)
    hop0(3)
    product_eight(2)
    hidden_back(2)
    line(0, 2)
    product_four(2)
    active_back(3)
    hop0(4)
    hop0(5)
    product_eight(3)
    line(3, 1)
    hidden_back(3)
    hop1(2)
    product_four(3)
    middle_back()
    hop0(6)
    hop0(7)
    attended_back()
    product_three()
    hop1(4)
    line(3, 2)
    attend_back_part(0)
    line(7, 1)
    hop1(1)
    hop2(2)
    attend_back_part(1)
    hop0(8)
    for i in range(3, F):
        line(0, i)
    hop2(1)
    attend_back_part(2)
    hop1(5)
    hop1(6)
    for i in range(3, F):
        line(3, i)
    line(7, 2)
    hop1(8)
    attend_back_part(3)
    pairs_arrive()
    hop2(5)
    product_first(0)
    hop1(0)
    for i in range(3, F):
        line(7, i)
    hop1(3)
    hop2(4)
    hop0(9)
    product_first(1)
    hop3(5)
    hop0(10)
    hop3(1)
    hop2(8)
    product_first(2)
    first_back(0)
    hop1(9)
    first_back(1)
    first_back(2)
    hop2(6)
    hop0(11)
    input_back()
    hop1(10)
    small_start()
    small_send()
    hop3(2)
    hop2(9)
    small_plane()
    hop3(6)
    hop3(4)
    hop2(10)
    hop1(11)
    hop1(7)
    small_share_start()
    back_start(1)
    hop3(3)
    hop3(9)
    cond_start()
    hop3(0)
    hop2(11)
    cond_plane()
    hop3(7)
    hop3(8)
    hop3(10)
    hop3(11)

    swap_da(at.c).wait_send()
    for p in (2, 3):
        for n in range(3):
            pair_to(p, n, at.c).wait_send()
    for r in range(K):
        if r >= K - 2:
            c_copy(r).wait_send()
        if r in finals[-2:]:
            out_done(r)
        for i in range(1, G):
            out_from(r, i).wait_recv()
        b_copy(r, at.sb, 0).wait_send()
        b_copy(r, sd, 1).wait_send()
        a_copy(r).wait_send()
        for i in range(F - 1 if r in LINED else 0):
            line_sends(r, i, lambda copy: copy.wait_send())
        for i in range(1, 0 if r in LINED else F):
            z_to(r, i).wait_send()
    back_finish(0)
    back_finish(1)
    for i in range(1, lines):
        small_to(i).wait_send()
    for n, s in enumerate(plane):
        small_across(n, at.s, s).wait_send()
    small_share(at.c).wait_send()
    loop(2 * F - 1, lambda i: cond_to(i + 1).wait_send())
    for n, s in enumerate(plane):
        cond_across(n, at.s, s).wait_send()
        cond_across(n, s, s).wait_recv()
    cond_own.wait()


def backward(sizes, *arrays):
    S, F, G = sizes
    bank, tok = arrays[0], arrays[3]
    K, _, _, _, half, width = bank.shape
    tokens = tok.shape[0]
    quarter, part, length = tokens // 2, width // 2, 2 * tokens
    count = S * F * G
    low = lambda *shape: pltpu.VMEM(shape, BF16)
    high = lambda *shape: pltpu.VMEM(shape, F32)
    specs = [ANY] * len(arrays)
    specs[2] = specs[-1] = VMEM
    return pl.pallas_call(
        functools.partial(backward_kernel, sizes),
        out_shape=(
            jax.ShapeDtypeStruct((G // 2, K, 2, half, width), F32),
            jax.ShapeDtypeStruct((S, F, G // 2, 16, width), BF16),
            jax.ShapeDtypeStruct((S, 2 * F, 8, 128), F32),
            jax.ShapeDtypeStruct((2, quarter, width), BF16),
            jax.ShapeDtypeStruct((2, quarter, width), BF16),
        ),
        in_specs=specs,
        out_specs=(ANY,) * 5,
        scratch_shapes=[
            low(K, S, F, half, width),
            low(2, S, F, half, width),
            low(RING, S, F, half, width),
            low(K - len(LINED), 2, F, half, width),
            low(K - len(LINED), F, half, width),
            low(K - len(LINED), F - 1, half, width),
            low(len(LINED), F + 1, S, half, width),
            low(len(LINED), 2, half, width),
            low(len(LINED), half, width),
            high(2, half, width),
            low(2, S, F, 2, half, width),
            low(tokens, width),
            low(tokens, width),
            high(tokens, width),
            high(tokens, width),
            low(tokens, width),
            low(tokens, width),
            low(tokens, width),
            high(tokens, width),
            low(tokens, width),
            low(tokens, part),
            low(length, part),
            low(2, 4, length, 2 * HD),
            high(2, length, 2 * HD),
            low(2, 3, length, 2 * HD),
            low(3, tokens, width),
            high(14, 8, width),
            high(16, width),
            high(16, width),
            high(16, width),
            low(16, width),
            low(S, F, 16, width),
            high(S * F, 128),
            high(2 * F, 8, 128),
            DMA((K,)),
            DMA((K,)),
            DMA((K, 2)),
            DMA((K, 2)),
            DMA((K,)),
            DMA((K,)),
            DMA((K, F)),
            DMA((K, F)),
            DMA((len(LINED), 2, F)),
            DMA((len(LINED), 2, F)),
            DMA((K,)),
            DMA((K, G)),
            DMA((K, G)),
            pltpu.SemaphoreType.REGULAR,
            DMA,
            DMA,
            DMA((count // 2,)),
            DMA((count // 2,)),
            DMA,
            DMA((3,)),
            DMA((3,)),
            DMA,
            DMA,
            DMA((2 * F,)),
            DMA((2 * F,)),
            DMA((2,)),
            DMA((3,)),
            DMA((3,)),
            DMA((2, 2)),
            DMA((2, 2)),
            DMA((2,)),
            DMA((20,)),
            DMA,
            DMA,
            DMA((4, 3)),
            DMA((4, 3)),
        ],
        compiler_params=params(3, 63),
        name="backward",
    )(*arrays)


def per_device(
    sizes,
    latents,
    conditioning,
    cotangent,
    owner_list,
    master,
    moment_one,
    moment_two,
    biases,
    bias_moment_one,
    bias_moment_two,
):
    S, F, G = sizes
    rows, width = master.shape[1:]
    half = rows // 2
    s, f, g = lax.axis_index("seq"), lax.axis_index("fsdp"), lax.axis_index("grp")
    core = g % 2

    picked = pick_blocks(master, owner_list)
    cond_rows = conditioning.reshape(2 * width // 128, 128)
    saved = forward(sizes, picked, cond_rows, latents[:, 0], cotangent[:, 0], biases)
    saved = (saved[0], saved[1].reshape(-1, width)) + tuple(saved[2:])
    silu = jax.nn.silu(lax.dynamic_index_in_dim(conditioning, s // 2, 0, keepdims=False))
    silu = jnp.where(core == s % 2, silu.astype(BF16).astype(F32), 0.0)
    silu = jnp.pad(silu, ((0, 7), (0, 0)))
    reduced, smalls, cond_all, out_lat, in_lat = backward(sizes, *saved, silu)

    linear_grads = jnp.sum(reduced, axis=0, keepdims=True) if G > 2 else reduced
    (
        new_master, new_one, new_two, new_copies, new_biases, new_bias_one, new_bias_two, output, input_grad,
    ) = adam_slots(
        sizes, owner_list, master, linear_grads, smalls.reshape(-1, width), moment_one, moment_two,
        biases, bias_moment_one, bias_moment_two, out_lat, in_lat,
    )

    first = (f % 2) * 4 + core * 2
    cond_mine = lax.dynamic_slice_in_dim(cond_all, first, 2, 2).reshape(S * F * 2, 2, 128)
    cond_mine = cond_mine.reshape(S * F * 2, 2, 128 // half, half).sum(axis=2)
    cond_mine = cond_mine.transpose(1, 0, 2).reshape(2, width)
    _, silu_pull = jax.vjp(jax.nn.silu, conditioning)
    cond_grad = silu_pull(cond_mine[:, None])[0]

    return (
        output[:, None],
        input_grad[:, None],
        cond_grad,
        new_master,
        new_one,
        new_two,
        new_copies,
        new_biases,
        new_bias_one,
        new_bias_two,
    )


def solution(mesh):
    sizes = (mesh.shape["seq"], mesh.shape["fsdp"], mesh.shape["grp"])
    tokens = P(None, ("fsdp", "grp"), "seq", None)
    vector = P(None, ("fsdp", "grp"), None)
    slots = P("grp", ("seq", "fsdp"), None)
    in_specs = (tokens, vector, tokens, P(), slots, slots, slots, P(), P(), P())
    out_specs = (tokens, tokens, vector, slots, slots, slots, slots, P(), P(), P())
    return jax.shard_map(
        functools.partial(per_device, sizes),
        mesh=mesh,
        in_specs=in_specs,
        out_specs=out_specs,
        check_vma=False,
    )
```
